32 devices in a mesh: heads: 4 (over z), batch: 8 (over y, x, core).
Axes of the slice: x: 2, y: 2, z: 4, core: 2. Of those that a mesh axis runs over, the one named last changes fastest.
Arguments:
- student_rows: bfloat16 [32, 1024, 384], P(('batch', 'heads')), may hold values from -6 to 6
- teacher_rows: bfloat16 [32, 1024, 768], P(('batch', 'heads')), may hold values from -6 to 6
- valid_length: int32 [32], P('batch'), may hold values from 512 to 1024, as said below
- split_point: int32 [32], P('batch'), may hold values from 2 to 1022, as said below
- project_five: bfloat16 [384, 3, 384], P(None, None, 'heads'), may hold values from -0.3125 to 0.3125
- bias_five: bfloat16 [2, 384], P(None, 'heads'), may hold values from -3 to 3
- output_five: bfloat16 [384, 384], P('heads'), may hold values from -1.25 to 1.25
- branch_bias: float32 [2, 384], replicated, may hold values from -2 to 2
- norm_gain: float32 [2, 384], replicated, may hold values from 0.5 to 1.5
- norm_bias: float32 [2, 384], replicated, may hold values from -2 to 2
- widen_weight: bfloat16 [384, 1536], P(None, 'heads'), may hold values from -0.3125 to 0.3125
- widen_bias: bfloat16 [1536], P('heads'), may hold values from -3 to 3
- narrow_weight: bfloat16 [1536, 384], P('heads'), may hold values from -0.15625 to 0.15625
- project_six: bfloat16 [384, 3, 384], P(None, None, 'heads'), may hold values from -0.3125 to 0.3125
- bias_six: bfloat16 [2, 384], P(None, 'heads'), may hold values from -3 to 3
- teacher_project: bfloat16 [768, 3, 768], P(None, None, 'heads'), may hold values from -0.21875 to 0.21875
- teacher_bias: bfloat16 [2, 768], P(None, 'heads'), may hold values from -3 to 3
Outputs:
- block_out: bfloat16 [32, 1024, 384], P(('batch', 'heads'))
- grad_in: float32 [32, 1024, 384], P(('batch', 'heads'))
- grad_project_five: float32 [384, 3, 384], P(None, None, 'heads')
- grad_bias_five: float32 [2, 384], P(None, 'heads')
- grad_output_five: float32 [384, 384], P('heads')
- grad_branch_bias: float32 [2, 384], replicated
- grad_norm_gain: float32 [2, 384], replicated
- grad_norm_bias: float32 [2, 384], replicated
- grad_widen_weight: float32 [384, 1536], P(None, 'heads')
- grad_widen_bias: float32 [1536], P('heads')
- grad_narrow_weight: float32 [1536, 384], P('heads')
- grad_project_six: float32 [384, 3, 384], P(None, None, 'heads')
- grad_bias_six: float32 [2, 384], P(None, 'heads')
- summary: float32 [4], replicated
The draws below stay inside these ranges and needn't reach their ends.
Inputs may be any that keep to these rules, and one draw needn't show every extreme that they name: `valid_length`: in each group of 4 sequences that share an index of batch, one has length 1024; one sequence of the whole batch has length 512. 2 <= split_point <= valid_length - 2 for each sequence.
All inputs are finite; a program needn't handle non-finite values.
Results may differ from the reference program's by a relative error of at most 0.033.
Values may be sent and summed in bfloat16 or wider, within the bound.
No kernel may reach another device: no remote copies, remote signals or barrier semaphores. Data moves between devices by JAX's collectives and lax.ppermute only.
A program may use at most 192 MiB of HBM per device.

```python
import math
import jax
import jax.numpy as jnp
from jax import lax

D = 384
TEACHER_D = 768
FF = 1536
HEADS = 12
HEAD_DIM = 32
TEACHER_HEAD_DIM = 64
SEQ_LEN = 1024
SEQ_DEV = 1
SEQS = 32
N_HEADS = 4


def shared_lengths(key):
    group = N_HEADS * SEQ_DEV
    count = SEQS // group
    base = jax.random.randint(jax.random.fold_in(key, 101), (count, group), SEQ_LEN // 2, SEQ_LEN + 1)
    picked = jax.random.randint(jax.random.fold_in(key, 102), (count, 1), 0, group)
    short_group = jax.random.randint(jax.random.fold_in(key, 103), (), 0, count)
    slots = jnp.arange(group, dtype=jnp.int32)[None, :]
    groups = jnp.arange(count, dtype=jnp.int32)[:, None]
    full_rows = slots == picked
    short_rows = (slots == (picked + 1) % group) & (groups == short_group)
    lengths = jnp.where(full_rows, SEQ_LEN, jnp.where(short_rows, SEQ_LEN // 2, base))
    return lengths.reshape(SEQS).astype(jnp.int32)


def draw_valid_length(key, part):
    lengths = shared_lengths(key)
    return lengths


def draw_split_point(key, part):
    lengths = shared_lengths(key)
    key = jax.random.fold_in(key, 5)
    return jax.random.randint(key, (SEQS,), 2, lengths - 1).astype(jnp.int32)


def block_levels(key, extent, cuts, smallest, top_value):
    def one(dim, blocks):
        heights = jax.random.uniform(jax.random.fold_in(jax.random.fold_in(key, 6), dim), (blocks,), jnp.float32, smallest / len(cuts), top_value / len(cuts))
        return jnp.repeat(jnp.exp(heights), extent[dim] // blocks).reshape((-1,) + (1,) * (len(extent) - dim - 1))

    level = one(*cuts[0])
    for cut in cuts[1:]:
        level = level * one(*cut)
    return level


def bell_draw(stream_key, shape, scale, bound, cuts=(), kind=jnp.bfloat16):
    drawn = jax.random.normal(stream_key, shape, jnp.float32) * scale
    if len(cuts) > 0:
        drawn = block_levels(stream_key, shape, cuts, -0.22, 0.18) * drawn
    return jnp.clip(drawn, min=-bound, max=bound).astype(kind)


def setup_inputs(seed: int = 0) -> dict:
    splits = jax.random.split(jax.random.key(seed), 18)
    return {
        "student_rows": bell_draw(splits[0], (SEQS, SEQ_LEN, D), 1.0, 6.0, ((0, 32),)),
        "teacher_rows": bell_draw(splits[1], (SEQS, SEQ_LEN, TEACHER_D), 1.0, 6.0, ((0, 32),)),
        "valid_length": draw_valid_length(jax.random.fold_in(splits[17], 71), 0),
        "split_point": draw_split_point(jax.random.fold_in(splits[17], 71), 0),
        "project_five": bell_draw(splits[4], (D, 3, D), D ** -0.5, 0.3125, ((2, 4),)),
        "bias_five": bell_draw(splits[5], (2, D), 0.5, 3.0, ((1, 4),)),
        "output_five": bell_draw(splits[6], (D, D), (D // 16) ** -0.5, 1.25, ((0, 4),)),
        "branch_bias": bell_draw(splits[7], (2, D), 0.3, 2.0, (), jnp.float32),
        "norm_gain": jnp.clip(1.0 + 0.1 * jax.random.normal(splits[8], (2, D), jnp.float32), 0.5, 1.5),
        "norm_bias": bell_draw(splits[9], (2, D), 0.3, 2.0, (), jnp.float32),
        "widen_weight": bell_draw(splits[10], (D, FF), D ** -0.5, 0.3125, ((1, 4),)),
        "widen_bias": bell_draw(splits[11], (FF,), 0.5, 3.0, ((0, 4),)),
        "narrow_weight": bell_draw(splits[12], (FF, D), FF ** -0.5, 0.15625, ((0, 4),)),
        "project_six": bell_draw(splits[13], (D, 3, D), D ** -0.5, 0.3125, ((2, 4),)),
        "bias_six": bell_draw(splits[14], (2, D), 0.5, 3.0, ((1, 4),)),
        "teacher_project": bell_draw(splits[15], (TEACHER_D, 3, TEACHER_D), TEACHER_D ** -0.5, 0.21875, ((2, 4),)),
        "teacher_bias": bell_draw(splits[16], (2, TEACHER_D), 0.5, 3.0, ((1, 4),)),
    }


@jax.custom_vjp
def low(v):
    return lax.optimization_barrier(v.astype(jnp.bfloat16)).astype(jnp.float32)

@jax.custom_vjp
def low_back(v):
    return v

def low_keep(v):
    return (low(v), None)

def low_pass(kept, grad):
    return (grad,)

def back_keep(v):
    return (v, None)

def back_low(kept, grad):
    return (low(grad),)
low.defvjp(low_keep, low_pass)
low_back.defvjp(back_keep, back_low)
NEG_LARGE = -1e+30
NORM_EPS = 1e-12
HIGHEST_PRECISION = lax.Precision.HIGHEST

def as_float(values):
    return values.astype(jnp.float32)

def matmul(left, right):
    return jnp.dot(left, right, precision=HIGHEST_PRECISION, preferred_element_type=jnp.float32)

def layer_norm(rows, gain, shift):
    center = lax.optimization_barrier(jnp.mean(rows, axis=-1, keepdims=True))
    offsets = rows - center
    spread = lax.optimization_barrier(jnp.mean(offsets * offsets, axis=-1, keepdims=True))
    return offsets * lax.rsqrt(spread + NORM_EPS) * gain + shift

def split_heads(rows, size):
    return rows.reshape(rows.shape[0], rows.shape[1] // size, size)

def pair_logits(left, right, size):
    product = jnp.einsum('qhd,khd->hqk', split_heads(left, size), split_heads(right, size), precision=HIGHEST_PRECISION)
    return product * (1.0 / math.sqrt(size))

def mask_keys(logits, key_valid):
    return jnp.where(key_valid[None, None, :], logits, NEG_LARGE)

def log_softmax(logits):
    highest = lax.optimization_barrier(jnp.max(logits, axis=-1, keepdims=True))
    shifted = logits - highest
    return shifted - jnp.log(lax.optimization_barrier(jnp.sum(jnp.exp(shifted), axis=-1, keepdims=True)))

def attend(queries, key_rows, value_rows, key_valid):
    logits = mask_keys(low_back(pair_logits(queries, key_rows, HEAD_DIM)), key_valid)
    highest = lax.optimization_barrier(jnp.max(logits, axis=-1, keepdims=True))
    weights = jnp.exp(logits - highest)
    probability = low(weights / lax.optimization_barrier(jnp.sum(weights, axis=-1, keepdims=True)))
    mixing = jnp.einsum('hqk,khd->qhd', probability, split_heads(value_rows, HEAD_DIM), precision=HIGHEST_PRECISION)
    return mixing.reshape(queries.shape[0], -1)

def relation(left, right, teacher_left, teacher_right, key_valid, row_weight):
    student_log = log_softmax(mask_keys(low_back(pair_logits(left, right, HEAD_DIM)), key_valid))
    teacher_log = log_softmax(mask_keys(pair_logits(teacher_left, teacher_right, TEACHER_HEAD_DIM), key_valid))
    teacher_prob = jnp.exp(teacher_log)
    diverge = lax.optimization_barrier(jnp.sum(jnp.where(key_valid[None, None, :], teacher_prob * (teacher_log - student_log), 0.0), axis=-1))
    return jnp.sum(diverge * row_weight[None, :])

def sequence_terms(params, rows, teacher_rows, length, split, teacher):
    teacher_weight, teacher_shift = teacher
    positions = jnp.arange(SEQ_LEN, dtype=jnp.int32)
    key_valid = positions < length
    loss_rows = key_valid & (positions != 0) & (positions != split - 1) & (positions != length - 1)
    row_weight = jnp.where(loss_rows, 1.0, 0.0).astype(jnp.float32) / ((length - 3).astype(jnp.float32) * (SEQS * HEADS))
    five = matmul(rows, params['project_five'].reshape(D, 3 * D))
    queries = low_back(low(five[:, :D] + params['bias_five'][0]))
    key_rows = low_back(low(five[:, D:2 * D]))
    value_rows = low_back(low(five[:, 2 * D:] + params['bias_five'][1]))
    attended_rows = low_back(low(attend(queries, key_rows, value_rows, key_valid)))
    mixing = low_back(matmul(attended_rows, params['output_five']) + params['branch_bias'][0])
    middle = layer_norm(rows + mixing, params['norm_gain'][0], params['norm_bias'][0])
    pre_act = low_back(matmul(low(middle), params['widen_weight']) + params['widen_bias'])
    activated = low(jax.nn.gelu(pre_act, approximate=False))
    branch_two = low_back(matmul(activated, params['narrow_weight']) + params['branch_bias'][1])
    block = low(layer_norm(middle + branch_two, params['norm_gain'][1], params['norm_bias'][1]))
    six = matmul(block, params['project_six'].reshape(D, 3 * D))
    query_six = low_back(low(six[:, :D] + params['bias_six'][0]))
    key_six = low_back(low(six[:, D:2 * D]))
    value_six = low_back(low(six[:, 2 * D:] + params['bias_six'][1]))
    teacher_all = matmul(teacher_rows, teacher_weight.reshape(TEACHER_D, 3 * TEACHER_D))
    teacher_query = low(teacher_all[:, :TEACHER_D] + teacher_shift[0])
    teacher_key = low(teacher_all[:, TEACHER_D:2 * TEACHER_D])
    teacher_value = low(teacher_all[:, 2 * TEACHER_D:] + teacher_shift[1])
    divergence = relation(query_six, key_six, teacher_query, teacher_key, key_valid, row_weight)
    divergence = divergence + relation(value_six, value_six, teacher_value, teacher_value, key_valid, row_weight)
    valid = key_valid.astype(jnp.float32)[:, None]
    squares = jnp.stack((jnp.sum(valid * rows * rows), jnp.sum(valid * mixing * mixing), jnp.sum(valid * branch_two * branch_two), jnp.sum(valid)))
    return (divergence, squares, block)

def reference(student_rows, teacher_rows, valid_length, split_point, project_five, bias_five, output_five, branch_bias, norm_gain, norm_bias, widen_weight, widen_bias, narrow_weight, project_six, bias_six, teacher_project, teacher_bias):
    params = {'project_five': as_float(project_five), 'bias_five': as_float(bias_five), 'output_five': as_float(output_five), 'branch_bias': as_float(branch_bias), 'norm_gain': as_float(norm_gain), 'norm_bias': as_float(norm_bias), 'widen_weight': as_float(widen_weight), 'widen_bias': as_float(widen_bias), 'narrow_weight': as_float(narrow_weight), 'project_six': as_float(project_six), 'bias_six': as_float(bias_six)}
    teacher = (as_float(teacher_project), as_float(teacher_bias))
    teacher_float = as_float(teacher_rows)

    def total(weights, rows):

        def single(inner, row_part, teacher_part, length, split):
            return sequence_terms(inner, row_part, teacher_part, length, split, teacher)
        piece = jax.checkpoint(single)

        def advance(running, inputs):
            divergence, squares, block = piece(weights, inputs[0], inputs[1], inputs[2], inputs[3])
            return ((running[0] + divergence, running[1] + squares), block)
        initial = (jnp.zeros((), jnp.float32), jnp.zeros((4,), jnp.float32))
        (divergence, squares), blocks = lax.scan(advance, initial, (rows, teacher_float, valid_length, split_point))
        return (divergence, (squares, blocks))
    divergence, pullback, (squares, blocks) = jax.vjp(total, params, as_float(student_rows), has_aux=True)
    gradients, grad_rows = pullback(jnp.ones((), jnp.float32))
    counted = squares[3] * D
    summary = jnp.stack((divergence, jnp.sqrt(squares[0] / counted), jnp.sqrt(squares[1] / counted), jnp.sqrt(squares[2] / counted)))
    return (blocks.astype(jnp.bfloat16), grad_rows, gradients['project_five'], gradients['bias_five'], gradients['output_five'], gradients['branch_bias'], gradients['norm_gain'], gradients['norm_bias'], gradients['widen_weight'], gradients['widen_bias'], gradients['narrow_weight'], gradients['project_six'], gradients['bias_six'], summary)
```

```python
import functools
import math

import jax
import jax.numpy as jnp
from jax import lax
from jax.experimental import pallas as pl
from jax.experimental.pallas import tpu as pltpu
from jax.sharding import PartitionSpec as P

D = 384
HEADS = 12
HEAD_DIM = 32
TEACHER_HEAD_DIM = 64
GROUP = 4
TILE = 256
NORM_EPS = 1e-12
MASKED = -1e30
LOG2E = math.log2(math.e)
LN2 = math.log(2.0)
STUDENT_SCALE = 1.0 / math.sqrt(HEAD_DIM)
TEACHER_SCALE = 1.0 / math.sqrt(TEACHER_HEAD_DIM)
VMEM = 56 * 2**20

f32 = jnp.float32
bf16 = jnp.bfloat16

NN = (((1,), (0,)), ((), ()))
NT = (((1,), (1,)), ((), ()))


def dot(left, right, dims=NN):
    return lax.dot_general(left, right, dims, preferred_element_type=f32)


def lanes(shape):
    return lax.broadcasted_iota(jnp.int32, shape, 1)


def split_rows(rows, head, size, scale):
    lane = lanes(rows.shape)
    inside = (lane >= head * size) & (lane < (head + 1) * size)
    extra = lax.rem(head + 1, 128 // size) * size
    scaled = rows.astype(f32) * scale
    high = scaled.astype(bf16).astype(f32)
    low = scaled - high
    first = jnp.where(inside, high, jnp.where(lane == extra, 1.0, 0.0))
    second = jnp.where(inside, low, 0.0)
    return jnp.concatenate([first.astype(bf16), second.astype(bf16)], axis=1)


def key_columns(rows, head, size, bias):
    lane = lanes(rows.shape)
    extra = lax.rem(head + 1, 128 // size) * size
    wide = rows.astype(f32)
    return jnp.concatenate([jnp.where(lane == extra, bias, wide).astype(bf16), rows], axis=1)


def key_bias(rows, length):
    position = lax.broadcasted_iota(jnp.int32, (rows, 1), 0)
    return jnp.where(position < length, 0.0, MASKED)


def attend_forward_kernel(length_ref, q_ref, k_ref, v_ref, e_ref, r_ref, o_ref, lhs, rhs):
    rows = q_ref.shape[0]
    tile = min(TILE, rows)
    bias = key_bias(rows, length_ref[0])

    def one_head(head, carry):
        lhs[...] = split_rows(q_ref[...], head, HEAD_DIM, STUDENT_SCALE * LOG2E)
        rhs[...] = key_columns(k_ref[...], head, HEAD_DIM, bias)

        def one_tile(step, carry):
            span = pl.ds(pl.multiple_of(step * tile, tile), tile)
            logits = dot(lhs[span, :], rhs[...], NT)
            weights = jnp.exp2(logits - jnp.max(logits, axis=1, keepdims=True))
            inverse = 1.0 / jnp.sum(weights, axis=1, keepdims=True)
            low = weights.astype(bf16)
            e_ref[head, span, :] = low
            mixed = dot(low, v_ref[...]) * inverse
            lane = lanes(mixed.shape)
            inside = (lane >= head * HEAD_DIM) & (lane < (head + 1) * HEAD_DIM)
            o_ref[span, :] = jnp.where(inside, mixed, o_ref[span, :].astype(f32)).astype(bf16)
            r_ref[span, :] = jnp.where(inside, inverse, r_ref[span, :])
            return carry

        return lax.fori_loop(0, rows // tile, one_tile, carry)

    lax.fori_loop(0, GROUP, one_head, 0)


def attend_forward(length, q, k, v):
    rows, width = q.shape
    groups = width // 128
    wide = pl.BlockSpec((rows, 128), lambda g: (0, g))
    return pl.pallas_call(
        attend_forward_kernel,
        grid=(groups,),
        in_specs=[pl.BlockSpec(memory_space=pltpu.SMEM), wide, wide, wide],
        out_specs=[pl.BlockSpec((GROUP, rows, rows), lambda g: (g, 0, 0)), wide, wide],
        out_shape=[
            jax.ShapeDtypeStruct((groups * GROUP, rows, rows), bf16),
            jax.ShapeDtypeStruct((rows, width), f32),
            jax.ShapeDtypeStruct((rows, width), bf16),
        ],
        scratch_shapes=[pltpu.VMEM((rows, 256), bf16), pltpu.VMEM((rows, 256), bf16)],
        compiler_params=pltpu.CompilerParams(vmem_limit_bytes=VMEM),
        name="attend_forward",
    )(length, q, k, v)


def attend_backward_kernel(
    q_ref, k_ref, v_ref, e_ref, r_ref, a_ref, d_ref, dq_ref, dk_ref, dv_ref, lhs, rhs, qt, dt, dkt, dvt
):
    rows = q_ref.shape[0]
    tile = min(TILE, rows)
    scaled = r_ref[...] * d_ref[...].astype(f32)
    qt[...] = q_ref[...].T
    dt[...] = scaled.astype(bf16).T
    dkt[...] = jnp.zeros_like(dkt)
    dvt[...] = jnp.zeros_like(dvt)

    def one_head(head, carry):
        lane = lanes((rows, 128))
        inside = (lane >= head * HEAD_DIM) & (lane < (head + 1) * HEAD_DIM)
        extra = lax.rem(head + 1, GROUP) * HEAD_DIM
        grads = r_ref[...] * d_ref[...].astype(f32)
        shift = -jnp.sum(jnp.where(inside, grads * a_ref[...].astype(f32), 0.0), axis=1, keepdims=True)
        high = grads.astype(bf16).astype(f32)
        shift_high = shift.astype(bf16).astype(f32)
        spare = jnp.where(lane == extra, shift_high, jnp.where(lane == extra + 1, shift - shift_high, 0.0))
        lhs[...] = jnp.concatenate(
            [
                jnp.where(inside, high, spare).astype(bf16),
                jnp.where(inside, grads - high, 0.0).astype(bf16),
            ],
            axis=1,
        )
        ones = (lane == extra) | (lane == extra + 1)
        rhs[...] = jnp.concatenate(
            [jnp.where(ones, 1.0, v_ref[...].astype(f32)).astype(bf16), v_ref[...]], axis=1
        )
        head_rows = pl.ds(pl.multiple_of(head * HEAD_DIM, HEAD_DIM), HEAD_DIM)

        def one_tile(step, carry):
            span = pl.ds(pl.multiple_of(step * tile, tile), tile)
            weights = e_ref[head, span, :]
            change = dot(lhs[span, :], rhs[...], NT)
            grad = (weights.astype(f32) * change).astype(bf16)
            found = dot(grad, k_ref[...]) * STUDENT_SCALE
            here = lanes(found.shape)
            held = (here >= head * HEAD_DIM) & (here < (head + 1) * HEAD_DIM)
            dq_ref[span, :] = jnp.where(held, found, dq_ref[span, :].astype(f32)).astype(bf16)
            dkt[head_rows, :] += dot(qt[head_rows, span], grad)
            dvt[head_rows, :] += dot(dt[head_rows, span], weights)
            return carry

        return lax.fori_loop(0, rows // tile, one_tile, carry)

    lax.fori_loop(0, GROUP, one_head, 0)
    dk_ref[...] = (dkt[...] * STUDENT_SCALE).T.astype(bf16)
    dv_ref[...] = dvt[...].T.astype(bf16)


def attend_backward(q, k, v, e, r, attended, d_attended):
    rows, width = q.shape
    groups = width // 128
    wide = pl.BlockSpec((rows, 128), lambda g: (0, g))
    return pl.pallas_call(
        attend_backward_kernel,
        grid=(groups,),
        in_specs=[wide, wide, wide, pl.BlockSpec((GROUP, rows, rows), lambda g: (g, 0, 0)), wide, wide, wide],
        out_specs=[wide, wide, wide],
        out_shape=[jax.ShapeDtypeStruct((rows, width), bf16)] * 3,
        scratch_shapes=[
            pltpu.VMEM((rows, 256), bf16),
            pltpu.VMEM((rows, 256), bf16),
            pltpu.VMEM((128, rows), bf16),
            pltpu.VMEM((128, rows), bf16),
            pltpu.VMEM((128, rows), f32),
            pltpu.VMEM((128, rows), f32),
        ],
        compiler_params=pltpu.CompilerParams(vmem_limit_bytes=VMEM),
        name="attend_backward",
    )(q, k, v, e, r, attended, d_attended)


def relation_kernel(
    length_ref, q_ref, k_ref, v_ref, tq_ref, tk_ref, tv_ref, w_ref,
    dq_ref, dk_ref, dv_ref, kl_ref, lhs, rhs, tlhs, trhs, lt, right_t, left_sum,
):
    rows = q_ref.shape[0]
    tile = min(TILE, rows)
    bias = key_bias(rows, length_ref[0])

    @pl.when(pl.program_id(0) == 0)
    def _():
        kl_ref[...] = jnp.zeros_like(kl_ref)

    def relate(left_ref, right_ref, tleft_ref, tright_ref):
        lt[...] = left_ref[...].T
        right_t[...] = jnp.zeros_like(right_t)

        def one_head(head, carry):
            lhs[...] = split_rows(left_ref[...], head, HEAD_DIM, STUDENT_SCALE * LOG2E)
            rhs[...] = key_columns(right_ref[...], head, HEAD_DIM, bias)
            part = pl.ds(pl.multiple_of((head // 2) * 128, 128), 128)
            own = lax.rem(head, 2)
            tlhs[...] = split_rows(tleft_ref[:, part], own, TEACHER_HEAD_DIM, TEACHER_SCALE * LOG2E)
            trhs[...] = key_columns(tright_ref[:, part], own, TEACHER_HEAD_DIM, bias)
            head_rows = pl.ds(pl.multiple_of(head * HEAD_DIM, HEAD_DIM), HEAD_DIM)

            def one_tile(step, carry):
                span = pl.ds(pl.multiple_of(step * tile, tile), tile)
                student = dot(lhs[span, :], rhs[...], NT)
                student = student - jnp.max(student, axis=1, keepdims=True)
                teacher = dot(tlhs[span, :], trhs[...], NT)
                teacher = teacher - jnp.max(teacher, axis=1, keepdims=True)
                es = jnp.exp2(student)
                et = jnp.exp2(teacher)
                sum_s = jnp.sum(es, axis=1, keepdims=True)
                sum_t = jnp.sum(et, axis=1, keepdims=True)
                cross = jnp.sum(et * (teacher - student), axis=1, keepdims=True)
                weight = w_ref[span, :]
                kl_ref[span, :] += weight * (LN2 * cross / sum_t + jnp.log(sum_s) - jnp.log(sum_t))
                grad = (es * (weight / sum_s) - et * (weight / sum_t)).astype(bf16)
                found = dot(grad, right_ref[...]) * STUDENT_SCALE
                here = lanes(found.shape)
                held = (here >= head * HEAD_DIM) & (here < (head + 1) * HEAD_DIM)
                left_sum[span, :] = jnp.where(held, found, left_sum[span, :])
                right_t[head_rows, :] += dot(lt[head_rows, span], grad)
                return carry

            return lax.fori_loop(0, rows // tile, one_tile, carry)

        lax.fori_loop(0, GROUP, one_head, 0)

    relate(q_ref, k_ref, tq_ref, tk_ref)
    dq_ref[...] = left_sum[...].astype(bf16)
    dk_ref[...] = (right_t[...] * STUDENT_SCALE).T.astype(bf16)
    relate(v_ref, v_ref, tv_ref, tv_ref)
    dv_ref[...] = (left_sum[...] + (right_t[...] * STUDENT_SCALE).T).astype(bf16)


def relations(length, q, k, v, tq, tk, tv, weight):
    rows, width = q.shape
    groups = width // 128
    wide = pl.BlockSpec((rows, 128), lambda g: (0, g))
    double = pl.BlockSpec((rows, 256), lambda g: (0, g))
    single = pl.BlockSpec((rows, 1), lambda g: (0, 0))
    return pl.pallas_call(
        relation_kernel,
        grid=(groups,),
        in_specs=[pl.BlockSpec(memory_space=pltpu.SMEM), wide, wide, wide, double, double, double, single],
        out_specs=[wide, wide, wide, single],
        out_shape=[jax.ShapeDtypeStruct((rows, width), bf16)] * 3 + [jax.ShapeDtypeStruct((rows, 1), f32)],
        scratch_shapes=[
            pltpu.VMEM((rows, 256), bf16),
            pltpu.VMEM((rows, 256), bf16),
            pltpu.VMEM((rows, 256), bf16),
            pltpu.VMEM((rows, 256), bf16),
            pltpu.VMEM((128, rows), bf16),
            pltpu.VMEM((128, rows), f32),
            pltpu.VMEM((rows, 128), f32),
        ],
        compiler_params=pltpu.CompilerParams(vmem_limit_bytes=VMEM),
        name="relations",
    )(length, q, k, v, tq, tk, tv, weight)


def project(rows, weight, biases):
    width = weight.shape[2]
    flat = dot(rows, weight.reshape(weight.shape[0], 3 * width))
    q = (flat[:, :width] + biases[0].astype(f32)).astype(bf16)
    k = flat[:, width : 2 * width].astype(bf16)
    v = (flat[:, 2 * width :] + biases[1].astype(f32)).astype(bf16)
    return q, k, v


def norm_forward(rows, gain, shift):
    center = jnp.mean(rows, axis=-1, keepdims=True)
    offsets = rows - center
    rstd = lax.rsqrt(jnp.mean(offsets * offsets, axis=-1, keepdims=True) + NORM_EPS)
    normed = offsets * rstd
    return normed * gain + shift, normed, rstd


def norm_backward(grad, normed, rstd, gain):
    inner = grad * gain
    mean = jnp.mean(inner, axis=-1, keepdims=True)
    slope = jnp.mean(inner * normed, axis=-1, keepdims=True)
    down = rstd * (inner - mean - normed * slope)
    return down, jnp.sum(grad * normed, axis=0), jnp.sum(grad, axis=0)


def exact_gelu(values):
    return jax.nn.gelu(values, approximate=False)


def reduce_pieces(pieces):
    shares = pieces[0].shape[0]
    batch = lax.axis_size("batch")
    flat = jnp.concatenate([p.astype(bf16).reshape(shares, -1) for p in pieces], axis=1)
    size = flat.shape[1]
    pad = -size % (batch * 128)
    if pad:
        flat = jnp.pad(flat, ((0, 0), (0, pad)))
    flat = lax.psum_scatter(flat, "batch", scatter_dimension=1, tiled=True)
    flat = lax.psum_scatter(flat, "heads", scatter_dimension=0, tiled=True)
    flat = lax.all_gather(flat, "batch", axis=1, tiled=True)[0].astype(f32)
    out = []
    offset = 0
    for p in pieces:
        count = math.prod(p.shape[1:])
        out.append(flat[offset : offset + count].reshape(p.shape[1:]))
        offset += count
    return out


def body(
    student_rows, teacher_rows, valid_length, split_point, project_five, bias_five, output_five, branch_bias,
    norm_gain, norm_bias, widen_weight, widen_bias, narrow_weight, project_six, bias_six, teacher_project,
    teacher_bias,
):
    shares = lax.axis_size("heads")
    me = lax.axis_index("heads")
    all_seqs = shares * lax.axis_size("batch")
    x = student_rows[0]
    rows = x.shape[0]
    length = lax.dynamic_slice_in_dim(valid_length, me, 1)
    split = lax.dynamic_slice_in_dim(split_point, me, 1)

    def gather(weight, axis):
        return lax.all_gather(weight, "heads", axis=axis, tiled=True)

    w_five, b_five, w_out = gather(project_five, 2), gather(bias_five, 1), gather(output_five, 0)
    w_wide, b_wide, w_narrow = gather(widen_weight, 1), gather(widen_bias, 0), gather(narrow_weight, 0)
    w_six, b_six = gather(project_six, 2), gather(bias_six, 1)
    w_teacher, b_teacher = gather(teacher_project, 2), gather(teacher_bias, 1)

    positions = jnp.arange(rows, dtype=jnp.int32)[:, None]
    valid = positions < length
    counted_rows = valid & (positions != 0) & (positions != split - 1) & (positions != length - 1)
    row_weight = jnp.where(counted_rows, 1.0, 0.0).astype(f32) / (
        (length - 3).astype(f32) * float(all_seqs * HEADS)
    )

    q, k, v = project(x, w_five, b_five)
    weights, inverse, attended = attend_forward(length, q, k, v)
    x_wide = x.astype(f32)
    mixing = dot(attended, w_out) + branch_bias[0]
    middle, normed_one, rstd_one = norm_forward(x_wide + mixing, norm_gain[0], norm_bias[0])
    middle_low = middle.astype(bf16)
    pre_act = dot(middle_low, w_wide) + b_wide.astype(f32)
    activated, gelu_back = jax.vjp(exact_gelu, pre_act)
    activated = activated.astype(bf16)
    branch_two = dot(activated, w_narrow) + branch_bias[1]
    block, normed_two, rstd_two = norm_forward(middle + branch_two, norm_gain[1], norm_bias[1])
    block = block.astype(bf16)

    q6, k6, v6 = project(block, w_six, b_six)
    tq, tk, tv = project(teacher_rows[0], w_teacher, b_teacher)
    dq6, dk6, dv6, divergence = relations(length, q6, k6, v6, tq, tk, tv, row_weight)

    g6 = jnp.concatenate((dq6, dk6, dv6), axis=1)
    grad_six = dot(block.T, g6)
    flat_six = w_six.reshape(w_six.shape[0], -1)
    d_block = dot(g6, flat_six, NT)
    d_sum_two, gain_two, shift_two = norm_backward(d_block, normed_two, rstd_two, norm_gain[1])
    d_branch = d_sum_two.astype(bf16)
    grad_narrow = dot(activated.T, d_branch)
    d_pre = gelu_back(dot(d_branch, w_narrow, NT))[0].astype(bf16)
    grad_wide = dot(middle_low.T, d_pre)
    d_middle = d_sum_two + dot(d_pre, w_wide, NT)
    d_sum_one, gain_one, shift_one = norm_backward(d_middle, normed_one, rstd_one, norm_gain[0])
    d_mixing = d_sum_one.astype(bf16)
    grad_out = dot(attended.T, d_mixing)
    d_attended = dot(d_mixing, w_out, NT).astype(bf16)

    dq5, dk5, dv5 = attend_backward(q, k, v, weights, inverse, attended, d_attended)
    g5 = jnp.concatenate((dq5, dk5, dv5), axis=1)
    grad_five = dot(x.T, g5)
    flat_five = w_five.reshape(w_five.shape[0], -1)
    grad_in = d_sum_one + dot(g5, flat_five, NT)

    def by_share(grad, parts):
        r, width = grad.shape[0], grad.shape[1] // parts
        return jnp.transpose(grad.reshape(r, parts, shares, width // shares), (2, 0, 1, 3))

    (six,) = reduce_pieces([by_share(grad_six, 3)])
    wide, narrow, out = reduce_pieces(
        [
            by_share(grad_wide, 1)[:, :, 0],
            grad_narrow.reshape(shares, -1, D),
            grad_out.reshape(shares, -1, D),
        ]
    )
    (five,) = reduce_pieces([by_share(grad_five, 3)])

    def column_sums(grad):
        return jnp.sum(grad, axis=0, dtype=f32)

    kept = valid.astype(f32)
    partials = jnp.stack(
        (
            jnp.sum(divergence),
            jnp.sum(kept * x_wide * x_wide),
            jnp.sum(kept * mixing * mixing),
            jnp.sum(kept * branch_two * branch_two),
            jnp.sum(kept),
        )
    )
    vectors = (
        partials,
        jnp.stack((column_sums(d_mixing), column_sums(d_branch))),
        jnp.stack((gain_one, gain_two)),
        jnp.stack((shift_one, shift_two)),
        jnp.stack((column_sums(dq5), column_sums(dv5))),
        column_sums(d_pre)[None],
        jnp.stack((column_sums(dq6), column_sums(dv6))),
    )
    flat = lax.psum(jnp.concatenate([p.reshape(-1) for p in vectors]), ("heads", "batch"))
    summed = []
    offset = 0
    for p in vectors:
        summed.append(flat[offset : offset + p.size].reshape(p.shape))
        offset += p.size

    def own(grad):
        width = grad.shape[1] // shares
        return lax.dynamic_slice_in_dim(grad, me * width, width, axis=1)

    totals = summed[0]
    counted = totals[4] * D
    summary = jnp.stack(
        (
            totals[0],
            jnp.sqrt(totals[1] / counted),
            jnp.sqrt(totals[2] / counted),
            jnp.sqrt(totals[3] / counted),
        )
    )
    return (
        block[None], grad_in[None], five, own(summed[4]), out, summed[1], summed[2], summed[3],
        wide, own(summed[5])[0], narrow, six, own(summed[6]), summary,
    )


def solution(mesh):
    return jax.shard_map(
        body,
        mesh=mesh,
        in_specs=(
            P(("batch", "heads"), None, None),
            P(("batch", "heads"), None, None),
            P("batch"),
            P("batch"),
            P(None, None, "heads"),
            P(None, "heads"),
            P("heads", None),
            P(),
            P(),
            P(),
            P(None, "heads"),
            P("heads"),
            P("heads", None),
            P(None, None, "heads"),
            P(None, "heads"),
            P(None, None, "heads"),
            P(None, "heads"),
        ),
        out_specs=(
            P(("batch", "heads"), None, None),
            P(("batch", "heads"), None, None),
            P(None, None, "heads"),
            P(None, "heads"),
            P("heads", None),
            P(),
            P(),
            P(),
            P(None, "heads"),
            P("heads"),
            P("heads", None),
            P(None, None, "heads"),
            P(None, "heads"),
            P(),
        ),
        check_vma=False,
    )
```

```python
import functools
import math

import jax
import jax.numpy as jnp
from jax import lax
from jax.experimental import pallas as pl
from jax.experimental.pallas import tpu as pltpu
from jax.sharding import PartitionSpec as P

D = 384
HEADS = 12
HEAD_DIM = 32
TEACHER_HEAD_DIM = 64
PART = 3
TILE = 256
STRIP = 16
NORM_EPS = 1e-12
MASKED = -1e30
SAFE = 64.0
LN2 = math.log(2.0)
STUDENT_SCALE = 1.0 / math.sqrt(HEAD_DIM)
STUDENT_LOG = math.log2(math.e) / math.sqrt(HEAD_DIM)
TEACHER_LOG = math.log2(math.e) / math.sqrt(TEACHER_HEAD_DIM)
VMEM = 56 * 2**20

f32 = jnp.float32
bf16 = jnp.bfloat16

NN = (((1,), (0,)), ((), ()))
NT = (((1,), (1,)), ((), ()))
TN = (((0,), (0,)), ((), ()))


def dot(left, right, dims=NN):
    return lax.dot_general(left, right, dims, preferred_element_type=f32)


def lanes(shape):
    return lax.broadcasted_iota(jnp.int32, shape, 1)


def wide_rows(rows):
    return jnp.concatenate([rows, jnp.zeros((rows.shape[0], 128 - rows.shape[1]), rows.dtype)], axis=1)


def in_head(lane, head, size=HEAD_DIM):
    return (lane >= head * size) & (lane < (head + 1) * size)


def split_terms(rows, head, size, extra):
    inside = in_head(lanes(rows.shape), head, size)
    high = rows.astype(bf16).astype(f32)
    first = jnp.where(inside, high, extra).astype(bf16)
    second = jnp.where(inside, rows - high, 0.0).astype(bf16)
    return jnp.concatenate([first, second], axis=1)


def key_bias(rows, length):
    position = lax.broadcasted_iota(jnp.int32, (rows, 1), 0)
    return jnp.where(position < length, 0.0, MASKED)


def fold(tile, combine):
    total = tile[:, :128]
    for column in range(128, tile.shape[1], 128):
        total = combine(total, tile[:, column : column + 128])
    return total


def row_sum(tile):
    return jnp.sum(fold(tile, jnp.add), axis=1, keepdims=True)


def weave(first, second):
    done = 0
    for index, step in enumerate(second):
        while done < len(first) and done * len(second) < len(first) * (index + 1):
            first[done]()
            done += 1
        step()
    for step in first[done:]:
        step()


def step_place(step, tile, per_head):
    head = step // per_head
    return head, pl.ds(pl.multiple_of(lax.rem(step, per_head) * tile, tile), tile)


def run_pipeline(steps, logits, vector, back, enter=None):
    def stage(step, slot, before, after):
        if enter is not None:
            enter(step)
        ahead = logits(step + 1, 1 - slot) if after else []
        behind = back(step - 1, 1 - slot) if before else []
        weave(ahead + behind, vector(step, slot))

    for chunk in logits(jnp.int32(0), 0):
        chunk()
    stage(jnp.int32(0), 0, False, True)

    def pair(index, carry):
        stage(2 * index + 1, 1, True, True)
        stage(2 * index + 2, 0, True, True)
        return carry

    lax.fori_loop(0, (steps - 2) // 2, pair, 0)
    stage(jnp.int32(steps - 1), 1, True, False)
    for chunk in back(jnp.int32(steps - 1), 1):
        chunk()


def project_part(x, w_ref, index, bias):
    flat = dot(x, w_ref[index * 96 : (index + 1) * 96, :], NT)
    if bias is not None:
        flat = flat + bias
    return wide_rows(flat).astype(bf16)


def attend_forward_kernel(
    length_ref, x_ref, w_ref, b_ref, q_ref, k_ref, v_ref, e_hbm, r_ref, o_ref, lhs, rhs, mixer, zs, e_all, sems
):
    rows = x_ref.shape[0]
    tile = min(TILE, rows)
    per_head = rows // tile
    steps = PART * per_head
    x = x_ref[...]
    q = project_part(x, w_ref, 0, b_ref[0:1, :96])
    k = project_part(x, w_ref, 1, None)
    v = project_part(x, w_ref, 2, b_ref[1:2, :96])
    q_ref[...] = q
    k_ref[...] = k
    v_ref[...] = v
    lane = lanes((rows, 128))
    one = jnp.where(lane == 96, 1.0, 0.0)
    for head in range(PART):
        lhs[head] = jnp.where(in_head(lane, head), q.astype(f32), one).astype(bf16)
    rhs[...] = jnp.where(lane == 96, key_bias(rows, length_ref[0]), k.astype(f32)).astype(bf16)
    mixer[...] = jnp.where(lane == 96, 1.0, v.astype(f32)).astype(bf16)
    o_ref[...] = jnp.zeros_like(o_ref)
    r_ref[...] = jnp.zeros_like(r_ref)

    def out_copy(step):
        head, span = step_place(step, tile, per_head)
        return pltpu.make_async_copy(e_all.at[head, span], e_hbm.at[head, span], sems.at[step])

    def logits(step, slot):
        head, span = step_place(step, tile, per_head)

        def chunk(start):
            zs[slot, :, start : start + 256] = dot(lhs[head, span, :], rhs[start : start + 256, :], NT)

        return [functools.partial(chunk, start) for start in range(0, rows, 256)]

    def vector(step, slot):
        head, span = step_place(step, tile, per_head)
        base = lax.rem(step, per_head) * tile

        def strip(start):
            z = zs[slot, start : start + STRIP, :]
            highest = jnp.max(fold(z, jnp.maximum), axis=1, keepdims=True)
            here = pl.ds(pl.multiple_of(base + start, STRIP), STRIP)
            e_all[head, here, :] = jnp.exp2((z - highest) * STUDENT_LOG).astype(bf16)

        return [functools.partial(strip, start) for start in range(0, tile, STRIP)]

    def back(step, slot):
        head, span = step_place(step, tile, per_head)

        def mix():
            mixed = dot(e_all[head, span, :], mixer[...])
            inverse = 1.0 / mixed[:, 96:97]
            inside = in_head(lanes(mixed.shape), head)
            o_ref[span, :] = jnp.where(inside, mixed * inverse, o_ref[span, :].astype(f32)).astype(bf16)
            r_ref[span, :] = jnp.where(inside, inverse, r_ref[span, :])

        return [mix]

    def enter(step):
        @pl.when(step > 0)
        def _():
            out_copy(step - 1).start()

    run_pipeline(steps, logits, vector, back, enter)
    out_copy(jnp.int32(steps - 1)).start()

    def finish(step, carry):
        out_copy(step).wait()
        return carry

    lax.fori_loop(0, steps, finish, 0)


def whole(shape):
    return pl.BlockSpec(shape, lambda *_: (0,) * len(shape))


SMEM = pl.BlockSpec(memory_space=pltpu.SMEM)
ANY = pl.BlockSpec(memory_space=pl.ANY)


def cost(micros):
    return pl.CostEstimate(flops=int(micros * 1.1e9), bytes_accessed=1024, transcendentals=0)


def attend_forward(length, x, w, b):
    rows = x.shape[0]
    narrow = jax.ShapeDtypeStruct((rows, 128), bf16)
    steps = PART * (rows // min(TILE, rows))
    return pl.pallas_call(
        attend_forward_kernel,
        grid=(1,),
        in_specs=[SMEM, whole(x.shape), whole(w.shape), whole(b.shape)],
        out_specs=[whole((rows, 128))] * 3 + [ANY] + [whole((rows, 128))] * 2,
        out_shape=[
            narrow, narrow, narrow, jax.ShapeDtypeStruct((PART, rows, rows), bf16),
            jax.ShapeDtypeStruct((rows, 128), f32), narrow,
        ],
        scratch_shapes=[
            pltpu.VMEM((PART, rows, 128), bf16),
            pltpu.VMEM((rows, 128), bf16),
            pltpu.VMEM((rows, 128), bf16),
            pltpu.VMEM((2, min(TILE, rows), rows), f32),
            pltpu.VMEM((PART, rows, rows), bf16),
            pltpu.SemaphoreType.DMA((steps,)),
        ],
        compiler_params=pltpu.CompilerParams(vmem_limit_bytes=VMEM),
        cost_estimate=cost(9),
        name="attend_forward",
    )(length, x, w, b)


def attend_backward_kernel(
    q_ref, k_ref, v_ref, e_hbm, r_ref, a_ref, d_ref, x_ref, w_ref, acc_ref, g_ref, in_ref,
    lhs, rhs, keys, qt, dt, zs, gs, dq, dkt, dvt, e_all, sems,
):
    rows = q_ref.shape[0]
    tile = min(TILE, rows)
    per_head = rows // tile
    steps = PART * per_head

    def in_copy(step):
        head, span = step_place(step, tile, per_head)
        return pltpu.make_async_copy(e_hbm.at[head, span], e_all.at[head, span], sems.at[step])

    def begin(step, carry):
        in_copy(step).start()
        return carry

    lax.fori_loop(0, steps, begin, 0)
    lane = lanes((rows, 128))
    grads = r_ref[...] * d_ref[...].astype(f32)
    shifts = grads * a_ref[...].astype(f32)
    k = k_ref[...].astype(f32)
    for head in range(PART):
        inside = in_head(lane, head)
        shift = -jnp.sum(jnp.where(inside, shifts, 0.0), axis=1, keepdims=True)
        high = shift.astype(bf16).astype(f32)
        lhs[head] = split_terms(
            grads, head, HEAD_DIM, jnp.where(lane == 96, high, jnp.where(lane == 97, shift - high, 0.0))
        )
        keys[head] = jnp.where(inside, k, 0.0).astype(bf16)
    rhs[:, :128] = jnp.where((lane == 96) | (lane == 97), 1.0, v_ref[...].astype(f32)).astype(bf16)
    rhs[:, 128:] = v_ref[...]
    qt[...] = q_ref[...].T
    dt[...] = grads.astype(bf16).T
    dq[...] = jnp.zeros_like(dq)
    dkt[...] = jnp.zeros_like(dkt)
    dvt[...] = jnp.zeros_like(dvt)

    def logits(step, slot):
        head, span = step_place(step, tile, per_head)

        def chunk(start):
            zs[slot, :, start : start + 256] = dot(lhs[head, span, :], rhs[start : start + 256, :], NT)

        return [functools.partial(chunk, start) for start in range(0, rows, 256)]

    def vector(step, slot):
        head, span = step_place(step, tile, per_head)
        base = lax.rem(step, per_head) * tile

        def strip(start):
            here = pl.ds(pl.multiple_of(base + start, STRIP), STRIP)
            weights = e_all[head, here, :].astype(f32)
            gs[slot, start : start + STRIP, :] = (weights * zs[slot, start : start + STRIP, :]).astype(bf16)

        return [functools.partial(strip, start) for start in range(0, tile, STRIP)]

    def back(step, slot):
        head, span = step_place(step, tile, per_head)
        own = pl.ds(pl.multiple_of(head * HEAD_DIM, HEAD_DIM), HEAD_DIM)

        def first():
            dq[span, :] += dot(gs[slot], keys[head])

        def second(start):
            part = slice(start, start + 256)
            dkt[own, part] += dot(qt[own, span], gs[slot, :, part])

        def third(start):
            part = slice(start, start + 256)
            dvt[own, part] += dot(dt[own, span], e_all[head, span, part])

        starts = range(0, rows, 256)
        return [first] + [functools.partial(second, s) for s in starts] + [functools.partial(third, s) for s in starts]

    run_pipeline(steps, logits, vector, back, lambda step: in_copy(step).wait())
    grads = (
        (dq[...] * STUDENT_SCALE).astype(bf16),
        (dkt[...] * STUDENT_SCALE).T.astype(bf16),
        dvt[...].T.astype(bf16),
    )
    weight_grads(grads, x_ref[...], g_ref)
    in_ref[...] = acc_ref[...] + spread(grads, w_ref)


def weight_grads(grads, x, g_ref):
    for index, grad in enumerate(grads):
        g_ref[index * 96 : (index + 1) * 96, :] = dot(grad, x, TN)[:96].astype(bf16)
    ones = jnp.ones((8, x.shape[0]), bf16)
    row = lax.broadcasted_iota(jnp.int32, (8, 128), 0)
    sums = jnp.where(row == 0, dot(ones, grads[0]), jnp.where(row == 1, dot(ones, grads[2]), 0.0))
    sums = jnp.concatenate([sums, jnp.zeros((8, x.shape[1] - 128), f32)], axis=1)
    g_ref[288:304, :] = jnp.concatenate([sums, jnp.zeros_like(sums)], axis=0).astype(bf16)


def spread(grads, w_ref):
    total = None
    for index, grad in enumerate(grads):
        term = dot(grad[:, :96], w_ref[index * 96 : (index + 1) * 96, :])
        total = term if total is None else total + term
    return total


def attend_backward(q, k, v, e, r, attended, d_attended, x, w, grad_in):
    rows = x.shape[0]
    tile = min(TILE, rows)
    row = whole((rows, 128))
    return pl.pallas_call(
        attend_backward_kernel,
        grid=(1,),
        in_specs=[row, row, row, ANY, row, row, row, whole(x.shape), whole(w.shape), whole(x.shape)],
        out_specs=[whole((304, x.shape[1])), whole(x.shape)],
        out_shape=[jax.ShapeDtypeStruct((304, x.shape[1]), bf16), jax.ShapeDtypeStruct(x.shape, f32)],
        scratch_shapes=[
            pltpu.VMEM((PART, rows, 256), bf16),
            pltpu.VMEM((rows, 256), bf16),
            pltpu.VMEM((PART, rows, 128), bf16),
            pltpu.VMEM((128, rows), bf16),
            pltpu.VMEM((128, rows), bf16),
            pltpu.VMEM((2, tile, rows), f32),
            pltpu.VMEM((2, tile, rows), bf16),
            pltpu.VMEM((rows, 128), f32),
            pltpu.VMEM((128, rows), f32),
            pltpu.VMEM((128, rows), f32),
            pltpu.VMEM((PART, rows, rows), bf16),
            pltpu.SemaphoreType.DMA((PART * (rows // tile),)),
        ],
        compiler_params=pltpu.CompilerParams(vmem_limit_bytes=VMEM),
        cost_estimate=cost(10),
        name="attend_backward",
    )(q, k, v, e, r, attended, d_attended, x, w, grad_in)


def relation_kernel(
    numbers, block_ref, teacher_ref, w_ref, b_ref, tw_ref, tb_ref, d_ref, g_ref, kl_ref,
    ls, rs, lt, rt, keys, left_t, zs, zt, gs, left_sum, right_t, es_all, et_all, weight, grads_s, *, all_rows,
):
    rows = block_ref.shape[0]
    tile = min(TILE, rows)
    per_head = rows // tile
    steps = PART * per_head
    length, split = numbers[0], numbers[1]
    block = block_ref[...]
    teacher = teacher_ref[...]
    w_ref, b_ref, tw_ref, tb_ref, g_ref = (r.at[0] for r in (w_ref, b_ref, tw_ref, tb_ref, g_ref))
    lane = lanes((rows, 128))
    position = lax.broadcasted_iota(jnp.int32, (rows, 1), 0)
    bias = key_bias(rows, length)

    @pl.when(pl.program_id(0) == 0)
    def _():
        counted = (position < length) & (position != 0) & (position != split - 1) & (position != length - 1)
        share = 1.0 / ((length - 3).astype(f32) * float(all_rows))
        weight[...] = jnp.where(counted, share, 0.0)
        kl_ref[...] = jnp.zeros_like(kl_ref)
        d_ref[...] = jnp.zeros_like(d_ref)

    def teacher_part(index, b):
        flat = dot(teacher, tw_ref[index * 192 : (index + 1) * 192, :], NT)
        if b is not None:
            flat = flat + b
        flat = flat.astype(bf16)
        return flat[:, :128], wide_rows(flat[:, 128:])

    def largest(rows_low, size, blocks):
        square = rows_low.astype(f32)
        square = (square * square).astype(bf16)
        feature = lax.broadcasted_iota(jnp.int32, (128, 128), 0) // size
        same = feature == lanes((128, 128)) // size
        return jnp.max(dot(square, jnp.where(same, 1.0, 0.0).astype(bf16)), axis=0, keepdims=True)

    def relate(left, right, t_left, t_right, symmetric):
        left_sum[...] = jnp.zeros_like(left_sum)
        right_t[...] = jnp.zeros_like(right_t)
        left_t[...] = left.T
        left_wide = left.astype(f32) * STUDENT_LOG
        right_wide = right.astype(f32)
        one = jnp.where(lane == 96, 1.0, 0.0)
        if symmetric:
            one = jnp.where(lane == 97, bias, one)
        first = jnp.where(lane == 96, bias, right_wide)
        if symmetric:
            first = jnp.where(lane == 97, 1.0, first)
        rs[:, :128] = first.astype(bf16)
        rs[:, 128:] = right
        for head in range(PART):
            ls[head] = split_terms(left_wide, head, HEAD_DIM, one)
            keys[head] = jnp.where(in_head(lane, head), right_wide, 0.0).astype(bf16)
            own = head % 2
            spare = (1 - own) * TEACHER_HEAD_DIM
            one_t = jnp.where(lane == spare, 1.0, 0.0)
            wide_t = t_right[head // 2].astype(f32)
            first_t = jnp.where(lane == spare, bias, wide_t)
            if symmetric:
                one_t = jnp.where(lane == spare + 1, bias, one_t)
                first_t = jnp.where(lane == spare + 1, 1.0, first_t)
            lt[head] = split_terms(t_left[head // 2].astype(f32) * TEACHER_LOG, own, TEACHER_HEAD_DIM, one_t)
            rt[head, :, :128] = first_t.astype(bf16)
            rt[head, :, 128:] = t_right[head // 2]
        student_bound = largest(left, HEAD_DIM, 4) * largest(right, HEAD_DIM, 4) * STUDENT_LOG**2
        bound = jnp.max(student_bound)
        for part in range(2):
            t_bound = largest(t_left[part], TEACHER_HEAD_DIM, 2) * largest(t_right[part], TEACHER_HEAD_DIM, 2)
            bound = jnp.maximum(bound, jnp.max(t_bound * TEACHER_LOG**2))
        near = bound < SAFE * SAFE

        @pl.when(near)
        def _():
            if symmetric:
                symmetric_pass()
            else:
                plain_pass()

        @pl.when(jnp.logical_not(near))
        def _():
            for head in range(PART):
                own = head % 2
                spare = (1 - own) * TEACHER_HEAD_DIM
                ls[head] = split_terms(left.astype(f32), head, HEAD_DIM, jnp.where(lane == 96, 1.0, 0.0))
                lt[head] = split_terms(
                    t_left[head // 2].astype(f32), own, TEACHER_HEAD_DIM, jnp.where(lane == spare, 1.0, 0.0)
                )
            shifted_pass()

    def plain_pass():
        def logits(step, slot):
            head, span = step_place(step, tile, per_head)

            def student(start):
                zs[slot, :, start : start + 256] = dot(ls[head, span, :], rs[start : start + 256, :], NT)

            def taught(start):
                zt[slot, :, start : start + 256] = dot(lt[head, span, :], rt[head, start : start + 256, :], NT)

            chunks = []
            for start in range(0, rows, 256):
                chunks += [functools.partial(student, start), functools.partial(taught, start)]
            return chunks

        def vector(step, slot):
            base = lax.rem(step, per_head) * tile

            def strip(start):
                here = pl.ds(pl.multiple_of(base + start, STRIP), STRIP)
                student = zs[slot, start : start + STRIP, :]
                taught = zt[slot, start : start + STRIP, :]
                es = jnp.exp2(student)
                et = jnp.exp2(taught)
                sum_s = row_sum(es)
                sum_t = row_sum(et)
                cross = row_sum(et * (taught - student))
                w = weight[here, :]
                inverse = 1.0 / sum_t
                kl_ref[here, :] += w * (LN2 * cross * inverse + jnp.log(sum_s) - jnp.log(sum_t))
                gs[slot, start : start + STRIP, :] = (es * (w / sum_s) - et * (w * inverse)).astype(bf16)

            return [functools.partial(strip, start) for start in range(0, tile, STRIP)]

        run_pipeline(steps, logits, vector, grad_products)

    def grad_products(step, slot):
        head, span = step_place(step, tile, per_head)
        own = pl.ds(pl.multiple_of(head * HEAD_DIM, HEAD_DIM), HEAD_DIM)

        def first():
            left_sum[span, :] += dot(gs[slot], keys[head])

        def second(start):
            part = slice(start, start + 256)
            right_t[own, part] += dot(left_t[own, span], gs[slot, :, part])

        return [first] + [functools.partial(second, start) for start in range(0, rows, 256)]

    def shifted_pass():
        def one(step, carry):
            head, span = step_place(step, tile, per_head)
            student = dot(ls[head, span, :], rs[...], NT)
            student = (student - jnp.max(student, axis=1, keepdims=True)) * STUDENT_LOG
            taught = dot(lt[head, span, :], rt[head], NT)
            taught = (taught - jnp.max(taught, axis=1, keepdims=True)) * TEACHER_LOG
            es = jnp.exp2(student)
            et = jnp.exp2(taught)
            sum_s = jnp.sum(es, axis=1, keepdims=True)
            sum_t = jnp.sum(et, axis=1, keepdims=True)
            cross = jnp.sum(et * (taught - student), axis=1, keepdims=True)
            w = weight[span, :]
            row = LN2 * cross / sum_t + jnp.log(sum_s) - jnp.log(sum_t)
            kl_ref[span, :] += jnp.where(w > 0.0, w * row, 0.0)
            gs[0] = (es * (w / sum_s) - et * (w / sum_t)).astype(bf16)
            for chunk in grad_products(step, 0):
                chunk()
            return carry

        lax.fori_loop(0, steps, one, 0)

    def symmetric_pass():
        size = tile
        count = rows // size

        def column(row):
            return jnp.broadcast_to(row, (128, size)).T[:, :1]

        def row_of(value):
            return jnp.broadcast_to(value, (size, 128)).T[:1, :]

        def one_head(head, carry):
            own = pl.ds(pl.multiple_of(head * HEAD_DIM, HEAD_DIM), HEAD_DIM)
            by_row = []
            by_column = [[jnp.zeros((1, size), f32)] * 3 for _ in range(count)]
            for i in range(count):
                here = slice(i * size, (i + 1) * size)
                after = slice(i * size, rows)
                student = dot(ls[head, here, :], rs[after, :], NT)
                taught = dot(lt[head, here, :], rt[head, after, :], NT)
                es = jnp.exp2(student)
                et = jnp.exp2(taught)
                cross = et * (taught - student)
                es_all[here, after] = es
                et_all[here, after] = et
                by_row.append([row_sum(t) for t in (es, et, cross)])
                for j in range(i + 1, count):
                    part = slice((j - i) * size, (j - i + 1) * size)
                    by_column[j] = [
                        c + jnp.sum(t[:, part], axis=0, keepdims=True)
                        for c, t in zip(by_column[j], (es, et, cross))
                    ]
            a, b = [], []
            for i in range(count):
                here = slice(i * size, (i + 1) * size)
                sum_s, sum_t, cross = (r + column(c) for r, c in zip(by_row[i], by_column[i]))
                w = weight[here, :]
                sum_s = jnp.where(w > 0.0, sum_s, 1.0)
                sum_t = jnp.where(w > 0.0, sum_t, 1.0)
                inverse = 1.0 / sum_t
                kl_ref[here, :] += w * (LN2 * cross * inverse + jnp.log(sum_s) - jnp.log(sum_t))
                a.append(w / sum_s)
                b.append(w * inverse)
            a_row = jnp.concatenate([row_of(t) for t in a], axis=1)
            b_row = jnp.concatenate([row_of(t) for t in b], axis=1)
            for i in range(count):
                here = slice(i * size, (i + 1) * size)
                after = slice(i * size, rows)
                both = es_all[here, after] * (a[i] + a_row[:, after])
                both = (both - et_all[here, after] * (b[i] + b_row[:, after])).astype(bf16)
                left_sum[here, :] += dot(both, keys[head, after, :])
                if i + 1 < count:
                    right_t[own, (i + 1) * size :] += dot(left_t[own, here], both[:, size:])
            return carry

        lax.fori_loop(0, PART, one_head, 0)

    q = project_part(block, w_ref, 0, b_ref[0:1, :96])
    k = project_part(block, w_ref, 1, None)
    tq = teacher_part(0, tb_ref[0:1, :192])
    tk = teacher_part(1, None)
    relate(q, k, tq, tk, False)
    grads_s[0] = (left_sum[...] * STUDENT_SCALE).astype(bf16)
    grads_s[1] = (right_t[...] * STUDENT_SCALE).T.astype(bf16)
    v = project_part(block, w_ref, 2, b_ref[1:2, :96])
    tv = teacher_part(2, tb_ref[1:2, :192])
    relate(v, v, tv, tv, True)
    grads_s[2] = ((left_sum[...] + right_t[...].T) * STUDENT_SCALE).astype(bf16)
    grads = tuple(grads_s[i] for i in range(3))
    weight_grads(grads, block, g_ref)
    d_ref[...] += spread(grads, w_ref)


def relations(numbers, block, teacher, w, b, tw, tb, all_rows):
    rows = block.shape[0]
    tile = min(TILE, rows)
    shares = w.shape[0]

    def share(shape):
        return pl.BlockSpec((1,) + shape[1:], lambda s: (s,) + (0,) * (len(shape) - 1))

    return pl.pallas_call(
        functools.partial(relation_kernel, all_rows=all_rows),
        grid=(shares,),
        in_specs=[
            SMEM, whole(block.shape), whole(teacher.shape), share(w.shape), share(b.shape), share(tw.shape),
            share(tb.shape),
        ],
        out_specs=[whole(block.shape), share((shares, 304, D)), whole((rows, 1))],
        out_shape=[
            jax.ShapeDtypeStruct(block.shape, f32),
            jax.ShapeDtypeStruct((shares, 304, D), bf16),
            jax.ShapeDtypeStruct((rows, 1), f32),
        ],
        scratch_shapes=[
            pltpu.VMEM((PART, rows, 256), bf16),
            pltpu.VMEM((rows, 256), bf16),
            pltpu.VMEM((PART, rows, 256), bf16),
            pltpu.VMEM((PART, rows, 256), bf16),
            pltpu.VMEM((PART, rows, 128), bf16),
            pltpu.VMEM((128, rows), bf16),
            pltpu.VMEM((2, tile, rows), f32),
            pltpu.VMEM((2, tile, rows), f32),
            pltpu.VMEM((2, tile, rows), bf16),
            pltpu.VMEM((rows, 128), f32),
            pltpu.VMEM((128, rows), f32),
            pltpu.VMEM((rows, rows), f32),
            pltpu.VMEM((rows, rows), f32),
            pltpu.VMEM((rows, 1), f32),
            pltpu.VMEM((3, rows, 128), bf16),
        ],
        compiler_params=pltpu.CompilerParams(vmem_limit_bytes=VMEM),
        cost_estimate=cost(110),
        name="relations",
    )(numbers, block, teacher, w, b, tw, tb)


def norm_forward(rows, gain, shift):
    center = jnp.mean(rows, axis=1, keepdims=True)
    offsets = rows - center
    rstd = lax.rsqrt(jnp.mean(offsets * offsets, axis=1, keepdims=True) + NORM_EPS)
    normed = offsets * rstd
    return normed * gain + shift, normed, rstd


def norm_backward(grad, normed, rstd, gain):
    inner = grad * gain
    mean = jnp.mean(inner, axis=1, keepdims=True)
    slope = jnp.mean(inner * normed, axis=1, keepdims=True)
    return rstd * (inner - mean - normed * slope)


def gelu_terms(x):
    size = jnp.abs(x) * math.sqrt(0.5)
    t = 1.0 / (1.0 + 0.3275911 * size)
    bell = jnp.exp(-0.5 * x * x)
    poly = t * (0.254829592 + t * (-0.284496736 + t * (1.421413741 + t * (-1.453152027 + t * 1.061405429))))
    tail = 0.5 * poly * bell
    share = jnp.where(x >= 0.0, 1.0 - tail, tail)
    return x * share, share + x * bell * (1.0 / math.sqrt(2.0 * math.pi))


def block_kernel(
    numbers, x_ref, a_ref, out_ref, wide_ref, wide_b_ref, narrow_ref, branch_ref, gain_ref, shift_ref,
    block_ref, n1_ref, r1_ref, n2_ref, r2_ref, act_ref, slope_ref, sums_ref,
):
    shares = a_ref.shape[0]
    tile = x_ref.shape[0]
    x = x_ref[...].astype(f32)
    mixing = branch_ref[0:1, :]
    for s in range(shares):
        mixing = mixing + dot(a_ref[s, :, :96], out_ref[s, :96, :])
    middle, normed, rstd = norm_forward(x + mixing, gain_ref[0:1, :], shift_ref[0:1, :])
    n1_ref[...] = normed
    r1_ref[...] = rstd
    low = middle.astype(bf16)
    branch = branch_ref[1:2, :]
    width = wide_ref.shape[2]
    for s in range(shares):
        value, slope = gelu_terms(dot(low, wide_ref[s]) + wide_b_ref[s, 0:1, :])
        value = value.astype(bf16)
        act_ref[:, s * width : (s + 1) * width] = value
        slope_ref[:, s * width : (s + 1) * width] = slope.astype(bf16)
        branch = branch + dot(value, narrow_ref[s])
    block, normed, rstd = norm_forward(middle + branch, gain_ref[1:2, :], shift_ref[1:2, :])
    n2_ref[...] = normed
    r2_ref[...] = rstd
    block_ref[...] = block.astype(bf16)
    position = lax.broadcasted_iota(jnp.int32, (tile, 1), 0) + pl.program_id(0) * tile
    kept = jnp.where(position < numbers[0], 1.0, 0.0)
    row = lax.broadcasted_iota(jnp.int32, (8, x.shape[1]), 0)
    total = jnp.zeros((8, x.shape[1]), f32)
    for index, part in enumerate((x, mixing, branch)):
        total = jnp.where(row == index, jnp.sum(kept * part * part, axis=0, keepdims=True), total)

    @pl.when(pl.program_id(0) == 0)
    def _():
        sums_ref[...] = jnp.zeros_like(sums_ref)

    sums_ref[...] += total


def by_tile(tile, width):
    return pl.BlockSpec((tile, width), lambda i: (i, 0))


def block_forward(numbers, x, attended, w_out, w_wide, b_wide, w_narrow, branch_bias, gain, shift):
    rows, width = x.shape
    tile = min(TILE, rows)
    shares = attended.shape[0]
    units = shares * w_wide.shape[2]
    row, column = by_tile(tile, width), by_tile(tile, 1)
    return pl.pallas_call(
        block_kernel,
        grid=(rows // tile,),
        in_specs=[
            SMEM, row, pl.BlockSpec((shares, tile, 128), lambda i: (0, i, 0)), whole(w_out.shape),
            whole(w_wide.shape), whole(b_wide.shape), whole(w_narrow.shape), whole(branch_bias.shape),
            whole(gain.shape), whole(shift.shape),
        ],
        out_specs=[row, row, column, row, column, by_tile(tile, units), by_tile(tile, units), whole((8, width))],
        out_shape=[
            jax.ShapeDtypeStruct((rows, width), bf16),
            jax.ShapeDtypeStruct((rows, width), f32),
            jax.ShapeDtypeStruct((rows, 1), f32),
            jax.ShapeDtypeStruct((rows, width), f32),
            jax.ShapeDtypeStruct((rows, 1), f32),
            jax.ShapeDtypeStruct((rows, units), bf16),
            jax.ShapeDtypeStruct((rows, units), bf16),
            jax.ShapeDtypeStruct((8, width), f32),
        ],
        compiler_params=pltpu.CompilerParams(vmem_limit_bytes=VMEM),
        cost_estimate=cost(20),
        name="block_forward",
    )(numbers, x, attended, w_out, w_wide, b_wide, w_narrow, branch_bias, gain, shift)


def block_backward_kernel(
    d_ref, n1_ref, r1_ref, n2_ref, r2_ref, act_ref, slope_ref, a_ref, out_ref, wide_ref, narrow_ref, gain_ref,
    shift_ref, sum_ref, da_ref, g_ref, vec_ref, g_sum, low_s, branch_s, pre_s, mix_s,
):
    step = pl.program_id(0)
    shares = a_ref.shape[0]
    tile, width = d_ref.shape
    units = wide_ref.shape[2]
    span = pl.ds(pl.multiple_of(step * tile, tile), tile)

    @pl.when(step == 0)
    def _():
        vec_ref[...] = jnp.zeros_like(vec_ref)
        g_sum[...] = jnp.zeros_like(g_sum)

    def column(value):
        return jnp.sum(value, axis=0, keepdims=True)

    row = lax.broadcasted_iota(jnp.int32, (8, width), 0)
    d_block = d_ref[...]
    normed_two = n2_ref[...]
    d_two = norm_backward(d_block, normed_two, r2_ref[...], gain_ref[1:2, :])
    d_branch = d_two.astype(bf16)
    branch_s[span, :] = d_branch
    normed_one = n1_ref[...]
    low = (normed_one * gain_ref[0:1, :] + shift_ref[0:1, :]).astype(bf16)
    low_s[span, :] = low
    d_middle = d_two
    for s in range(shares):
        grad = dot(d_branch, narrow_ref[s], NT) * slope_ref[:, s * units : (s + 1) * units].astype(f32)
        grad = grad.astype(bf16)
        pre_s[span, s * units : (s + 1) * units] = grad
        g_sum[s : s + 1, :] += column(grad.astype(f32))
        d_middle = d_middle + dot(grad, wide_ref[s], NT)
    d_one = norm_backward(d_middle, normed_one, r1_ref[...], gain_ref[0:1, :])
    sum_ref[...] = d_one
    d_mixing = d_one.astype(bf16)
    mix_s[span, :] = d_mixing
    for s in range(shares):
        da_ref[s] = wide_rows(dot(d_mixing, out_ref[s, :96, :], NT)).astype(bf16)
    parts = (
        d_mixing.astype(f32), d_branch.astype(f32), d_middle * normed_one, d_block * normed_two, d_middle, d_block,
    )
    total = jnp.zeros((8, width), f32)
    for index, part in enumerate(parts):
        total = jnp.where(row == index, column(part), total)
    vec_ref[...] += total

    @pl.when(step == pl.num_programs(0) - 1)
    def _():
        for s in range(shares):
            part = slice(s * units, (s + 1) * units)
            g_ref[s, 0:units, :] = dot(act_ref[:, part], branch_s[...], TN).astype(bf16)
            g_ref[s, units : 2 * units, :] = dot(low_s[...], pre_s[:, part], TN).astype(bf16)
            g_ref[s, 2 * units : 2 * units + 96, :] = dot(a_ref[s], mix_s[...], TN)[:96].astype(bf16)
            first = lax.broadcasted_iota(jnp.int32, (32, units), 0) == 0
            g_ref[s, 2 * units + 96 : 2 * units + 128, :] = jnp.where(first, g_sum[s : s + 1, :], 0.0).astype(bf16)


def block_backward(d_block, n1, r1, n2, r2, act, slope, attended, w_out, w_wide, w_narrow, gain, shift):
    rows, width = d_block.shape
    tile = min(TILE, rows)
    shares, units = attended.shape[0], w_wide.shape[2]
    row, column = by_tile(tile, width), by_tile(tile, 1)
    return pl.pallas_call(
        block_backward_kernel,
        grid=(rows // tile,),
        in_specs=[
            row, row, column, row, column, whole(act.shape), by_tile(tile, shares * units), whole(attended.shape),
            whole(w_out.shape), whole(w_wide.shape), whole(w_narrow.shape), whole(gain.shape), whole(shift.shape),
        ],
        out_specs=[
            row,
            pl.BlockSpec((shares, tile, 128), lambda i: (0, i, 0)),
            whole((shares, 2 * units + 128, width)),
            whole((8, width)),
        ],
        out_shape=[
            jax.ShapeDtypeStruct((rows, width), f32),
            jax.ShapeDtypeStruct((shares, rows, 128), bf16),
            jax.ShapeDtypeStruct((shares, 2 * units + 128, width), bf16),
            jax.ShapeDtypeStruct((8, width), f32),
        ],
        scratch_shapes=[
            pltpu.VMEM((8, units), f32),
            pltpu.VMEM((rows, width), bf16),
            pltpu.VMEM((rows, width), bf16),
            pltpu.VMEM((rows, shares * units), bf16),
            pltpu.VMEM((rows, width), bf16),
        ],
        compiler_params=pltpu.CompilerParams(vmem_limit_bytes=VMEM),
        cost_estimate=cost(25),
        name="block_backward",
    )(d_block, n1, r1, n2, r2, act, slope, attended, w_out, w_wide, w_narrow, gain, shift)


def shift_shares(value, by):
    shares = lax.axis_size("heads")
    return lax.ppermute(value, "heads", [((i + by) % shares, i) for i in range(shares)])


def exchange(value, bit):
    size = lax.axis_size("batch")
    return lax.ppermute(value, "batch", [(i, i ^ bit) for i in range(size)])


def batch_sum(value):
    bit = 1
    while bit < lax.axis_size("batch"):
        low = value.astype(bf16) if value.dtype != f32 else value
        value = low.astype(f32) + exchange(low, bit).astype(f32)
        bit *= 2
        if low.dtype == bf16 and bit < lax.axis_size("batch"):
            value = value.astype(bf16)
    return value


def body(
    student_rows, teacher_rows, valid_length, split_point, project_five, bias_five, output_five, branch_bias,
    norm_gain, norm_bias, widen_weight, widen_bias, narrow_weight, project_six, bias_six, teacher_project,
    teacher_bias,
):
    shares = lax.axis_size("heads")
    batch = lax.axis_size("batch")
    me = lax.axis_index("heads")
    place = lax.axis_index("batch")
    all_rows = shares * batch * HEADS
    x = student_rows[0]
    teacher = teacher_rows[0]
    length = lax.dynamic_slice_in_dim(valid_length, me, 1)
    numbers = jnp.concatenate([length, lax.dynamic_slice_in_dim(split_point, me, 1)])

    def turned(weight):
        return jnp.transpose(weight, (1, 2, 0)).reshape(-1, weight.shape[0])

    def pad(rows, width):
        return jnp.pad(rows, ((0, 0), (0, width - rows.shape[1])))

    small = jnp.concatenate(
        [pad(bias_five, D), pad(bias_six, D), widen_bias[None], pad(teacher_bias, D), jnp.zeros((1, D), bf16)], axis=0
    )
    five = turned(project_five)
    fives = [five] + [shift_shares(five, by) for by in range(1, shares)]
    smalls = [small] + [shift_shares(small, by) for by in range(1, shares)]
    smalls = [s.astype(f32) for s in smalls]

    def eighth(rows):
        count = -(-rows.shape[0] // batch)
        rows = jnp.pad(rows, ((0, count * batch - rows.shape[0]), (0, 0)))
        return lax.dynamic_slice_in_dim(rows, place * count, count)

    def gather(rows):
        part = eighth(rows)
        parts = [shift_shares(part, by) for by in range(1, shares)]
        return [rows] + [lax.all_gather(p, "batch", axis=0, tiled=True)[: rows.shape[0]] for p in parts]

    units = widen_weight.shape[1]
    mid = jnp.concatenate([widen_weight, narrow_weight, jnp.pad(output_five, ((0, 32), (0, 0)))], axis=0)
    mids = gather(mid)
    sixes = gather(turned(project_six))
    taughts = gather(turned(teacher_project))

    heads = []
    for s in range(shares):
        heads.append(attend_forward(length, x, fives[s], smalls[s][0:2]))
    attended = jnp.stack([h[5] for h in heads])
    mids = jnp.stack(mids)
    smalls = jnp.stack(smalls)
    w_wide, w_narrow, w_out = mids[:, :D], mids[:, D : D + units], mids[:, D + units :]
    block, n1, r1, n2, r2, act, slope, squares = block_forward(
        numbers, x, attended, w_out, w_wide, smalls[:, 4:5], w_narrow, branch_bias, norm_gain, norm_bias
    )
    d_block, g_six, divergence = relations(
        numbers, block, teacher, jnp.stack(sixes), smalls[:, 2:4], jnp.stack(taughts), smalls[:, 5:7], all_rows
    )
    d_sum_one, d_attended, g_mid, vectors = block_backward(
        d_block, n1, r1, n2, r2, act, slope, attended, w_out, w_wide, w_narrow, norm_gain, norm_bias
    )

    def to_owner(parts):
        total = parts[0].astype(f32)
        for by in range(1, shares):
            total = total + shift_shares(parts[by], shares - by).astype(f32)
        return total.astype(bf16)

    six = batch_sum(to_owner([g_six[s] for s in range(shares)]))

    counts = g_mid.shape[1] // batch
    mid_part = lax.psum_scatter(g_mid, "batch", scatter_dimension=1, tiled=True)
    mid_part = to_owner([mid_part[s] for s in range(shares)])
    mid_sum = lax.all_gather(mid_part, "batch", axis=0, tiled=True).astype(f32)

    kept = jnp.sum(jnp.where(jnp.arange(x.shape[0]) < length, 1.0, 0.0))
    scalars = jnp.stack([jnp.sum(divergence), jnp.sum(squares[0]), jnp.sum(squares[1]), jnp.sum(squares[2]), kept])
    vectors = lax.dynamic_update_slice(vectors, pad(scalars[None], D), (6, 0))
    bit = 1
    while bit < shares:
        vectors = vectors + lax.ppermute(vectors, "heads", [(i, i ^ bit) for i in range(shares)])
        bit *= 2
    vectors = batch_sum(vectors)

    grad_in = d_sum_one
    g_five = [None] * shares
    for s in list(range(1, shares)) + [0]:
        q, k, v, e, r, a = heads[s]
        g_five[s], grad_in = attend_backward(q, k, v, e, r, a, d_attended[s], x, fives[s], grad_in)
    five_sum = batch_sum(to_owner(g_five))

    def unturned(grad):
        return jnp.transpose(grad[: 3 * 96].reshape(3, 96, -1), (2, 0, 1))

    totals = vectors[6]
    counted = totals[4] * D
    summary = jnp.concatenate([totals[:1], jnp.sqrt(totals[1:4] / counted)])
    return (
        block[None], grad_in[None], unturned(five_sum), five_sum[288:290, :96],
        mid_sum[2 * units : 2 * units + 96], vectors[0:2], vectors[2:4], vectors[4:6],
        mid_sum[units : 2 * units], mid_sum[2 * units + 96], mid_sum[:units],
        unturned(six), six[288:290, :96], summary,
    )


def solution(mesh):
    return jax.shard_map(
        body,
        mesh=mesh,
        in_specs=(
            P(("batch", "heads"), None, None),
            P(("batch", "heads"), None, None),
            P("batch"),
            P("batch"),
            P(None, None, "heads"),
            P(None, "heads"),
            P("heads", None),
            P(),
            P(),
            P(),
            P(None, "heads"),
            P("heads"),
            P("heads", None),
            P(None, None, "heads"),
            P(None, "heads"),
            P(None, None, "heads"),
            P(None, "heads"),
        ),
        out_specs=(
            P(("batch", "heads"), None, None),
            P(("batch", "heads"), None, None),
            P(None, None, "heads"),
            P(None, "heads"),
            P("heads", None),
            P(),
            P(),
            P(),
            P(None, "heads"),
            P("heads"),
            P("heads", None),
            P(None, None, "heads"),
            P(None, "heads"),
            P(),
        ),
        check_vma=False,
    )
```

```python
import functools
import math

import jax
import jax.numpy as jnp
from jax import lax
from jax.experimental import pallas as pl
from jax.experimental.pallas import tpu as pltpu
from jax.sharding import PartitionSpec as P

D = 384
HEADS = 12
HEAD_DIM = 32
TEACHER_HEAD_DIM = 64
PART = 3
TILE = 256
STRIP = 16
NORM_EPS = 1e-12
MASKED = -1e30
SAFE = 64.0
LN2 = math.log(2.0)
STUDENT_SCALE = 1.0 / math.sqrt(HEAD_DIM)
STUDENT_LOG = math.log2(math.e) / math.sqrt(HEAD_DIM)
TEACHER_LOG = math.log2(math.e) / math.sqrt(TEACHER_HEAD_DIM)
VMEM = 56 * 2**20

f32 = jnp.float32
bf16 = jnp.bfloat16

NN = (((1,), (0,)), ((), ()))
NT = (((1,), (1,)), ((), ()))
TN = (((0,), (0,)), ((), ()))


def dot(left, right, dims=NN):
    return lax.dot_general(left, right, dims, preferred_element_type=f32)


def lanes(shape):
    return lax.broadcasted_iota(jnp.int32, shape, 1)


def wide_rows(rows):
    return jnp.concatenate([rows, jnp.zeros((rows.shape[0], 128 - rows.shape[1]), rows.dtype)], axis=1)


def in_head(lane, head, size=HEAD_DIM):
    return (lane >= head * size) & (lane < (head + 1) * size)


def split_terms(rows, head, size, extra):
    inside = in_head(lanes(rows.shape), head, size)
    high = rows.astype(bf16).astype(f32)
    first = jnp.where(inside, high, extra).astype(bf16)
    second = jnp.where(inside, rows - high, 0.0).astype(bf16)
    return jnp.concatenate([first, second], axis=1)


def own_number(ref):
    return ref[lax.axis_index("heads")]


def key_bias(rows, length):
    position = lax.broadcasted_iota(jnp.int32, (rows, 1), 0)
    return jnp.where(position < length, 0.0, MASKED)


def fold(tile, combine):
    total = tile[:, :128]
    for column in range(128, tile.shape[1], 128):
        total = combine(total, tile[:, column : column + 128])
    return total


def row_sum(tile):
    return jnp.sum(fold(tile, jnp.add), axis=1, keepdims=True)


def weave(first, second):
    done = 0
    for index, step in enumerate(second):
        while done < len(first) and done * len(second) < len(first) * (index + 1):
            first[done]()
            done += 1
        step()
    for step in first[done:]:
        step()


def step_place(step, tile, per_head):
    head = step // per_head
    return head, pl.ds(pl.multiple_of(lax.rem(step, per_head) * tile, tile), tile)


def run_pipeline(steps, logits, vector, back, enter=None):
    def stage(step, slot, before, after):
        if enter is not None:
            enter(step)
        ahead = logits(step + 1, 1 - slot) if after else []
        behind = back(step - 1, 1 - slot) if before else []
        weave(ahead + behind, vector(step, slot))

    for chunk in logits(jnp.int32(0), 0):
        chunk()
    stage(jnp.int32(0), 0, False, True)

    def pair(index, carry):
        stage(2 * index + 1, 1, True, True)
        stage(2 * index + 2, 0, True, True)
        return carry

    lax.fori_loop(0, (steps - 2) // 2, pair, 0)
    stage(jnp.int32(steps - 1), 1, True, False)
    for chunk in back(jnp.int32(steps - 1), 1):
        chunk()


def project_part(x, w_ref, index, bias):
    flat = dot(x, w_ref[index * 96 : (index + 1) * 96, :], NT)
    if bias is not None:
        flat = flat + bias
    return wide_rows(flat).astype(bf16)


def attend_forward_kernel(
    length_ref, x_ref, w_ref, b_ref, q_ref, k_ref, v_ref, e_hbm, r_ref, o_ref, lhs, rhs, mixer, zs, e_all, sems
):
    rows = x_ref.shape[0]
    tile = min(TILE, rows)
    per_head = rows // tile
    steps = PART * per_head
    x = x_ref[...]
    q = project_part(x, w_ref, 0, b_ref[0:1, :96])
    k = project_part(x, w_ref, 1, None)
    v = project_part(x, w_ref, 2, b_ref[1:2, :96])
    q_ref[...] = q
    k_ref[...] = k
    v_ref[...] = v
    lane = lanes((rows, 128))
    one = jnp.where(lane == 96, 1.0, 0.0)
    for head in range(PART):
        lhs[head] = jnp.where(in_head(lane, head), q.astype(f32), one).astype(bf16)
    rhs[...] = jnp.where(lane == 96, key_bias(rows, own_number(length_ref)), k.astype(f32)).astype(bf16)
    mixer[...] = jnp.where(lane == 96, 1.0, v.astype(f32)).astype(bf16)
    o_ref[...] = jnp.zeros_like(o_ref)
    r_ref[...] = jnp.zeros_like(r_ref)

    def out_copy(step):
        head, span = step_place(step, tile, per_head)
        return pltpu.make_async_copy(e_all.at[head, span], e_hbm.at[head, span], sems.at[step])

    def logits(step, slot):
        head, span = step_place(step, tile, per_head)

        def chunk(start):
            zs[slot, :, start : start + 256] = dot(lhs[head, span, :], rhs[start : start + 256, :], NT)

        return [functools.partial(chunk, start) for start in range(0, rows, 256)]

    def vector(step, slot):
        head, span = step_place(step, tile, per_head)
        base = lax.rem(step, per_head) * tile

        def strip(start):
            z = zs[slot, start : start + STRIP, :]
            highest = jnp.max(fold(z, jnp.maximum), axis=1, keepdims=True)
            here = pl.ds(pl.multiple_of(base + start, STRIP), STRIP)
            e_all[head, here, :] = jnp.exp2((z - highest) * STUDENT_LOG).astype(bf16)

        return [functools.partial(strip, start) for start in range(0, tile, STRIP)]

    def back(step, slot):
        head, span = step_place(step, tile, per_head)

        def mix():
            mixed = dot(e_all[head, span, :], mixer[...])
            inverse = 1.0 / mixed[:, 96:97]
            inside = in_head(lanes(mixed.shape), head)
            o_ref[span, :] = jnp.where(inside, mixed * inverse, o_ref[span, :].astype(f32)).astype(bf16)
            r_ref[span, :] = jnp.where(inside, inverse, r_ref[span, :])

        return [mix]

    def enter(step):
        @pl.when(step > 0)
        def _():
            out_copy(step - 1).start()

    run_pipeline(steps, logits, vector, back, enter)
    out_copy(jnp.int32(steps - 1)).start()

    def finish(step, carry):
        out_copy(step).wait()
        return carry

    lax.fori_loop(0, steps, finish, 0)


def whole(shape):
    return pl.BlockSpec(shape, lambda *_: (0,) * len(shape))


SMEM = pl.BlockSpec(memory_space=pltpu.SMEM)
ANY = pl.BlockSpec(memory_space=pl.ANY)


def cost(micros):
    return pl.CostEstimate(flops=int(micros * 1.1e9), bytes_accessed=1024, transcendentals=0)


def attend_forward(length, x, w, b):
    rows = x.shape[0]
    narrow = jax.ShapeDtypeStruct((rows, 128), bf16)
    steps = PART * (rows // min(TILE, rows))
    return pl.pallas_call(
        attend_forward_kernel,
        grid=(1,),
        in_specs=[SMEM, whole(x.shape), whole(w.shape), whole(b.shape)],
        out_specs=[whole((rows, 128))] * 3 + [ANY] + [whole((rows, 128))] * 2,
        out_shape=[
            narrow, narrow, narrow, jax.ShapeDtypeStruct((PART, rows, rows), bf16),
            jax.ShapeDtypeStruct((rows, 128), f32), narrow,
        ],
        scratch_shapes=[
            pltpu.VMEM((PART, rows, 128), bf16),
            pltpu.VMEM((rows, 128), bf16),
            pltpu.VMEM((rows, 128), bf16),
            pltpu.VMEM((2, min(TILE, rows), rows), f32),
            pltpu.VMEM((PART, rows, rows), bf16),
            pltpu.SemaphoreType.DMA((steps,)),
        ],
        compiler_params=pltpu.CompilerParams(vmem_limit_bytes=VMEM),
        cost_estimate=cost(9),
        name="attend_forward",
    )(length, x, w, b)


def attend_backward_kernel(
    q_ref, k_ref, v_ref, e_hbm, r_ref, a_ref, d_ref, x_ref, w_ref, acc_ref, tail_ref, g_ref, in_ref,
    lhs, rhs, keys, qt, dt, zs, gs, dq, dkt, dvt, e_all, sems,
):
    rows = q_ref.shape[0]
    tile = min(TILE, rows)
    per_head = rows // tile
    steps = PART * per_head

    def in_copy(step):
        head, span = step_place(step, tile, per_head)
        return pltpu.make_async_copy(e_hbm.at[head, span], e_all.at[head, span], sems.at[step])

    def begin(step, carry):
        in_copy(step).start()
        return carry

    lax.fori_loop(0, steps, begin, 0)
    lane = lanes((rows, 128))
    grads = r_ref[...] * d_ref[...].astype(f32)
    shifts = grads * a_ref[...].astype(f32)
    k = k_ref[...].astype(f32)
    for head in range(PART):
        inside = in_head(lane, head)
        shift = -jnp.sum(jnp.where(inside, shifts, 0.0), axis=1, keepdims=True)
        high = shift.astype(bf16).astype(f32)
        lhs[head] = split_terms(
            grads, head, HEAD_DIM, jnp.where(lane == 96, high, jnp.where(lane == 97, shift - high, 0.0))
        )
        keys[head] = jnp.where(inside, k, 0.0).astype(bf16)
    rhs[:, :128] = jnp.where((lane == 96) | (lane == 97), 1.0, v_ref[...].astype(f32)).astype(bf16)
    rhs[:, 128:] = v_ref[...]
    qt[...] = q_ref[...].T
    dt[...] = grads.astype(bf16).T
    dq[...] = jnp.zeros_like(dq)
    dkt[...] = jnp.zeros_like(dkt)
    dvt[...] = jnp.zeros_like(dvt)

    def logits(step, slot):
        head, span = step_place(step, tile, per_head)

        def chunk(start):
            zs[slot, :, start : start + 256] = dot(lhs[head, span, :], rhs[start : start + 256, :], NT)

        return [functools.partial(chunk, start) for start in range(0, rows, 256)]

    def vector(step, slot):
        head, span = step_place(step, tile, per_head)
        base = lax.rem(step, per_head) * tile

        def strip(start):
            here = pl.ds(pl.multiple_of(base + start, STRIP), STRIP)
            weights = e_all[head, here, :].astype(f32)
            gs[slot, start : start + STRIP, :] = (weights * zs[slot, start : start + STRIP, :]).astype(bf16)

        return [functools.partial(strip, start) for start in range(0, tile, STRIP)]

    def back(step, slot):
        head, span = step_place(step, tile, per_head)
        own = pl.ds(pl.multiple_of(head * HEAD_DIM, HEAD_DIM), HEAD_DIM)

        def first():
            dq[span, :] += dot(gs[slot], keys[head])

        def second(start):
            part = slice(start, start + 256)
            dkt[own, part] += dot(qt[own, span], gs[slot, :, part])

        def third(start):
            part = slice(start, start + 256)
            dvt[own, part] += dot(dt[own, span], e_all[head, span, part])

        starts = range(0, rows, 256)
        return [first] + [functools.partial(second, s) for s in starts] + [functools.partial(third, s) for s in starts]

    run_pipeline(steps, logits, vector, back, lambda step: in_copy(step).wait())
    grads = (
        (dq[...] * STUDENT_SCALE).astype(bf16),
        (dkt[...] * STUDENT_SCALE).T.astype(bf16),
        dvt[...].T.astype(bf16),
    )
    weight_grads(grads, x_ref[...], g_ref, tail_ref[:16, :].astype(f32), tail_ref[16:, :].astype(f32))
    in_ref[...] = acc_ref[...] + spread(grads, w_ref)


def weight_grads(grads, x, g_ref, tail_high=0.0, tail_low=0.0):
    for index, grad in enumerate(grads):
        g_ref[index * 96 : (index + 1) * 96, :] = dot(grad, x, TN)[:96].astype(bf16)
    ones = jnp.ones((16, x.shape[0]), bf16)
    row = lax.broadcasted_iota(jnp.int32, (16, 128), 0)
    sums = jnp.where(row == 0, dot(ones, grads[0]), jnp.where(row == 1, dot(ones, grads[2]), 0.0))
    sums = jnp.concatenate([sums, jnp.zeros((16, x.shape[1] - 128), f32)], axis=1) + tail_high
    high = sums.astype(bf16).astype(f32)
    g_ref[288:304, :] = high.astype(bf16)
    g_ref[304:320, :] = (sums - high + tail_low).astype(bf16)


def spread(grads, w_ref):
    total = None
    for index, grad in enumerate(grads):
        term = dot(grad[:, :96], w_ref[index * 96 : (index + 1) * 96, :])
        total = term if total is None else total + term
    return total


def attend_backward(q, k, v, e, r, attended, d_attended, x, w, grad_in, tail):
    rows = x.shape[0]
    tile = min(TILE, rows)
    row = whole((rows, 128))
    return pl.pallas_call(
        attend_backward_kernel,
        grid=(1,),
        in_specs=[row, row, row, ANY, row, row, row, whole(x.shape), whole(w.shape), whole(x.shape), whole(tail.shape)],
        out_specs=[whole((320, x.shape[1])), whole(x.shape)],
        out_shape=[jax.ShapeDtypeStruct((320, x.shape[1]), bf16), jax.ShapeDtypeStruct(x.shape, f32)],
        scratch_shapes=[
            pltpu.VMEM((PART, rows, 256), bf16),
            pltpu.VMEM((rows, 256), bf16),
            pltpu.VMEM((PART, rows, 128), bf16),
            pltpu.VMEM((128, rows), bf16),
            pltpu.VMEM((128, rows), bf16),
            pltpu.VMEM((2, tile, rows), f32),
            pltpu.VMEM((2, tile, rows), bf16),
            pltpu.VMEM((rows, 128), f32),
            pltpu.VMEM((128, rows), f32),
            pltpu.VMEM((128, rows), f32),
            pltpu.VMEM((PART, rows, rows), bf16),
            pltpu.SemaphoreType.DMA((PART * (rows // tile),)),
        ],
        compiler_params=pltpu.CompilerParams(vmem_limit_bytes=VMEM),
        cost_estimate=cost(10),
        name="attend_backward",
    )(q, k, v, e, r, attended, d_attended, x, w, grad_in, tail)


def relation_kernel(
    length_ref, split_ref, block_ref, teacher_ref, w_ref, b_ref, tw_ref, tb_ref, d_ref, g_ref, kl_ref,
    ls, rs, lt, rt, keys, left_t, zs, zt, gs, left_sum, right_t, es_all, et_all, weight, grads_s, *, all_rows,
):
    rows = block_ref.shape[0]
    tile = min(TILE, rows)
    per_head = rows // tile
    steps = PART * per_head
    length, split = own_number(length_ref), own_number(split_ref)
    block = block_ref[...]
    teacher = teacher_ref[...]
    w_ref, b_ref, tw_ref, tb_ref, g_ref = (r.at[0] for r in (w_ref, b_ref, tw_ref, tb_ref, g_ref))
    lane = lanes((rows, 128))
    position = lax.broadcasted_iota(jnp.int32, (rows, 1), 0)
    bias = key_bias(rows, length)

    @pl.when(pl.program_id(0) == 0)
    def _():
        counted = (position < length) & (position != 0) & (position != split - 1) & (position != length - 1)
        share = 1.0 / ((length - 3).astype(f32) * float(all_rows))
        weight[...] = jnp.where(counted, share, 0.0)
        kl_ref[...] = jnp.zeros_like(kl_ref)
        d_ref[...] = jnp.zeros_like(d_ref)

    def teacher_part(index, b):
        flat = dot(teacher, tw_ref[index * 192 : (index + 1) * 192, :], NT)
        if b is not None:
            flat = flat + b
        flat = flat.astype(bf16)
        return flat[:, :128], wide_rows(flat[:, 128:])

    def largest(rows_low, size, blocks):
        square = rows_low.astype(f32)
        square = (square * square).astype(bf16)
        feature = lax.broadcasted_iota(jnp.int32, (128, 128), 0) // size
        same = feature == lanes((128, 128)) // size
        return jnp.max(dot(square, jnp.where(same, 1.0, 0.0).astype(bf16)), axis=0, keepdims=True)

    def relate(left, right, t_left, t_right, symmetric):
        left_sum[...] = jnp.zeros_like(left_sum)
        right_t[...] = jnp.zeros_like(right_t)
        left_t[...] = left.T
        left_wide = left.astype(f32) * STUDENT_LOG
        right_wide = right.astype(f32)
        one = jnp.where(lane == 96, 1.0, 0.0)
        if symmetric:
            one = jnp.where(lane == 97, bias, one)
        first = jnp.where(lane == 96, bias, right_wide)
        if symmetric:
            first = jnp.where(lane == 97, 1.0, first)
        rs[:, :128] = first.astype(bf16)
        rs[:, 128:] = right
        for head in range(PART):
            ls[head] = split_terms(left_wide, head, HEAD_DIM, one)
            keys[head] = jnp.where(in_head(lane, head), right_wide, 0.0).astype(bf16)
            own = head % 2
            spare = (1 - own) * TEACHER_HEAD_DIM
            one_t = jnp.where(lane == spare, 1.0, 0.0)
            wide_t = t_right[head // 2].astype(f32)
            first_t = jnp.where(lane == spare, bias, wide_t)
            if symmetric:
                one_t = jnp.where(lane == spare + 1, bias, one_t)
                first_t = jnp.where(lane == spare + 1, 1.0, first_t)
            lt[head] = split_terms(t_left[head // 2].astype(f32) * TEACHER_LOG, own, TEACHER_HEAD_DIM, one_t)
            rt[head, :, :128] = first_t.astype(bf16)
            rt[head, :, 128:] = t_right[head // 2]
        student_bound = largest(left, HEAD_DIM, 4) * largest(right, HEAD_DIM, 4) * STUDENT_LOG**2
        bound = jnp.max(student_bound)
        for part in range(2):
            t_bound = largest(t_left[part], TEACHER_HEAD_DIM, 2) * largest(t_right[part], TEACHER_HEAD_DIM, 2)
            bound = jnp.maximum(bound, jnp.max(t_bound * TEACHER_LOG**2))
        near = bound < SAFE * SAFE

        @pl.when(near)
        def _():
            if symmetric:
                symmetric_pass()
            else:
                plain_pass()

        @pl.when(jnp.logical_not(near))
        def _():
            for head in range(PART):
                own = head % 2
                spare = (1 - own) * TEACHER_HEAD_DIM
                ls[head] = split_terms(left.astype(f32), head, HEAD_DIM, jnp.where(lane == 96, 1.0, 0.0))
                lt[head] = split_terms(
                    t_left[head // 2].astype(f32), own, TEACHER_HEAD_DIM, jnp.where(lane == spare, 1.0, 0.0)
                )
            shifted_pass()

    def plain_pass():
        def logits(step, slot):
            head, span = step_place(step, tile, per_head)

            def student(start):
                zs[slot, :, start : start + 256] = dot(ls[head, span, :], rs[start : start + 256, :], NT)

            def taught(start):
                zt[slot, :, start : start + 256] = dot(lt[head, span, :], rt[head, start : start + 256, :], NT)

            chunks = []
            for start in range(0, rows, 256):
                chunks += [functools.partial(student, start), functools.partial(taught, start)]
            return chunks

        def vector(step, slot):
            base = lax.rem(step, per_head) * tile

            def strip(start):
                here = pl.ds(pl.multiple_of(base + start, STRIP), STRIP)
                student = zs[slot, start : start + STRIP, :]
                taught = zt[slot, start : start + STRIP, :]
                es = jnp.exp2(student)
                et = jnp.exp2(taught)
                sum_s = row_sum(es)
                sum_t = row_sum(et)
                cross = row_sum(et * (taught - student))
                w = weight[here, :]
                inverse = 1.0 / sum_t
                kl_ref[here, :] += w * (LN2 * cross * inverse + jnp.log(sum_s) - jnp.log(sum_t))
                gs[slot, start : start + STRIP, :] = (es * (w / sum_s) - et * (w * inverse)).astype(bf16)

            return [functools.partial(strip, start) for start in range(0, tile, STRIP)]

        run_pipeline(steps, logits, vector, grad_products)

    def grad_products(step, slot):
        head, span = step_place(step, tile, per_head)
        own = pl.ds(pl.multiple_of(head * HEAD_DIM, HEAD_DIM), HEAD_DIM)

        def first():
            left_sum[span, :] += dot(gs[slot], keys[head])

        def second(start):
            part = slice(start, start + 256)
            right_t[own, part] += dot(left_t[own, span], gs[slot, :, part])

        return [first] + [functools.partial(second, start) for start in range(0, rows, 256)]

    def shifted_pass():
        def one(step, carry):
            head, span = step_place(step, tile, per_head)
            student = dot(ls[head, span, :], rs[...], NT)
            student = (student - jnp.max(student, axis=1, keepdims=True)) * STUDENT_LOG
            taught = dot(lt[head, span, :], rt[head], NT)
            taught = (taught - jnp.max(taught, axis=1, keepdims=True)) * TEACHER_LOG
            es = jnp.exp2(student)
            et = jnp.exp2(taught)
            sum_s = jnp.sum(es, axis=1, keepdims=True)
            sum_t = jnp.sum(et, axis=1, keepdims=True)
            cross = jnp.sum(et * (taught - student), axis=1, keepdims=True)
            w = weight[span, :]
            row = LN2 * cross / sum_t + jnp.log(sum_s) - jnp.log(sum_t)
            kl_ref[span, :] += jnp.where(w > 0.0, w * row, 0.0)
            gs[0] = (es * (w / sum_s) - et * (w / sum_t)).astype(bf16)
            for chunk in grad_products(step, 0):
                chunk()
            return carry

        lax.fori_loop(0, steps, one, 0)

    def symmetric_pass():
        size = tile
        count = rows // size

        def column(row):
            return jnp.broadcast_to(row, (128, size)).T[:, :1]

        def row_of(value):
            return jnp.broadcast_to(value, (size, 128)).T[:1, :]

        def one_head(head, carry):
            own = pl.ds(pl.multiple_of(head * HEAD_DIM, HEAD_DIM), HEAD_DIM)
            by_row = []
            by_column = [[jnp.zeros((1, size), f32)] * 3 for _ in range(count)]
            for i in range(count):
                here = slice(i * size, (i + 1) * size)
                after = slice(i * size, rows)
                student = dot(ls[head, here, :], rs[after, :], NT)
                taught = dot(lt[head, here, :], rt[head, after, :], NT)
                es = jnp.exp2(student)
                et = jnp.exp2(taught)
                cross = et * (taught - student)
                es_all[here, after] = es
                et_all[here, after] = et
                by_row.append([row_sum(t) for t in (es, et, cross)])
                for j in range(i + 1, count):
                    part = slice((j - i) * size, (j - i + 1) * size)
                    by_column[j] = [
                        c + jnp.sum(t[:, part], axis=0, keepdims=True)
                        for c, t in zip(by_column[j], (es, et, cross))
                    ]
            a, b = [], []
            for i in range(count):
                here = slice(i * size, (i + 1) * size)
                sum_s, sum_t, cross = (r + column(c) for r, c in zip(by_row[i], by_column[i]))
                w = weight[here, :]
                sum_s = jnp.where(w > 0.0, sum_s, 1.0)
                sum_t = jnp.where(w > 0.0, sum_t, 1.0)
                inverse = 1.0 / sum_t
                kl_ref[here, :] += w * (LN2 * cross * inverse + jnp.log(sum_s) - jnp.log(sum_t))
                a.append(w / sum_s)
                b.append(w * inverse)
            a_row = jnp.concatenate([row_of(t) for t in a], axis=1)
            b_row = jnp.concatenate([row_of(t) for t in b], axis=1)
            for i in range(count):
                here = slice(i * size, (i + 1) * size)
                after = slice(i * size, rows)
                both = es_all[here, after] * (a[i] + a_row[:, after])
                both = (both - et_all[here, after] * (b[i] + b_row[:, after])).astype(bf16)
                left_sum[here, :] += dot(both, keys[head, after, :])
                if i + 1 < count:
                    right_t[own, (i + 1) * size :] += dot(left_t[own, here], both[:, size:])
            return carry

        lax.fori_loop(0, PART, one_head, 0)

    q = project_part(block, w_ref, 0, b_ref[0:1, :96])
    k = project_part(block, w_ref, 1, None)
    tq = teacher_part(0, tb_ref[0:1, :192])
    tk = teacher_part(1, None)
    relate(q, k, tq, tk, False)
    grads_s[0] = (left_sum[...] * STUDENT_SCALE).astype(bf16)
    grads_s[1] = (right_t[...] * STUDENT_SCALE).T.astype(bf16)
    v = project_part(block, w_ref, 2, b_ref[1:2, :96])
    tv = teacher_part(2, tb_ref[1:2, :192])
    relate(v, v, tv, tv, True)
    grads_s[2] = ((left_sum[...] + right_t[...].T) * STUDENT_SCALE).astype(bf16)
    grads = tuple(grads_s[i] for i in range(3))
    weight_grads(grads, block, g_ref)
    d_ref[...] += spread(grads, w_ref)


def relations(length, split, block, teacher, w, b, tw, tb, all_rows):
    rows = block.shape[0]
    tile = min(TILE, rows)
    shares = w.shape[0]

    def share(shape):
        return pl.BlockSpec((1,) + shape[1:], lambda s: (s,) + (0,) * (len(shape) - 1))

    return pl.pallas_call(
        functools.partial(relation_kernel, all_rows=all_rows),
        grid=(shares,),
        in_specs=[
            SMEM, SMEM, whole(block.shape), whole(teacher.shape), share(w.shape), share(b.shape), share(tw.shape),
            share(tb.shape),
        ],
        out_specs=[whole(block.shape), share((shares, 320, D)), whole((rows, 1))],
        out_shape=[
            jax.ShapeDtypeStruct(block.shape, f32),
            jax.ShapeDtypeStruct((shares, 320, D), bf16),
            jax.ShapeDtypeStruct((rows, 1), f32),
        ],
        scratch_shapes=[
            pltpu.VMEM((PART, rows, 256), bf16),
            pltpu.VMEM((rows, 256), bf16),
            pltpu.VMEM((PART, rows, 256), bf16),
            pltpu.VMEM((PART, rows, 256), bf16),
            pltpu.VMEM((PART, rows, 128), bf16),
            pltpu.VMEM((128, rows), bf16),
            pltpu.VMEM((2, tile, rows), f32),
            pltpu.VMEM((2, tile, rows), f32),
            pltpu.VMEM((2, tile, rows), bf16),
            pltpu.VMEM((rows, 128), f32),
            pltpu.VMEM((128, rows), f32),
            pltpu.VMEM((rows, rows), f32),
            pltpu.VMEM((rows, rows), f32),
            pltpu.VMEM((rows, 1), f32),
            pltpu.VMEM((3, rows, 128), bf16),
        ],
        compiler_params=pltpu.CompilerParams(vmem_limit_bytes=VMEM),
        cost_estimate=cost(110),
        name="relations",
    )(length, split, block, teacher, w, b, tw, tb)


def norm_forward(rows, gain, shift):
    center = jnp.mean(rows, axis=1, keepdims=True)
    offsets = rows - center
    rstd = lax.rsqrt(jnp.mean(offsets * offsets, axis=1, keepdims=True) + NORM_EPS)
    normed = offsets * rstd
    return normed * gain + shift, normed, rstd


def norm_backward(grad, normed, rstd, gain):
    inner = grad * gain
    mean = jnp.mean(inner, axis=1, keepdims=True)
    slope = jnp.mean(inner * normed, axis=1, keepdims=True)
    return rstd * (inner - mean - normed * slope)


def gelu_terms(x):
    size = jnp.abs(x) * math.sqrt(0.5)
    t = 1.0 / (1.0 + 0.3275911 * size)
    bell = jnp.exp(-0.5 * x * x)
    poly = t * (0.254829592 + t * (-0.284496736 + t * (1.421413741 + t * (-1.453152027 + t * 1.061405429))))
    tail = 0.5 * poly * bell
    share = jnp.where(x >= 0.0, 1.0 - tail, tail)
    return x * share, share + x * bell * (1.0 / math.sqrt(2.0 * math.pi))


def block_kernel(
    length_ref, x_ref, out_ref, wide_ref, wide_b_ref, narrow_ref, branch_ref, gain_ref, shift_ref, *rest,
):
    shares = out_ref.shape[0]
    a_refs = rest[:shares]
    block_ref, n1_ref, r1_ref, n2_ref, r2_ref, act_ref, slope_ref, sums_ref = rest[shares:]
    tile = x_ref.shape[0]
    x = x_ref[...].astype(f32)
    mixing = branch_ref[0:1, :]
    for s in range(shares):
        mixing = mixing + dot(a_refs[s][:, :96], out_ref[s, :96, :])
    middle, normed, rstd = norm_forward(x + mixing, gain_ref[0:1, :], shift_ref[0:1, :])
    n1_ref[...] = normed
    r1_ref[...] = rstd
    low = middle.astype(bf16)
    branch = branch_ref[1:2, :]
    width = wide_ref.shape[2]
    for s in range(shares):
        value, slope = gelu_terms(dot(low, wide_ref[s]) + wide_b_ref[s, 0:1, :])
        value = value.astype(bf16)
        act_ref[:, s * width : (s + 1) * width] = value
        slope_ref[:, s * width : (s + 1) * width] = slope.astype(bf16)
        branch = branch + dot(value, narrow_ref[s])
    block, normed, rstd = norm_forward(middle + branch, gain_ref[1:2, :], shift_ref[1:2, :])
    n2_ref[...] = normed
    r2_ref[...] = rstd
    block_ref[...] = block.astype(bf16)
    position = lax.broadcasted_iota(jnp.int32, (tile, 1), 0) + pl.program_id(0) * tile
    kept = jnp.where(position < own_number(length_ref), 1.0, 0.0)
    row = lax.broadcasted_iota(jnp.int32, (8, x.shape[1]), 0)
    total = jnp.zeros((8, x.shape[1]), f32)
    for index, part in enumerate((x, mixing, branch)):
        total = jnp.where(row == index, jnp.sum(kept * part * part, axis=0, keepdims=True), total)

    @pl.when(pl.program_id(0) == 0)
    def _():
        sums_ref[...] = jnp.zeros_like(sums_ref)

    sums_ref[...] += total


def by_tile(tile, width):
    return pl.BlockSpec((tile, width), lambda i: (i, 0))


def block_forward(length, x, attended, w_out, w_wide, b_wide, w_narrow, branch_bias, gain, shift):
    rows, width = x.shape
    tile = min(TILE, rows)
    shares = len(attended)
    units = shares * w_wide.shape[2]
    row, column = by_tile(tile, width), by_tile(tile, 1)
    return pl.pallas_call(
        block_kernel,
        grid=(rows // tile,),
        in_specs=[
            SMEM, row, whole(w_out.shape), whole(w_wide.shape), whole(b_wide.shape), whole(w_narrow.shape),
            whole(branch_bias.shape), whole(gain.shape), whole(shift.shape),
        ] + [by_tile(tile, 128)] * shares,
        out_specs=[row, row, column, row, column, by_tile(tile, units), by_tile(tile, units), whole((8, width))],
        out_shape=[
            jax.ShapeDtypeStruct((rows, width), bf16),
            jax.ShapeDtypeStruct((rows, width), f32),
            jax.ShapeDtypeStruct((rows, 1), f32),
            jax.ShapeDtypeStruct((rows, width), f32),
            jax.ShapeDtypeStruct((rows, 1), f32),
            jax.ShapeDtypeStruct((rows, units), bf16),
            jax.ShapeDtypeStruct((rows, units), bf16),
            jax.ShapeDtypeStruct((8, width), f32),
        ],
        compiler_params=pltpu.CompilerParams(vmem_limit_bytes=VMEM),
        cost_estimate=cost(20),
        name="block_forward",
    )(length, x, w_out, w_wide, b_wide, w_narrow, branch_bias, gain, shift, *attended)


def block_backward_kernel(
    length_ref, d_ref, n1_ref, r1_ref, n2_ref, r2_ref, act_ref, slope_ref, out_ref, wide_ref, narrow_ref, gain_ref,
    shift_ref, kl_ref, square_ref, *rest,
):
    step = pl.program_id(0)
    shares = out_ref.shape[0]
    a_refs, sum_ref, da_refs = rest[:shares], rest[shares], rest[shares + 1 : 2 * shares + 1]
    g_ref, tail_ref, vec_ref, g_sum, low_s, branch_s, pre_s, mix_s = rest[2 * shares + 1 :]
    tile, width = d_ref.shape
    units = wide_ref.shape[2]
    span = pl.ds(pl.multiple_of(step * tile, tile), tile)

    @pl.when(step == 0)
    def _():
        vec_ref[...] = jnp.zeros_like(vec_ref)
        g_sum[...] = jnp.zeros_like(g_sum)

    def column(value):
        return jnp.sum(value, axis=0, keepdims=True)

    row = lax.broadcasted_iota(jnp.int32, (8, width), 0)
    d_block = d_ref[...]
    normed_two = n2_ref[...]
    d_two = norm_backward(d_block, normed_two, r2_ref[...], gain_ref[1:2, :])
    d_branch = d_two.astype(bf16)
    branch_s[span, :] = d_branch
    normed_one = n1_ref[...]
    low = (normed_one * gain_ref[0:1, :] + shift_ref[0:1, :]).astype(bf16)
    low_s[span, :] = low
    d_middle = d_two
    for s in range(shares):
        grad = dot(d_branch, narrow_ref[s], NT) * slope_ref[:, s * units : (s + 1) * units].astype(f32)
        grad = grad.astype(bf16)
        pre_s[span, s * units : (s + 1) * units] = grad
        g_sum[s : s + 1, :] += column(grad.astype(f32))
        d_middle = d_middle + dot(grad, wide_ref[s], NT)
    d_one = norm_backward(d_middle, normed_one, r1_ref[...], gain_ref[0:1, :])
    sum_ref[...] = d_one
    d_mixing = d_one.astype(bf16)
    mix_s[span, :] = d_mixing
    for s in range(shares):
        da_refs[s][...] = wide_rows(dot(d_mixing, out_ref[s, :96, :], NT)).astype(bf16)
    parts = (
        d_mixing.astype(f32), d_branch.astype(f32), d_middle * normed_one, d_block * normed_two, d_middle, d_block,
    )
    total = jnp.zeros((8, width), f32)
    for index, part in enumerate(parts):
        total = jnp.where(row == index, column(part), total)
    vec_ref[...] += total

    @pl.when(step == pl.num_programs(0) - 1)
    def _():
        for s in range(shares):
            part = slice(s * units, (s + 1) * units)
            g_ref[s, 0:units, :] = dot(act_ref[:, part], branch_s[...], TN).astype(bf16)
            g_ref[s, units : 2 * units, :] = dot(low_s[...], pre_s[:, part], TN).astype(bf16)
            g_ref[s, 2 * units : 2 * units + 96, :] = dot(a_refs[s][...], mix_s[...], TN)[:96].astype(bf16)
            first = lax.broadcasted_iota(jnp.int32, (32, units), 0) == 0
            g_ref[s, 2 * units + 96 : 2 * units + 128, :] = jnp.where(first, g_sum[s : s + 1, :], 0.0).astype(bf16)
        scalars = [jnp.sum(kl_ref[...], axis=0, keepdims=True)]
        scalars += [jnp.sum(square_ref[i : i + 1, :], axis=1, keepdims=True) for i in range(3)]
        scalars += [jnp.broadcast_to(own_number(length_ref).astype(f32), (1, 1))]
        lane = lanes((8, width))
        total = vec_ref[...]
        for index, value in enumerate(scalars):
            total = jnp.where((row == 6) & (lane == index), value, total)
        total = jnp.concatenate([jnp.zeros_like(total), total], axis=0)
        high = total.astype(bf16).astype(f32)
        tail_ref[:16, :] = high.astype(bf16)
        tail_ref[16:, :] = (total - high).astype(bf16)


def block_backward(
    length, d_block, n1, r1, n2, r2, act, slope, attended, w_out, w_wide, w_narrow, gain, shift, divergence, squares
):
    rows, width = d_block.shape
    tile = min(TILE, rows)
    shares, units = len(attended), w_wide.shape[2]
    row, column = by_tile(tile, width), by_tile(tile, 1)
    return pl.pallas_call(
        block_backward_kernel,
        grid=(rows // tile,),
        in_specs=[
            SMEM, row, row, column, row, column, whole(act.shape), by_tile(tile, shares * units), whole(w_out.shape),
            whole(w_wide.shape), whole(w_narrow.shape), whole(gain.shape), whole(shift.shape),
            whole(divergence.shape), whole(squares.shape),
        ] + [whole((rows, 128))] * shares,
        out_specs=[
            row, *[by_tile(tile, 128)] * shares, whole((shares, 2 * units + 128, width)), whole((32, width)),
        ],
        out_shape=[
            jax.ShapeDtypeStruct((rows, width), f32),
            *[jax.ShapeDtypeStruct((rows, 128), bf16)] * shares,
            jax.ShapeDtypeStruct((shares, 2 * units + 128, width), bf16),
            jax.ShapeDtypeStruct((32, width), bf16),
        ],
        scratch_shapes=[
            pltpu.VMEM((8, width), f32),
            pltpu.VMEM((8, units), f32),
            pltpu.VMEM((rows, width), bf16),
            pltpu.VMEM((rows, width), bf16),
            pltpu.VMEM((rows, shares * units), bf16),
            pltpu.VMEM((rows, width), bf16),
        ],
        compiler_params=pltpu.CompilerParams(vmem_limit_bytes=VMEM),
        cost_estimate=cost(25),
        name="block_backward",
    )(
        length, d_block, n1, r1, n2, r2, act, slope, w_out, w_wide, w_narrow, gain, shift, divergence, squares, *attended
    )


def shift_shares(value, by):
    shares = lax.axis_size("heads")
    return lax.ppermute(value, "heads", [((i + by) % shares, i) for i in range(shares)])


def exchange(value, bit):
    size = lax.axis_size("batch")
    return lax.ppermute(value, "batch", [(i, i ^ bit) for i in range(size)])


def merge_kernel(*refs):
    out_ref = refs[-1]
    total = refs[0][...].astype(f32)
    for ref in refs[1:-1]:
        total = total + ref[...].astype(f32)
    end = total.shape[0] - 32
    sums = total[end : end + 16] + total[end + 16 :]
    if out_ref.dtype == f32:
        out_ref[:end, :] = total[:end]
        out_ref[end:, :] = sums
    else:
        high = sums.astype(bf16).astype(f32)
        out_ref[:end, :] = total[:end].astype(bf16)
        out_ref[end : end + 16, :] = high.astype(bf16)
        out_ref[end + 16 :, :] = (sums - high).astype(bf16)


def merge(parts, last=False):
    rows, width = parts[0].shape
    shape = jax.ShapeDtypeStruct((rows - 16, width), f32) if last else jax.ShapeDtypeStruct((rows, width), bf16)
    return pl.pallas_call(
        merge_kernel, out_shape=shape, cost_estimate=cost(1), name="merge",
        compiler_params=pltpu.CompilerParams(vmem_limit_bytes=VMEM),
    )(*parts)


def batch_sum(value):
    size = lax.axis_size("batch")
    bit = 1
    while bit < size:
        value = merge([value, exchange(value, bit)], last=2 * bit >= size)
        bit *= 2
    return value


def body(
    student_rows, teacher_rows, valid_length, split_point, project_five, bias_five, output_five, branch_bias,
    norm_gain, norm_bias, widen_weight, widen_bias, narrow_weight, project_six, bias_six, teacher_project,
    teacher_bias,
):
    shares = lax.axis_size("heads")
    batch = lax.axis_size("batch")
    place = lax.axis_index("batch")
    all_rows = shares * batch * HEADS
    x = student_rows[0]
    teacher = teacher_rows[0]

    def turned(weight):
        return jnp.transpose(weight, (1, 2, 0)).reshape(-1, weight.shape[0])

    def pad(rows, width):
        return jnp.pad(rows, ((0, 0), (0, width - rows.shape[1])))

    small = jnp.concatenate(
        [pad(bias_five, D), pad(bias_six, D), widen_bias[None], pad(teacher_bias, D), jnp.zeros((1, D), bf16)], axis=0
    )
    five = jnp.concatenate([turned(project_five), small], axis=0)
    fives = [five] + [shift_shares(five, by) for by in range(1, shares)]
    smalls = [w[288:].astype(f32) for w in fives]

    def part_of(rows):
        count = -(-rows.shape[0] // batch)
        rows = jnp.pad(rows, ((0, count * batch - rows.shape[0]), (0, 0)))
        return lax.dynamic_slice_in_dim(rows, place * count, count)

    def whole_of(own, gathered, start, count):
        others = jnp.swapaxes(gathered[:, :, start : start + count], 0, 1).reshape(shares - 1, -1, own.shape[1])
        return jnp.concatenate([own[None], others[:, : own.shape[0]]], axis=0)

    units = widen_weight.shape[1]
    mid = jnp.concatenate([widen_weight, narrow_weight, jnp.pad(output_five, ((0, 32), (0, 0)))], axis=0)
    six = turned(project_six)
    taught = turned(teacher_project)
    parts = [part_of(mid), part_of(six), part_of(taught).reshape(-1, D)]
    sizes = [p.shape[0] for p in parts]
    parts = jnp.concatenate(parts, axis=0)
    parts = jnp.stack([shift_shares(parts, by) for by in range(1, shares)])
    first = sizes[0] + sizes[1]
    near = lax.all_gather(parts[:, :first], "batch", axis=0)
    far = lax.all_gather(parts[:, first:], "batch", axis=0)

    heads = []
    for s in range(shares):
        heads.append(attend_forward(valid_length, x, fives[s], smalls[s][0:2]))
    attended = [h[5] for h in heads]
    mids = whole_of(mid, near, 0, sizes[0])
    smalls = jnp.stack(smalls)
    w_wide, w_narrow, w_out = mids[:, :D], mids[:, D : D + units], mids[:, D + units :]
    block, n1, r1, n2, r2, act, slope, squares = block_forward(
        valid_length, x, attended, w_out, w_wide, smalls[:, 4:5], w_narrow, branch_bias, norm_gain, norm_bias
    )
    sixes = whole_of(six, near, sizes[0], sizes[1])
    taughts = whole_of(taught, far.reshape(batch, shares - 1, -1, taught.shape[1]), 0, sizes[2])
    d_block, g_six, divergence = relations(
        valid_length, split_point, block, teacher, sixes, smalls[:, 2:4], taughts, smalls[:, 5:7], all_rows
    )
    result = block_backward(
        valid_length, d_block, n1, r1, n2, r2, act, slope, attended, w_out, w_wide, w_narrow, norm_gain, norm_bias,
        divergence, squares,
    )
    d_sum_one, d_attended, (g_mid, tail) = result[0], result[1 : 1 + shares], result[1 + shares :]

    def to_owner(parts):
        return [parts[0]] + [shift_shares(parts[by], shares - by) for by in range(1, shares)]

    six_part = lax.psum_scatter(g_six, "batch", scatter_dimension=1, tiled=True)
    mid_part = lax.psum_scatter(g_mid, "batch", scatter_dimension=1, tiled=True)
    six_rows = six_part.shape[1]
    both = jnp.concatenate([six_part, mid_part], axis=1)

    grad_in = d_sum_one
    g_five = [None] * shares
    for s in list(range(1, shares)) + [0]:
        q, k, v, e, r, a = heads[s]
        g_five[s], grad_in = attend_backward(q, k, v, e, r, a, d_attended[s], x, fives[s], grad_in, tail)

    both = sum(p.astype(f32) for p in to_owner([both[s] for s in range(shares)])).astype(bf16)
    both = lax.all_gather(both, "batch", axis=0).astype(f32)
    six_sum = both[:, :six_rows].reshape(-1, D)
    mid_sum = both[:, six_rows:].reshape(-1, D)
    five_sum = batch_sum(merge(to_owner(g_five)))

    def unturned(grad):
        return jnp.transpose(grad[: 3 * 96].reshape(3, 96, -1), (2, 0, 1))

    vectors = five_sum[296:304]
    totals = vectors[6]
    counted = totals[4] * D
    summary = jnp.concatenate([totals[:1], jnp.sqrt(totals[1:4] / counted)])
    six_bias = six_sum[288:290, :96] + six_sum[304:306, :96]
    return (
        block[None], grad_in[None], unturned(five_sum), five_sum[288:290, :96],
        mid_sum[2 * units : 2 * units + 96], vectors[0:2], vectors[2:4], vectors[4:6],
        mid_sum[units : 2 * units], mid_sum[2 * units + 96], mid_sum[:units],
        unturned(six_sum), six_bias, summary,
    )


def solution(mesh):
    return jax.shard_map(
        body,
        mesh=mesh,
        in_specs=(
            P(("batch", "heads"), None, None),
            P(("batch", "heads"), None, None),
            P("batch"),
            P("batch"),
            P(None, None, "heads"),
            P(None, "heads"),
            P("heads", None),
            P(),
            P(),
            P(),
            P(None, "heads"),
            P("heads"),
            P("heads", None),
            P(None, None, "heads"),
            P(None, "heads"),
            P(None, None, "heads"),
            P(None, "heads"),
        ),
        out_specs=(
            P(("batch", "heads"), None, None),
            P(("batch", "heads"), None, None),
            P(None, None, "heads"),
            P(None, "heads"),
            P("heads", None),
            P(),
            P(),
            P(),
            P(None, "heads"),
            P("heads"),
            P("heads", None),
            P(None, None, "heads"),
            P(None, "heads"),
            P(),
        ),
        check_vma=False,
    )
```

```python
import functools
import math

import jax
import jax.numpy as jnp
from jax import lax
from jax.experimental import pallas as pl
from jax.experimental.pallas import tpu as pltpu
from jax.sharding import PartitionSpec as P

D = 384
HEADS = 12
HEAD_DIM = 32
TEACHER_HEAD_DIM = 64
PART = 3
TILE = 512
STRIP = 16
NORM_EPS = 1e-12
MASKED = -1e30
SAFE = 64.0
LN2 = math.log(2.0)
STUDENT_SCALE = 1.0 / math.sqrt(HEAD_DIM)
STUDENT_LOG = math.log2(math.e) / math.sqrt(HEAD_DIM)
TEACHER_LOG = math.log2(math.e) / math.sqrt(TEACHER_HEAD_DIM)
VMEM = 56 * 2**20

f32 = jnp.float32
bf16 = jnp.bfloat16

NN = (((1,), (0,)), ((), ()))
NT = (((1,), (1,)), ((), ()))
TN = (((0,), (0,)), ((), ()))


def dot(left, right, dims=NN):
    return lax.dot_general(left, right, dims, preferred_element_type=f32)


def lanes(shape):
    return lax.broadcasted_iota(jnp.int32, shape, 1)


def wide_rows(rows):
    return jnp.concatenate([rows, jnp.zeros((rows.shape[0], 128 - rows.shape[1]), rows.dtype)], axis=1)


def in_head(lane, head, size=HEAD_DIM):
    return (lane >= head * size) & (lane < (head + 1) * size)


def split_terms(rows, head, size, extra):
    inside = in_head(lanes(rows.shape), head, size)
    high = rows.astype(bf16).astype(f32)
    first = jnp.where(inside, high, extra).astype(bf16)
    second = jnp.where(inside, rows - high, 0.0).astype(bf16)
    return jnp.concatenate([first, second], axis=1)


def own_number(ref):
    return ref[lax.axis_index("heads")]


def key_bias(rows, length):
    position = lax.broadcasted_iota(jnp.int32, (rows, 1), 0)
    return jnp.where(position < length, 0.0, MASKED)


def fold(tile, combine):
    total = tile[:, :128]
    for column in range(128, tile.shape[1], 128):
        total = combine(total, tile[:, column : column + 128])
    return total


def row_sum(tile):
    return jnp.sum(fold(tile, jnp.add), axis=1, keepdims=True)


def weave(first, second):
    done = 0
    for index, step in enumerate(second):
        while done < len(first) and done * len(second) < len(first) * (index + 1):
            first[done]()
            done += 1
        step()
    for step in first[done:]:
        step()


def step_place(step, tile, per_head):
    head = step // per_head
    return head, pl.ds(pl.multiple_of(lax.rem(step, per_head) * tile, tile), tile)


def run_pipeline(steps, logits, vector, back, enter=None):
    def stage(step, slot, before, after, second=False):
        if enter is not None:
            enter(step, slot, not before, second)
        ahead = logits(step + 1, 1 - slot) if after else []
        behind = back(step - 1, 1 - slot) if before else []
        weave(ahead + behind, vector(step, slot))

    for chunk in logits(jnp.int32(0), 0):
        chunk()
    stage(jnp.int32(0), 0, False, True)
    stage(jnp.int32(1), 1, True, True, second=True)

    def pair(index, carry):
        stage(2 * index + 2, 0, True, True)
        stage(2 * index + 3, 1, True, True)
        return carry

    lax.fori_loop(0, (steps - 4) // 2, pair, 0)
    stage(jnp.int32(steps - 2), 0, True, True)
    stage(jnp.int32(steps - 1), 1, True, False)
    for chunk in back(jnp.int32(steps - 1), 1):
        chunk()


def project_part(x, w_ref, index, bias):
    flat = dot(x, w_ref[index * 96 : (index + 1) * 96, :], NT)
    if bias is not None:
        flat = flat + bias
    return wide_rows(flat).astype(bf16)


def attend_forward_kernel(
    length_ref, x_ref, w_ref, q_ref, k_ref, v_ref, e_hbm, r_ref, o_ref, lhs, rhs, mixer, zs, es, sems
):
    rows = x_ref.shape[0]
    tile = zs.shape[1]
    per_head = rows // tile
    steps = PART * per_head
    x = x_ref[...]
    small = w_ref[288:304, :].astype(f32)
    q = project_part(x, w_ref, 0, small[0:1, :96])
    k = project_part(x, w_ref, 1, None)
    v = project_part(x, w_ref, 2, small[1:2, :96])
    q_ref[...] = q
    k_ref[...] = k
    v_ref[...] = v
    lane = lanes((rows, 128))
    one = jnp.where(lane == 96, 1.0, 0.0)
    for head in range(PART):
        lhs[head] = jnp.where(in_head(lane, head), q.astype(f32), one).astype(bf16)
    rhs[...] = jnp.where(lane == 96, key_bias(rows, own_number(length_ref)), k.astype(f32)).astype(bf16)
    mixer[...] = jnp.where(lane == 96, 1.0, v.astype(f32)).astype(bf16)
    o_ref[...] = jnp.zeros_like(o_ref)
    r_ref[...] = jnp.zeros_like(r_ref)

    def out_copy(step, slot):
        head, span = step_place(step, tile, per_head)
        return pltpu.make_async_copy(es.at[slot], e_hbm.at[head, span], sems.at[slot])

    def logits(step, slot):
        head, span = step_place(step, tile, per_head)

        def chunk(start):
            zs[slot, :, start : start + 256] = dot(lhs[head, span, :], rhs[start : start + 256, :], NT)

        return [functools.partial(chunk, start) for start in range(0, rows, 256)]

    def vector(step, slot):
        def strip(start):
            z = zs[slot, start : start + STRIP, :]
            highest = jnp.max(fold(z, jnp.maximum), axis=1, keepdims=True)
            es[slot, start : start + STRIP, :] = jnp.exp2((z - highest) * STUDENT_LOG).astype(bf16)

        return [functools.partial(strip, start) for start in range(0, tile, STRIP)]

    def back(step, slot):
        head, span = step_place(step, tile, per_head)

        sums = []

        def part(start):
            sums.append(dot(es[slot, :, start : start + 256], mixer[start : start + 256, :]))

        def mix():
            mixed = functools.reduce(jnp.add, sums)
            inverse = 1.0 / mixed[:, 96:97]
            inside = in_head(lanes(mixed.shape), head)
            o_ref[span, :] = jnp.where(inside, mixed * inverse, o_ref[span, :].astype(f32)).astype(bf16)
            r_ref[span, :] = jnp.where(inside, inverse, r_ref[span, :])

        return [functools.partial(part, start) for start in range(0, rows, 256)] + [mix]

    def enter(step, slot, first, second):
        if not first:
            out_copy(step - 1, 1 - slot).start()
        if not (first or second):
            out_copy(step - 2, slot).wait()

    run_pipeline(steps, logits, vector, back, enter)
    out_copy(jnp.int32(steps - 1), 1).start()
    out_copy(jnp.int32(steps - 2), 0).wait()
    out_copy(jnp.int32(steps - 1), 1).wait()


def whole(shape):
    return pl.BlockSpec(shape, lambda *_: (0,) * len(shape))


SMEM = pl.BlockSpec(memory_space=pltpu.SMEM)
ANY = pl.BlockSpec(memory_space=pl.ANY)


def cost(micros):
    return pl.CostEstimate(flops=int(micros * 0.04e9), bytes_accessed=1024, transcendentals=0)


def attend_forward(length, x, w):
    rows = x.shape[0]
    narrow = jax.ShapeDtypeStruct((rows, 128), bf16)
    tile = min(TILE, rows // 2)
    return pl.pallas_call(
        attend_forward_kernel,
        grid=(1,),
        in_specs=[SMEM, whole(x.shape), whole(w.shape)],
        out_specs=[whole((rows, 128))] * 3 + [ANY] + [whole((rows, 128))] * 2,
        out_shape=[
            narrow, narrow, narrow, jax.ShapeDtypeStruct((PART, rows, rows), bf16),
            jax.ShapeDtypeStruct((rows, 128), f32), narrow,
        ],
        scratch_shapes=[
            pltpu.VMEM((PART, rows, 128), bf16),
            pltpu.VMEM((rows, 128), bf16),
            pltpu.VMEM((rows, 128), bf16),
            pltpu.VMEM((2, tile, rows), f32),
            pltpu.VMEM((2, tile, rows), bf16),
            pltpu.SemaphoreType.DMA((2,)),
        ],
        compiler_params=pltpu.CompilerParams(vmem_limit_bytes=VMEM),
        cost_estimate=cost(9),
        name="attend_forward",
    )(length, x, w)


def attend_backward_kernel(
    q_ref, k_ref, v_ref, e_hbm, r_ref, a_ref, d_ref, x_hbm, w_hbm, acc_hbm, tail_ref, g_ref, in_ref,
    lhs, rhs, keys, qt, dt, zs, gs, dq, dkt, dvt, e_all, x_ref, w_ref, acc_ref, sems, late,
):
    rows = q_ref.shape[0]
    tile = zs.shape[1]
    per_head = rows // tile
    steps = PART * per_head

    def in_copy(step):
        head, span = step_place(step, tile, per_head)
        return pltpu.make_async_copy(e_hbm.at[head, span], e_all.at[head, span], sems.at[step])

    def begin(step, carry):
        in_copy(step).start()
        return carry

    lax.fori_loop(0, steps, begin, 0)
    late_copies = [
        pltpu.make_async_copy(source, target, late.at[index])
        for index, (source, target) in enumerate(((x_hbm, x_ref), (w_hbm, w_ref), (acc_hbm, acc_ref)))
    ]
    for copy in late_copies:
        copy.start()
    lane = lanes((rows, 128))
    grads = r_ref[...] * d_ref[...].astype(f32)
    shifts = grads * a_ref[...].astype(f32)
    k = k_ref[...].astype(f32)
    for head in range(PART):
        inside = in_head(lane, head)
        shift = -jnp.sum(jnp.where(inside, shifts, 0.0), axis=1, keepdims=True)
        high = shift.astype(bf16).astype(f32)
        lhs[head] = split_terms(
            grads, head, HEAD_DIM, jnp.where(lane == 96, high, jnp.where(lane == 97, shift - high, 0.0))
        )
        keys[head] = jnp.where(inside, k, 0.0).astype(bf16)
    rhs[:, :128] = jnp.where((lane == 96) | (lane == 97), 1.0, v_ref[...].astype(f32)).astype(bf16)
    rhs[:, 128:] = v_ref[...]
    qt[...] = q_ref[...].T
    dt[...] = grads.astype(bf16).T
    dq[...] = jnp.zeros_like(dq)
    dkt[...] = jnp.zeros_like(dkt)
    dvt[...] = jnp.zeros_like(dvt)

    def logits(step, slot):
        head, span = step_place(step, tile, per_head)

        def chunk(start):
            zs[slot, :, start : start + 256] = dot(lhs[head, span, :], rhs[start : start + 256, :], NT)

        return [functools.partial(chunk, start) for start in range(0, rows, 256)]

    def vector(step, slot):
        head, span = step_place(step, tile, per_head)
        base = lax.rem(step, per_head) * tile

        def strip(start):
            here = pl.ds(pl.multiple_of(base + start, STRIP), STRIP)
            weights = e_all[head, here, :].astype(f32)
            gs[slot, start : start + STRIP, :] = (weights * zs[slot, start : start + STRIP, :]).astype(bf16)

        return [functools.partial(strip, start) for start in range(0, tile, STRIP)]

    def back(step, slot):
        head, span = step_place(step, tile, per_head)
        own = pl.ds(pl.multiple_of(head * HEAD_DIM, HEAD_DIM), HEAD_DIM)

        def first():
            dq[span, :] += dot(gs[slot], keys[head])

        def second(start):
            part = slice(start, start + 256)
            dkt[own, part] += dot(qt[own, span], gs[slot, :, part])

        def third(start):
            part = slice(start, start + 256)
            dvt[own, part] += dot(dt[own, span], e_all[head, span, part])

        starts = range(0, rows, 256)
        return [first] + [functools.partial(second, s) for s in starts] + [functools.partial(third, s) for s in starts]

    run_pipeline(steps, logits, vector, back, lambda step, slot, first, second: in_copy(step).wait())
    for copy in late_copies:
        copy.wait()
    grads = (
        (dq[...] * STUDENT_SCALE).astype(bf16),
        (dkt[...] * STUDENT_SCALE).T.astype(bf16),
        dvt[...].T.astype(bf16),
    )
    weight_grads(grads, x_ref[...], g_ref, tail_ref[:16, :].astype(f32), tail_ref[16:, :].astype(f32))
    in_ref[...] = acc_ref[...] + spread(grads, w_ref)


def weight_grads(grads, x, g_ref, tail_high=0.0, tail_low=0.0):
    for index, grad in enumerate(grads):
        g_ref[index * 96 : (index + 1) * 96, :] = dot(grad, x, TN)[:96].astype(bf16)
    ones = jnp.ones((16, x.shape[0]), bf16)
    row = lax.broadcasted_iota(jnp.int32, (16, 128), 0)
    sums = jnp.where(row == 0, dot(ones, grads[0]), jnp.where(row == 1, dot(ones, grads[2]), 0.0))
    sums = jnp.concatenate([sums, jnp.zeros((16, x.shape[1] - 128), f32)], axis=1) + tail_high
    high = sums.astype(bf16).astype(f32)
    g_ref[288:304, :] = high.astype(bf16)
    g_ref[304:320, :] = (sums - high + tail_low).astype(bf16)


def spread(grads, w_ref):
    total = None
    for index, grad in enumerate(grads):
        term = dot(grad[:, :96], w_ref[index * 96 : (index + 1) * 96, :])
        total = term if total is None else total + term
    return total


def attend_backward(q, k, v, e, r, attended, d_attended, x, w, grad_in, tail):
    rows = x.shape[0]
    tile = min(TILE, rows // 2)
    row = whole((rows, 128))
    return pl.pallas_call(
        attend_backward_kernel,
        grid=(1,),
        in_specs=[row, row, row, ANY, row, row, row, ANY, ANY, ANY, whole(tail.shape)],
        out_specs=[whole((320, x.shape[1])), whole(x.shape)],
        out_shape=[jax.ShapeDtypeStruct((320, x.shape[1]), bf16), jax.ShapeDtypeStruct(x.shape, f32)],
        scratch_shapes=[
            pltpu.VMEM((PART, rows, 256), bf16),
            pltpu.VMEM((rows, 256), bf16),
            pltpu.VMEM((PART, rows, 128), bf16),
            pltpu.VMEM((128, rows), bf16),
            pltpu.VMEM((128, rows), bf16),
            pltpu.VMEM((2, tile, rows), f32),
            pltpu.VMEM((2, tile, rows), bf16),
            pltpu.VMEM((rows, 128), f32),
            pltpu.VMEM((128, rows), f32),
            pltpu.VMEM((128, rows), f32),
            pltpu.VMEM((PART, rows, rows), bf16),
            pltpu.VMEM(x.shape, bf16),
            pltpu.VMEM(w.shape, bf16),
            pltpu.VMEM(x.shape, f32),
            pltpu.SemaphoreType.DMA((PART * (rows // tile),)),
            pltpu.SemaphoreType.DMA((3,)),
        ],
        compiler_params=pltpu.CompilerParams(vmem_limit_bytes=VMEM),
        cost_estimate=cost(10),
        name="attend_backward",
    )(q, k, v, e, r, attended, d_attended, x, w, grad_in, tail)


def relation_kernel(
    length_ref, split_ref, block_ref, teacher_ref, packed_ref, small_ref, *rest, all_rows, gathered,
):
    if gathered:
        d_before, kl_before, *rest = rest
    (
    d_ref, g_ref, kl_ref, pack, ls, rs, lt, rt, keys, left_t, zs, zt, gs, left_sum, right_t, es_all, et_all, weight, grads_s,
    ) = rest
    rows = block_ref.shape[0]
    tile = zs.shape[1]
    per_head = rows // tile
    steps = PART * per_head
    length, split = own_number(length_ref), own_number(split_ref)
    block = block_ref[...]
    teacher = teacher_ref[...]
    if gathered:
        unpack(packed_ref, 0, pack)
    else:
        pack[...] = packed_ref[...]
    w_ref, g_ref = pack, g_ref.at[0]
    small = small_ref[0].astype(f32)
    lane = lanes((rows, 128))
    position = lax.broadcasted_iota(jnp.int32, (rows, 1), 0)
    bias = key_bias(rows, length)

    @pl.when(pl.program_id(0) == 0)
    def _():
        counted = (position < length) & (position != 0) & (position != split - 1) & (position != length - 1)
        share = 1.0 / ((length - 3).astype(f32) * float(all_rows))
        weight[...] = jnp.where(counted, share, 0.0)
        kl_ref[...] = kl_before[...] if gathered else jnp.zeros_like(kl_ref)
        d_ref[...] = d_before[...] if gathered else jnp.zeros_like(d_ref)

    def teacher_part(index, b):
        start = 288 + index * 192
        flat = dot(teacher[:, :D], pack[start : start + 192, :], NT)
        flat = flat + dot(teacher[:, D:], pack[start + 576 : start + 768, :], NT)
        if b is not None:
            flat = flat + b
        flat = flat.astype(bf16)
        return flat[:, :128], wide_rows(flat[:, 128:])

    def largest(rows_low, size, blocks):
        square = rows_low.astype(f32)
        square = (square * square).astype(bf16)
        feature = lax.broadcasted_iota(jnp.int32, (128, 128), 0) // size
        same = feature == lanes((128, 128)) // size
        return jnp.max(dot(square, jnp.where(same, 1.0, 0.0).astype(bf16)), axis=0, keepdims=True)

    def relate(left, right, t_left, t_right, symmetric):
        left_sum[...] = jnp.zeros_like(left_sum)
        right_t[...] = jnp.zeros_like(right_t)
        left_t[...] = left.T
        left_wide = left.astype(f32) * STUDENT_LOG
        right_wide = right.astype(f32)
        one = jnp.where(lane == 96, 1.0, 0.0)
        if symmetric:
            one = jnp.where(lane == 97, bias, one)
        first = jnp.where(lane == 96, bias, right_wide)
        if symmetric:
            first = jnp.where(lane == 97, 1.0, first)
        rs[:, :128] = first.astype(bf16)
        rs[:, 128:] = right
        for head in range(PART):
            ls[head] = split_terms(left_wide, head, HEAD_DIM, one)
            keys[head] = jnp.where(in_head(lane, head), right_wide, 0.0).astype(bf16)
            own = head % 2
            spare = (1 - own) * TEACHER_HEAD_DIM
            one_t = jnp.where(lane == spare, 1.0, 0.0)
            wide_t = t_right[head // 2].astype(f32)
            first_t = jnp.where(lane == spare, bias, wide_t)
            if symmetric:
                one_t = jnp.where(lane == spare + 1, bias, one_t)
                first_t = jnp.where(lane == spare + 1, 1.0, first_t)
            lt[head] = split_terms(t_left[head // 2].astype(f32) * TEACHER_LOG, own, TEACHER_HEAD_DIM, one_t)
            rt[head, :, :128] = first_t.astype(bf16)
            rt[head, :, 128:] = t_right[head // 2]
        student_bound = largest(left, HEAD_DIM, 4) * largest(right, HEAD_DIM, 4) * STUDENT_LOG**2
        bound = jnp.max(student_bound)
        for part in range(2):
            t_bound = largest(t_left[part], TEACHER_HEAD_DIM, 2) * largest(t_right[part], TEACHER_HEAD_DIM, 2)
            bound = jnp.maximum(bound, jnp.max(t_bound * TEACHER_LOG**2))
        near = bound < SAFE * SAFE

        @pl.when(near)
        def _():
            if symmetric:
                symmetric_pass()
            else:
                plain_pass()

        @pl.when(jnp.logical_not(near))
        def _():
            for head in range(PART):
                own = head % 2
                spare = (1 - own) * TEACHER_HEAD_DIM
                ls[head] = split_terms(left.astype(f32), head, HEAD_DIM, jnp.where(lane == 96, 1.0, 0.0))
                lt[head] = split_terms(
                    t_left[head // 2].astype(f32), own, TEACHER_HEAD_DIM, jnp.where(lane == spare, 1.0, 0.0)
                )
            shifted_pass()

    def plain_pass():
        def logits(step, slot):
            head, span = step_place(step, tile, per_head)

            def student(start):
                zs[slot, :, start : start + 256] = dot(ls[head, span, :], rs[start : start + 256, :], NT)

            def taught(start):
                zt[slot, :, start : start + 256] = dot(lt[head, span, :], rt[head, start : start + 256, :], NT)

            chunks = []
            for start in range(0, rows, 256):
                chunks += [functools.partial(student, start), functools.partial(taught, start)]
            return chunks

        def vector(step, slot):
            base = lax.rem(step, per_head) * tile

            def strip(start):
                here = pl.ds(pl.multiple_of(base + start, STRIP), STRIP)
                student = zs[slot, start : start + STRIP, :]
                taught = zt[slot, start : start + STRIP, :]
                es = jnp.exp2(student)
                et = jnp.exp2(taught)
                sum_s = row_sum(es)
                sum_t = row_sum(et)
                cross = row_sum(et * (taught - student))
                w = weight[here, :]
                inverse = 1.0 / sum_t
                kl_ref[here, :] += w * (LN2 * cross * inverse + jnp.log(sum_s) - jnp.log(sum_t))
                gs[slot, start : start + STRIP, :] = (es * (w / sum_s) - et * (w * inverse)).astype(bf16)

            return [functools.partial(strip, start) for start in range(0, tile, STRIP)]

        run_pipeline(steps, logits, vector, grad_products)

    def grad_products(step, slot):
        head, span = step_place(step, tile, per_head)
        own = pl.ds(pl.multiple_of(head * HEAD_DIM, HEAD_DIM), HEAD_DIM)

        def first():
            left_sum[span, :] += dot(gs[slot], keys[head])

        def second(start):
            part = slice(start, start + 256)
            right_t[own, part] += dot(left_t[own, span], gs[slot, :, part])

        return [first] + [functools.partial(second, start) for start in range(0, rows, 256)]

    def shifted_pass():
        def one(step, carry):
            head, span = step_place(step, tile, per_head)
            student = dot(ls[head, span, :], rs[...], NT)
            student = (student - jnp.max(student, axis=1, keepdims=True)) * STUDENT_LOG
            taught = dot(lt[head, span, :], rt[head], NT)
            taught = (taught - jnp.max(taught, axis=1, keepdims=True)) * TEACHER_LOG
            es = jnp.exp2(student)
            et = jnp.exp2(taught)
            sum_s = jnp.sum(es, axis=1, keepdims=True)
            sum_t = jnp.sum(et, axis=1, keepdims=True)
            cross = jnp.sum(et * (taught - student), axis=1, keepdims=True)
            w = weight[span, :]
            row = LN2 * cross / sum_t + jnp.log(sum_s) - jnp.log(sum_t)
            kl_ref[span, :] += jnp.where(w > 0.0, w * row, 0.0)
            gs[0] = (es * (w / sum_s) - et * (w / sum_t)).astype(bf16)
            for chunk in grad_products(step, 0):
                chunk()
            return carry

        lax.fori_loop(0, steps, one, 0)

    def symmetric_pass():
        size = min(256, rows)
        count = rows // size

        def column(row):
            return jnp.broadcast_to(row, (128, size)).T[:, :1]

        def row_of(value):
            return jnp.broadcast_to(value, (size, 128)).T[:1, :]

        def one_head(head, carry):
            own = pl.ds(pl.multiple_of(head * HEAD_DIM, HEAD_DIM), HEAD_DIM)
            by_row = []
            by_column = [[jnp.zeros((1, size), f32)] * 3 for _ in range(count)]
            for i in range(count):
                here = slice(i * size, (i + 1) * size)
                after = slice(i * size, rows)
                student = dot(ls[head, here, :], rs[after, :], NT)
                taught = dot(lt[head, here, :], rt[head, after, :], NT)
                es = jnp.exp2(student)
                et = jnp.exp2(taught)
                cross = et * (taught - student)
                es_all[here, after] = es
                et_all[here, after] = et
                by_row.append([row_sum(t) for t in (es, et, cross)])
                for j in range(i + 1, count):
                    part = slice((j - i) * size, (j - i + 1) * size)
                    by_column[j] = [
                        c + jnp.sum(t[:, part], axis=0, keepdims=True)
                        for c, t in zip(by_column[j], (es, et, cross))
                    ]
            a, b = [], []
            for i in range(count):
                here = slice(i * size, (i + 1) * size)
                sum_s, sum_t, cross = (r + column(c) for r, c in zip(by_row[i], by_column[i]))
                w = weight[here, :]
                sum_s = jnp.where(w > 0.0, sum_s, 1.0)
                sum_t = jnp.where(w > 0.0, sum_t, 1.0)
                inverse = 1.0 / sum_t
                kl_ref[here, :] += w * (LN2 * cross * inverse + jnp.log(sum_s) - jnp.log(sum_t))
                a.append(w / sum_s)
                b.append(w * inverse)
            a_row = jnp.concatenate([row_of(t) for t in a], axis=1)
            b_row = jnp.concatenate([row_of(t) for t in b], axis=1)
            for i in range(count):
                here = slice(i * size, (i + 1) * size)
                after = slice(i * size, rows)
                both = es_all[here, after] * (a[i] + a_row[:, after])
                both = (both - et_all[here, after] * (b[i] + b_row[:, after])).astype(bf16)
                left_sum[here, :] += dot(both, keys[head, after, :])
                if i + 1 < count:
                    right_t[own, (i + 1) * size :] += dot(left_t[own, here], both[:, size:])
            return carry

        lax.fori_loop(0, PART, one_head, 0)

    q = project_part(block, w_ref, 0, small[2:3, :96])
    k = project_part(block, w_ref, 1, None)
    tq = teacher_part(0, small[5:6, :192])
    tk = teacher_part(1, None)
    relate(q, k, tq, tk, False)
    grads_s[0] = (left_sum[...] * STUDENT_SCALE).astype(bf16)
    grads_s[1] = (right_t[...] * STUDENT_SCALE).T.astype(bf16)
    v = project_part(block, w_ref, 2, small[3:4, :96])
    tv = teacher_part(2, small[6:7, :192])
    relate(v, v, tv, tv, True)
    grads_s[2] = ((left_sum[...] + right_t[...].T) * STUDENT_SCALE).astype(bf16)
    grads = tuple(grads_s[i] for i in range(3))
    weight_grads(grads, block, g_ref)
    d_ref[...] += spread(grads, w_ref)


def unpack(packed_ref, share, target):
    rows, part = target.shape[0], packed_ref.shape[2]
    for start in range(0, rows, part):
        size = min(part, rows - start)
        target[start : start + size, :] = packed_ref[start // part, share, :size, :]


def relations(length, split, block, teacher, packed, small, all_rows, before=None):
    rows = block.shape[0]
    tile = min(TILE, rows // 2)
    gathered = before is not None
    shares = small.shape[0]

    def share(shape):
        return pl.BlockSpec((1,) + shape[1:], lambda s: (s,) + (0,) * (len(shape) - 1))

    if gathered:
        place = pl.BlockSpec((packed.shape[0], 1) + packed.shape[2:], lambda s: (0, s + 1, 0, 0))
    else:
        place = whole(packed.shape)
    return pl.pallas_call(
        functools.partial(relation_kernel, all_rows=all_rows, gathered=gathered),
        grid=(shares,),
        in_specs=[SMEM, SMEM, whole(block.shape), whole(teacher.shape), place, share(small.shape)]
        + [whole(b.shape) for b in before or ()],
        out_specs=[whole(block.shape), share((shares, 320, D)), whole((rows, 1))],
        out_shape=[
            jax.ShapeDtypeStruct(block.shape, f32),
            jax.ShapeDtypeStruct((shares, 320, D), bf16),
            jax.ShapeDtypeStruct((rows, 1), f32),
        ],
        scratch_shapes=[
            pltpu.VMEM((1440, D), bf16),
            pltpu.VMEM((PART, rows, 256), bf16),
            pltpu.VMEM((rows, 256), bf16),
            pltpu.VMEM((PART, rows, 256), bf16),
            pltpu.VMEM((PART, rows, 256), bf16),
            pltpu.VMEM((PART, rows, 128), bf16),
            pltpu.VMEM((128, rows), bf16),
            pltpu.VMEM((2, tile, rows), f32),
            pltpu.VMEM((2, tile, rows), f32),
            pltpu.VMEM((2, tile, rows), bf16),
            pltpu.VMEM((rows, 128), f32),
            pltpu.VMEM((128, rows), f32),
            pltpu.VMEM((rows, rows), f32),
            pltpu.VMEM((rows, rows), f32),
            pltpu.VMEM((rows, 1), f32),
            pltpu.VMEM((3, rows, 128), bf16),
        ],
        compiler_params=pltpu.CompilerParams(vmem_limit_bytes=VMEM),
        cost_estimate=cost(30 * shares),
        name="relations",
    )(length, split, block, teacher, packed, small, *(before or ()))


def norm_forward(rows, gain, shift):
    center = jnp.mean(rows, axis=1, keepdims=True)
    offsets = rows - center
    rstd = lax.rsqrt(jnp.mean(offsets * offsets, axis=1, keepdims=True) + NORM_EPS)
    normed = offsets * rstd
    return normed * gain + shift, normed, rstd


def norm_backward(grad, normed, rstd, gain):
    inner = grad * gain
    mean = jnp.mean(inner, axis=1, keepdims=True)
    slope = jnp.mean(inner * normed, axis=1, keepdims=True)
    return rstd * (inner - mean - normed * slope)


def gelu_terms(x):
    size = jnp.abs(x) * math.sqrt(0.5)
    t = 1.0 / (1.0 + 0.3275911 * size)
    bell = jnp.exp(-0.5 * x * x)
    poly = t * (0.254829592 + t * (-0.284496736 + t * (1.421413741 + t * (-1.453152027 + t * 1.061405429))))
    tail = 0.5 * poly * bell
    share = jnp.where(x >= 0.0, 1.0 - tail, tail)
    return x * share, share + x * bell * (1.0 / math.sqrt(2.0 * math.pi))


def unpack_all(packed_ref, pack):
    for share in range(pack.shape[0]):
        unpack(packed_ref, share, pack.at[share])


def split_pack(pack):
    return pack.at[:, :D], pack.at[:, D : 2 * D], pack.at[:, 2 * D :]


def block_kernel(
    length_ref, x_ref, packed_ref, small_ref, branch_ref, gain_ref, shift_ref, *rest,
):
    shares = small_ref.shape[0]
    a_refs = rest[:shares]
    block_ref, n1_ref, r1_ref, n2_ref, r2_ref, act_ref, slope_ref, sums_ref, pack = rest[shares:]
    tile = x_ref.shape[0]

    @pl.when(pl.program_id(0) == 0)
    def _():
        unpack_all(packed_ref, pack)

    wide_ref, narrow_ref, out_ref = split_pack(pack)
    x = x_ref[...].astype(f32)
    mixing = branch_ref[0:1, :]
    for s in range(shares):
        mixing = mixing + dot(a_refs[s][:, :96], out_ref[s, :96, :])
    middle, normed, rstd = norm_forward(x + mixing, gain_ref[0:1, :], shift_ref[0:1, :])
    n1_ref[...] = normed
    r1_ref[...] = rstd
    low = middle.astype(bf16)
    branch = branch_ref[1:2, :]
    width = D
    for s in range(shares):
        value, slope = gelu_terms(dot(low, wide_ref[s]) + small_ref[s, 4:5, :].astype(f32))
        value = value.astype(bf16)
        act_ref[:, s * width : (s + 1) * width] = value
        slope_ref[:, s * width : (s + 1) * width] = slope.astype(bf16)
        branch = branch + dot(value, narrow_ref[s])
    block, normed, rstd = norm_forward(middle + branch, gain_ref[1:2, :], shift_ref[1:2, :])
    n2_ref[...] = normed
    r2_ref[...] = rstd
    block_ref[...] = block.astype(bf16)
    position = lax.broadcasted_iota(jnp.int32, (tile, 1), 0) + pl.program_id(0) * tile
    kept = jnp.where(position < own_number(length_ref), 1.0, 0.0)
    row = lax.broadcasted_iota(jnp.int32, (8, x.shape[1]), 0)
    total = jnp.zeros((8, x.shape[1]), f32)
    for index, part in enumerate((x, mixing, branch)):
        total = jnp.where(row == index, jnp.sum(kept * part * part, axis=0, keepdims=True), total)

    @pl.when(pl.program_id(0) == 0)
    def _():
        sums_ref[...] = jnp.zeros_like(sums_ref)

    sums_ref[...] += total


def by_tile(tile, width):
    return pl.BlockSpec((tile, width), lambda i: (i, 0))


def block_forward(length, x, attended, packed, small, branch_bias, gain, shift):
    rows, width = x.shape
    tile = min(256, rows)
    shares = len(attended)
    units = shares * D
    row, column = by_tile(tile, width), by_tile(tile, 1)
    return pl.pallas_call(
        block_kernel,
        grid=(rows // tile,),
        in_specs=[
            SMEM, row, whole(packed.shape), whole(small.shape), whole(branch_bias.shape), whole(gain.shape), whole(shift.shape),
        ] + [by_tile(tile, 128)] * shares,
        out_specs=[row, row, column, row, column, by_tile(tile, units), by_tile(tile, units), whole((8, width))],
        out_shape=[
            jax.ShapeDtypeStruct((rows, width), bf16),
            jax.ShapeDtypeStruct((rows, width), f32),
            jax.ShapeDtypeStruct((rows, 1), f32),
            jax.ShapeDtypeStruct((rows, width), f32),
            jax.ShapeDtypeStruct((rows, 1), f32),
            jax.ShapeDtypeStruct((rows, units), bf16),
            jax.ShapeDtypeStruct((rows, units), bf16),
            jax.ShapeDtypeStruct((8, width), f32),
        ],
        scratch_shapes=[pltpu.VMEM((shares, 2 * D + 128, D), bf16)],
        compiler_params=pltpu.CompilerParams(vmem_limit_bytes=VMEM),
        cost_estimate=cost(20),
        name="block_forward",
    )(length, x, packed, small, branch_bias, gain, shift, *attended)


def block_backward_kernel(
    length_ref, d_ref, n1_ref, r1_ref, n2_ref, r2_ref, act_ref, slope_ref, packed_ref, gain_ref,
    shift_ref, kl_ref, square_ref, six_own_ref, six_ref, *rest,
):
    step = pl.program_id(0)
    pack = rest[-1]
    shares = pack.shape[0]
    a_refs, sum_ref, da_refs = rest[:shares], rest[shares], rest[shares + 1 : 2 * shares + 1]
    g_ref, tail_ref, vec_ref, g_sum, low_s, branch_s, pre_s, mix_s = rest[2 * shares + 1 : -1]
    tile, width = d_ref.shape
    units = D
    span = pl.ds(pl.multiple_of(step * tile, tile), tile)

    @pl.when(step == 0)
    def _():
        unpack_all(packed_ref, pack)
        vec_ref[...] = jnp.zeros_like(vec_ref)
        g_sum[...] = jnp.zeros_like(g_sum)

    wide_ref, narrow_ref, out_ref = split_pack(pack)

    def column(value):
        return jnp.sum(value, axis=0, keepdims=True)

    row = lax.broadcasted_iota(jnp.int32, (8, width), 0)
    d_block = d_ref[...]
    normed_two = n2_ref[...]
    d_two = norm_backward(d_block, normed_two, r2_ref[...], gain_ref[1:2, :])
    d_branch = d_two.astype(bf16)
    branch_s[span, :] = d_branch
    normed_one = n1_ref[...]
    low = (normed_one * gain_ref[0:1, :] + shift_ref[0:1, :]).astype(bf16)
    low_s[span, :] = low
    d_middle = d_two
    for s in range(shares):
        grad = dot(d_branch, narrow_ref[s], NT) * slope_ref[:, s * units : (s + 1) * units].astype(f32)
        grad = grad.astype(bf16)
        pre_s[span, s * units : (s + 1) * units] = grad
        g_sum[s : s + 1, :] += column(grad.astype(f32))
        d_middle = d_middle + dot(grad, wide_ref[s], NT)
    d_one = norm_backward(d_middle, normed_one, r1_ref[...], gain_ref[0:1, :])
    sum_ref[...] = d_one
    d_mixing = d_one.astype(bf16)
    mix_s[span, :] = d_mixing
    for s in range(shares):
        da_refs[s][...] = wide_rows(dot(d_mixing, out_ref[s, :96, :], NT)).astype(bf16)
    parts = (
        d_mixing.astype(f32), d_branch.astype(f32), d_middle * normed_one, d_block * normed_two, d_middle, d_block,
    )
    total = jnp.zeros((8, width), f32)
    for index, part in enumerate(parts):
        total = jnp.where(row == index, column(part), total)
    vec_ref[...] += total

    @pl.when(step == pl.num_programs(0) - 1)
    def _():
        for s in range(shares):
            part = slice(s * units, (s + 1) * units)
            own = slice(s * width, (s + 1) * width)
            g_ref[0:units, own] = dot(act_ref[:, part], branch_s[...], TN).astype(bf16)
            g_ref[units : 2 * units, own] = dot(low_s[...], pre_s[:, part], TN).astype(bf16)
            g_ref[2 * units : 2 * units + 96, own] = dot(a_refs[s][...], mix_s[...], TN)[:96].astype(bf16)
            g_ref[2 * units + 128 :, own] = six_own_ref[0] if s == 0 else six_ref[s - 1]
            first = lax.broadcasted_iota(jnp.int32, (32, units), 0) == 0
            g_ref[2 * units + 96 : 2 * units + 128, own] = jnp.where(first, g_sum[s : s + 1, :], 0.0).astype(bf16)
        scalars = [jnp.sum(kl_ref[...], axis=0, keepdims=True)]
        scalars += [jnp.sum(square_ref[i : i + 1, :], axis=1, keepdims=True) for i in range(3)]
        scalars += [jnp.broadcast_to(own_number(length_ref).astype(f32), (1, 1))]
        lane = lanes((8, width))
        total = vec_ref[...]
        for index, value in enumerate(scalars):
            total = jnp.where((row == 6) & (lane == index), value, total)
        total = jnp.concatenate([jnp.zeros((2, width), f32), total, jnp.zeros((6, width), f32)], axis=0)
        high = total.astype(bf16).astype(f32)
        tail_ref[:16, :] = high.astype(bf16)
        tail_ref[16:, :] = (total - high).astype(bf16)


def block_backward(
    length, d_block, n1, r1, n2, r2, act, slope, attended, packed, gain, shift, divergence, squares,
    six_own, six,
):
    rows, width = d_block.shape
    tile = min(256, rows)
    shares, units = len(attended), D
    row, column = by_tile(tile, width), by_tile(tile, 1)
    return pl.pallas_call(
        block_backward_kernel,
        grid=(rows // tile,),
        in_specs=[
            SMEM, row, row, column, row, column, whole(act.shape), by_tile(tile, shares * units), whole(packed.shape), whole(gain.shape), whole(shift.shape),
            whole(divergence.shape), whole(squares.shape), whole(six_own.shape), whole(six.shape),
        ] + [whole((rows, 128))] * shares,
        out_specs=[
            row, *[by_tile(tile, 128)] * shares, whole((2 * units + 448, shares * width)), whole((32, width)),
        ],
        out_shape=[
            jax.ShapeDtypeStruct((rows, width), f32),
            *[jax.ShapeDtypeStruct((rows, 128), bf16)] * shares,
            jax.ShapeDtypeStruct((2 * units + 448, shares * width), bf16),
            jax.ShapeDtypeStruct((32, width), bf16),
        ],
        scratch_shapes=[
            pltpu.VMEM((8, width), f32),
            pltpu.VMEM((8, units), f32),
            pltpu.VMEM((rows, width), bf16),
            pltpu.VMEM((rows, width), bf16),
            pltpu.VMEM((rows, shares * units), bf16),
            pltpu.VMEM((rows, width), bf16),
            pltpu.VMEM((shares, 2 * D + 128, D), bf16),
        ],
        compiler_params=pltpu.CompilerParams(vmem_limit_bytes=VMEM),
        cost_estimate=cost(25),
        name="block_backward",
    )(
        length, d_block, n1, r1, n2, r2, act, slope, packed, gain, shift, divergence, squares,
        six_own, six, *attended
    )


def after(value, *others):
    return lax.optimization_barrier((value,) + others)[0]


def shift_shares(value, by):
    shares = lax.axis_size("heads")
    return lax.ppermute(value, "heads", [((i + by) % shares, i) for i in range(shares)])


def exchange(value, bit):
    size = lax.axis_size("batch")
    return lax.ppermute(value, "batch", [(i, i ^ bit) for i in range(size)])


def merge_kernel(*refs, count):
    outs = refs[count:]
    total = refs[0][...].astype(f32)
    for ref in refs[1:count]:
        total = total + ref[...].astype(f32)
    end = total.shape[0] - 32
    sums = total[end : end + 16] + total[end + 16 :]
    if len(outs) == 2:
        put_turned(total[:end], outs[0])
        outs[1][...] = sums
    else:
        high = sums.astype(bf16).astype(f32)
        outs[0][:end, :] = total[:end].astype(bf16)
        outs[0][end : end + 16, :] = high.astype(bf16)
        outs[0][end + 16 :, :] = (sums - high).astype(bf16)


def put_turned(rows, out_ref):
    for part in range(3):
        out_ref[:, part, :] = rows[part * 96 : (part + 1) * 96].T


def merge(parts, last=False):
    rows, width = parts[0].shape
    if last:
        shape = [jax.ShapeDtypeStruct((width, 3, 96), f32), jax.ShapeDtypeStruct((16, width), f32)]
    else:
        shape = jax.ShapeDtypeStruct((rows, width), bf16)
    return pl.pallas_call(
        functools.partial(merge_kernel, count=len(parts)), out_shape=shape, cost_estimate=cost(1), name="merge",
        compiler_params=pltpu.CompilerParams(vmem_limit_bytes=VMEM),
    )(*parts)


def finish_mid_kernel(rows_ref, narrow_ref, wide_ref, out_ref, bias_ref, six_ref, sums_ref):
    units = narrow_ref.shape[0]
    narrow_ref[...] = rows_ref[:units, :].astype(f32)
    wide_ref[...] = rows_ref[units : 2 * units, :].astype(f32)
    out_ref[...] = rows_ref[2 * units : 2 * units + 96, :].astype(f32)
    bias_ref[...] = rows_ref[2 * units + 96 : 2 * units + 112, :].astype(f32)[:8]
    six = 2 * units + 128
    put_turned(rows_ref[six : six + 288, :].astype(f32), six_ref)
    sums_ref[...] = rows_ref[six + 288 : six + 304, :].astype(f32) + rows_ref[six + 304 :, :].astype(f32)


def finish_mid(rows):
    width = rows.shape[1]
    shapes = [(D, width), (D, width), (96, width), (8, width), (width, 3, 96), (16, width)]
    return pl.pallas_call(
        finish_mid_kernel, out_shape=[jax.ShapeDtypeStruct(s, f32) for s in shapes], cost_estimate=cost(1),
        name="finish_mid", compiler_params=pltpu.CompilerParams(vmem_limit_bytes=VMEM),
    )(rows)


def batch_sum(value):
    size = lax.axis_size("batch")
    bit = 1
    while bit < size:
        value = merge([value, exchange(value, bit)], last=2 * bit >= size)
        bit *= 2
    return value


def body(
    student_rows, teacher_rows, valid_length, split_point, project_five, bias_five, output_five, branch_bias,
    norm_gain, norm_bias, widen_weight, widen_bias, narrow_weight, project_six, bias_six, teacher_project,
    teacher_bias,
):
    shares = lax.axis_size("heads")
    batch = lax.axis_size("batch")
    place = lax.axis_index("batch")
    all_rows = shares * batch * HEADS
    x = student_rows[0]
    teacher = teacher_rows[0]

    def turned(weight):
        return jnp.transpose(weight, (1, 2, 0)).reshape(-1, weight.shape[0])

    def pad(rows, width):
        return jnp.pad(rows, ((0, 0), (0, width - rows.shape[1])))

    small = jnp.concatenate(
        [pad(bias_five, D), pad(bias_six, D), widen_bias[None], pad(teacher_bias, D), jnp.zeros((9, D), bf16)], axis=0
    )
    five = jnp.concatenate([turned(project_five), small], axis=0)

    def padded(rows):
        count = -(-rows.shape[0] // (16 * batch)) * 16
        return jnp.pad(rows, ((0, count * batch - rows.shape[0]), (0, 0)))

    def part_of(rows):
        rows = padded(rows)
        count = rows.shape[0] // batch
        return lax.dynamic_slice_in_dim(rows, place * count, count)

    def others(rows):
        return [shift_shares(rows, by) for by in range(1, shares)]

    half = five.shape[0] // 2
    core = lax.rem(place, 2)
    halves = jnp.stack(others(lax.dynamic_slice_in_dim(five, core * half, half)))
    mid = jnp.concatenate([widen_weight, narrow_weight, jnp.pad(output_five, ((0, 32), (0, 0)))], axis=0)
    mid_parts = others(part_of(mid))
    taught = turned(teacher_project)
    rest = jnp.concatenate([turned(project_six), taught[:, :D], taught[:, D:]], axis=0)

    first = attend_forward(valid_length, x, five)
    rest_parts = others(after(part_of(rest), first[5]))
    mid_parts = jnp.stack([after(p, first[5], halves) for p in mid_parts])
    halves = after(halves, first[5])
    swapped = exchange(halves, 1)
    low, high = jnp.where(core == 0, halves, swapped), jnp.where(core == 0, swapped, halves)
    fives = [five] + [jnp.concatenate([low[s], high[s]], axis=0) for s in range(shares - 1)]
    smalls = jnp.stack([w[288:] for w in fives])
    mid_all = lax.all_gather(mid_parts, "batch", axis=0)
    mid_all = jnp.concatenate([padded(mid).reshape(batch, 1, -1, D), mid_all], axis=1)
    heads = [first, attend_forward(valid_length, after(x, mid_parts), fives[1])]
    rest_parts = jnp.stack([after(p, heads[1][5]) for p in rest_parts])
    rest_all = lax.all_gather(rest_parts, "batch", axis=0)
    rest_all = jnp.concatenate([padded(rest).reshape(batch, 1, -1, D), rest_all], axis=1)
    for s in range(2, shares):
        heads.append(attend_forward(valid_length, after(x, rest_parts), fives[s]))
    attended = [h[5] for h in heads]
    block, n1, r1, n2, r2, act, slope, squares = block_forward(
        valid_length, x, attended, mid_all, smalls, branch_bias, norm_gain, norm_bias
    )
    d_block, g_six_own, divergence = relations(
        valid_length, split_point, block, teacher, rest, smalls[:1], all_rows
    )
    d_block, g_six, divergence = relations(
        valid_length, split_point, block, teacher, rest_all, smalls[1:], all_rows, (d_block, divergence)
    )
    result = block_backward(
        valid_length, d_block, n1, r1, n2, r2, act, slope, attended, mid_all, norm_gain, norm_bias,
        divergence, squares, g_six_own, g_six,
    )
    d_sum_one, d_attended, (g_both, tail) = result[0], result[1 : 1 + shares], result[1 + shares :]

    def to_owner(parts):
        return [parts[0]] + [shift_shares(parts[by], shares - by) for by in range(1, shares)]

    units = widen_weight.shape[1]
    both = lax.psum_scatter(g_both, "batch", scatter_dimension=0, tiled=True)

    grad_in = d_sum_one
    g_five = [None] * shares
    for s in list(range(1, shares)) + [0]:
        q, k, v, e, r, a = heads[s]
        g_five[s], grad_in = attend_backward(q, k, v, e, r, a, d_attended[s], x, fives[s], grad_in, tail)

    both = to_owner([both[:, s * D : (s + 1) * D] for s in range(shares)])
    both = sum(p.astype(f32) for p in both).astype(bf16)
    both = lax.all_gather(both, "batch", axis=0, tiled=True)
    grad_narrow, grad_wide, grad_out, wide_bias, grad_six, six_sums = finish_mid(both)
    grad_five, five_sums = batch_sum(merge(to_owner(g_five)))
    totals = five_sums[8]
    counted = totals[4] * D
    summary = jnp.concatenate([totals[:1], jnp.sqrt(totals[1:4] / counted)])
    return (
        block[None], grad_in[None], grad_five, five_sums[0:2, :96],
        grad_out, five_sums[2:4], five_sums[4:6], five_sums[6:8],
        grad_wide, wide_bias[0], grad_narrow, grad_six, six_sums[0:2, :96], summary,
    )


def solution(mesh):
    return jax.shard_map(
        body,
        mesh=mesh,
        in_specs=(
            P(("batch", "heads"), None, None),
            P(("batch", "heads"), None, None),
            P("batch"),
            P("batch"),
            P(None, None, "heads"),
            P(None, "heads"),
            P("heads", None),
            P(),
            P(),
            P(),
            P(None, "heads"),
            P("heads"),
            P("heads", None),
            P(None, None, "heads"),
            P(None, "heads"),
            P(None, None, "heads"),
            P(None, "heads"),
        ),
        out_specs=(
            P(("batch", "heads"), None, None),
            P(("batch", "heads"), None, None),
            P(None, None, "heads"),
            P(None, "heads"),
            P("heads", None),
            P(),
            P(),
            P(),
            P(None, "heads"),
            P("heads"),
            P("heads", None),
            P(None, None, "heads"),
            P(None, "heads"),
            P(),
        ),
        check_vma=False,
    )
```

```python
import functools
import math

import jax
import jax.numpy as jnp
from jax import lax
from jax.experimental import pallas as pl
from jax.experimental.pallas import tpu as pltpu
from jax.sharding import PartitionSpec as P

D = 384
HEADS = 12
HEAD_DIM = 32
TEACHER_HEAD_DIM = 64
PART = 3
TILE = 512
MID_ROWS = 2 * D + 128
STRIP = 16
NORM_EPS = 1e-12
MASKED = -1e30
SAFE = 64.0
LN2 = math.log(2.0)
STUDENT_SCALE = 1.0 / math.sqrt(HEAD_DIM)
STUDENT_LOG = math.log2(math.e) / math.sqrt(HEAD_DIM)
TEACHER_LOG = math.log2(math.e) / math.sqrt(TEACHER_HEAD_DIM)
VMEM = 56 * 2**20

f32 = jnp.float32
bf16 = jnp.bfloat16

NN = (((1,), (0,)), ((), ()))
NT = (((1,), (1,)), ((), ()))
TN = (((0,), (0,)), ((), ()))


def dot(left, right, dims=NN):
    return lax.dot_general(left, right, dims, preferred_element_type=f32)


def lanes(shape):
    return lax.broadcasted_iota(jnp.int32, shape, 1)


def wide_rows(rows):
    return jnp.concatenate([rows, jnp.zeros((rows.shape[0], 128 - rows.shape[1]), rows.dtype)], axis=1)


def in_head(lane, head, size=HEAD_DIM):
    return (lane >= head * size) & (lane < (head + 1) * size)


def split_terms(rows, head, size, extra):
    inside = in_head(lanes(rows.shape), head, size)
    high = rows.astype(bf16).astype(f32)
    first = jnp.where(inside, high, extra).astype(bf16)
    second = jnp.where(inside, rows - high, 0.0).astype(bf16)
    return jnp.concatenate([first, second], axis=1)


def own_number(ref):
    return ref[lax.axis_index("heads")]


def key_bias(rows, length):
    position = lax.broadcasted_iota(jnp.int32, (rows, 1), 0)
    return jnp.where(position < length, 0.0, MASKED)


def fold(tile, combine):
    total = tile[:, :128]
    for column in range(128, tile.shape[1], 128):
        total = combine(total, tile[:, column : column + 128])
    return total


def row_sum(tile):
    return jnp.sum(fold(tile, jnp.add), axis=1, keepdims=True)


def weave(first, second):
    done = 0
    for index, step in enumerate(second):
        while done < len(first) and done * len(second) < len(first) * (index + 1):
            first[done]()
            done += 1
        step()
    for step in first[done:]:
        step()


def step_place(step, tile, per_head):
    head = step // per_head
    return head, pl.ds(pl.multiple_of(lax.rem(step, per_head) * tile, tile), tile)


def run_pipeline(steps, logits, vector, back, enter=None):
    def stage(step, slot, before, after, second=False):
        if enter is not None:
            enter(step, slot, not before, second)
        ahead = logits(step + 1, 1 - slot) if after else []
        behind = back(step - 1, 1 - slot) if before else []
        weave(ahead + behind, vector(step, slot))

    for chunk in logits(jnp.int32(0), 0):
        chunk()
    stage(jnp.int32(0), 0, False, True)
    stage(jnp.int32(1), 1, True, True, second=True)

    def pair(index, carry):
        stage(2 * index + 2, 0, True, True)
        stage(2 * index + 3, 1, True, True)
        return carry

    lax.fori_loop(0, (steps - 4) // 2, pair, 0)
    stage(jnp.int32(steps - 2), 0, True, True)
    stage(jnp.int32(steps - 1), 1, True, False)
    for chunk in back(jnp.int32(steps - 1), 1):
        chunk()


def project_part(x, w_ref, index, bias):
    flat = dot(x, w_ref[index * 96 : (index + 1) * 96, :], NT)
    if bias is not None:
        flat = flat + bias
    return wide_rows(flat).astype(bf16)


def attend_forward_kernel(
    length_ref, x_ref, w_ref, q_ref, k_ref, v_ref, e_hbm, r_ref, o_ref, lhs, rhs, mixer, zs0, zs1, es0, es1, sems
):
    share = pl.program_id(0)
    w_ref, q_ref, k_ref, v_ref, r_ref, o_ref = (t.at[0] for t in (w_ref, q_ref, k_ref, v_ref, r_ref, o_ref))
    zs, es = (zs0, zs1), (es0, es1)
    rows = x_ref.shape[0]
    tile = zs0.shape[0]
    per_head = rows // tile
    steps = PART * per_head
    x = x_ref[...]
    small = w_ref[288:304, :].astype(f32)
    q = project_part(x, w_ref, 0, small[0:1, :96])
    k = project_part(x, w_ref, 1, None)
    v = project_part(x, w_ref, 2, small[1:2, :96])
    q_ref[...] = q
    k_ref[...] = k
    v_ref[...] = v
    lane = lanes((rows, 128))
    one = jnp.where(lane == 96, 1.0, 0.0)
    for head in range(PART):
        lhs[head] = jnp.where(in_head(lane, head), q.astype(f32), one).astype(bf16)
    rhs[...] = jnp.where(lane == 96, key_bias(rows, own_number(length_ref)), k.astype(f32)).astype(bf16)
    mixer[...] = jnp.where(lane == 96, 1.0, v.astype(f32)).astype(bf16)
    o_ref[...] = jnp.zeros_like(o_ref)
    r_ref[...] = jnp.zeros_like(r_ref)

    def out_copy(step, slot):
        head, span = step_place(step, tile, per_head)
        return pltpu.make_async_copy(es[slot], e_hbm.at[share, head, span], sems.at[slot])

    def logits(step, slot):
        head, span = step_place(step, tile, per_head)

        def chunk(start):
            zs[slot][:, start : start + 256] = dot(lhs[head, span, :], rhs[start : start + 256, :], NT)

        return [functools.partial(chunk, start) for start in range(0, rows, 256)]

    def vector(step, slot):
        def strip(start):
            z = zs[slot][start : start + STRIP, :]
            highest = jnp.max(fold(z, jnp.maximum), axis=1, keepdims=True)
            es[slot][start : start + STRIP, :] = jnp.exp2((z - highest) * STUDENT_LOG).astype(bf16)

        return [functools.partial(strip, start) for start in range(0, tile, STRIP)]

    def back(step, slot):
        head, span = step_place(step, tile, per_head)

        sums = []

        def part(start):
            sums.append(dot(es[slot][:, start : start + 256], mixer[start : start + 256, :]))

        def mix():
            mixed = functools.reduce(jnp.add, sums)
            inverse = 1.0 / mixed[:, 96:97]
            inside = in_head(lanes(mixed.shape), head)
            o_ref[span, :] = jnp.where(inside, mixed * inverse, o_ref[span, :].astype(f32)).astype(bf16)
            r_ref[span, :] = jnp.where(inside, inverse, r_ref[span, :])

        return [functools.partial(part, start) for start in range(0, rows, 256)] + [mix]

    def enter(step, slot, first, second):
        if not first:
            out_copy(step - 1, 1 - slot).start()
        if not (first or second):
            out_copy(step - 2, slot).wait()

    run_pipeline(steps, logits, vector, back, enter)
    out_copy(jnp.int32(steps - 1), 1).start()
    out_copy(jnp.int32(steps - 2), 0).wait()
    out_copy(jnp.int32(steps - 1), 1).wait()


def whole(shape):
    return pl.BlockSpec(shape, lambda *_: (0,) * len(shape))


SMEM = pl.BlockSpec(memory_space=pltpu.SMEM)
ANY = pl.BlockSpec(memory_space=pl.ANY)


def cost(micros):
    return pl.CostEstimate(flops=int(micros * 0.04e9), bytes_accessed=1024, transcendentals=0)


def attend_forward(length, x, w):
    rows, count = x.shape[0], w.shape[0]
    tile = min(TILE, rows // 2)
    narrow = jax.ShapeDtypeStruct((count, rows, 128), bf16)

    def share(shape):
        return pl.BlockSpec((1,) + shape, lambda s: (s,) + (0,) * len(shape))

    row = share((rows, 128))
    return pl.pallas_call(
        attend_forward_kernel,
        grid=(count,),
        in_specs=[SMEM, whole(x.shape), share(w.shape[1:])],
        out_specs=[row] * 3 + [ANY] + [row] * 2,
        out_shape=[
            narrow, narrow, narrow, jax.ShapeDtypeStruct((count, PART, rows, rows), bf16),
            jax.ShapeDtypeStruct((count, rows, 128), f32), narrow,
        ],
        scratch_shapes=[
            pltpu.VMEM((PART, rows, 128), bf16),
            pltpu.VMEM((rows, 128), bf16),
            pltpu.VMEM((rows, 128), bf16),
            pltpu.VMEM((tile, rows), f32),
            pltpu.VMEM((tile, rows), f32),
            pltpu.VMEM((tile, rows), bf16),
            pltpu.VMEM((tile, rows), bf16),
            pltpu.SemaphoreType.DMA((2,)),
        ],
        compiler_params=pltpu.CompilerParams(vmem_limit_bytes=VMEM),
        cost_estimate=cost(9 * count),
        name="attend_forward",
    )(length, x, w)


def attend_backward_kernel(
    q_ref, k_ref, v_ref, e_hbm, r_ref, a_ref, d_ref, x_hbm, w_hbm, acc_hbm, tail_ref, g_ref, in_ref,
    lhs, rhs, keys, qt, dt, zs0, zs1, gs0, gs1, dq, dkt, dvt, e_all, x_ref, w_ref, acc_ref, sems, late, *, share,
):
    q_ref, k_ref, v_ref, r_ref, a_ref = (t.at[0] for t in (q_ref, k_ref, v_ref, r_ref, a_ref))
    rows = q_ref.shape[0]
    zs, gs = (zs0, zs1), (gs0, gs1)
    tile = zs0.shape[0]
    per_head = rows // tile
    steps = PART * per_head

    def in_copy(step):
        head, span = step_place(step, tile, per_head)
        return pltpu.make_async_copy(e_hbm.at[share, head, span], e_all.at[head, span], sems.at[step])

    def begin(step, carry):
        in_copy(step).start()
        return carry

    lax.fori_loop(0, steps, begin, 0)
    late_copies = [
        pltpu.make_async_copy(source, target, late.at[index])
        for index, (source, target) in enumerate(((x_hbm, x_ref), (w_hbm.at[share], w_ref), (acc_hbm, acc_ref)))
    ]
    for copy in late_copies:
        copy.start()
    lane = lanes((rows, 128))
    grads = r_ref[...] * d_ref[...].astype(f32)
    shifts = grads * a_ref[...].astype(f32)
    k = k_ref[...].astype(f32)
    for head in range(PART):
        inside = in_head(lane, head)
        shift = -jnp.sum(jnp.where(inside, shifts, 0.0), axis=1, keepdims=True)
        high = shift.astype(bf16).astype(f32)
        lhs[head] = split_terms(
            grads, head, HEAD_DIM, jnp.where(lane == 96, high, jnp.where(lane == 97, shift - high, 0.0))
        )
        keys[head] = jnp.where(inside, k, 0.0).astype(bf16)
    rhs[:, :128] = jnp.where((lane == 96) | (lane == 97), 1.0, v_ref[...].astype(f32)).astype(bf16)
    rhs[:, 128:] = v_ref[...]
    qt[...] = q_ref[...].T
    dt[...] = grads.astype(bf16).T
    dq[...] = jnp.zeros_like(dq)
    dkt[...] = jnp.zeros_like(dkt)
    dvt[...] = jnp.zeros_like(dvt)

    def logits(step, slot):
        head, span = step_place(step, tile, per_head)

        def chunk(start):
            zs[slot][:, start : start + 256] = dot(lhs[head, span, :], rhs[start : start + 256, :], NT)

        return [functools.partial(chunk, start) for start in range(0, rows, 256)]

    def vector(step, slot):
        head, span = step_place(step, tile, per_head)
        base = lax.rem(step, per_head) * tile

        def strip(start):
            here = pl.ds(pl.multiple_of(base + start, STRIP), STRIP)
            weights = e_all[head, here, :].astype(f32)
            gs[slot][start : start + STRIP, :] = (weights * zs[slot][start : start + STRIP, :]).astype(bf16)

        return [functools.partial(strip, start) for start in range(0, tile, STRIP)]

    def back(step, slot):
        head, span = step_place(step, tile, per_head)
        own = pl.ds(pl.multiple_of(head * HEAD_DIM, HEAD_DIM), HEAD_DIM)

        def first():
            dq[span, :] += dot(gs[slot][...], keys[head])

        def second(start):
            part = slice(start, start + 256)
            dkt[own, part] += dot(qt[own, span], gs[slot][:, part])

        def third(start):
            part = slice(start, start + 256)
            dvt[own, part] += dot(dt[own, span], e_all[head, span, part])

        starts = range(0, rows, 256)
        return [first] + [functools.partial(second, s) for s in starts] + [functools.partial(third, s) for s in starts]

    run_pipeline(steps, logits, vector, back, lambda step, slot, first, second: in_copy(step).wait())
    for copy in late_copies:
        copy.wait()
    grads = (
        (dq[...] * STUDENT_SCALE).astype(bf16),
        (dkt[...] * STUDENT_SCALE).T.astype(bf16),
        dvt[...].T.astype(bf16),
    )
    weight_grads(grads, x_ref[...], g_ref, tail_ref[:16, :].astype(f32), tail_ref[16:, :].astype(f32))
    in_ref[...] = acc_ref[...] + spread(grads, w_ref)


def weight_grads(grads, x, g_ref, tail_high=0.0, tail_low=0.0):
    for index, grad in enumerate(grads):
        g_ref[index * 96 : (index + 1) * 96, :] = dot(grad, x, TN)[:96].astype(bf16)
    ones = jnp.ones((16, x.shape[0]), bf16)
    row = lax.broadcasted_iota(jnp.int32, (16, 128), 0)
    sums = jnp.where(row == 0, dot(ones, grads[0]), jnp.where(row == 1, dot(ones, grads[2]), 0.0))
    sums = jnp.concatenate([sums, jnp.zeros((16, x.shape[1] - 128), f32)], axis=1) + tail_high
    high = sums.astype(bf16).astype(f32)
    g_ref[288:304, :] = high.astype(bf16)
    g_ref[304:320, :] = (sums - high + tail_low).astype(bf16)


def spread(grads, w_ref):
    total = None
    for index, grad in enumerate(grads):
        term = dot(grad[:, :96], w_ref[index * 96 : (index + 1) * 96, :])
        total = term if total is None else total + term
    return total


def attend_backward(share, q, k, v, e, r, attended, d_attended, x, w, grad_in, tail):
    rows = x.shape[0]
    tile = min(TILE, rows // 2)
    row = pl.BlockSpec((1, rows, 128), lambda i: (share, 0, 0))
    return pl.pallas_call(
        functools.partial(attend_backward_kernel, share=share),
        grid=(1,),
        in_specs=[row, row, row, ANY, row, row, whole((rows, 128)), ANY, ANY, ANY, whole(tail.shape)],
        out_specs=[whole((320, x.shape[1])), whole(x.shape)],
        out_shape=[jax.ShapeDtypeStruct((320, x.shape[1]), bf16), jax.ShapeDtypeStruct(x.shape, f32)],
        scratch_shapes=[
            pltpu.VMEM((PART, rows, 256), bf16),
            pltpu.VMEM((rows, 256), bf16),
            pltpu.VMEM((PART, rows, 128), bf16),
            pltpu.VMEM((128, rows), bf16),
            pltpu.VMEM((128, rows), bf16),
            pltpu.VMEM((tile, rows), f32),
            pltpu.VMEM((tile, rows), f32),
            pltpu.VMEM((tile, rows), bf16),
            pltpu.VMEM((tile, rows), bf16),
            pltpu.VMEM((rows, 128), f32),
            pltpu.VMEM((128, rows), f32),
            pltpu.VMEM((128, rows), f32),
            pltpu.VMEM((PART, rows, rows), bf16),
            pltpu.VMEM(x.shape, bf16),
            pltpu.VMEM(w.shape[1:], bf16),
            pltpu.VMEM(x.shape, f32),
            pltpu.SemaphoreType.DMA((PART * (rows // tile),)),
            pltpu.SemaphoreType.DMA((3,)),
        ],
        compiler_params=pltpu.CompilerParams(vmem_limit_bytes=VMEM),
        cost_estimate=cost(10),
        name="attend_backward",
    )(q, k, v, e, r, attended, d_attended, x, w, grad_in, tail)


def relation_kernel(
    length_ref, split_ref, block_ref, teacher_ref, own_ref, packed_ref, small_ref, d_ref, g_ref, kl_ref, pack, ls, rs, lt, rt, keys, left_t, zs, zt, gs, left_sum, right_t, es_all, et_all, weight, grads_s,
    *, all_rows,
):
    rows = block_ref.shape[0]
    tile = zs.shape[1]
    per_head = rows // tile
    steps = PART * per_head
    length, split = own_number(length_ref), own_number(split_ref)
    block = block_ref[...]
    teacher = teacher_ref[...]
    @pl.when(pl.program_id(0) == 0)
    def _():
        pack[...] = own_ref[...]

    @pl.when(pl.program_id(0) > 0)
    def _():
        unpack(packed_ref, 0, pack, MID_ROWS)

    w_ref, g_ref = pack, g_ref.at[0]
    small = small_ref[0].astype(f32)
    lane = lanes((rows, 128))
    position = lax.broadcasted_iota(jnp.int32, (rows, 1), 0)
    bias = key_bias(rows, length)

    @pl.when(pl.program_id(0) == 0)
    def _():
        counted = (position < length) & (position != 0) & (position != split - 1) & (position != length - 1)
        share = 1.0 / ((length - 3).astype(f32) * float(all_rows))
        weight[...] = jnp.where(counted, share, 0.0)
        kl_ref[...] = jnp.zeros_like(kl_ref)
        d_ref[...] = jnp.zeros_like(d_ref)

    def teacher_part(index, b):
        start = 288 + index * 192
        flat = dot(teacher[:, :D], pack[start : start + 192, :], NT)
        flat = flat + dot(teacher[:, D:], pack[start + 576 : start + 768, :], NT)
        if b is not None:
            flat = flat + b
        flat = flat.astype(bf16)
        return flat[:, :128], wide_rows(flat[:, 128:])

    def largest(rows_low, size, blocks):
        square = rows_low.astype(f32)
        square = (square * square).astype(bf16)
        feature = lax.broadcasted_iota(jnp.int32, (128, 128), 0) // size
        same = feature == lanes((128, 128)) // size
        return jnp.max(dot(square, jnp.where(same, 1.0, 0.0).astype(bf16)), axis=0, keepdims=True)

    def relate(left, right, t_left, t_right, symmetric):
        left_sum[...] = jnp.zeros_like(left_sum)
        right_t[...] = jnp.zeros_like(right_t)
        left_t[...] = left.T
        left_wide = left.astype(f32) * STUDENT_LOG
        right_wide = right.astype(f32)
        one = jnp.where(lane == 96, 1.0, 0.0)
        if symmetric:
            one = jnp.where(lane == 97, bias, one)
        first = jnp.where(lane == 96, bias, right_wide)
        if symmetric:
            first = jnp.where(lane == 97, 1.0, first)
        rs[:, :128] = first.astype(bf16)
        rs[:, 128:] = right
        for head in range(PART):
            ls[head] = split_terms(left_wide, head, HEAD_DIM, one)
            keys[head] = jnp.where(in_head(lane, head), right_wide, 0.0).astype(bf16)
            own = head % 2
            spare = (1 - own) * TEACHER_HEAD_DIM
            one_t = jnp.where(lane == spare, 1.0, 0.0)
            wide_t = t_right[head // 2].astype(f32)
            first_t = jnp.where(lane == spare, bias, wide_t)
            if symmetric:
                one_t = jnp.where(lane == spare + 1, bias, one_t)
                first_t = jnp.where(lane == spare + 1, 1.0, first_t)
            lt[head] = split_terms(t_left[head // 2].astype(f32) * TEACHER_LOG, own, TEACHER_HEAD_DIM, one_t)
            rt[head, :, :128] = first_t.astype(bf16)
            rt[head, :, 128:] = t_right[head // 2]
        student_bound = largest(left, HEAD_DIM, 4) * largest(right, HEAD_DIM, 4) * STUDENT_LOG**2
        bound = jnp.max(student_bound)
        for part in range(2):
            t_bound = largest(t_left[part], TEACHER_HEAD_DIM, 2) * largest(t_right[part], TEACHER_HEAD_DIM, 2)
            bound = jnp.maximum(bound, jnp.max(t_bound * TEACHER_LOG**2))
        near = bound < SAFE * SAFE

        @pl.when(near)
        def _():
            if symmetric:
                symmetric_pass()
            else:
                plain_pass()

        @pl.when(jnp.logical_not(near))
        def _():
            for head in range(PART):
                own = head % 2
                spare = (1 - own) * TEACHER_HEAD_DIM
                ls[head] = split_terms(left.astype(f32), head, HEAD_DIM, jnp.where(lane == 96, 1.0, 0.0))
                lt[head] = split_terms(
                    t_left[head // 2].astype(f32), own, TEACHER_HEAD_DIM, jnp.where(lane == spare, 1.0, 0.0)
                )
            shifted_pass()

    def plain_pass():
        def logits(step, slot):
            head, span = step_place(step, tile, per_head)

            def student(start):
                zs[slot, :, start : start + 256] = dot(ls[head, span, :], rs[start : start + 256, :], NT)

            def taught(start):
                zt[slot, :, start : start + 256] = dot(lt[head, span, :], rt[head, start : start + 256, :], NT)

            chunks = []
            for start in range(0, rows, 256):
                chunks += [functools.partial(student, start), functools.partial(taught, start)]
            return chunks

        def vector(step, slot):
            base = lax.rem(step, per_head) * tile

            def strip(start):
                here = pl.ds(pl.multiple_of(base + start, STRIP), STRIP)
                student = zs[slot, start : start + STRIP, :]
                taught = zt[slot, start : start + STRIP, :]
                es = jnp.exp2(student)
                et = jnp.exp2(taught)
                sum_s = row_sum(es)
                sum_t = row_sum(et)
                cross = row_sum(et * (taught - student))
                w = weight[here, :]
                inverse = 1.0 / sum_t
                kl_ref[here, :] += w * (LN2 * cross * inverse + jnp.log(sum_s) - jnp.log(sum_t))
                gs[slot, start : start + STRIP, :] = (es * (w / sum_s) - et * (w * inverse)).astype(bf16)

            return [functools.partial(strip, start) for start in range(0, tile, STRIP)]

        run_pipeline(steps, logits, vector, grad_products)

    def grad_products(step, slot):
        head, span = step_place(step, tile, per_head)
        own = pl.ds(pl.multiple_of(head * HEAD_DIM, HEAD_DIM), HEAD_DIM)

        def first():
            left_sum[span, :] += dot(gs[slot], keys[head])

        def second(start):
            part = slice(start, start + 256)
            right_t[own, part] += dot(left_t[own, span], gs[slot, :, part])

        return [first] + [functools.partial(second, start) for start in range(0, rows, 256)]

    def shifted_pass():
        def one(step, carry):
            head, span = step_place(step, tile, per_head)
            student = dot(ls[head, span, :], rs[...], NT)
            student = (student - jnp.max(student, axis=1, keepdims=True)) * STUDENT_LOG
            taught = dot(lt[head, span, :], rt[head], NT)
            taught = (taught - jnp.max(taught, axis=1, keepdims=True)) * TEACHER_LOG
            es = jnp.exp2(student)
            et = jnp.exp2(taught)
            sum_s = jnp.sum(es, axis=1, keepdims=True)
            sum_t = jnp.sum(et, axis=1, keepdims=True)
            cross = jnp.sum(et * (taught - student), axis=1, keepdims=True)
            w = weight[span, :]
            row = LN2 * cross / sum_t + jnp.log(sum_s) - jnp.log(sum_t)
            kl_ref[span, :] += jnp.where(w > 0.0, w * row, 0.0)
            gs[0] = (es * (w / sum_s) - et * (w / sum_t)).astype(bf16)
            for chunk in grad_products(step, 0):
                chunk()
            return carry

        lax.fori_loop(0, steps, one, 0)

    def symmetric_pass():
        size = min(256, rows)
        count = rows // size

        def column(row):
            return jnp.broadcast_to(row, (128, size)).T[:, :1]

        def row_of(value):
            return jnp.broadcast_to(value, (size, 128)).T[:1, :]

        def one_head(head, carry):
            own = pl.ds(pl.multiple_of(head * HEAD_DIM, HEAD_DIM), HEAD_DIM)
            by_row = []
            by_column = [[jnp.zeros((1, size), f32)] * 3 for _ in range(count)]
            for i in range(count):
                here = slice(i * size, (i + 1) * size)
                after = slice(i * size, rows)
                student = dot(ls[head, here, :], rs[after, :], NT)
                taught = dot(lt[head, here, :], rt[head, after, :], NT)
                es = jnp.exp2(student)
                et = jnp.exp2(taught)
                cross = et * (taught - student)
                es_all[here, after] = es
                et_all[here, after] = et
                by_row.append([row_sum(t) for t in (es, et, cross)])
                for j in range(i + 1, count):
                    part = slice((j - i) * size, (j - i + 1) * size)
                    by_column[j] = [
                        c + jnp.sum(t[:, part], axis=0, keepdims=True)
                        for c, t in zip(by_column[j], (es, et, cross))
                    ]
            a, b = [], []
            for i in range(count):
                here = slice(i * size, (i + 1) * size)
                sum_s, sum_t, cross = (r + column(c) for r, c in zip(by_row[i], by_column[i]))
                w = weight[here, :]
                sum_s = jnp.where(w > 0.0, sum_s, 1.0)
                sum_t = jnp.where(w > 0.0, sum_t, 1.0)
                inverse = 1.0 / sum_t
                kl_ref[here, :] += w * (LN2 * cross * inverse + jnp.log(sum_s) - jnp.log(sum_t))
                a.append(w / sum_s)
                b.append(w * inverse)
            a_row = jnp.concatenate([row_of(t) for t in a], axis=1)
            b_row = jnp.concatenate([row_of(t) for t in b], axis=1)
            for i in range(count):
                here = slice(i * size, (i + 1) * size)
                after = slice(i * size, rows)
                both = es_all[here, after] * (a[i] + a_row[:, after])
                both = (both - et_all[here, after] * (b[i] + b_row[:, after])).astype(bf16)
                left_sum[here, :] += dot(both, keys[head, after, :])
                if i + 1 < count:
                    right_t[own, (i + 1) * size :] += dot(left_t[own, here], both[:, size:])
            return carry

        lax.fori_loop(0, PART, one_head, 0)

    q = project_part(block, w_ref, 0, small[2:3, :96])
    k = project_part(block, w_ref, 1, None)
    tq = teacher_part(0, small[5:6, :192])
    tk = teacher_part(1, None)
    relate(q, k, tq, tk, False)
    grads_s[0] = (left_sum[...] * STUDENT_SCALE).astype(bf16)
    grads_s[1] = (right_t[...] * STUDENT_SCALE).T.astype(bf16)
    v = project_part(block, w_ref, 2, small[3:4, :96])
    tv = teacher_part(2, small[6:7, :192])
    relate(v, v, tv, tv, True)
    grads_s[2] = ((left_sum[...] + right_t[...].T) * STUDENT_SCALE).astype(bf16)
    grads = tuple(grads_s[i] for i in range(3))
    weight_grads(grads, block, g_ref)
    d_ref[...] += spread(grads, w_ref)


def part_rows(rows, batch):
    return -(-rows // (16 * batch)) * 16


def unpack(packed_ref, share, target, before=0):
    rows, batch = target.shape[0], packed_ref.shape[0]
    part = part_rows(rows, batch)
    offset = part_rows(before, batch)
    for start in range(0, rows, part):
        size = min(part, rows - start)
        target[start : start + size, :] = packed_ref[start // part, share, offset : offset + size, :]


def relations(length, split, block, teacher, own, packed, small, all_rows):
    rows = block.shape[0]
    tile = min(TILE, rows // 2)
    shares = small.shape[0]

    def share(shape):
        return pl.BlockSpec((1,) + shape[1:], lambda s: (s,) + (0,) * (len(shape) - 1))

    place = pl.BlockSpec((packed.shape[0], 1) + packed.shape[2:], lambda s: (0, jnp.maximum(s - 1, 0), 0, 0))
    return pl.pallas_call(
        functools.partial(relation_kernel, all_rows=all_rows),
        grid=(shares,),
        in_specs=[
            SMEM, SMEM, whole(block.shape), whole(teacher.shape), whole(own.shape), place, share(small.shape),
        ],
        out_specs=[whole(block.shape), share((shares, 320, D)), whole((rows, 1))],
        out_shape=[
            jax.ShapeDtypeStruct(block.shape, f32),
            jax.ShapeDtypeStruct((shares, 320, D), bf16),
            jax.ShapeDtypeStruct((rows, 1), f32),
        ],
        scratch_shapes=[
            pltpu.VMEM((1440, D), bf16),
            pltpu.VMEM((PART, rows, 256), bf16),
            pltpu.VMEM((rows, 256), bf16),
            pltpu.VMEM((PART, rows, 256), bf16),
            pltpu.VMEM((PART, rows, 256), bf16),
            pltpu.VMEM((PART, rows, 128), bf16),
            pltpu.VMEM((128, rows), bf16),
            pltpu.VMEM((2, tile, rows), f32),
            pltpu.VMEM((2, tile, rows), f32),
            pltpu.VMEM((2, tile, rows), bf16),
            pltpu.VMEM((rows, 128), f32),
            pltpu.VMEM((128, rows), f32),
            pltpu.VMEM((rows, rows), f32),
            pltpu.VMEM((rows, rows), f32),
            pltpu.VMEM((rows, 1), f32),
            pltpu.VMEM((3, rows, 128), bf16),
        ],
        compiler_params=pltpu.CompilerParams(vmem_limit_bytes=VMEM),
        cost_estimate=cost(30 * shares),
        name="relations",
    )(length, split, block, teacher, own, packed, small)


def norm_forward(rows, gain, shift):
    center = jnp.mean(rows, axis=1, keepdims=True)
    offsets = rows - center
    rstd = lax.rsqrt(jnp.mean(offsets * offsets, axis=1, keepdims=True) + NORM_EPS)
    normed = offsets * rstd
    return normed * gain + shift, normed, rstd


def norm_backward(grad, normed, rstd, gain):
    inner = grad * gain
    mean = jnp.mean(inner, axis=1, keepdims=True)
    slope = jnp.mean(inner * normed, axis=1, keepdims=True)
    return rstd * (inner - mean - normed * slope)


def gelu_terms(x):
    size = jnp.abs(x) * math.sqrt(0.5)
    t = 1.0 / (1.0 + 0.3275911 * size)
    bell = jnp.exp(-0.5 * x * x)
    poly = t * (0.254829592 + t * (-0.284496736 + t * (1.421413741 + t * (-1.453152027 + t * 1.061405429))))
    tail = 0.5 * poly * bell
    share = jnp.where(x >= 0.0, 1.0 - tail, tail)
    return x * share, share + x * bell * (1.0 / math.sqrt(2.0 * math.pi))


def unpack_all(own_ref, packed_ref, pack):
    pack[0] = own_ref[...]
    for share in range(1, pack.shape[0]):
        unpack(packed_ref, share - 1, pack.at[share])


def mid_part(packed):
    return whole(packed.shape[:2] + (part_rows(MID_ROWS, packed.shape[0]), packed.shape[3]))


def split_pack(pack):
    return pack.at[:, :D], pack.at[:, D : 2 * D], pack.at[:, 2 * D :]


def block_kernel(
    length_ref, x_ref, own_ref, packed_ref, small_ref, branch_ref, gain_ref, shift_ref, first_ref, other_ref,
    block_ref, n1_ref, r1_ref, n2_ref, r2_ref, act_ref, slope_ref, sums_ref, pack,
):
    shares = small_ref.shape[0]
    a_refs = [first_ref.at[0]] + [other_ref.at[s] for s in range(shares - 1)]
    tile = x_ref.shape[0]

    @pl.when(pl.program_id(0) == 0)
    def _():
        unpack_all(own_ref, packed_ref, pack)

    wide_ref, narrow_ref, out_ref = split_pack(pack)
    x = x_ref[...].astype(f32)
    mixing = branch_ref[0:1, :]
    for s in range(shares):
        mixing = mixing + dot(a_refs[s][:, :96], out_ref[s, :96, :])
    middle, normed, rstd = norm_forward(x + mixing, gain_ref[0:1, :], shift_ref[0:1, :])
    n1_ref[...] = normed
    r1_ref[...] = rstd
    low = middle.astype(bf16)
    branch = branch_ref[1:2, :]
    width = D
    for s in range(shares):
        value, slope = gelu_terms(dot(low, wide_ref[s]) + small_ref[s, 4:5, :].astype(f32))
        value = value.astype(bf16)
        act_ref[:, s * width : (s + 1) * width] = value
        slope_ref[:, s * width : (s + 1) * width] = slope.astype(bf16)
        branch = branch + dot(value, narrow_ref[s])
    block, normed, rstd = norm_forward(middle + branch, gain_ref[1:2, :], shift_ref[1:2, :])
    n2_ref[...] = normed
    r2_ref[...] = rstd
    block_ref[...] = block.astype(bf16)
    position = lax.broadcasted_iota(jnp.int32, (tile, 1), 0) + pl.program_id(0) * tile
    kept = jnp.where(position < own_number(length_ref), 1.0, 0.0)
    row = lax.broadcasted_iota(jnp.int32, (8, x.shape[1]), 0)
    total = jnp.zeros((8, x.shape[1]), f32)
    for index, part in enumerate((x, mixing, branch)):
        total = jnp.where(row == index, jnp.sum(kept * part * part, axis=0, keepdims=True), total)

    @pl.when(pl.program_id(0) == 0)
    def _():
        sums_ref[...] = jnp.zeros_like(sums_ref)

    sums_ref[...] += total


def by_tile(tile, width):
    return pl.BlockSpec((tile, width), lambda i: (i, 0))


def block_forward(length, x, attended, own, packed, small, branch_bias, gain, shift):
    rows, width = x.shape
    tile = min(256, rows)
    shares = small.shape[0]
    units = shares * D
    row, column = by_tile(tile, width), by_tile(tile, 1)
    return pl.pallas_call(
        block_kernel,
        grid=(rows // tile,),
        in_specs=[
            SMEM, row, whole(own.shape), mid_part(packed), whole(small.shape), whole(branch_bias.shape), whole(gain.shape), whole(shift.shape),
        ] + [pl.BlockSpec((a.shape[0], tile, 128), lambda i: (0, i, 0)) for a in attended],
        out_specs=[row, row, column, row, column, by_tile(tile, units), by_tile(tile, units), whole((8, width))],
        out_shape=[
            jax.ShapeDtypeStruct((rows, width), bf16),
            jax.ShapeDtypeStruct((rows, width), f32),
            jax.ShapeDtypeStruct((rows, 1), f32),
            jax.ShapeDtypeStruct((rows, width), f32),
            jax.ShapeDtypeStruct((rows, 1), f32),
            jax.ShapeDtypeStruct((rows, units), bf16),
            jax.ShapeDtypeStruct((rows, units), bf16),
            jax.ShapeDtypeStruct((8, width), f32),
        ],
        scratch_shapes=[pltpu.VMEM((shares, 2 * D + 128, D), bf16)],
        compiler_params=pltpu.CompilerParams(vmem_limit_bytes=VMEM),
        cost_estimate=cost(20),
        name="block_forward",
    )(length, x, own, packed, small, branch_bias, gain, shift, *attended)


def block_backward_kernel(
    length_ref, d_ref, n1_ref, r1_ref, n2_ref, r2_ref, act_ref, slope_ref, own_ref, packed_ref, gain_ref,
    shift_ref, kl_ref, square_ref, six_ref, first_ref, other_ref, *rest,
):
    step = pl.program_id(0)
    pack = rest[-1]
    shares = pack.shape[0]
    a_refs = [first_ref.at[0]] + [other_ref.at[s] for s in range(shares - 1)]
    sum_ref, da_refs = rest[0], rest[1 : shares + 1]
    g_ref, tail_ref, vec_ref, g_sum, low_s, branch_s, pre_s, mix_s = rest[shares + 1 : -1]
    tile, width = d_ref.shape
    units = D
    span = pl.ds(pl.multiple_of(step * tile, tile), tile)

    @pl.when(step == 0)
    def _():
        unpack_all(own_ref, packed_ref, pack)
        vec_ref[...] = jnp.zeros_like(vec_ref)
        g_sum[...] = jnp.zeros_like(g_sum)

    wide_ref, narrow_ref, out_ref = split_pack(pack)

    def column(value):
        return jnp.sum(value, axis=0, keepdims=True)

    row = lax.broadcasted_iota(jnp.int32, (8, width), 0)
    d_block = d_ref[...]
    normed_two = n2_ref[...]
    d_two = norm_backward(d_block, normed_two, r2_ref[...], gain_ref[1:2, :])
    d_branch = d_two.astype(bf16)
    branch_s[span, :] = d_branch
    normed_one = n1_ref[...]
    low = (normed_one * gain_ref[0:1, :] + shift_ref[0:1, :]).astype(bf16)
    low_s[span, :] = low
    d_middle = d_two
    for s in range(shares):
        grad = dot(d_branch, narrow_ref[s], NT) * slope_ref[:, s * units : (s + 1) * units].astype(f32)
        grad = grad.astype(bf16)
        pre_s[span, s * units : (s + 1) * units] = grad
        g_sum[s : s + 1, :] += column(grad.astype(f32))
        d_middle = d_middle + dot(grad, wide_ref[s], NT)
    d_one = norm_backward(d_middle, normed_one, r1_ref[...], gain_ref[0:1, :])
    sum_ref[...] = d_one
    d_mixing = d_one.astype(bf16)
    mix_s[span, :] = d_mixing
    for s in range(shares):
        da_refs[s][...] = wide_rows(dot(d_mixing, out_ref[s, :96, :], NT)).astype(bf16)
    parts = (
        d_mixing.astype(f32), d_branch.astype(f32), d_middle * normed_one, d_block * normed_two, d_middle, d_block,
    )
    total = jnp.zeros((8, width), f32)
    for index, part in enumerate(parts):
        total = jnp.where(row == index, column(part), total)
    vec_ref[...] += total

    @pl.when(step == pl.num_programs(0) - 1)
    def _():
        for s in range(shares):
            part = slice(s * units, (s + 1) * units)
            own = slice(s * width, (s + 1) * width)
            g_ref[0:units, own] = dot(act_ref[:, part], branch_s[...], TN).astype(bf16)
            g_ref[units : 2 * units, own] = dot(low_s[...], pre_s[:, part], TN).astype(bf16)
            g_ref[2 * units : 2 * units + 96, own] = dot(a_refs[s][...], mix_s[...], TN)[:96].astype(bf16)
            g_ref[2 * units + 128 :, own] = six_ref[s]
            first = lax.broadcasted_iota(jnp.int32, (32, units), 0) == 0
            g_ref[2 * units + 96 : 2 * units + 128, own] = jnp.where(first, g_sum[s : s + 1, :], 0.0).astype(bf16)
        scalars = [jnp.sum(kl_ref[...], axis=0, keepdims=True)]
        scalars += [jnp.sum(square_ref[i : i + 1, :], axis=1, keepdims=True) for i in range(3)]
        scalars += [jnp.broadcast_to(own_number(length_ref).astype(f32), (1, 1))]
        lane = lanes((8, width))
        total = vec_ref[...]
        for index, value in enumerate(scalars):
            total = jnp.where((row == 6) & (lane == index), value, total)
        total = jnp.concatenate([jnp.zeros((2, width), f32), total, jnp.zeros((6, width), f32)], axis=0)
        high = total.astype(bf16).astype(f32)
        tail_ref[:16, :] = high.astype(bf16)
        tail_ref[16:, :] = (total - high).astype(bf16)


def block_backward(
    length, d_block, n1, r1, n2, r2, act, slope, attended, own, packed, gain, shift, divergence, squares, six,
):
    rows, width = d_block.shape
    tile = min(256, rows)
    shares, units = six.shape[0], D
    row, column = by_tile(tile, width), by_tile(tile, 1)
    return pl.pallas_call(
        block_backward_kernel,
        grid=(rows // tile,),
        in_specs=[
            SMEM, row, row, column, row, column, whole(act.shape), by_tile(tile, shares * units), whole(own.shape), mid_part(packed), whole(gain.shape), whole(shift.shape),
            whole(divergence.shape), whole(squares.shape), whole(six.shape),
        ] + [whole(a.shape) for a in attended],
        out_specs=[
            row, *[by_tile(tile, 128)] * shares, whole((2 * units + 448, shares * width)), whole((32, width)),
        ],
        out_shape=[
            jax.ShapeDtypeStruct((rows, width), f32),
            *[jax.ShapeDtypeStruct((rows, 128), bf16)] * shares,
            jax.ShapeDtypeStruct((2 * units + 448, shares * width), bf16),
            jax.ShapeDtypeStruct((32, width), bf16),
        ],
        scratch_shapes=[
            pltpu.VMEM((8, width), f32),
            pltpu.VMEM((8, units), f32),
            pltpu.VMEM((rows, width), bf16),
            pltpu.VMEM((rows, width), bf16),
            pltpu.VMEM((rows, shares * units), bf16),
            pltpu.VMEM((rows, width), bf16),
            pltpu.VMEM((shares, 2 * D + 128, D), bf16),
        ],
        compiler_params=pltpu.CompilerParams(vmem_limit_bytes=VMEM),
        cost_estimate=cost(25),
        name="block_backward",
    )(
        length, d_block, n1, r1, n2, r2, act, slope, own, packed, gain, shift, divergence, squares, six, *attended
    )


def after(value, *others):
    return lax.optimization_barrier((value,) + others)[0]


def shift_shares(value, by):
    shares = lax.axis_size("heads")
    return lax.ppermute(value, "heads", [((i + by) % shares, i) for i in range(shares)])


def exchange(value, bit):
    size = lax.axis_size("batch")
    return lax.ppermute(value, "batch", [(i, i ^ bit) for i in range(size)])


def merge_kernel(*refs, count):
    outs = refs[count:]
    total = refs[0][...].astype(f32)
    for ref in refs[1:count]:
        total = total + ref[...].astype(f32)
    end = total.shape[0] - 32
    sums = total[end : end + 16] + total[end + 16 :]
    if len(outs) == 2:
        put_turned(total[:end], outs[0])
        outs[1][...] = sums
    else:
        high = sums.astype(bf16).astype(f32)
        outs[0][:end, :] = total[:end].astype(bf16)
        outs[0][end : end + 16, :] = high.astype(bf16)
        outs[0][end + 16 :, :] = (sums - high).astype(bf16)


def put_turned(rows, out_ref):
    for part in range(3):
        out_ref[:, part, :] = rows[part * 96 : (part + 1) * 96].T


def merge(parts, last=False):
    rows, width = parts[0].shape
    if last:
        shape = [jax.ShapeDtypeStruct((width, 3, 96), f32), jax.ShapeDtypeStruct((16, width), f32)]
    else:
        shape = jax.ShapeDtypeStruct((rows, width), bf16)
    return pl.pallas_call(
        functools.partial(merge_kernel, count=len(parts)), out_shape=shape, cost_estimate=cost(1), name="merge",
        compiler_params=pltpu.CompilerParams(vmem_limit_bytes=VMEM),
    )(*parts)


def finish_mid_kernel(rows_ref, narrow_ref, wide_ref, out_ref, bias_ref, six_ref, sums_ref):
    units = narrow_ref.shape[0]
    narrow_ref[...] = rows_ref[:units, :].astype(f32)
    wide_ref[...] = rows_ref[units : 2 * units, :].astype(f32)
    out_ref[...] = rows_ref[2 * units : 2 * units + 96, :].astype(f32)
    bias_ref[...] = rows_ref[2 * units + 96 : 2 * units + 112, :].astype(f32)[:8]
    six = 2 * units + 128
    put_turned(rows_ref[six : six + 288, :].astype(f32), six_ref)
    sums_ref[...] = rows_ref[six + 288 : six + 304, :].astype(f32) + rows_ref[six + 304 :, :].astype(f32)


def finish_mid(rows):
    width = rows.shape[1]
    shapes = [(D, width), (D, width), (96, width), (8, width), (width, 3, 96), (16, width)]
    return pl.pallas_call(
        finish_mid_kernel, out_shape=[jax.ShapeDtypeStruct(s, f32) for s in shapes], cost_estimate=cost(1),
        name="finish_mid", compiler_params=pltpu.CompilerParams(vmem_limit_bytes=VMEM),
    )(rows)


def body(
    student_rows, teacher_rows, valid_length, split_point, project_five, bias_five, output_five, branch_bias,
    norm_gain, norm_bias, widen_weight, widen_bias, narrow_weight, project_six, bias_six, teacher_project,
    teacher_bias,
):
    shares = lax.axis_size("heads")
    batch = lax.axis_size("batch")
    place = lax.axis_index("batch")
    all_rows = shares * batch * HEADS
    x = student_rows[0]
    teacher = teacher_rows[0]

    def turned(weight):
        return jnp.transpose(weight, (1, 2, 0)).reshape(-1, weight.shape[0])

    def pad(rows, width):
        return jnp.pad(rows, ((0, 0), (0, width - rows.shape[1])))

    small = jnp.concatenate(
        [pad(bias_five, D), pad(bias_six, D), widen_bias[None], pad(teacher_bias, D), jnp.zeros((9, D), bf16)], axis=0
    )
    five = jnp.concatenate([turned(project_five), small], axis=0)

    def part_of(rows):
        count = part_rows(rows.shape[0], batch)
        rows = jnp.pad(rows, ((0, count * batch - rows.shape[0]), (0, 0)))
        return lax.dynamic_slice_in_dim(rows, place * count, count)

    def others(rows):
        return [shift_shares(rows, by) for by in range(1, shares)]

    half = five.shape[0] // 2
    core = lax.rem(place, 2)
    halves = others(lax.dynamic_slice_in_dim(five, core * half, half))
    mid = jnp.concatenate([widen_weight, narrow_weight, jnp.pad(output_five, ((0, 32), (0, 0)))], axis=0)
    taught = turned(teacher_project)
    rest = jnp.concatenate([turned(project_six), taught[:, :D], taught[:, D:]], axis=0)
    parts = others(after(jnp.concatenate([part_of(mid), part_of(rest)], axis=0), five))

    first = attend_forward(valid_length, x, five[None])
    halves = jnp.stack([after(p, first[5]) for p in halves])
    swapped = exchange(halves, 1)
    parts = jnp.stack([after(p, first[5], halves) for p in parts])
    parts_all = lax.all_gather(parts, "batch", axis=0)
    low, high = jnp.where(core == 0, halves, swapped), jnp.where(core == 0, swapped, halves)
    fives = jnp.concatenate([low, high], axis=1)
    smalls = jnp.concatenate([five[None, 288:], fives[:, 288:]], axis=0)
    other = attend_forward(valid_length, after(x, parts), fives)
    attended = (first[5], other[5])
    block, n1, r1, n2, r2, act, slope, squares = block_forward(
        valid_length, x, attended, mid, parts_all, smalls, branch_bias, norm_gain, norm_bias
    )
    d_block, g_six, divergence = relations(
        valid_length, split_point, block, teacher, rest, parts_all, smalls, all_rows
    )
    result = block_backward(
        valid_length, d_block, n1, r1, n2, r2, act, slope, attended, mid, parts_all, norm_gain, norm_bias,
        divergence, squares, g_six,
    )
    d_sum_one, d_attended, (g_both, tail) = result[0], result[1 : 1 + shares], result[1 + shares :]

    def to_owner(parts):
        return [parts[0]] + [shift_shares(parts[by], shares - by) for by in range(1, shares)]

    units = widen_weight.shape[1]
    both = lax.psum_scatter(g_both, "batch", scatter_dimension=0, tiled=True)

    grad_in = d_sum_one
    g_five = [None] * shares
    for s in list(range(1, shares)) + [0]:
        q, k, v, e, r, a = other if s else first
        rows, w = after(x, *g_five[1 : shares - 1]) if s == 0 else x, fives if s else five[None]
        grad, grad_in = attend_backward(max(s - 1, 0), q, k, v, e, r, a, d_attended[s], rows, w, grad_in, tail)
        g_five[s] = shift_shares(grad, shares - s) if s else grad

    five_sum = merge(g_five)
    both = after(both, five_sum)
    both = to_owner([both[:, s * D : (s + 1) * D] for s in range(shares)])
    bit = 1
    while 2 * bit < batch:
        five_sum = merge([five_sum, exchange(five_sum, bit)])
        if bit == 1:
            both = [after(p, five_sum) for p in both]
        bit *= 2
    both = sum(p.astype(f32) for p in both).astype(bf16)
    both = lax.all_gather(both, "batch", axis=0, tiled=True)
    grad_five, five_sums = merge([five_sum, exchange(five_sum, bit)], last=True)
    grad_narrow, grad_wide, grad_out, wide_bias, grad_six, six_sums = finish_mid(both)
    totals = five_sums[8]
    counted = totals[4] * D
    summary = jnp.concatenate([totals[:1], jnp.sqrt(totals[1:4] / counted)])
    return (
        block[None], grad_in[None], grad_five, five_sums[0:2, :96],
        grad_out, five_sums[2:4], five_sums[4:6], five_sums[6:8],
        grad_wide, wide_bias[0], grad_narrow, grad_six, six_sums[0:2, :96], summary,
    )


def solution(mesh):
    return jax.shard_map(
        body,
        mesh=mesh,
        in_specs=(
            P(("batch", "heads"), None, None),
            P(("batch", "heads"), None, None),
            P("batch"),
            P("batch"),
            P(None, None, "heads"),
            P(None, "heads"),
            P("heads", None),
            P(),
            P(),
            P(),
            P(None, "heads"),
            P("heads"),
            P("heads", None),
            P(None, None, "heads"),
            P(None, "heads"),
            P(None, None, "heads"),
            P(None, "heads"),
        ),
        out_specs=(
            P(("batch", "heads"), None, None),
            P(("batch", "heads"), None, None),
            P(None, None, "heads"),
            P(None, "heads"),
            P("heads", None),
            P(),
            P(),
            P(),
            P(None, "heads"),
            P("heads"),
            P("heads", None),
            P(None, None, "heads"),
            P(None, "heads"),
            P(),
        ),
        check_vma=False,
    )
```

```python
import functools
import math

import jax
import jax.numpy as jnp
from jax import lax
from jax.experimental import pallas as pl
from jax.experimental.pallas import tpu as pltpu
from jax.sharding import PartitionSpec as P

D = 384
HEADS = 12
HEAD_DIM = 32
TEACHER_HEAD_DIM = 64
PART = 3
TILE = 512
MID_ROWS = 2 * D + 128
STRIP = 16
NORM_EPS = 1e-12
MASKED = -1e30
SAFE = 64.0
LN2 = math.log(2.0)
STUDENT_SCALE = 1.0 / math.sqrt(HEAD_DIM)
STUDENT_LOG = math.log2(math.e) / math.sqrt(HEAD_DIM)
TEACHER_LOG = math.log2(math.e) / math.sqrt(TEACHER_HEAD_DIM)
VMEM = 56 * 2**20

f32 = jnp.float32
bf16 = jnp.bfloat16

NN = (((1,), (0,)), ((), ()))
NT = (((1,), (1,)), ((), ()))
TN = (((0,), (0,)), ((), ()))


def dot(left, right, dims=NN):
    return lax.dot_general(left, right, dims, preferred_element_type=f32)


def lanes(shape):
    return lax.broadcasted_iota(jnp.int32, shape, 1)


def wide_rows(rows):
    return jnp.concatenate([rows, jnp.zeros((rows.shape[0], 128 - rows.shape[1]), rows.dtype)], axis=1)


def in_head(lane, head, size=HEAD_DIM):
    return (lane >= head * size) & (lane < (head + 1) * size)


def split_terms(rows, head, size, extra):
    inside = in_head(lanes(rows.shape), head, size)
    high = rows.astype(bf16).astype(f32)
    first = jnp.where(inside, high, extra).astype(bf16)
    second = jnp.where(inside, rows - high, 0.0).astype(bf16)
    return jnp.concatenate([first, second], axis=1)


def own_number(ref):
    return ref[lax.axis_index("heads")]


def key_bias(rows, length):
    position = lax.broadcasted_iota(jnp.int32, (rows, 1), 0)
    return jnp.where(position < length, 0.0, MASKED)


def fold(tile, combine):
    total = tile[:, :128]
    for column in range(128, tile.shape[1], 128):
        total = combine(total, tile[:, column : column + 128])
    return total


def row_sum(tile):
    return jnp.sum(fold(tile, jnp.add), axis=1, keepdims=True)


def weave(first, second):
    done = 0
    for index, step in enumerate(second):
        while done < len(first) and done * len(second) < len(first) * (index + 1):
            first[done]()
            done += 1
        step()
    for step in first[done:]:
        step()


def step_place(step, tile, per_head):
    head = step // per_head
    return head, pl.ds(pl.multiple_of(lax.rem(step, per_head) * tile, tile), tile)


def skew(first, second):
    steps = [first[0]]
    for index in range(1, len(first)):
        steps += [first[index], second[index - 1]]
    return steps + [second[-1]]


def run_rolled(steps, logits, vector, back, reset=None, enter=None):
    def pair(index, carry):
        for slot in range(2):
            step = 2 * index + slot
            if enter is not None:
                enter(step, slot, index)
            ahead = logits(jnp.minimum(step + 1, steps - 1), 1 - slot)
            weave(ahead + back(jnp.maximum(step - 1, 0), 1 - slot), vector(step, slot))
            if slot == 0 and reset is not None:
                pl.when(index == 0)(reset)
        return carry

    for chunk in logits(jnp.int32(0), 0):
        chunk()
    lax.fori_loop(0, steps // 2, pair, 0)
    for chunk in back(jnp.int32(steps - 1), 1):
        chunk()


def run_pipeline(steps, logits, vector, back, enter=None):
    def stage(step, slot, before, after, second=False):
        if enter is not None:
            enter(step, slot, not before, second)
        ahead = logits(step + 1, 1 - slot) if after else []
        behind = back(step - 1, 1 - slot) if before else []
        weave(ahead + behind, vector(step, slot))

    for chunk in logits(jnp.int32(0), 0):
        chunk()
    stage(jnp.int32(0), 0, False, True)
    stage(jnp.int32(1), 1, True, True, second=True)

    def pair(index, carry):
        stage(2 * index + 2, 0, True, True)
        stage(2 * index + 3, 1, True, True)
        return carry

    lax.fori_loop(0, (steps - 4) // 2, pair, 0)
    stage(jnp.int32(steps - 2), 0, True, True)
    stage(jnp.int32(steps - 1), 1, True, False)
    for chunk in back(jnp.int32(steps - 1), 1):
        chunk()


def project_part(x, w_ref, index, bias):
    flat = dot(x, w_ref[index * 96 : (index + 1) * 96, :], NT)
    if bias is not None:
        flat = flat + bias
    return wide_rows(flat).astype(bf16)


def attend_forward_kernel(
    length_ref, x_ref, w_ref, q_ref, k_ref, v_ref, e_hbm, r_ref, o_ref, lhs, rhs, mixer, zs0, zs1, es0, es1, sems
):
    share = pl.program_id(0)
    w_ref, q_ref, k_ref, v_ref, r_ref, o_ref = (t.at[0] for t in (w_ref, q_ref, k_ref, v_ref, r_ref, o_ref))
    zs, es = (zs0, zs1), (es0, es1)
    rows = x_ref.shape[0]
    tile = zs0.shape[0]
    per_head = rows // tile
    steps = PART * per_head
    x = x_ref[...]
    small = w_ref[288:304, :].astype(f32)
    q = project_part(x, w_ref, 0, small[0:1, :96])
    k = project_part(x, w_ref, 1, None)
    v = project_part(x, w_ref, 2, small[1:2, :96])
    q_ref[...] = q
    k_ref[...] = k
    v_ref[...] = v
    lane = lanes((rows, 128))
    one = jnp.where(lane == 96, 1.0, 0.0)
    for head in range(PART):
        lhs[head] = jnp.where(in_head(lane, head), q.astype(f32), one).astype(bf16)
    rhs[...] = jnp.where(lane == 96, key_bias(rows, own_number(length_ref)), k.astype(f32)).astype(bf16)
    mixer[...] = jnp.where(lane == 96, 1.0, v.astype(f32)).astype(bf16)
    o_ref[...] = jnp.zeros_like(o_ref)
    r_ref[...] = jnp.zeros_like(r_ref)

    def out_copy(step, slot):
        head, span = step_place(step, tile, per_head)
        return pltpu.make_async_copy(es[slot], e_hbm.at[share, head, span], sems.at[slot])

    def logits(step, slot):
        head, span = step_place(step, tile, per_head)

        def chunk(start):
            zs[slot][:, start : start + 256] = dot(lhs[head, span, :], rhs[start : start + 256, :], NT)

        return [functools.partial(chunk, start) for start in range(0, rows, 256)]

    def vector(step, slot):
        def strip(start):
            z = zs[slot][start : start + STRIP, :]
            highest = jnp.max(fold(z, jnp.maximum), axis=1, keepdims=True)
            es[slot][start : start + STRIP, :] = jnp.exp2((z - highest) * STUDENT_LOG).astype(bf16)

        return [functools.partial(strip, start) for start in range(0, tile, STRIP)]

    def back(step, slot):
        head, span = step_place(step, tile, per_head)

        sums = []

        def part(start):
            sums.append(dot(es[slot][:, start : start + 256], mixer[start : start + 256, :]))

        def mix():
            mixed = functools.reduce(jnp.add, sums)
            inverse = 1.0 / mixed[:, 96:97]
            inside = in_head(lanes(mixed.shape), head)
            o_ref[span, :] = jnp.where(inside, mixed * inverse, o_ref[span, :].astype(f32)).astype(bf16)
            r_ref[span, :] = jnp.where(inside, inverse, r_ref[span, :])

        return [functools.partial(part, start) for start in range(0, rows, 256)] + [mix]

    def enter(step, slot, first, second):
        if not first:
            out_copy(step - 1, 1 - slot).start()
        if not (first or second):
            out_copy(step - 2, slot).wait()

    run_pipeline(steps, logits, vector, back, enter)
    out_copy(jnp.int32(steps - 1), 1).start()
    out_copy(jnp.int32(steps - 2), 0).wait()
    out_copy(jnp.int32(steps - 1), 1).wait()


def whole(shape):
    return pl.BlockSpec(shape, lambda *_: (0,) * len(shape))


SMEM = pl.BlockSpec(memory_space=pltpu.SMEM)
ANY = pl.BlockSpec(memory_space=pl.ANY)


def cost(micros):
    return pl.CostEstimate(flops=int(micros * 0.04e9), bytes_accessed=1024, transcendentals=0)


def attend_forward(length, x, w):
    rows, count = x.shape[0], w.shape[0]
    tile = min(TILE, rows // 2)
    narrow = jax.ShapeDtypeStruct((count, rows, 128), bf16)

    def share(shape):
        return pl.BlockSpec((1,) + shape, lambda s: (s,) + (0,) * len(shape))

    row = share((rows, 128))
    return pl.pallas_call(
        attend_forward_kernel,
        grid=(count,),
        in_specs=[SMEM, whole(x.shape), share(w.shape[1:])],
        out_specs=[row] * 3 + [ANY] + [row] * 2,
        out_shape=[
            narrow, narrow, narrow, jax.ShapeDtypeStruct((count, PART, rows, rows), bf16),
            jax.ShapeDtypeStruct((count, rows, 128), f32), narrow,
        ],
        scratch_shapes=[
            pltpu.VMEM((PART, rows, 128), bf16),
            pltpu.VMEM((rows, 128), bf16),
            pltpu.VMEM((rows, 128), bf16),
            pltpu.VMEM((tile, rows), f32),
            pltpu.VMEM((tile, rows), f32),
            pltpu.VMEM((tile, rows), bf16),
            pltpu.VMEM((tile, rows), bf16),
            pltpu.SemaphoreType.DMA((2,)),
        ],
        compiler_params=pltpu.CompilerParams(vmem_limit_bytes=VMEM),
        cost_estimate=cost(9 * count),
        name="attend_forward",
    )(length, x, w)


def attend_backward_kernel(
    q_ref, k_ref, v_ref, e_hbm, r_ref, a_ref, d_ref, x_hbm, w_hbm, acc_hbm, tail_ref, g_ref, in_ref,
    lhs, rhs, keys, qt, dt, zs0, zs1, gs0, gs1, dq, dkt, dvt, e_all, x_ref, w_ref, acc_ref, sems, late, *, share,
):
    q_ref, k_ref, v_ref, r_ref, a_ref = (t.at[0] for t in (q_ref, k_ref, v_ref, r_ref, a_ref))
    rows = q_ref.shape[0]
    zs, gs = (zs0, zs1), (gs0, gs1)
    tile = zs0.shape[0]
    per_head = rows // tile
    steps = PART * per_head

    def in_copy(step):
        head, span = step_place(step, tile, per_head)
        return pltpu.make_async_copy(e_hbm.at[share, head, span], e_all.at[head, span], sems.at[step])

    def begin(step, carry):
        in_copy(step).start()
        return carry

    lax.fori_loop(0, steps, begin, 0)
    late_copies = [
        pltpu.make_async_copy(source, target, late.at[index])
        for index, (source, target) in enumerate(((x_hbm, x_ref), (w_hbm.at[share], w_ref), (acc_hbm, acc_ref)))
    ]
    for copy in late_copies:
        copy.start()
    lane = lanes((rows, 128))
    grads = r_ref[...] * d_ref[...].astype(f32)
    shifts = grads * a_ref[...].astype(f32)
    k = k_ref[...].astype(f32)
    def one_head(head, carry):
        inside = in_head(lane, head)
        shift = -jnp.sum(jnp.where(inside, shifts, 0.0), axis=1, keepdims=True)
        high = shift.astype(bf16).astype(f32)
        lhs[head] = split_terms(
            grads, head, HEAD_DIM, jnp.where(lane == 96, high, jnp.where(lane == 97, shift - high, 0.0))
        )
        keys[head] = jnp.where(inside, k, 0.0).astype(bf16)
        return carry

    lax.fori_loop(0, PART, one_head, 0)
    rhs[:, :128] = jnp.where((lane == 96) | (lane == 97), 1.0, v_ref[...].astype(f32)).astype(bf16)
    rhs[:, 128:] = v_ref[...]
    qt[...] = q_ref[...].T
    dt[...] = grads.astype(bf16).T

    def reset():
        dq[...] = jnp.zeros_like(dq)
        dkt[...] = jnp.zeros_like(dkt)
        dvt[...] = jnp.zeros_like(dvt)

    reset()

    def logits(step, slot):
        head, span = step_place(step, tile, per_head)

        def chunk(start):
            zs[slot][:, start : start + 256] = dot(lhs[head, span, :], rhs[start : start + 256, :], NT)

        return [functools.partial(chunk, start) for start in range(0, rows, 256)]

    def vector(step, slot):
        head, span = step_place(step, tile, per_head)
        base = lax.rem(step, per_head) * tile

        def strip(start):
            here = pl.ds(pl.multiple_of(base + start, STRIP), STRIP)
            weights = e_all[head, here, :].astype(f32)
            gs[slot][start : start + STRIP, :] = (weights * zs[slot][start : start + STRIP, :]).astype(bf16)

        return [functools.partial(strip, start) for start in range(0, tile, STRIP)]

    def back(step, slot):
        head, span = step_place(step, tile, per_head)
        own = pl.ds(pl.multiple_of(head * HEAD_DIM, HEAD_DIM), HEAD_DIM)

        def first():
            dq[span, :] += dot(gs[slot][...], keys[head])

        def second(start):
            part = slice(start, start + 256)
            dkt[own, part] += dot(qt[own, span], gs[slot][:, part])

        def third(start):
            part = slice(start, start + 256)
            dvt[own, part] += dot(dt[own, span], e_all[head, span, part])

        starts = range(0, rows, 256)
        return [first] + [functools.partial(second, s) for s in starts] + [functools.partial(third, s) for s in starts]

    run_pipeline(steps, logits, vector, back, lambda step, slot, first, second: in_copy(step).wait())
    for copy in late_copies:
        copy.wait()
    grads = (
        (dq[...] * STUDENT_SCALE).astype(bf16),
        (dkt[...] * STUDENT_SCALE).T.astype(bf16),
        dvt[...].T.astype(bf16),
    )
    weight_grads(grads, x_ref[...], g_ref, tail_ref[:16, :].astype(f32), tail_ref[16:, :].astype(f32))
    in_ref[...] = acc_ref[...] + spread(grads, w_ref)


def weight_grads(grads, x, g_ref, tail_high=0.0, tail_low=0.0):
    for index, grad in enumerate(grads):
        g_ref[index * 96 : (index + 1) * 96, :] = dot(grad, x, TN)[:96].astype(bf16)
    ones = jnp.ones((16, x.shape[0]), bf16)
    row = lax.broadcasted_iota(jnp.int32, (16, 128), 0)
    sums = jnp.where(row == 0, dot(ones, grads[0]), jnp.where(row == 1, dot(ones, grads[2]), 0.0))
    sums = jnp.concatenate([sums, jnp.zeros((16, x.shape[1] - 128), f32)], axis=1) + tail_high
    high = sums.astype(bf16).astype(f32)
    g_ref[288:304, :] = high.astype(bf16)
    g_ref[304:320, :] = (sums - high + tail_low).astype(bf16)


def spread(grads, w_ref):
    total = None
    for index, grad in enumerate(grads):
        term = dot(grad[:, :96], w_ref[index * 96 : (index + 1) * 96, :])
        total = term if total is None else total + term
    return total


def attend_backward(share, q, k, v, e, r, attended, d_attended, x, w, grad_in, tail):
    rows = x.shape[0]
    tile = min(TILE, rows // 2)
    row = pl.BlockSpec((1, rows, 128), lambda i: (share, 0, 0))
    return pl.pallas_call(
        functools.partial(attend_backward_kernel, share=share),
        grid=(1,),
        in_specs=[row, row, row, ANY, row, row, whole((rows, 128)), ANY, ANY, ANY, whole(tail.shape)],
        out_specs=[whole((320, x.shape[1])), whole(x.shape)],
        out_shape=[jax.ShapeDtypeStruct((320, x.shape[1]), bf16), jax.ShapeDtypeStruct(x.shape, f32)],
        scratch_shapes=[
            pltpu.VMEM((PART, rows, 256), bf16),
            pltpu.VMEM((rows, 256), bf16),
            pltpu.VMEM((PART, rows, 128), bf16),
            pltpu.VMEM((128, rows), bf16),
            pltpu.VMEM((128, rows), bf16),
            pltpu.VMEM((tile, rows), f32),
            pltpu.VMEM((tile, rows), f32),
            pltpu.VMEM((tile, rows), bf16),
            pltpu.VMEM((tile, rows), bf16),
            pltpu.VMEM((rows, 128), f32),
            pltpu.VMEM((128, rows), f32),
            pltpu.VMEM((128, rows), f32),
            pltpu.VMEM((PART, rows, rows), bf16),
            pltpu.VMEM(x.shape, bf16),
            pltpu.VMEM(w.shape[1:], bf16),
            pltpu.VMEM(x.shape, f32),
            pltpu.SemaphoreType.DMA((PART * (rows // tile),)),
            pltpu.SemaphoreType.DMA((3,)),
        ],
        compiler_params=pltpu.CompilerParams(vmem_limit_bytes=VMEM),
        cost_estimate=cost(10),
        name="attend_backward",
    )(q, k, v, e, r, attended, d_attended, x, w, grad_in, tail)


def relation_kernel(
    length_ref, split_ref, block_ref, teacher_ref, own_ref, packed_ref, small_ref, d_ref, g_ref, kl_ref, kl_row_ref,
    pack, lefts, rights, t_lefts, t_rights, ls, rs, lt, rt, keys, left_t, zs0, zs1, zt0, zt1, gs0, gs1,
    left_sum, right_t, es_all, et_all, parts, columns, factors, rows_s, weight, weight_row, grads_s, *, all_rows,
):
    rows = block_ref.shape[0]
    tile = zs0.shape[0]
    per_head = rows // tile
    steps = PART * per_head
    zs, zt, gs = (zs0, zs1), (zt0, zt1), (gs0.at[:tile], gs1)
    length, split = own_number(length_ref), own_number(split_ref)

    @pl.when(pl.program_id(0) == 0)
    def _():
        pack[...] = own_ref[...]
        position = lax.broadcasted_iota(jnp.int32, (rows, 1), 0)
        counted = (position < length) & (position != 0) & (position != split - 1) & (position != length - 1)
        share = 1.0 / ((length - 3).astype(f32) * float(all_rows))
        weight[...] = jnp.where(counted, share, 0.0)
        position = lanes((1, rows))
        counted = (position < length) & (position != 0) & (position != split - 1) & (position != length - 1)
        weight_row[...] = jnp.where(counted, share, 0.0)
        kl_ref[...] = jnp.zeros_like(kl_ref)
        kl_row_ref[...] = jnp.zeros_like(kl_row_ref)
        d_ref[...] = jnp.zeros_like(d_ref)

    @pl.when(pl.program_id(0) > 0)
    def _():
        unpack(packed_ref, 0, pack, MID_ROWS)

    g_ref = g_ref.at[0]
    small = small_ref[0].astype(f32)

    def largest(low, size):
        square = low.astype(f32)
        same = lax.broadcasted_iota(jnp.int32, (128, 128), 0) // size == lanes((128, 128)) // size
        return jnp.max(dot((square * square).astype(bf16), jnp.where(same, 1.0, 0.0).astype(bf16)), axis=0, keepdims=True)

    def project(index, carry):
        here = pl.ds(pl.multiple_of(index * tile, tile), tile)
        block, teacher = block_ref[here, :], teacher_ref[here, :]

        def student(part, b):
            flat = dot(block, pack[part * 96 : (part + 1) * 96, :], NT)
            return wide_rows(flat if b is None else flat + b).astype(bf16)

        def taught(part, b):
            start = 288 + part * 192
            flat = dot(teacher[:, :D], pack[start : start + 192, :], NT)
            flat = flat + dot(teacher[:, D:], pack[start + 576 : start + 768, :], NT)
            flat = (flat if b is None else flat + b).astype(bf16)
            return flat[:, :128], wide_rows(flat[:, 128:])

        q, k, v = student(0, small[2:3, :96]), student(1, None), student(2, small[3:4, :96])
        lefts[0, here, :] = q
        rights[0, here, :] = k
        lefts[1, here, :] = v
        rights[1, here, :] = v
        tq, tk, tv = taught(0, small[5:6, :192]), taught(1, None), taught(2, small[6:7, :192])
        for half in range(2):
            t_lefts[0, half, here, :] = tq[half]
            t_rights[0, half, here, :] = tk[half]
            t_lefts[1, half, here, :] = tv[half]
            t_rights[1, half, here, :] = tv[half]
        found = [largest(value, HEAD_DIM) for value in (q, k, v)]
        found += [largest(value, TEACHER_HEAD_DIM) for value in tq + tk + tv]
        return tuple(jnp.maximum(old, new) for old, new in zip(carry, found))

    top = lax.fori_loop(0, rows // tile, project, (jnp.zeros((1, 128), f32),) * 9)
    bounds = []
    for s_left, s_right, t_left, t_right in ((0, 1, 3, 5), (2, 2, 7, 7)):
        bound = jnp.max(top[s_left] * top[s_right]) * STUDENT_LOG**2
        for half in range(2):
            bound = jnp.maximum(bound, jnp.max(top[t_left + half] * top[t_right + half]) * TEACHER_LOG**2)
        bounds.append(bound)

    def operands(relation, student_scale, teacher_scale, row_bias, everything):
        band = min(128, rows)
        line = lanes((1, 128))

        def terms(value, inside, extra):
            high, low = value
            return jnp.where(inside, high, extra).astype(bf16), jnp.where(inside, low, 0.0).astype(bf16)

        def halves(value, scale):
            value = value * scale
            high = value.astype(bf16).astype(f32)
            return high, value - high

        def one_band(index, carry):
            here = pl.ds(pl.multiple_of(index * band, band), band)
            position = lax.broadcasted_iota(jnp.int32, (band, 128), 0) + index * band
            bias = jnp.where(position < length, 0.0, MASKED)
            row = jnp.where(row_bias, bias, 0.0)
            left, right = lefts[relation, here, :].astype(f32), rights[relation, here, :].astype(f32)
            value = halves(left, student_scale)
            extra = jnp.where(line == 97, row, jnp.where(line == 96, 1.0, 0.0))
            if everything:
                rs[here, :128] = jnp.where(line == 97, 1.0, jnp.where(line == 96, bias, right)).astype(bf16)
                rs[here, 128:] = rights[relation, here, :]
            for head in range(PART):
                inside = in_head(line, head)
                ls[head, here, :128], ls[head, here, 128:] = terms(value, inside, extra)
                if everything:
                    keys[head, here, :] = jnp.where(inside, right, 0.0).astype(bf16)
            for half in range(2):
                t_left = t_lefts[relation, half, here, :].astype(f32)
                t_right = t_rights[relation, half, here, :].astype(f32)
                value = halves(t_left, teacher_scale)
                for head in range(2 * half, min(2 * half + 2, PART)):
                    own = head % 2
                    spare = (1 - own) * TEACHER_HEAD_DIM
                    extra = jnp.where(line == spare + 1, row, jnp.where(line == spare, 1.0, 0.0))
                    inside = in_head(line, own, TEACHER_HEAD_DIM)
                    lt[head, here, :128], lt[head, here, 128:] = terms(value, inside, extra)
                    if everything:
                        first = jnp.where(line == spare + 1, 1.0, jnp.where(line == spare, bias, t_right))
                        rt[head, here, :128] = first.astype(bf16)
                        rt[head, here, 128:] = t_rights[relation, half, here, :]
            return carry

        lax.fori_loop(0, rows // band, one_band, 0)

    def relate(relation, carry):
        symmetric = relation == 1
        left_t[...] = lefts[relation].T
        operands(relation, STUDENT_LOG, TEACHER_LOG, symmetric, True)
        near = jnp.where(symmetric, bounds[1], bounds[0]) < SAFE * SAFE
        reset()

        @pl.when(near & jnp.logical_not(symmetric))
        def _():
            run_pipeline(steps, logits, vector, grad_products)

        @pl.when(near & symmetric)
        def _():
            lax.fori_loop(0, PART, symmetric_head, 0)

        @pl.when(jnp.logical_not(near))
        def _():
            operands(relation, 1.0, 1.0, False, False)
            lax.fori_loop(0, steps, shifted_step, 0)

        @pl.when(jnp.logical_not(symmetric))
        def _():
            grads_s[0] = (left_sum[...] * STUDENT_SCALE).astype(bf16)
            grads_s[1] = (right_t[...] * STUDENT_SCALE).T.astype(bf16)

        @pl.when(symmetric)
        def _():
            grads_s[2] = ((left_sum[...] + right_t[...].T) * STUDENT_SCALE).astype(bf16)

        return carry

    def reset():
        left_sum[...] = jnp.zeros_like(left_sum)
        right_t[...] = jnp.zeros_like(right_t)

    def logits(step, slot):
        head, span = step_place(step, tile, per_head)

        def student(start):
            zs[slot][:, start : start + 256] = dot(ls[head, span, :], rs[start : start + 256, :], NT)

        def taught(start):
            zt[slot][:, start : start + 256] = dot(lt[head, span, :], rt[head, start : start + 256, :], NT)

        chunks = []
        for start in range(0, rows, 256):
            chunks += [functools.partial(student, start), functools.partial(taught, start)]
        return chunks

    def vector(step, slot):
        base = lax.rem(step, per_head) * tile
        z, t, g = zs[slot], zt[slot], gs[slot]
        scales = {}

        def weigh(start):
            strip = slice(start, start + STRIP)
            sum_s = sum_t = cross = 0.0
            for column in range(0, rows, 128):
                part = slice(column, column + 128)
                student, taught = z[strip, part], t[strip, part]
                es, et = jnp.exp2(student), jnp.exp2(taught)
                z[strip, part] = es
                t[strip, part] = et
                sum_s, sum_t, cross = sum_s + es, sum_t + et, cross + et * (taught - student)
            here = pl.ds(pl.multiple_of(base + start, STRIP), STRIP)
            sum_s, sum_t, cross = (jnp.sum(v, axis=1, keepdims=True) for v in (sum_s, sum_t, cross))
            w = weight[here, :]
            inverse = 1.0 / sum_t
            kl_ref[here, :] += w * (LN2 * cross * inverse + jnp.log(sum_s) - jnp.log(sum_t))
            scales[start] = w / sum_s, w * inverse

        def grad(start):
            strip = slice(start, start + STRIP)
            a, b = scales[start]
            for column in range(0, rows, 128):
                part = slice(column, column + 128)
                g[strip, part] = (z[strip, part] * a - t[strip, part] * b).astype(bf16)

        starts = range(0, tile, STRIP)
        return skew([functools.partial(weigh, s) for s in starts], [functools.partial(grad, s) for s in starts])

    def grad_products(step, slot):
        head, span = step_place(step, tile, per_head)
        own = pl.ds(pl.multiple_of(head * HEAD_DIM, HEAD_DIM), HEAD_DIM)

        def first():
            left_sum[span, :] += dot(gs[slot][...], keys[head])

        def second(start):
            part = slice(start, start + 256)
            right_t[own, part] += dot(left_t[own, span], gs[slot][:, part])

        return [first] + [functools.partial(second, start) for start in range(0, rows, 256)]

    def shifted_step(step, carry):
        head, span = step_place(step, tile, per_head)
        student = dot(ls[head, span, :], rs[...], NT)
        zs0[...] = (student - jnp.max(student, axis=1, keepdims=True)) * STUDENT_LOG
        taught = dot(lt[head, span, :], rt[head], NT)
        zt0[...] = (taught - jnp.max(taught, axis=1, keepdims=True)) * TEACHER_LOG

        def strip(index, carry):
            here = pl.ds(pl.multiple_of(index * STRIP, STRIP), STRIP)
            student, taught = zs0[here, :], zt0[here, :]
            es, et = jnp.exp2(student), jnp.exp2(taught)
            sum_s, sum_t = row_sum(es), row_sum(et)
            cross = row_sum(et * (taught - student))
            there = pl.ds(pl.multiple_of(lax.rem(step, per_head) * tile + index * STRIP, STRIP), STRIP)
            w = weight[there, :]
            row = LN2 * cross / sum_t + jnp.log(sum_s) - jnp.log(sum_t)
            kl_ref[there, :] += jnp.where(w > 0.0, w * row, 0.0)
            gs0[here, :] = (es * (w / sum_s) - et * (w / sum_t)).astype(bf16)
            return carry

        lax.fori_loop(0, tile // STRIP, strip, 0)
        for chunk in grad_products(step, 0):
            chunk()
        return carry

    def symmetric_head(head, carry):
        size, band = min(256, rows), 32
        count = rows // size
        own = pl.ds(pl.multiple_of(head * HEAD_DIM, HEAD_DIM), HEAD_DIM)
        columns[...] = jnp.zeros_like(columns)

        def logit_chunks(i):
            here = slice(i * size, (i + 1) * size)

            def student(part):
                es_all[here, part] = dot(ls[head, here, :], rs[part, :], NT)

            def taught(part):
                et_all[here, part] = dot(lt[head, here, :], rt[head, part, :], NT)

            chunks = []
            for j in range(i, count):
                part = slice(j * size, (j + 1) * size)
                chunks += [functools.partial(student, part), functools.partial(taught, part)]
            return chunks

        def weigh(i, start):
            strip = slice(start, start + band)
            totals = [0.0, 0.0, 0.0]
            for column in range(i * size, rows, 128):
                part = slice(column, column + 128)
                student, taught = es_all[strip, part], et_all[strip, part]
                es, et = jnp.exp2(student), jnp.exp2(taught)
                es_all[strip, part] = es
                et_all[strip, part] = et
                for index, value in enumerate((es, et, et * (taught - student))):
                    totals[index] = totals[index] + value
                    if column >= (i + 1) * size:
                        eight = value[:8]
                        for line in range(8, band, 8):
                            eight = eight + value[line : line + 8]
                        columns[index, :, part] += eight
            for index in range(3):
                parts[index, strip, :] = totals[index]

        def combine(i, start):
            strip = slice(start, start + STRIP)
            a, b = factors[0, strip, :], factors[1, strip, :]
            for column in range(i * size, rows, 128):
                part = slice(column, column + 128)
                both = es_all[strip, part] * (a + rows_s[0, :, part])
                both = both - et_all[strip, part] * (b + rows_s[1, :, part])
                gs0[strip, part] = both.astype(bf16)

        def products(i):
            here = slice(i * size, (i + 1) * size)

            def first(j):
                part = slice(j * size, (j + 1) * size)
                left_sum[here, :] += dot(gs_all[here, part], keys[head, part, :])

            def second(j):
                part = slice(j * size, (j + 1) * size)
                right_t[own, part] += dot(left_t[own, here], gs_all[here, part])

            chunks = [functools.partial(first, j) for j in range(i, count)]
            return chunks + [functools.partial(second, j) for j in range(i + 1, count)]

        gs_all = gs0
        for chunk in logit_chunks(0):
            chunk()
        for i in range(count):
            ahead = logit_chunks(i + 1) if i + 1 < count else []
            weave(ahead, [functools.partial(weigh, i, s) for s in range(i * size, (i + 1) * size, band)])
        sums = [
            jnp.sum(parts[index].T, axis=0, keepdims=True) + jnp.sum(columns[index], axis=0, keepdims=True)
            for index in range(3)
        ]
        w = weight_row[...]
        sum_s, sum_t = (jnp.where(w > 0.0, value, 1.0) for value in sums[:2])
        inverse = 1.0 / sum_t
        kl_row_ref[...] += w * (LN2 * sums[2] * inverse + jnp.log(sum_s) - jnp.log(sum_t))
        for index, value in enumerate((w / sum_s, w * inverse)):
            factors[index] = jnp.broadcast_to(value, (128, rows)).T
            rows_s[index] = jnp.broadcast_to(value, (STRIP, rows))
        for i in range(count):
            behind = products(i - 1) if i else []
            weave(behind, [functools.partial(combine, i, s) for s in range(i * size, (i + 1) * size, STRIP)])
        for chunk in products(count - 1):
            chunk()
        return carry

    lax.fori_loop(0, 2, relate, 0)
    grads = tuple(grads_s[i] for i in range(3))
    weight_grads(grads, block_ref[...], g_ref)
    d_ref[...] += spread(grads, pack)


def part_rows(rows, batch):
    return -(-rows // (16 * batch)) * 16


def unpack(packed_ref, share, target, before=0):
    rows, batch = target.shape[0], packed_ref.shape[0]
    part = part_rows(rows, batch)
    offset = part_rows(before, batch)
    for start in range(0, rows, part):
        size = min(part, rows - start)
        target[start : start + size, :] = packed_ref[start // part, share, offset : offset + size, :]


def relations(length, split, block, teacher, own, packed, small, all_rows):
    rows = block.shape[0]
    tile = min(TILE, rows // 2)
    shares = small.shape[0]

    def share(shape):
        return pl.BlockSpec((1,) + shape[1:], lambda s: (s,) + (0,) * (len(shape) - 1))

    place = pl.BlockSpec((packed.shape[0], 1) + packed.shape[2:], lambda s: (0, jnp.maximum(s - 1, 0), 0, 0))
    return pl.pallas_call(
        functools.partial(relation_kernel, all_rows=all_rows),
        grid=(shares,),
        in_specs=[
            SMEM, SMEM, whole(block.shape), whole(teacher.shape), whole(own.shape), place, share(small.shape),
        ],
        out_specs=[whole(block.shape), share((shares, 320, D)), whole((rows, 1)), whole((1, rows))],
        out_shape=[
            jax.ShapeDtypeStruct(block.shape, f32),
            jax.ShapeDtypeStruct((shares, 320, D), bf16),
            jax.ShapeDtypeStruct((rows, 1), f32),
            jax.ShapeDtypeStruct((1, rows), f32),
        ],
        scratch_shapes=[
            pltpu.VMEM((1440, D), bf16),
            pltpu.VMEM((2, rows, 128), bf16),
            pltpu.VMEM((2, rows, 128), bf16),
            pltpu.VMEM((2, 2, rows, 128), bf16),
            pltpu.VMEM((2, 2, rows, 128), bf16),
            pltpu.VMEM((PART, rows, 256), bf16),
            pltpu.VMEM((rows, 256), bf16),
            pltpu.VMEM((PART, rows, 256), bf16),
            pltpu.VMEM((PART, rows, 256), bf16),
            pltpu.VMEM((PART, rows, 128), bf16),
            pltpu.VMEM((128, rows), bf16),
            pltpu.VMEM((tile, rows), f32),
            pltpu.VMEM((tile, rows), f32),
            pltpu.VMEM((tile, rows), f32),
            pltpu.VMEM((tile, rows), f32),
            pltpu.VMEM((rows, rows), bf16),
            pltpu.VMEM((tile, rows), bf16),
            pltpu.VMEM((rows, 128), f32),
            pltpu.VMEM((128, rows), f32),
            pltpu.VMEM((rows, rows), f32),
            pltpu.VMEM((rows, rows), f32),
            pltpu.VMEM((3, rows, 128), f32),
            pltpu.VMEM((3, 8, rows), f32),
            pltpu.VMEM((2, rows, 128), f32),
            pltpu.VMEM((2, STRIP, rows), f32),
            pltpu.VMEM((rows, 1), f32),
            pltpu.VMEM((1, rows), f32),
            pltpu.VMEM((3, rows, 128), bf16),
        ],
        compiler_params=pltpu.CompilerParams(vmem_limit_bytes=VMEM),
        cost_estimate=cost(30 * shares),
        name="relations",
    )(length, split, block, teacher, own, packed, small)


def norm_forward(rows, gain, shift):
    center = jnp.mean(rows, axis=1, keepdims=True)
    offsets = rows - center
    rstd = lax.rsqrt(jnp.mean(offsets * offsets, axis=1, keepdims=True) + NORM_EPS)
    normed = offsets * rstd
    return normed * gain + shift, normed, rstd


def norm_backward(grad, normed, rstd, gain):
    inner = grad * gain
    mean = jnp.mean(inner, axis=1, keepdims=True)
    slope = jnp.mean(inner * normed, axis=1, keepdims=True)
    return rstd * (inner - mean - normed * slope)


def gelu_terms(x):
    size = jnp.abs(x) * math.sqrt(0.5)
    t = 1.0 / (1.0 + 0.3275911 * size)
    bell = jnp.exp(-0.5 * x * x)
    poly = t * (0.254829592 + t * (-0.284496736 + t * (1.421413741 + t * (-1.453152027 + t * 1.061405429))))
    tail = 0.5 * poly * bell
    share = jnp.where(x >= 0.0, 1.0 - tail, tail)
    return x * share, share + x * bell * (1.0 / math.sqrt(2.0 * math.pi))


def unpack_all(own_ref, packed_ref, pack):
    pack[0] = own_ref[...]
    for share in range(1, pack.shape[0]):
        unpack(packed_ref, share - 1, pack.at[share])


def mid_part(packed):
    return whole(packed.shape[:2] + (part_rows(MID_ROWS, packed.shape[0]), packed.shape[3]))


def split_pack(pack):
    return pack.at[:, :D], pack.at[:, D : 2 * D], pack.at[:, 2 * D :]


def block_kernel(
    length_ref, x_ref, own_ref, packed_ref, small_ref, branch_ref, gain_ref, shift_ref, first_ref, other_ref,
    block_ref, n1_ref, r1_ref, n2_ref, r2_ref, act_ref, slope_ref, sums_ref, pack,
):
    shares = small_ref.shape[0]
    a_refs = [first_ref.at[0]] + [other_ref.at[s] for s in range(shares - 1)]
    tile = x_ref.shape[0]

    @pl.when(pl.program_id(0) == 0)
    def _():
        unpack_all(own_ref, packed_ref, pack)

    wide_ref, narrow_ref, out_ref = split_pack(pack)
    x = x_ref[...].astype(f32)
    mixing = branch_ref[0:1, :]
    for s in range(shares):
        mixing = mixing + dot(a_refs[s][:, :96], out_ref[s, :96, :])
    middle, normed, rstd = norm_forward(x + mixing, gain_ref[0:1, :], shift_ref[0:1, :])
    n1_ref[...] = normed
    r1_ref[...] = rstd
    low = middle.astype(bf16)
    branch = branch_ref[1:2, :]
    width = D
    for s in range(shares):
        value, slope = gelu_terms(dot(low, wide_ref[s]) + small_ref[s, 4:5, :].astype(f32))
        value = value.astype(bf16)
        act_ref[:, s * width : (s + 1) * width] = value
        slope_ref[:, s * width : (s + 1) * width] = slope.astype(bf16)
        branch = branch + dot(value, narrow_ref[s])
    block, normed, rstd = norm_forward(middle + branch, gain_ref[1:2, :], shift_ref[1:2, :])
    n2_ref[...] = normed
    r2_ref[...] = rstd
    block_ref[...] = block.astype(bf16)
    position = lax.broadcasted_iota(jnp.int32, (tile, 1), 0) + pl.program_id(0) * tile
    kept = jnp.where(position < own_number(length_ref), 1.0, 0.0)
    row = lax.broadcasted_iota(jnp.int32, (8, x.shape[1]), 0)
    total = jnp.zeros((8, x.shape[1]), f32)
    for index, part in enumerate((x, mixing, branch)):
        total = jnp.where(row == index, jnp.sum(kept * part * part, axis=0, keepdims=True), total)

    @pl.when(pl.program_id(0) == 0)
    def _():
        sums_ref[...] = jnp.zeros_like(sums_ref)

    sums_ref[...] += total


def by_tile(tile, width):
    return pl.BlockSpec((tile, width), lambda i: (i, 0))


def block_forward(length, x, attended, own, packed, small, branch_bias, gain, shift):
    rows, width = x.shape
    tile = min(256, rows)
    shares = small.shape[0]
    units = shares * D
    row, column = by_tile(tile, width), by_tile(tile, 1)
    return pl.pallas_call(
        block_kernel,
        grid=(rows // tile,),
        in_specs=[
            SMEM, row, whole(own.shape), mid_part(packed), whole(small.shape), whole(branch_bias.shape), whole(gain.shape), whole(shift.shape),
        ] + [pl.BlockSpec((a.shape[0], tile, 128), lambda i: (0, i, 0)) for a in attended],
        out_specs=[row, row, column, row, column, by_tile(tile, units), by_tile(tile, units), whole((8, width))],
        out_shape=[
            jax.ShapeDtypeStruct((rows, width), bf16),
            jax.ShapeDtypeStruct((rows, width), f32),
            jax.ShapeDtypeStruct((rows, 1), f32),
            jax.ShapeDtypeStruct((rows, width), f32),
            jax.ShapeDtypeStruct((rows, 1), f32),
            jax.ShapeDtypeStruct((rows, units), bf16),
            jax.ShapeDtypeStruct((rows, units), bf16),
            jax.ShapeDtypeStruct((8, width), f32),
        ],
        scratch_shapes=[pltpu.VMEM((shares, 2 * D + 128, D), bf16)],
        compiler_params=pltpu.CompilerParams(vmem_limit_bytes=VMEM),
        cost_estimate=cost(20),
        name="block_forward",
    )(length, x, own, packed, small, branch_bias, gain, shift, *attended)


def block_backward_kernel(
    length_ref, d_ref, n1_ref, r1_ref, n2_ref, r2_ref, act_ref, slope_ref, own_ref, packed_ref, gain_ref,
    shift_ref, kl_ref, kl_row_ref, square_ref, six_ref, first_ref, other_ref, *rest,
):
    step = pl.program_id(0)
    pack = rest[-1]
    shares = pack.shape[0]
    a_refs = [first_ref.at[0]] + [other_ref.at[s] for s in range(shares - 1)]
    sum_ref, da_refs = rest[0], rest[1 : shares + 1]
    g_ref, tail_ref, vec_ref, g_sum, low_s, branch_s, pre_s, mix_s = rest[shares + 1 : -1]
    tile, width = d_ref.shape
    units = D
    span = pl.ds(pl.multiple_of(step * tile, tile), tile)

    @pl.when(step == 0)
    def _():
        unpack_all(own_ref, packed_ref, pack)
        vec_ref[...] = jnp.zeros_like(vec_ref)
        g_sum[...] = jnp.zeros_like(g_sum)

    wide_ref, narrow_ref, out_ref = split_pack(pack)

    def column(value):
        return jnp.sum(value, axis=0, keepdims=True)

    row = lax.broadcasted_iota(jnp.int32, (8, width), 0)
    d_block = d_ref[...]
    normed_two = n2_ref[...]
    d_two = norm_backward(d_block, normed_two, r2_ref[...], gain_ref[1:2, :])
    d_branch = d_two.astype(bf16)
    branch_s[span, :] = d_branch
    normed_one = n1_ref[...]
    low = (normed_one * gain_ref[0:1, :] + shift_ref[0:1, :]).astype(bf16)
    low_s[span, :] = low
    d_middle = d_two
    for s in range(shares):
        grad = dot(d_branch, narrow_ref[s], NT) * slope_ref[:, s * units : (s + 1) * units].astype(f32)
        grad = grad.astype(bf16)
        pre_s[span, s * units : (s + 1) * units] = grad
        g_sum[s : s + 1, :] += column(grad.astype(f32))
        d_middle = d_middle + dot(grad, wide_ref[s], NT)
    d_one = norm_backward(d_middle, normed_one, r1_ref[...], gain_ref[0:1, :])
    sum_ref[...] = d_one
    d_mixing = d_one.astype(bf16)
    mix_s[span, :] = d_mixing
    for s in range(shares):
        da_refs[s][...] = wide_rows(dot(d_mixing, out_ref[s, :96, :], NT)).astype(bf16)
    parts = (
        d_mixing.astype(f32), d_branch.astype(f32), d_middle * normed_one, d_block * normed_two, d_middle, d_block,
    )
    total = jnp.zeros((8, width), f32)
    for index, part in enumerate(parts):
        total = jnp.where(row == index, column(part), total)
    vec_ref[...] += total

    @pl.when(step == pl.num_programs(0) - 1)
    def _():
        for s in range(shares):
            part = slice(s * units, (s + 1) * units)
            own = slice(s * width, (s + 1) * width)
            g_ref[0:units, own] = dot(act_ref[:, part], branch_s[...], TN).astype(bf16)
            g_ref[units : 2 * units, own] = dot(low_s[...], pre_s[:, part], TN).astype(bf16)
            g_ref[2 * units : 2 * units + 96, own] = dot(a_refs[s][...], mix_s[...], TN)[:96].astype(bf16)
            g_ref[2 * units + 128 :, own] = six_ref[s]
            first = lax.broadcasted_iota(jnp.int32, (32, units), 0) == 0
            g_ref[2 * units + 96 : 2 * units + 128, own] = jnp.where(first, g_sum[s : s + 1, :], 0.0).astype(bf16)
        scalars = [jnp.sum(kl_ref[...], axis=0, keepdims=True) + jnp.sum(kl_row_ref[...], axis=1, keepdims=True)]
        scalars += [jnp.sum(square_ref[i : i + 1, :], axis=1, keepdims=True) for i in range(3)]
        scalars += [jnp.broadcast_to(own_number(length_ref).astype(f32), (1, 1))]
        lane = lanes((8, width))
        total = vec_ref[...]
        for index, value in enumerate(scalars):
            total = jnp.where((row == 6) & (lane == index), value, total)
        total = jnp.concatenate([jnp.zeros((2, width), f32), total, jnp.zeros((6, width), f32)], axis=0)
        high = total.astype(bf16).astype(f32)
        tail_ref[:16, :] = high.astype(bf16)
        tail_ref[16:, :] = (total - high).astype(bf16)


def block_backward(
    length, d_block, n1, r1, n2, r2, act, slope, attended, own, packed, gain, shift, divergence, squares, six,
):
    rows, width = d_block.shape
    tile = min(256, rows)
    shares, units = six.shape[0], D
    row, column = by_tile(tile, width), by_tile(tile, 1)
    return pl.pallas_call(
        block_backward_kernel,
        grid=(rows // tile,),
        in_specs=[
            SMEM, row, row, column, row, column, whole(act.shape), by_tile(tile, shares * units), whole(own.shape), mid_part(packed), whole(gain.shape), whole(shift.shape),
            whole(divergence[0].shape), whole(divergence[1].shape), whole(squares.shape), whole(six.shape),
        ] + [whole(a.shape) for a in attended],
        out_specs=[
            row, *[by_tile(tile, 128)] * shares, whole((2 * units + 448, shares * width)), whole((32, width)),
        ],
        out_shape=[
            jax.ShapeDtypeStruct((rows, width), f32),
            *[jax.ShapeDtypeStruct((rows, 128), bf16)] * shares,
            jax.ShapeDtypeStruct((2 * units + 448, shares * width), bf16),
            jax.ShapeDtypeStruct((32, width), bf16),
        ],
        scratch_shapes=[
            pltpu.VMEM((8, width), f32),
            pltpu.VMEM((8, units), f32),
            pltpu.VMEM((rows, width), bf16),
            pltpu.VMEM((rows, width), bf16),
            pltpu.VMEM((rows, shares * units), bf16),
            pltpu.VMEM((rows, width), bf16),
            pltpu.VMEM((shares, 2 * D + 128, D), bf16),
        ],
        compiler_params=pltpu.CompilerParams(vmem_limit_bytes=VMEM),
        cost_estimate=cost(25),
        name="block_backward",
    )(
        length, d_block, n1, r1, n2, r2, act, slope, own, packed, gain, shift, *divergence, squares, six, *attended
    )


def after(value, *others):
    return lax.optimization_barrier((value,) + others)[0]


def shift_shares(value, by):
    shares = lax.axis_size("heads")
    return lax.ppermute(value, "heads", [((i + by) % shares, i) for i in range(shares)])


def exchange(value, bit):
    size = lax.axis_size("batch")
    return lax.ppermute(value, "batch", [(i, i ^ bit) for i in range(size)])


def merge_kernel(*refs, count):
    outs = refs[count:]
    total = refs[0][...].astype(f32)
    for ref in refs[1:count]:
        total = total + ref[...].astype(f32)
    end = total.shape[0] - 32
    sums = total[end : end + 16] + total[end + 16 :]
    if len(outs) == 2:
        put_turned(total[:end], outs[0])
        outs[1][...] = sums
    else:
        high = sums.astype(bf16).astype(f32)
        outs[0][:end, :] = total[:end].astype(bf16)
        outs[0][end : end + 16, :] = high.astype(bf16)
        outs[0][end + 16 :, :] = (sums - high).astype(bf16)


def put_turned(rows, out_ref):
    for part in range(3):
        out_ref[:, part, :] = rows[part * 96 : (part + 1) * 96].T


def merge(parts, last=False):
    rows, width = parts[0].shape
    if last:
        shape = [jax.ShapeDtypeStruct((width, 3, 96), f32), jax.ShapeDtypeStruct((16, width), f32)]
    else:
        shape = jax.ShapeDtypeStruct((rows, width), bf16)
    return pl.pallas_call(
        functools.partial(merge_kernel, count=len(parts)), out_shape=shape, cost_estimate=cost(1), name="merge",
        compiler_params=pltpu.CompilerParams(vmem_limit_bytes=VMEM),
    )(*parts)


def finish_mid_kernel(rows_ref, narrow_ref, wide_ref, out_ref, bias_ref, six_ref, sums_ref):
    units = narrow_ref.shape[0]
    narrow_ref[...] = rows_ref[:units, :].astype(f32)
    wide_ref[...] = rows_ref[units : 2 * units, :].astype(f32)
    out_ref[...] = rows_ref[2 * units : 2 * units + 96, :].astype(f32)
    bias_ref[...] = rows_ref[2 * units + 96 : 2 * units + 112, :].astype(f32)[:8]
    six = 2 * units + 128
    put_turned(rows_ref[six : six + 288, :].astype(f32), six_ref)
    sums_ref[...] = rows_ref[six + 288 : six + 304, :].astype(f32) + rows_ref[six + 304 :, :].astype(f32)


def finish_mid(rows):
    width = rows.shape[1]
    shapes = [(D, width), (D, width), (96, width), (8, width), (width, 3, 96), (16, width)]
    return pl.pallas_call(
        finish_mid_kernel, out_shape=[jax.ShapeDtypeStruct(s, f32) for s in shapes], cost_estimate=cost(1),
        name="finish_mid", compiler_params=pltpu.CompilerParams(vmem_limit_bytes=VMEM),
    )(rows)


def body(
    student_rows, teacher_rows, valid_length, split_point, project_five, bias_five, output_five, branch_bias,
    norm_gain, norm_bias, widen_weight, widen_bias, narrow_weight, project_six, bias_six, teacher_project,
    teacher_bias,
):
    shares = lax.axis_size("heads")
    batch = lax.axis_size("batch")
    place = lax.axis_index("batch")
    all_rows = shares * batch * HEADS
    x = student_rows[0]
    teacher = teacher_rows[0]

    def turned(weight):
        return jnp.transpose(weight, (1, 2, 0)).reshape(-1, weight.shape[0])

    def pad(rows, width):
        return jnp.pad(rows, ((0, 0), (0, width - rows.shape[1])))

    small = jnp.concatenate(
        [pad(bias_five, D), pad(bias_six, D), widen_bias[None], pad(teacher_bias, D), jnp.zeros((9, D), bf16)], axis=0
    )
    five = jnp.concatenate([turned(project_five), small], axis=0)

    def part_of(rows):
        count = part_rows(rows.shape[0], batch)
        rows = jnp.pad(rows, ((0, count * batch - rows.shape[0]), (0, 0)))
        return lax.dynamic_slice_in_dim(rows, place * count, count)

    def others(rows):
        return [shift_shares(rows, by) for by in range(1, shares)]

    half = five.shape[0] // 2
    core = lax.rem(place, 2)
    halves = others(lax.dynamic_slice_in_dim(five, core * half, half))
    mid = jnp.concatenate([widen_weight, narrow_weight, jnp.pad(output_five, ((0, 32), (0, 0)))], axis=0)
    taught = turned(teacher_project)
    rest = jnp.concatenate([turned(project_six), taught[:, :D], taught[:, D:]], axis=0)
    parts = others(after(jnp.concatenate([part_of(mid), part_of(rest)], axis=0), five))

    first = attend_forward(valid_length, x, five[None])
    halves = jnp.stack([after(p, first[5]) for p in halves])
    swapped = exchange(halves, 1)
    parts = jnp.stack([after(p, first[5], halves) for p in parts])
    parts_all = lax.all_gather(parts, "batch", axis=0)
    low, high = jnp.where(core == 0, halves, swapped), jnp.where(core == 0, swapped, halves)
    fives = jnp.concatenate([low, high], axis=1)
    smalls = jnp.concatenate([five[None, 288:], fives[:, 288:]], axis=0)
    other = attend_forward(valid_length, after(x, parts), fives)
    attended = (first[5], other[5])
    block, n1, r1, n2, r2, act, slope, squares = block_forward(
        valid_length, x, attended, mid, parts_all, smalls, branch_bias, norm_gain, norm_bias
    )
    d_block, g_six, *divergence = relations(
        valid_length, split_point, block, teacher, rest, parts_all, smalls, all_rows
    )
    result = block_backward(
        valid_length, d_block, n1, r1, n2, r2, act, slope, attended, mid, parts_all, norm_gain, norm_bias,
        divergence, squares, g_six,
    )
    d_sum_one, d_attended, (g_both, tail) = result[0], result[1 : 1 + shares], result[1 + shares :]

    def to_owner(parts):
        return [parts[0]] + [shift_shares(parts[by], shares - by) for by in range(1, shares)]

    units = widen_weight.shape[1]
    both = lax.psum_scatter(g_both, "batch", scatter_dimension=0, tiled=True)

    grad_in = d_sum_one
    g_five = [None] * shares
    for s in list(range(1, shares)) + [0]:
        q, k, v, e, r, a = other if s else first
        rows, w = after(x, *g_five[1 : shares - 1]) if s == 0 else x, fives if s else five[None]
        grad, grad_in = attend_backward(max(s - 1, 0), q, k, v, e, r, a, d_attended[s], rows, w, grad_in, tail)
        g_five[s] = shift_shares(grad, shares - s) if s else grad

    five_sum = merge(g_five)
    both = after(both, five_sum)
    both = to_owner([both[:, s * D : (s + 1) * D] for s in range(shares)])
    bits = [1 << i for i in range(batch.bit_length() - 1)]
    for index, bit in enumerate(bits):
        received = exchange(five_sum, bit)
        if index == 1:
            both = [after(p, five_sum) for p in both]
            both = sum(p.astype(f32) for p in both).astype(bf16)
            five_sum = after(five_sum, both)
        if index == len(bits) - 1:
            both = lax.all_gather(after(both, five_sum), "batch", axis=0, tiled=True)
            five_sum = after(five_sum, both)
        five_sum = merge([five_sum, received], last=index == len(bits) - 1)
    grad_five, five_sums = five_sum
    grad_narrow, grad_wide, grad_out, wide_bias, grad_six, six_sums = finish_mid(both)
    totals = five_sums[8]
    counted = totals[4] * D
    summary = jnp.concatenate([totals[:1], jnp.sqrt(totals[1:4] / counted)])
    return (
        block[None], grad_in[None], grad_five, five_sums[0:2, :96],
        grad_out, five_sums[2:4], five_sums[4:6], five_sums[6:8],
        grad_wide, wide_bias[0], grad_narrow, grad_six, six_sums[0:2, :96], summary,
    )


def solution(mesh):
    return jax.shard_map(
        body,
        mesh=mesh,
        in_specs=(
            P(("batch", "heads"), None, None),
            P(("batch", "heads"), None, None),
            P("batch"),
            P("batch"),
            P(None, None, "heads"),
            P(None, "heads"),
            P("heads", None),
            P(),
            P(),
            P(),
            P(None, "heads"),
            P("heads"),
            P("heads", None),
            P(None, None, "heads"),
            P(None, "heads"),
            P(None, None, "heads"),
            P(None, "heads"),
        ),
        out_specs=(
            P(("batch", "heads"), None, None),
            P(("batch", "heads"), None, None),
            P(None, None, "heads"),
            P(None, "heads"),
            P("heads", None),
            P(),
            P(),
            P(),
            P(None, "heads"),
            P("heads"),
            P("heads", None),
            P(None, None, "heads"),
            P(None, "heads"),
            P(),
        ),
        check_vma=False,
    )
```

```python
import functools
import math

import jax
import jax.numpy as jnp
from jax import lax
from jax.experimental import pallas as pl
from jax.experimental.pallas import tpu as pltpu
from jax.sharding import PartitionSpec as P

D = 384
HEADS = 12
HEAD_DIM = 32
TEACHER_HEAD_DIM = 64
PART = 3
TILE = 512
STRIP = 16
NORM_EPS = 1e-12
MASKED = -1e30
SAFE = 64.0
LN2 = math.log(2.0)
STUDENT_SCALE = 1.0 / math.sqrt(HEAD_DIM)
STUDENT_LOG = math.log2(math.e) / math.sqrt(HEAD_DIM)
TEACHER_LOG = math.log2(math.e) / math.sqrt(TEACHER_HEAD_DIM)
VMEM = 56 * 2**20

f32 = jnp.float32
bf16 = jnp.bfloat16

NN = (((1,), (0,)), ((), ()))
NT = (((1,), (1,)), ((), ()))
TN = (((0,), (0,)), ((), ()))


def dot(left, right, dims=NN):
    return lax.dot_general(left, right, dims, preferred_element_type=f32)


def lanes(shape):
    return lax.broadcasted_iota(jnp.int32, shape, 1)


def wide_rows(rows):
    return jnp.concatenate([rows, jnp.zeros((rows.shape[0], 128 - rows.shape[1]), rows.dtype)], axis=1)


def in_head(lane, head, size=HEAD_DIM):
    return (lane >= head * size) & (lane < (head + 1) * size)


def split_terms(rows, head, size, extra):
    inside = in_head(lanes(rows.shape), head, size)
    high = rows.astype(bf16).astype(f32)
    first = jnp.where(inside, high, extra).astype(bf16)
    second = jnp.where(inside, rows - high, 0.0).astype(bf16)
    return jnp.concatenate([first, second], axis=1)


def own_number(ref):
    return ref[lax.axis_index("heads")]


def key_bias(rows, length):
    position = lax.broadcasted_iota(jnp.int32, (rows, 1), 0)
    return jnp.where(position < length, 0.0, MASKED)


def fold(tile, combine):
    total = tile[:, :128]
    for column in range(128, tile.shape[1], 128):
        total = combine(total, tile[:, column : column + 128])
    return total


def row_sum(tile):
    return jnp.sum(fold(tile, jnp.add), axis=1, keepdims=True)


def weave(first, second):
    done = 0
    for index, step in enumerate(second):
        while done < len(first) and done * len(second) < len(first) * (index + 1):
            first[done]()
            done += 1
        step()
    for step in first[done:]:
        step()


def step_place(step, tile, per_head):
    head = step // per_head
    return head, pl.ds(pl.multiple_of(lax.rem(step, per_head) * tile, tile), tile)


def skew(first, second):
    steps = [first[0]]
    for index in range(1, len(first)):
        steps += [first[index], second[index - 1]]
    return steps + [second[-1]]


def run_rolled(steps, logits, vector, back, reset=None, enter=None):
    def pair(index, carry):
        for slot in range(2):
            step = 2 * index + slot
            if enter is not None:
                enter(step, slot, index)
            ahead = logits(jnp.minimum(step + 1, steps - 1), 1 - slot)
            weave(ahead + back(jnp.maximum(step - 1, 0), 1 - slot), vector(step, slot))
            if slot == 0 and reset is not None:
                pl.when(index == 0)(reset)
        return carry

    for chunk in logits(jnp.int32(0), 0):
        chunk()
    lax.fori_loop(0, steps // 2, pair, 0)
    for chunk in back(jnp.int32(steps - 1), 1):
        chunk()


def run_pipeline(steps, logits, vector, back, enter=None):
    def stage(step, slot, before, after, second=False):
        if enter is not None:
            enter(step, slot, not before, second)
        ahead = logits(step + 1, 1 - slot) if after else []
        behind = back(step - 1, 1 - slot) if before else []
        weave(ahead + behind, vector(step, slot))

    for chunk in logits(jnp.int32(0), 0):
        chunk()
    stage(jnp.int32(0), 0, False, True)
    stage(jnp.int32(1), 1, True, True, second=True)

    def pair(index, carry):
        stage(2 * index + 2, 0, True, True)
        stage(2 * index + 3, 1, True, True)
        return carry

    lax.fori_loop(0, (steps - 4) // 2, pair, 0)
    stage(jnp.int32(steps - 2), 0, True, True)
    stage(jnp.int32(steps - 1), 1, True, False)
    for chunk in back(jnp.int32(steps - 1), 1):
        chunk()


def project_part(x, w_ref, index, bias):
    flat = dot(x, w_ref[index * 96 : (index + 1) * 96, :], NT)
    if bias is not None:
        flat = flat + bias
    return wide_rows(flat).astype(bf16)


def attend_forward_kernel(
    length_ref, x_ref, w_ref, q_ref, k_ref, v_ref, e_hbm, r_ref, o_ref, lhs, rhs, mixer, zs0, zs1, es0, es1, sems
):
    share = pl.program_id(0)
    w_ref, q_ref, k_ref, v_ref, r_ref, o_ref = (t.at[0] for t in (w_ref, q_ref, k_ref, v_ref, r_ref, o_ref))
    zs, es = (zs0, zs1), (es0, es1)
    rows = x_ref.shape[0]
    tile = zs0.shape[0]
    per_head = rows // tile
    steps = PART * per_head
    x = x_ref[...]
    small = w_ref[288:304, :].astype(f32)
    q = project_part(x, w_ref, 0, small[0:1, :96])
    k = project_part(x, w_ref, 1, None)
    v = project_part(x, w_ref, 2, small[1:2, :96])
    q_ref[...] = q
    k_ref[...] = k
    v_ref[...] = v
    lane = lanes((rows, 128))
    one = jnp.where(lane == 96, 1.0, 0.0)
    for head in range(PART):
        lhs[head] = jnp.where(in_head(lane, head), q.astype(f32), one).astype(bf16)
    rhs[...] = jnp.where(lane == 96, key_bias(rows, own_number(length_ref)), k.astype(f32)).astype(bf16)
    mixer[...] = jnp.where(lane == 96, 1.0, v.astype(f32)).astype(bf16)
    o_ref[...] = jnp.zeros_like(o_ref)
    r_ref[...] = jnp.zeros_like(r_ref)

    def out_copy(step, slot):
        head, span = step_place(step, tile, per_head)
        return pltpu.make_async_copy(es[slot], e_hbm.at[share, head, span], sems.at[slot])

    def logits(step, slot):
        head, span = step_place(step, tile, per_head)

        def chunk(start):
            zs[slot][:, start : start + 256] = dot(lhs[head, span, :], rhs[start : start + 256, :], NT)

        return [functools.partial(chunk, start) for start in range(0, rows, 256)]

    def vector(step, slot):
        def strip(start):
            z = zs[slot][start : start + STRIP, :]
            highest = jnp.max(fold(z, jnp.maximum), axis=1, keepdims=True)
            es[slot][start : start + STRIP, :] = jnp.exp2((z - highest) * STUDENT_LOG).astype(bf16)

        return [functools.partial(strip, start) for start in range(0, tile, STRIP)]

    def back(step, slot):
        head, span = step_place(step, tile, per_head)

        sums = []

        def part(start):
            sums.append(dot(es[slot][:, start : start + 256], mixer[start : start + 256, :]))

        def mix():
            mixed = functools.reduce(jnp.add, sums)
            inverse = 1.0 / mixed[:, 96:97]
            inside = in_head(lanes(mixed.shape), head)
            o_ref[span, :] = jnp.where(inside, mixed * inverse, o_ref[span, :].astype(f32)).astype(bf16)
            r_ref[span, :] = jnp.where(inside, inverse, r_ref[span, :])

        return [functools.partial(part, start) for start in range(0, rows, 256)] + [mix]

    def enter(step, slot, first, second):
        if not first:
            out_copy(step - 1, 1 - slot).start()
        if not (first or second):
            out_copy(step - 2, slot).wait()

    run_pipeline(steps, logits, vector, back, enter)
    out_copy(jnp.int32(steps - 1), 1).start()
    out_copy(jnp.int32(steps - 2), 0).wait()
    out_copy(jnp.int32(steps - 1), 1).wait()


def whole(shape):
    return pl.BlockSpec(shape, lambda *_: (0,) * len(shape))


SMEM = pl.BlockSpec(memory_space=pltpu.SMEM)
ANY = pl.BlockSpec(memory_space=pl.ANY)


def cost(micros):
    return pl.CostEstimate(flops=int(micros * 0.04e9), bytes_accessed=1024, transcendentals=0)


def attend_forward(length, x, w):
    rows, count = x.shape[0], w.shape[0]
    tile = min(TILE, rows // 2)
    narrow = jax.ShapeDtypeStruct((count, rows, 128), bf16)

    def share(shape):
        return pl.BlockSpec((1,) + shape, lambda s: (s,) + (0,) * len(shape))

    row = share((rows, 128))
    return pl.pallas_call(
        attend_forward_kernel,
        grid=(count,),
        in_specs=[SMEM, whole(x.shape), share(w.shape[1:])],
        out_specs=[row] * 3 + [ANY] + [row] * 2,
        out_shape=[
            narrow, narrow, narrow, jax.ShapeDtypeStruct((count, PART, rows, rows), bf16),
            jax.ShapeDtypeStruct((count, rows, 128), f32), narrow,
        ],
        scratch_shapes=[
            pltpu.VMEM((PART, rows, 128), bf16),
            pltpu.VMEM((rows, 128), bf16),
            pltpu.VMEM((rows, 128), bf16),
            pltpu.VMEM((tile, rows), f32),
            pltpu.VMEM((tile, rows), f32),
            pltpu.VMEM((tile, rows), bf16),
            pltpu.VMEM((tile, rows), bf16),
            pltpu.SemaphoreType.DMA((2,)),
        ],
        compiler_params=pltpu.CompilerParams(vmem_limit_bytes=VMEM),
        cost_estimate=cost(9 * count),
        name="attend_forward",
    )(length, x, w)


def attend_backward_kernel(
    q_ref, k_ref, v_ref, e_hbm, r_ref, a_ref, d_ref, x_hbm, w_hbm, acc_hbm, tail_ref, g_ref, in_ref,
    lhs, rhs, keys, qt, dt, zs0, zs1, gs0, gs1, dq, dkt, dvt, e_all, x_ref, w_ref, acc_ref, sems, late, *, share,
):
    q_ref, k_ref, v_ref, r_ref, a_ref = (t.at[0] for t in (q_ref, k_ref, v_ref, r_ref, a_ref))
    rows = q_ref.shape[0]
    zs, gs = (zs0, zs1), (gs0, gs1)
    tile = zs0.shape[0]
    per_head = rows // tile
    steps = PART * per_head

    def in_copy(step):
        head, span = step_place(step, tile, per_head)
        return pltpu.make_async_copy(e_hbm.at[share, head, span], e_all.at[head, span], sems.at[step])

    def begin(step, carry):
        in_copy(step).start()
        return carry

    lax.fori_loop(0, steps, begin, 0)
    late_copies = [
        pltpu.make_async_copy(source, target, late.at[index])
        for index, (source, target) in enumerate(((x_hbm, x_ref), (w_hbm.at[share], w_ref), (acc_hbm, acc_ref)))
    ]
    for copy in late_copies:
        copy.start()
    lane = lanes((rows, 128))
    grads = r_ref[...] * d_ref[...].astype(f32)
    shifts = grads * a_ref[...].astype(f32)
    k = k_ref[...].astype(f32)
    def one_head(head, carry):
        inside = in_head(lane, head)
        shift = -jnp.sum(jnp.where(inside, shifts, 0.0), axis=1, keepdims=True)
        high = shift.astype(bf16).astype(f32)
        lhs[head] = split_terms(
            grads, head, HEAD_DIM, jnp.where(lane == 96, high, jnp.where(lane == 97, shift - high, 0.0))
        )
        keys[head] = jnp.where(inside, k, 0.0).astype(bf16)
        return carry

    lax.fori_loop(0, PART, one_head, 0)
    rhs[:, :128] = jnp.where((lane == 96) | (lane == 97), 1.0, v_ref[...].astype(f32)).astype(bf16)
    rhs[:, 128:] = v_ref[...]
    qt[...] = q_ref[...].T
    dt[...] = grads.astype(bf16).T

    def reset():
        dq[...] = jnp.zeros_like(dq)
        dkt[...] = jnp.zeros_like(dkt)
        dvt[...] = jnp.zeros_like(dvt)

    reset()

    def logits(step, slot):
        head, span = step_place(step, tile, per_head)

        def chunk(start):
            zs[slot][:, start : start + 256] = dot(lhs[head, span, :], rhs[start : start + 256, :], NT)

        return [functools.partial(chunk, start) for start in range(0, rows, 256)]

    def vector(step, slot):
        head, span = step_place(step, tile, per_head)
        base = lax.rem(step, per_head) * tile

        def strip(start):
            here = pl.ds(pl.multiple_of(base + start, STRIP), STRIP)
            weights = e_all[head, here, :].astype(f32)
            gs[slot][start : start + STRIP, :] = (weights * zs[slot][start : start + STRIP, :]).astype(bf16)

        return [functools.partial(strip, start) for start in range(0, tile, STRIP)]

    def back(step, slot):
        head, span = step_place(step, tile, per_head)
        own = pl.ds(pl.multiple_of(head * HEAD_DIM, HEAD_DIM), HEAD_DIM)

        def first():
            dq[span, :] += dot(gs[slot][...], keys[head])

        def second(start):
            part = slice(start, start + 256)
            dkt[own, part] += dot(qt[own, span], gs[slot][:, part])

        def third(start):
            part = slice(start, start + 256)
            dvt[own, part] += dot(dt[own, span], e_all[head, span, part])

        starts = range(0, rows, 256)
        return [first] + [functools.partial(second, s) for s in starts] + [functools.partial(third, s) for s in starts]

    run_pipeline(steps, logits, vector, back, lambda step, slot, first, second: in_copy(step).wait())
    for copy in late_copies:
        copy.wait()
    grads = (
        (dq[...] * STUDENT_SCALE).astype(bf16),
        (dkt[...] * STUDENT_SCALE).T.astype(bf16),
        dvt[...].T.astype(bf16),
    )
    weight_grads(grads, x_ref[...], g_ref, tail_ref[:16, :].astype(f32), tail_ref[16:, :].astype(f32))
    in_ref[...] = acc_ref[...] + spread(grads, w_ref)


def weight_grads(grads, x, g_ref, tail_high=0.0, tail_low=0.0):
    for index, grad in enumerate(grads):
        g_ref[index * 96 : (index + 1) * 96, :] = dot(grad, x, TN)[:96].astype(bf16)
    ones = jnp.ones((16, x.shape[0]), bf16)
    row = lax.broadcasted_iota(jnp.int32, (16, 128), 0)
    sums = jnp.where(row == 0, dot(ones, grads[0]), jnp.where(row == 1, dot(ones, grads[2]), 0.0))
    sums = jnp.concatenate([sums, jnp.zeros((16, x.shape[1] - 128), f32)], axis=1) + tail_high
    high = sums.astype(bf16).astype(f32)
    g_ref[288:304, :] = high.astype(bf16)
    g_ref[304:320, :] = (sums - high + tail_low).astype(bf16)


def spread(grads, w_ref):
    total = None
    for index, grad in enumerate(grads):
        term = dot(grad[:, :96], w_ref[index * 96 : (index + 1) * 96, :])
        total = term if total is None else total + term
    return total


def attend_backward(share, q, k, v, e, r, attended, d_attended, x, w, grad_in, tail):
    rows = x.shape[0]
    tile = min(TILE, rows // 2)
    row = pl.BlockSpec((1, rows, 128), lambda i: (share, 0, 0))
    return pl.pallas_call(
        functools.partial(attend_backward_kernel, share=share),
        grid=(1,),
        in_specs=[row, row, row, ANY, row, row, whole((rows, 128)), ANY, ANY, ANY, whole(tail.shape)],
        out_specs=[whole((320, x.shape[1])), whole(x.shape)],
        out_shape=[jax.ShapeDtypeStruct((320, x.shape[1]), bf16), jax.ShapeDtypeStruct(x.shape, f32)],
        scratch_shapes=[
            pltpu.VMEM((PART, rows, 256), bf16),
            pltpu.VMEM((rows, 256), bf16),
            pltpu.VMEM((PART, rows, 128), bf16),
            pltpu.VMEM((128, rows), bf16),
            pltpu.VMEM((128, rows), bf16),
            pltpu.VMEM((tile, rows), f32),
            pltpu.VMEM((tile, rows), f32),
            pltpu.VMEM((tile, rows), bf16),
            pltpu.VMEM((tile, rows), bf16),
            pltpu.VMEM((rows, 128), f32),
            pltpu.VMEM((128, rows), f32),
            pltpu.VMEM((128, rows), f32),
            pltpu.VMEM((PART, rows, rows), bf16),
            pltpu.VMEM(x.shape, bf16),
            pltpu.VMEM(w.shape[1:], bf16),
            pltpu.VMEM(x.shape, f32),
            pltpu.SemaphoreType.DMA((PART * (rows // tile),)),
            pltpu.SemaphoreType.DMA((3,)),
        ],
        compiler_params=pltpu.CompilerParams(vmem_limit_bytes=VMEM),
        cost_estimate=cost(10),
        name="attend_backward",
    )(q, k, v, e, r, attended, d_attended, x, w, grad_in, tail)


def relation_kernel(
    length_ref, split_ref, block_ref, teacher_ref, packed_ref, small_ref, *rest, all_rows, gathered,
):
    before = None
    if gathered:
        before, rest = rest[:3], rest[3:]
    (
    d_ref, g_ref, kl_ref, kl_row_ref, pack, lefts, rights, t_lefts, t_rights, ls, rs, lt, rt, keys, left_t, zs0, zs1, zt0, zt1, gs0, gs1,
    left_sum, right_t, es_all, et_all, parts, columns, factors, rows_s, weight, weight_row, grads_s,
    ) = rest
    rows = block_ref.shape[0]
    tile = zs0.shape[0]
    per_head = rows // tile
    steps = PART * per_head
    zs, zt, gs = (zs0, zs1), (zt0, zt1), (gs0.at[:tile], gs1)
    length, split = own_number(length_ref), own_number(split_ref)

    @pl.when(pl.program_id(0) == 0)
    def _():
        position = lax.broadcasted_iota(jnp.int32, (rows, 1), 0)
        counted = (position < length) & (position != 0) & (position != split - 1) & (position != length - 1)
        share = 1.0 / ((length - 3).astype(f32) * float(all_rows))
        weight[...] = jnp.where(counted, share, 0.0)
        position = lanes((1, rows))
        counted = (position < length) & (position != 0) & (position != split - 1) & (position != length - 1)
        weight_row[...] = jnp.where(counted, share, 0.0)
        for index, ref in enumerate((d_ref, kl_ref, kl_row_ref)):
            ref[...] = before[index][...] if gathered else jnp.zeros_like(ref)

    if gathered:
        unpack(packed_ref, 0, pack)
    else:
        pack[...] = packed_ref[...]

    g_ref = g_ref.at[0]
    small = small_ref[0].astype(f32)

    def largest(low, size):
        square = low.astype(f32)
        same = lax.broadcasted_iota(jnp.int32, (128, 128), 0) // size == lanes((128, 128)) // size
        return jnp.max(dot((square * square).astype(bf16), jnp.where(same, 1.0, 0.0).astype(bf16)), axis=0, keepdims=True)

    def project(index, carry):
        here = pl.ds(pl.multiple_of(index * tile, tile), tile)
        block, teacher = block_ref[here, :], teacher_ref[here, :]

        def student(part, b):
            flat = dot(block, pack[part * 96 : (part + 1) * 96, :], NT)
            return wide_rows(flat if b is None else flat + b).astype(bf16)

        def taught(part, b):
            start = 288 + part * 192
            flat = dot(teacher[:, :D], pack[start : start + 192, :], NT)
            flat = flat + dot(teacher[:, D:], pack[start + 576 : start + 768, :], NT)
            flat = (flat if b is None else flat + b).astype(bf16)
            return flat[:, :128], wide_rows(flat[:, 128:])

        q, k, v = student(0, small[2:3, :96]), student(1, None), student(2, small[3:4, :96])
        lefts[0, here, :] = q
        rights[0, here, :] = k
        lefts[1, here, :] = v
        rights[1, here, :] = v
        tq, tk, tv = taught(0, small[5:6, :192]), taught(1, None), taught(2, small[6:7, :192])
        for half in range(2):
            t_lefts[0, half, here, :] = tq[half]
            t_rights[0, half, here, :] = tk[half]
            t_lefts[1, half, here, :] = tv[half]
            t_rights[1, half, here, :] = tv[half]
        found = [largest(value, HEAD_DIM) for value in (q, k, v)]
        found += [largest(value, TEACHER_HEAD_DIM) for value in tq + tk + tv]
        return tuple(jnp.maximum(old, new) for old, new in zip(carry, found))

    top = lax.fori_loop(0, rows // tile, project, (jnp.zeros((1, 128), f32),) * 9)
    bounds = []
    for s_left, s_right, t_left, t_right in ((0, 1, 3, 5), (2, 2, 7, 7)):
        bound = jnp.max(top[s_left] * top[s_right]) * STUDENT_LOG**2
        for half in range(2):
            bound = jnp.maximum(bound, jnp.max(top[t_left + half] * top[t_right + half]) * TEACHER_LOG**2)
        bounds.append(bound)

    def operands(relation, student_scale, teacher_scale, row_bias, everything):
        band = min(128, rows)
        line = lanes((1, 128))

        def terms(value, inside, extra):
            high, low = value
            return jnp.where(inside, high, extra).astype(bf16), jnp.where(inside, low, 0.0).astype(bf16)

        def halves(value, scale):
            value = value * scale
            high = value.astype(bf16).astype(f32)
            return high, value - high

        def one_band(index, carry):
            here = pl.ds(pl.multiple_of(index * band, band), band)
            position = lax.broadcasted_iota(jnp.int32, (band, 128), 0) + index * band
            bias = jnp.where(position < length, 0.0, MASKED)
            row = jnp.where(row_bias, bias, 0.0)
            left, right = lefts[relation, here, :].astype(f32), rights[relation, here, :].astype(f32)
            value = halves(left, student_scale)
            extra = jnp.where(line == 97, row, jnp.where(line == 96, 1.0, 0.0))
            if everything:
                rs[here, :128] = jnp.where(line == 97, 1.0, jnp.where(line == 96, bias, right)).astype(bf16)
                rs[here, 128:] = rights[relation, here, :]
            for head in range(PART):
                inside = in_head(line, head)
                ls[head, here, :128], ls[head, here, 128:] = terms(value, inside, extra)
                if everything:
                    keys[head, here, :] = jnp.where(inside, right, 0.0).astype(bf16)
            for half in range(2):
                t_left = t_lefts[relation, half, here, :].astype(f32)
                t_right = t_rights[relation, half, here, :].astype(f32)
                value = halves(t_left, teacher_scale)
                for head in range(2 * half, min(2 * half + 2, PART)):
                    own = head % 2
                    spare = (1 - own) * TEACHER_HEAD_DIM
                    extra = jnp.where(line == spare + 1, row, jnp.where(line == spare, 1.0, 0.0))
                    inside = in_head(line, own, TEACHER_HEAD_DIM)
                    lt[head, here, :128], lt[head, here, 128:] = terms(value, inside, extra)
                    if everything:
                        first = jnp.where(line == spare + 1, 1.0, jnp.where(line == spare, bias, t_right))
                        rt[head, here, :128] = first.astype(bf16)
                        rt[head, here, 128:] = t_rights[relation, half, here, :]
            return carry

        lax.fori_loop(0, rows // band, one_band, 0)

    def relate(relation, carry):
        symmetric = relation == 1
        left_t[...] = lefts[relation].T
        operands(relation, STUDENT_LOG, TEACHER_LOG, symmetric, True)
        near = jnp.where(symmetric, bounds[1], bounds[0]) < SAFE * SAFE
        reset()

        @pl.when(near & jnp.logical_not(symmetric))
        def _():
            run_pipeline(steps, logits, vector, grad_products)

        @pl.when(near & symmetric)
        def _():
            lax.fori_loop(0, PART, symmetric_head, 0)

        @pl.when(jnp.logical_not(near))
        def _():
            operands(relation, 1.0, 1.0, False, False)
            lax.fori_loop(0, steps, shifted_step, 0)

        @pl.when(jnp.logical_not(symmetric))
        def _():
            grads_s[0] = (left_sum[...] * STUDENT_SCALE).astype(bf16)
            grads_s[1] = (right_t[...] * STUDENT_SCALE).T.astype(bf16)

        @pl.when(symmetric)
        def _():
            grads_s[2] = ((left_sum[...] + right_t[...].T) * STUDENT_SCALE).astype(bf16)

        return carry

    def reset():
        left_sum[...] = jnp.zeros_like(left_sum)
        right_t[...] = jnp.zeros_like(right_t)

    def logits(step, slot):
        head, span = step_place(step, tile, per_head)

        def student(start):
            zs[slot][:, start : start + 256] = dot(ls[head, span, :], rs[start : start + 256, :], NT)

        def taught(start):
            zt[slot][:, start : start + 256] = dot(lt[head, span, :], rt[head, start : start + 256, :], NT)

        chunks = []
        for start in range(0, rows, 256):
            chunks += [functools.partial(student, start), functools.partial(taught, start)]
        return chunks

    def vector(step, slot):
        base = lax.rem(step, per_head) * tile
        z, t, g = zs[slot], zt[slot], gs[slot]
        scales = {}

        def weigh(start):
            strip = slice(start, start + STRIP)
            sum_s = sum_t = cross = 0.0
            for column in range(0, rows, 128):
                part = slice(column, column + 128)
                student, taught = z[strip, part], t[strip, part]
                es, et = jnp.exp2(student), jnp.exp2(taught)
                z[strip, part] = es
                t[strip, part] = et
                sum_s, sum_t, cross = sum_s + es, sum_t + et, cross + et * (taught - student)
            here = pl.ds(pl.multiple_of(base + start, STRIP), STRIP)
            sum_s, sum_t, cross = (jnp.sum(v, axis=1, keepdims=True) for v in (sum_s, sum_t, cross))
            w = weight[here, :]
            inverse = 1.0 / sum_t
            kl_ref[here, :] += w * (LN2 * cross * inverse + jnp.log(sum_s) - jnp.log(sum_t))
            scales[start] = w / sum_s, w * inverse

        def grad(start):
            strip = slice(start, start + STRIP)
            a, b = scales[start]
            for column in range(0, rows, 128):
                part = slice(column, column + 128)
                g[strip, part] = (z[strip, part] * a - t[strip, part] * b).astype(bf16)

        starts = range(0, tile, STRIP)
        return skew([functools.partial(weigh, s) for s in starts], [functools.partial(grad, s) for s in starts])

    def grad_products(step, slot):
        head, span = step_place(step, tile, per_head)
        own = pl.ds(pl.multiple_of(head * HEAD_DIM, HEAD_DIM), HEAD_DIM)

        def first():
            left_sum[span, :] += dot(gs[slot][...], keys[head])

        def second(start):
            part = slice(start, start + 256)
            right_t[own, part] += dot(left_t[own, span], gs[slot][:, part])

        return [first] + [functools.partial(second, start) for start in range(0, rows, 256)]

    def shifted_step(step, carry):
        head, span = step_place(step, tile, per_head)
        student = dot(ls[head, span, :], rs[...], NT)
        zs0[...] = (student - jnp.max(student, axis=1, keepdims=True)) * STUDENT_LOG
        taught = dot(lt[head, span, :], rt[head], NT)
        zt0[...] = (taught - jnp.max(taught, axis=1, keepdims=True)) * TEACHER_LOG

        def strip(index, carry):
            here = pl.ds(pl.multiple_of(index * STRIP, STRIP), STRIP)
            student, taught = zs0[here, :], zt0[here, :]
            es, et = jnp.exp2(student), jnp.exp2(taught)
            sum_s, sum_t = row_sum(es), row_sum(et)
            cross = row_sum(et * (taught - student))
            there = pl.ds(pl.multiple_of(lax.rem(step, per_head) * tile + index * STRIP, STRIP), STRIP)
            w = weight[there, :]
            row = LN2 * cross / sum_t + jnp.log(sum_s) - jnp.log(sum_t)
            kl_ref[there, :] += jnp.where(w > 0.0, w * row, 0.0)
            gs0[here, :] = (es * (w / sum_s) - et * (w / sum_t)).astype(bf16)
            return carry

        lax.fori_loop(0, tile // STRIP, strip, 0)
        for chunk in grad_products(step, 0):
            chunk()
        return carry

    def symmetric_head(head, carry):
        size, band = min(256, rows), 32
        count = rows // size
        own = pl.ds(pl.multiple_of(head * HEAD_DIM, HEAD_DIM), HEAD_DIM)
        columns[...] = jnp.zeros_like(columns)

        def logit_chunks(i):
            here = slice(i * size, (i + 1) * size)

            def student(part):
                es_all[here, part] = dot(ls[head, here, :], rs[part, :], NT)

            def taught(part):
                et_all[here, part] = dot(lt[head, here, :], rt[head, part, :], NT)

            chunks = []
            for j in range(i, count):
                part = slice(j * size, (j + 1) * size)
                chunks += [functools.partial(student, part), functools.partial(taught, part)]
            return chunks

        def weigh(i, start):
            strip = slice(start, start + band)
            totals = [0.0, 0.0, 0.0]
            for column in range(i * size, rows, 128):
                part = slice(column, column + 128)
                student, taught = es_all[strip, part], et_all[strip, part]
                es, et = jnp.exp2(student), jnp.exp2(taught)
                es_all[strip, part] = es
                et_all[strip, part] = et
                for index, value in enumerate((es, et, et * (taught - student))):
                    totals[index] = totals[index] + value
                    if column >= (i + 1) * size:
                        eight = value[:8]
                        for line in range(8, band, 8):
                            eight = eight + value[line : line + 8]
                        columns[index, :, part] += eight
            for index in range(3):
                parts[index, strip, :] = totals[index]

        def combine(i, start):
            strip = slice(start, start + STRIP)
            a, b = factors[0, strip, :], factors[1, strip, :]
            for column in range(i * size, rows, 128):
                part = slice(column, column + 128)
                both = es_all[strip, part] * (a + rows_s[0, :, part])
                both = both - et_all[strip, part] * (b + rows_s[1, :, part])
                gs0[strip, part] = both.astype(bf16)

        def products(i):
            here = slice(i * size, (i + 1) * size)

            def first(j):
                part = slice(j * size, (j + 1) * size)
                left_sum[here, :] += dot(gs_all[here, part], keys[head, part, :])

            def second(j):
                part = slice(j * size, (j + 1) * size)
                right_t[own, part] += dot(left_t[own, here], gs_all[here, part])

            chunks = [functools.partial(first, j) for j in range(i, count)]
            return chunks + [functools.partial(second, j) for j in range(i + 1, count)]

        gs_all = gs0
        for chunk in logit_chunks(0):
            chunk()
        for i in range(count):
            ahead = logit_chunks(i + 1) if i + 1 < count else []
            weave(ahead, [functools.partial(weigh, i, s) for s in range(i * size, (i + 1) * size, band)])
        sums = [
            jnp.sum(parts[index].T, axis=0, keepdims=True) + jnp.sum(columns[index], axis=0, keepdims=True)
            for index in range(3)
        ]
        w = weight_row[...]
        sum_s, sum_t = (jnp.where(w > 0.0, value, 1.0) for value in sums[:2])
        inverse = 1.0 / sum_t
        kl_row_ref[...] += w * (LN2 * sums[2] * inverse + jnp.log(sum_s) - jnp.log(sum_t))
        for index, value in enumerate((w / sum_s, w * inverse)):
            factors[index] = jnp.broadcast_to(value, (128, rows)).T
            rows_s[index] = jnp.broadcast_to(value, (STRIP, rows))
        for i in range(count):
            behind = products(i - 1) if i else []
            weave(behind, [functools.partial(combine, i, s) for s in range(i * size, (i + 1) * size, STRIP)])
        for chunk in products(count - 1):
            chunk()
        return carry

    lax.fori_loop(0, 2, relate, 0)
    grads = tuple(grads_s[i] for i in range(3))
    weight_grads(grads, block_ref[...], g_ref)
    d_ref[...] += spread(grads, pack)


def part_rows(rows, batch):
    return -(-rows // (16 * batch)) * 16


def unpack(packed_ref, share, target):
    rows, batch = target.shape[0], packed_ref.shape[0]
    part = part_rows(rows, batch)
    for start in range(0, rows, part):
        size = min(part, rows - start)
        target[start : start + size, :] = packed_ref[start // part, share, :size, :]


def relations(length, split, block, teacher, packed, small, all_rows, before=()):
    rows = block.shape[0]
    tile = min(TILE, rows // 2)
    shares = small.shape[0]

    def share(shape):
        return pl.BlockSpec((1,) + shape[1:], lambda s: (s,) + (0,) * (len(shape) - 1))

    gathered = len(before) > 0
    if gathered:
        place = pl.BlockSpec((packed.shape[0], 1) + packed.shape[2:], lambda s: (0, s, 0, 0))
    else:
        place = whole(packed.shape)
    return pl.pallas_call(
        functools.partial(relation_kernel, all_rows=all_rows, gathered=gathered),
        grid=(shares,),
        in_specs=[
            SMEM, SMEM, whole(block.shape), whole(teacher.shape), place, share(small.shape),
        ] + [whole(b.shape) for b in before],
        out_specs=[whole(block.shape), share((shares, 320, D)), whole((rows, 1)), whole((1, rows))],
        out_shape=[
            jax.ShapeDtypeStruct(block.shape, f32),
            jax.ShapeDtypeStruct((shares, 320, D), bf16),
            jax.ShapeDtypeStruct((rows, 1), f32),
            jax.ShapeDtypeStruct((1, rows), f32),
        ],
        scratch_shapes=[
            pltpu.VMEM((1440, D), bf16),
            pltpu.VMEM((2, rows, 128), bf16),
            pltpu.VMEM((2, rows, 128), bf16),
            pltpu.VMEM((2, 2, rows, 128), bf16),
            pltpu.VMEM((2, 2, rows, 128), bf16),
            pltpu.VMEM((PART, rows, 256), bf16),
            pltpu.VMEM((rows, 256), bf16),
            pltpu.VMEM((PART, rows, 256), bf16),
            pltpu.VMEM((PART, rows, 256), bf16),
            pltpu.VMEM((PART, rows, 128), bf16),
            pltpu.VMEM((128, rows), bf16),
            pltpu.VMEM((tile, rows), f32),
            pltpu.VMEM((tile, rows), f32),
            pltpu.VMEM((tile, rows), f32),
            pltpu.VMEM((tile, rows), f32),
            pltpu.VMEM((rows, rows), bf16),
            pltpu.VMEM((tile, rows), bf16),
            pltpu.VMEM((rows, 128), f32),
            pltpu.VMEM((128, rows), f32),
            pltpu.VMEM((rows, rows), f32),
            pltpu.VMEM((rows, rows), f32),
            pltpu.VMEM((3, rows, 128), f32),
            pltpu.VMEM((3, 8, rows), f32),
            pltpu.VMEM((2, rows, 128), f32),
            pltpu.VMEM((2, STRIP, rows), f32),
            pltpu.VMEM((rows, 1), f32),
            pltpu.VMEM((1, rows), f32),
            pltpu.VMEM((3, rows, 128), bf16),
        ],
        compiler_params=pltpu.CompilerParams(vmem_limit_bytes=VMEM),
        cost_estimate=cost(30 * shares),
        name="relations",
    )(length, split, block, teacher, packed, small, *before)


def norm_forward(rows, gain, shift):
    center = jnp.mean(rows, axis=1, keepdims=True)
    offsets = rows - center
    rstd = lax.rsqrt(jnp.mean(offsets * offsets, axis=1, keepdims=True) + NORM_EPS)
    normed = offsets * rstd
    return normed * gain + shift, normed, rstd


def norm_backward(grad, normed, rstd, gain):
    inner = grad * gain
    mean = jnp.mean(inner, axis=1, keepdims=True)
    slope = jnp.mean(inner * normed, axis=1, keepdims=True)
    return rstd * (inner - mean - normed * slope)


def gelu_terms(x):
    size = jnp.abs(x) * math.sqrt(0.5)
    t = 1.0 / (1.0 + 0.3275911 * size)
    bell = jnp.exp(-0.5 * x * x)
    poly = t * (0.254829592 + t * (-0.284496736 + t * (1.421413741 + t * (-1.453152027 + t * 1.061405429))))
    tail = 0.5 * poly * bell
    share = jnp.where(x >= 0.0, 1.0 - tail, tail)
    return x * share, share + x * bell * (1.0 / math.sqrt(2.0 * math.pi))


def unpack_all(own_ref, packed_ref, pack):
    pack[0] = own_ref[...]
    for share in range(1, pack.shape[0]):
        unpack(packed_ref, share - 1, pack.at[share])


def split_pack(pack):
    return pack.at[:, :D], pack.at[:, D : 2 * D], pack.at[:, 2 * D :]


def block_kernel(
    length_ref, x_ref, own_ref, packed_ref, small_ref, branch_ref, gain_ref, shift_ref, first_ref, other_ref,
    block_ref, n1_ref, r1_ref, n2_ref, r2_ref, act_ref, slope_ref, sums_ref, pack,
):
    shares = small_ref.shape[0]
    a_refs = [first_ref.at[0]] + [other_ref.at[s] for s in range(shares - 1)]
    tile = x_ref.shape[0]

    @pl.when(pl.program_id(0) == 0)
    def _():
        unpack_all(own_ref, packed_ref, pack)

    wide_ref, narrow_ref, out_ref = split_pack(pack)
    x = x_ref[...].astype(f32)
    mixing = branch_ref[0:1, :]
    for s in range(shares):
        mixing = mixing + dot(a_refs[s][:, :96], out_ref[s, :96, :])
    middle, normed, rstd = norm_forward(x + mixing, gain_ref[0:1, :], shift_ref[0:1, :])
    n1_ref[...] = normed
    r1_ref[...] = rstd
    low = middle.astype(bf16)
    branch = branch_ref[1:2, :]
    width = D
    for s in range(shares):
        value, slope = gelu_terms(dot(low, wide_ref[s]) + small_ref[s, 4:5, :].astype(f32))
        value = value.astype(bf16)
        act_ref[:, s * width : (s + 1) * width] = value
        slope_ref[:, s * width : (s + 1) * width] = slope.astype(bf16)
        branch = branch + dot(value, narrow_ref[s])
    block, normed, rstd = norm_forward(middle + branch, gain_ref[1:2, :], shift_ref[1:2, :])
    n2_ref[...] = normed
    r2_ref[...] = rstd
    block_ref[...] = block.astype(bf16)
    position = lax.broadcasted_iota(jnp.int32, (tile, 1), 0) + pl.program_id(0) * tile
    kept = jnp.where(position < own_number(length_ref), 1.0, 0.0)
    row = lax.broadcasted_iota(jnp.int32, (8, x.shape[1]), 0)
    total = jnp.zeros((8, x.shape[1]), f32)
    for index, part in enumerate((x, mixing, branch)):
        total = jnp.where(row == index, jnp.sum(kept * part * part, axis=0, keepdims=True), total)

    @pl.when(pl.program_id(0) == 0)
    def _():
        sums_ref[...] = jnp.zeros_like(sums_ref)

    sums_ref[...] += total


def by_tile(tile, width):
    return pl.BlockSpec((tile, width), lambda i: (i, 0))


def block_forward(length, x, attended, own, packed, small, branch_bias, gain, shift):
    rows, width = x.shape
    tile = min(256, rows)
    shares = small.shape[0]
    units = shares * D
    row, column = by_tile(tile, width), by_tile(tile, 1)
    return pl.pallas_call(
        block_kernel,
        grid=(rows // tile,),
        in_specs=[
            SMEM, row, whole(own.shape), whole(packed.shape), whole(small.shape), whole(branch_bias.shape), whole(gain.shape), whole(shift.shape),
        ] + [pl.BlockSpec((a.shape[0], tile, 128), lambda i: (0, i, 0)) for a in attended],
        out_specs=[row, row, column, row, column, by_tile(tile, units), by_tile(tile, units), whole((8, width))],
        out_shape=[
            jax.ShapeDtypeStruct((rows, width), bf16),
            jax.ShapeDtypeStruct((rows, width), f32),
            jax.ShapeDtypeStruct((rows, 1), f32),
            jax.ShapeDtypeStruct((rows, width), f32),
            jax.ShapeDtypeStruct((rows, 1), f32),
            jax.ShapeDtypeStruct((rows, units), bf16),
            jax.ShapeDtypeStruct((rows, units), bf16),
            jax.ShapeDtypeStruct((8, width), f32),
        ],
        scratch_shapes=[pltpu.VMEM((shares, 2 * D + 128, D), bf16)],
        compiler_params=pltpu.CompilerParams(vmem_limit_bytes=VMEM),
        cost_estimate=cost(20),
        name="block_forward",
    )(length, x, own, packed, small, branch_bias, gain, shift, *attended)


def block_backward_kernel(
    length_ref, d_ref, n1_ref, r1_ref, n2_ref, r2_ref, act_ref, slope_ref, own_ref, packed_ref, gain_ref,
    shift_ref, kl_ref, kl_row_ref, square_ref, six_own_ref, six_ref, first_ref, other_ref, *rest,
):
    step = pl.program_id(0)
    pack = rest[-1]
    shares = pack.shape[0]
    a_refs = [first_ref.at[0]] + [other_ref.at[s] for s in range(shares - 1)]
    sum_ref, da_refs = rest[0], rest[1 : shares + 1]
    g_ref, tail_ref, vec_ref, g_sum, low_s, branch_s, pre_s, mix_s = rest[shares + 1 : -1]
    tile, width = d_ref.shape
    units = D
    span = pl.ds(pl.multiple_of(step * tile, tile), tile)

    @pl.when(step == 0)
    def _():
        unpack_all(own_ref, packed_ref, pack)
        vec_ref[...] = jnp.zeros_like(vec_ref)
        g_sum[...] = jnp.zeros_like(g_sum)

    wide_ref, narrow_ref, out_ref = split_pack(pack)

    def column(value):
        return jnp.sum(value, axis=0, keepdims=True)

    row = lax.broadcasted_iota(jnp.int32, (8, width), 0)
    d_block = d_ref[...]
    normed_two = n2_ref[...]
    d_two = norm_backward(d_block, normed_two, r2_ref[...], gain_ref[1:2, :])
    d_branch = d_two.astype(bf16)
    branch_s[span, :] = d_branch
    normed_one = n1_ref[...]
    low = (normed_one * gain_ref[0:1, :] + shift_ref[0:1, :]).astype(bf16)
    low_s[span, :] = low
    d_middle = d_two
    for s in range(shares):
        grad = dot(d_branch, narrow_ref[s], NT) * slope_ref[:, s * units : (s + 1) * units].astype(f32)
        grad = grad.astype(bf16)
        pre_s[span, s * units : (s + 1) * units] = grad
        g_sum[s : s + 1, :] += column(grad.astype(f32))
        d_middle = d_middle + dot(grad, wide_ref[s], NT)
    d_one = norm_backward(d_middle, normed_one, r1_ref[...], gain_ref[0:1, :])
    sum_ref[...] = d_one
    d_mixing = d_one.astype(bf16)
    mix_s[span, :] = d_mixing
    for s in range(shares):
        da_refs[s][...] = wide_rows(dot(d_mixing, out_ref[s, :96, :], NT)).astype(bf16)
    parts = (
        d_mixing.astype(f32), d_branch.astype(f32), d_middle * normed_one, d_block * normed_two, d_middle, d_block,
    )
    total = jnp.zeros((8, width), f32)
    for index, part in enumerate(parts):
        total = jnp.where(row == index, column(part), total)
    vec_ref[...] += total

    @pl.when(step == pl.num_programs(0) - 1)
    def _():
        for s in range(shares):
            part = slice(s * units, (s + 1) * units)
            own = slice(s * width, (s + 1) * width)
            g_ref[0:units, own] = dot(act_ref[:, part], branch_s[...], TN).astype(bf16)
            g_ref[units : 2 * units, own] = dot(low_s[...], pre_s[:, part], TN).astype(bf16)
            g_ref[2 * units : 2 * units + 96, own] = dot(a_refs[s][...], mix_s[...], TN)[:96].astype(bf16)
            g_ref[2 * units + 128 :, own] = six_own_ref[0] if s == 0 else six_ref[s - 1]
            first = lax.broadcasted_iota(jnp.int32, (32, units), 0) == 0
            g_ref[2 * units + 96 : 2 * units + 128, own] = jnp.where(first, g_sum[s : s + 1, :], 0.0).astype(bf16)
        scalars = [jnp.sum(kl_ref[...], axis=0, keepdims=True) + jnp.sum(kl_row_ref[...], axis=1, keepdims=True)]
        scalars += [jnp.sum(square_ref[i : i + 1, :], axis=1, keepdims=True) for i in range(3)]
        scalars += [jnp.broadcast_to(own_number(length_ref).astype(f32), (1, 1))]
        lane = lanes((8, width))
        total = vec_ref[...]
        for index, value in enumerate(scalars):
            total = jnp.where((row == 6) & (lane == index), value, total)
        total = jnp.concatenate([jnp.zeros((2, width), f32), total, jnp.zeros((6, width), f32)], axis=0)
        high = total.astype(bf16).astype(f32)
        tail_ref[:16, :] = high.astype(bf16)
        tail_ref[16:, :] = (total - high).astype(bf16)


def block_backward(
    length, d_block, n1, r1, n2, r2, act, slope, attended, own, packed, gain, shift, divergence, squares, six_own, six,
):
    rows, width = d_block.shape
    tile = min(256, rows)
    shares, units = six.shape[0] + 1, D
    row, column = by_tile(tile, width), by_tile(tile, 1)
    return pl.pallas_call(
        block_backward_kernel,
        grid=(rows // tile,),
        in_specs=[
            SMEM, row, row, column, row, column, whole(act.shape), by_tile(tile, shares * units), whole(own.shape), whole(packed.shape), whole(gain.shape), whole(shift.shape),
            whole(divergence[0].shape), whole(divergence[1].shape), whole(squares.shape), whole(six_own.shape),
            whole(six.shape),
        ] + [whole(a.shape) for a in attended],
        out_specs=[
            row, *[by_tile(tile, 128)] * shares, whole((2 * units + 448, shares * width)), whole((32, width)),
        ],
        out_shape=[
            jax.ShapeDtypeStruct((rows, width), f32),
            *[jax.ShapeDtypeStruct((rows, 128), bf16)] * shares,
            jax.ShapeDtypeStruct((2 * units + 448, shares * width), bf16),
            jax.ShapeDtypeStruct((32, width), bf16),
        ],
        scratch_shapes=[
            pltpu.VMEM((8, width), f32),
            pltpu.VMEM((8, units), f32),
            pltpu.VMEM((rows, width), bf16),
            pltpu.VMEM((rows, width), bf16),
            pltpu.VMEM((rows, shares * units), bf16),
            pltpu.VMEM((rows, width), bf16),
            pltpu.VMEM((shares, 2 * D + 128, D), bf16),
        ],
        compiler_params=pltpu.CompilerParams(vmem_limit_bytes=VMEM),
        cost_estimate=cost(25),
        name="block_backward",
    )(
        length, d_block, n1, r1, n2, r2, act, slope, own, packed, gain, shift, *divergence, squares, six_own, six,
        *attended
    )


def after(value, *others):
    return lax.optimization_barrier((value,) + others)[0]


def shift_shares(value, by):
    shares = lax.axis_size("heads")
    return lax.ppermute(value, "heads", [((i + by) % shares, i) for i in range(shares)])


def exchange(value, bit):
    size = lax.axis_size("batch")
    return lax.ppermute(value, "batch", [(i, i ^ bit) for i in range(size)])


def merge_kernel(*refs, count):
    outs = refs[count:]
    total = refs[0][...].astype(f32)
    for ref in refs[1:count]:
        total = total + ref[...].astype(f32)
    end = total.shape[0] - 32
    sums = total[end : end + 16] + total[end + 16 :]
    if len(outs) > 1:
        grad_ref, bias_ref, branch_ref, gain_ref, shift_ref, summary_ref = outs
        grad_ref[...] = total[:end]
        bias_ref[...] = sums[0:2, :96]
        branch_ref[...] = sums[2:4]
        gain_ref[...] = sums[4:6]
        shift_ref[...] = sums[6:8]
        scalars = sums[8:9, :8]
        roots = jnp.sqrt(scalars / (scalars[:, 4:5] * D))
        summary_ref[...] = jnp.where(lanes((1, 8)) == 0, scalars, roots)[:, :4]
    else:
        high = sums.astype(bf16).astype(f32)
        outs[0][:end, :] = total[:end].astype(bf16)
        outs[0][end : end + 16, :] = high.astype(bf16)
        outs[0][end + 16 :, :] = (sums - high).astype(bf16)


def merge(parts, last=False):
    rows, width = parts[0].shape
    if last:
        shapes = [(rows - 32, width), (2, 96), (2, width), (2, width), (2, width), (1, 4)]
        shape = [jax.ShapeDtypeStruct(s, f32) for s in shapes]
    else:
        shape = jax.ShapeDtypeStruct((rows, width), bf16)
    return pl.pallas_call(
        functools.partial(merge_kernel, count=len(parts)), out_shape=shape, cost_estimate=cost(1), name="merge",
        compiler_params=pltpu.CompilerParams(vmem_limit_bytes=VMEM),
    )(*parts)


def finish_mid_kernel(rows_ref, narrow_ref, wide_ref, out_ref, bias_ref, six_ref, six_bias_ref):
    units = narrow_ref.shape[0]
    narrow_ref[...] = rows_ref[:units, :].astype(f32)
    wide_ref[...] = rows_ref[units : 2 * units, :].astype(f32)
    out_ref[...] = rows_ref[2 * units : 2 * units + 96, :].astype(f32)
    bias_ref[...] = rows_ref[2 * units + 96 : 2 * units + 112, :].astype(f32)[:1]
    six = 2 * units + 128
    six_ref[...] = rows_ref[six : six + 288, :].astype(f32)
    sums = rows_ref[six + 288 : six + 304, :].astype(f32) + rows_ref[six + 304 :, :].astype(f32)
    six_bias_ref[...] = sums[0:2, :96]


def finish_mid(rows):
    width = rows.shape[1]
    shapes = [(D, width), (D, width), (96, width), (1, width), (288, width), (2, 96)]
    return pl.pallas_call(
        finish_mid_kernel, out_shape=[jax.ShapeDtypeStruct(s, f32) for s in shapes], cost_estimate=cost(1),
        name="finish_mid", compiler_params=pltpu.CompilerParams(vmem_limit_bytes=VMEM),
    )(rows)


def body(
    student_rows, teacher_rows, valid_length, split_point, project_five, bias_five, output_five, branch_bias,
    norm_gain, norm_bias, widen_weight, widen_bias, narrow_weight, project_six, bias_six, teacher_project,
    teacher_bias,
):
    shares = lax.axis_size("heads")
    batch = lax.axis_size("batch")
    place = lax.axis_index("batch")
    all_rows = shares * batch * HEADS
    x = student_rows[0]
    teacher = teacher_rows[0]

    def turned(weight):
        return jnp.transpose(weight, (1, 2, 0)).reshape(-1, weight.shape[0])

    def pad(rows, width):
        return jnp.pad(rows, ((0, 0), (0, width - rows.shape[1])))

    small = jnp.concatenate(
        [pad(bias_five, D), pad(bias_six, D), widen_bias[None], pad(teacher_bias, D), jnp.zeros((9, D), bf16)], axis=0
    )
    five = jnp.concatenate([turned(project_five), small], axis=0)

    def part_of(rows):
        count = part_rows(rows.shape[0], batch)
        rows = jnp.pad(rows, ((0, count * batch - rows.shape[0]), (0, 0)))
        return lax.dynamic_slice_in_dim(rows, place * count, count)

    def others(rows):
        return [shift_shares(rows, by) for by in range(1, shares)]

    half = five.shape[0] // 2
    core = lax.rem(place, 2)
    mid = jnp.concatenate([widen_weight, narrow_weight, jnp.pad(output_five, ((0, 32), (0, 0)))], axis=0)
    taught = turned(teacher_project)
    rest = jnp.concatenate([turned(project_six), taught[:, :D], taught[:, D:]], axis=0)
    parts = others(jnp.concatenate([lax.dynamic_slice_in_dim(five, core * half, half), part_of(mid)], axis=0))

    first = attend_forward(valid_length, x, five[None])
    parts = jnp.stack([after(p, first[5]) for p in parts])
    halves, mid_parts = parts[:, :half], parts[:, half:]
    swapped = exchange(halves, 1)
    mid_all = lax.all_gather(mid_parts, "batch", axis=0)
    rest_parts = others(after(part_of(rest), mid_parts))
    low, high = jnp.where(core == 0, halves, swapped), jnp.where(core == 0, swapped, halves)
    fives = jnp.concatenate([low, high], axis=1)
    smalls = jnp.concatenate([five[None, 288:], fives[:, 288:]], axis=0)
    other = attend_forward(valid_length, after(x, mid_parts), fives)
    rest_parts = jnp.stack([after(p, other[5]) for p in rest_parts])
    rest_all = lax.all_gather(rest_parts, "batch", axis=0)
    attended = (first[5], other[5])
    block, n1, r1, n2, r2, act, slope, squares = block_forward(
        valid_length, after(x, rest_parts), attended, mid, mid_all, smalls, branch_bias, norm_gain, norm_bias
    )
    d_block, g_six_own, *divergence = relations(
        valid_length, split_point, block, teacher, rest, smalls[:1], all_rows
    )
    d_block, g_six, *divergence = relations(
        valid_length, split_point, block, teacher, rest_all, smalls[1:], all_rows, (d_block, *divergence)
    )
    result = block_backward(
        valid_length, d_block, n1, r1, n2, r2, act, slope, attended, mid, mid_all, norm_gain, norm_bias,
        divergence, squares, g_six_own, g_six,
    )
    d_sum_one, d_attended, (g_both, tail) = result[0], result[1 : 1 + shares], result[1 + shares :]

    def to_owner(parts):
        return [parts[0]] + [shift_shares(parts[by], shares - by) for by in range(1, shares)]

    units = widen_weight.shape[1]
    both = lax.psum_scatter(g_both, "batch", scatter_dimension=0, tiled=True)

    grad_in = d_sum_one
    g_five = [None] * shares
    for s in list(range(1, shares)) + [0]:
        q, k, v, e, r, a = other if s else first
        rows, w = after(x, *g_five[1 : shares - 1]) if s == 0 else x, fives if s else five[None]
        grad, grad_in = attend_backward(max(s - 1, 0), q, k, v, e, r, a, d_attended[s], rows, w, grad_in, tail)
        g_five[s] = shift_shares(grad, shares - s) if s else grad

    five_sum = merge(g_five)
    both = after(both, five_sum)
    both = to_owner([both[:, s * D : (s + 1) * D] for s in range(shares)])
    bits = [1 << i for i in range(batch.bit_length() - 1)]
    for index, bit in enumerate(bits):
        received = exchange(five_sum, bit)
        if index == 1:
            both = [after(p, five_sum) for p in both]
            both = sum(p.astype(f32) for p in both).astype(bf16)
            five_sum = after(five_sum, both)
        if index == len(bits) - 1:
            both = lax.all_gather(after(both, five_sum), "batch", axis=0, tiled=True)
            five_sum = after(five_sum, both)
        five_sum = merge([five_sum, received], last=index == len(bits) - 1)
    grad_five, five_bias, branch, gain, shift, summary = five_sum
    grad_narrow, grad_wide, grad_out, wide_bias, grad_six, six_bias = finish_mid(both)

    def unturned(grad):
        return jnp.transpose(grad.reshape(3, -1, grad.shape[1]), (2, 0, 1))

    return (
        block[None], grad_in[None], unturned(grad_five), five_bias, grad_out, branch, gain, shift,
        grad_wide, wide_bias[0], grad_narrow, unturned(grad_six), six_bias, summary[0],
    )


def solution(mesh):
    return jax.shard_map(
        body,
        mesh=mesh,
        in_specs=(
            P(("batch", "heads"), None, None),
            P(("batch", "heads"), None, None),
            P("batch"),
            P("batch"),
            P(None, None, "heads"),
            P(None, "heads"),
            P("heads", None),
            P(),
            P(),
            P(),
            P(None, "heads"),
            P("heads"),
            P("heads", None),
            P(None, None, "heads"),
            P(None, "heads"),
            P(None, None, "heads"),
            P(None, "heads"),
        ),
        out_specs=(
            P(("batch", "heads"), None, None),
            P(("batch", "heads"), None, None),
            P(None, None, "heads"),
            P(None, "heads"),
            P("heads", None),
            P(),
            P(),
            P(),
            P(None, "heads"),
            P("heads"),
            P("heads", None),
            P(None, None, "heads"),
            P(None, "heads"),
            P(),
        ),
        check_vma=False,
    )
```

```python
import functools
import math

import jax
import jax.numpy as jnp
from jax import lax
from jax.experimental import pallas as pl
from jax.experimental.pallas import tpu as pltpu
from jax.sharding import PartitionSpec as P

D = 384
HEADS = 12
HEAD_DIM = 32
TEACHER_HEAD_DIM = 64
PART = 3
TILE = 512
WIDE_TILE = 1024
STRIP = 16
NORM_EPS = 1e-12
MASKED = -1e30
SAFE = 64.0
LN2 = math.log(2.0)
STUDENT_SCALE = 1.0 / math.sqrt(HEAD_DIM)
STUDENT_LOG = math.log2(math.e) / math.sqrt(HEAD_DIM)
TEACHER_LOG = math.log2(math.e) / math.sqrt(TEACHER_HEAD_DIM)
VMEM = 56 * 2**20

f32 = jnp.float32
bf16 = jnp.bfloat16

NN = (((1,), (0,)), ((), ()))
NT = (((1,), (1,)), ((), ()))
TN = (((0,), (0,)), ((), ()))


def dot(left, right, dims=NN):
    return lax.dot_general(left, right, dims, preferred_element_type=f32)


def lanes(shape):
    return lax.broadcasted_iota(jnp.int32, shape, 1)


def wide_rows(rows):
    return jnp.concatenate([rows, jnp.zeros((rows.shape[0], 128 - rows.shape[1]), rows.dtype)], axis=1)


def in_head(lane, head, size=HEAD_DIM):
    return (lane >= head * size) & (lane < (head + 1) * size)


def split_terms(rows, head, size, extra):
    inside = in_head(lanes(rows.shape), head, size)
    high = rows.astype(bf16).astype(f32)
    first = jnp.where(inside, high, extra).astype(bf16)
    second = jnp.where(inside, rows - high, 0.0).astype(bf16)
    return jnp.concatenate([first, second], axis=1)


def own_number(ref):
    return ref[lax.axis_index("heads")]


def key_bias(rows, length):
    position = lax.broadcasted_iota(jnp.int32, (rows, 1), 0)
    return jnp.where(position < length, 0.0, MASKED)


def fold(tile, combine):
    total = tile[:, :128]
    for column in range(128, tile.shape[1], 128):
        total = combine(total, tile[:, column : column + 128])
    return total


def row_sum(tile):
    return jnp.sum(fold(tile, jnp.add), axis=1, keepdims=True)


def weave(first, second):
    done = 0
    for index, step in enumerate(second):
        while done < len(first) and done * len(second) < len(first) * (index + 1):
            first[done]()
            done += 1
        step()
    for step in first[done:]:
        step()


def step_place(step, tile, per_head):
    head = step // per_head
    return head, pl.ds(pl.multiple_of(lax.rem(step, per_head) * tile, tile), tile)


def skew(first, second):
    steps = [first[0]]
    for index in range(1, len(first)):
        steps += [first[index], second[index - 1]]
    return steps + [second[-1]]


def run_rolled(steps, logits, vector, back, reset=None, enter=None):
    def pair(index, carry):
        for slot in range(2):
            step = 2 * index + slot
            if enter is not None:
                enter(step, slot, index)
            ahead = logits(jnp.minimum(step + 1, steps - 1), 1 - slot)
            weave(ahead + back(jnp.maximum(step - 1, 0), 1 - slot), vector(step, slot))
            if slot == 0 and reset is not None:
                pl.when(index == 0)(reset)
        return carry

    for chunk in logits(jnp.int32(0), 0):
        chunk()
    lax.fori_loop(0, steps // 2, pair, 0)
    for chunk in back(jnp.int32(steps - 1), 1):
        chunk()


def run_pipeline(steps, logits, vector, back, enter=None):
    def stage(step, slot, before, after, second=False):
        if enter is not None:
            enter(step, slot, not before, second)
        ahead = logits(step + 1, 1 - slot) if after else []
        behind = back(step - 1, 1 - slot) if before else []
        weave(ahead + behind, vector(step, slot))

    for chunk in logits(jnp.int32(0), 0):
        chunk()
    if steps < 4:
        for step in range(steps):
            stage(jnp.int32(step), step % 2, step > 0, step + 1 < steps, second=step == 1)
        for chunk in back(jnp.int32(steps - 1), (steps - 1) % 2):
            chunk()
        return
    stage(jnp.int32(0), 0, False, True)
    stage(jnp.int32(1), 1, True, True, second=True)

    def pair(index, carry):
        stage(2 * index + 2, 0, True, True)
        stage(2 * index + 3, 1, True, True)
        return carry

    lax.fori_loop(0, (steps - 4) // 2, pair, 0)
    stage(jnp.int32(steps - 2), 0, True, True)
    stage(jnp.int32(steps - 1), 1, True, False)
    for chunk in back(jnp.int32(steps - 1), 1):
        chunk()


def project_part(x, w_ref, index, bias):
    flat = dot(x, w_ref[index * 96 : (index + 1) * 96, :], NT)
    if bias is not None:
        flat = flat + bias
    return wide_rows(flat).astype(bf16)


def attend_forward_kernel(
    length_ref, x_ref, w_ref, q_ref, k_ref, v_ref, e_hbm, r_ref, o_ref, lhs, rhs, mixer, zs0, zs1, es0, es1, sems
):
    share = pl.program_id(0)
    w_ref, q_ref, k_ref, v_ref, r_ref, o_ref = (t.at[0] for t in (w_ref, q_ref, k_ref, v_ref, r_ref, o_ref))
    zs, es = (zs0, zs1), (es0, es1)
    rows = x_ref.shape[0]
    tile = zs0.shape[0]
    per_head = rows // tile
    steps = PART * per_head
    x = x_ref[...]
    small = w_ref[288:304, :].astype(f32)
    q = project_part(x, w_ref, 0, small[0:1, :96])
    k = project_part(x, w_ref, 1, None)
    v = project_part(x, w_ref, 2, small[1:2, :96])
    q_ref[...] = q
    k_ref[...] = k
    v_ref[...] = v
    lane = lanes((rows, 128))
    one = jnp.where(lane == 96, 1.0, 0.0)
    for head in range(PART):
        lhs[head] = jnp.where(in_head(lane, head), q.astype(f32), one).astype(bf16)
    rhs[...] = jnp.where(lane == 96, key_bias(rows, own_number(length_ref)), k.astype(f32)).astype(bf16)
    mixer[...] = jnp.where(lane == 96, 1.0, v.astype(f32)).astype(bf16)
    o_ref[...] = jnp.zeros_like(o_ref)
    r_ref[...] = jnp.zeros_like(r_ref)

    def out_copy(step, slot):
        head, span = step_place(step, tile, per_head)
        return pltpu.make_async_copy(es[slot], e_hbm.at[share, head, span], sems.at[slot])

    def logits(step, slot):
        head, span = step_place(step, tile, per_head)

        def chunk(start):
            zs[slot][:, start : start + 256] = dot(lhs[head, span, :], rhs[start : start + 256, :], NT)

        return [functools.partial(chunk, start) for start in range(0, rows, 256)]

    def vector(step, slot):
        def strip(start):
            z = zs[slot][start : start + STRIP, :]
            highest = jnp.max(fold(z, jnp.maximum), axis=1, keepdims=True)
            es[slot][start : start + STRIP, :] = jnp.exp2((z - highest) * STUDENT_LOG).astype(bf16)

        return [functools.partial(strip, start) for start in range(0, tile, STRIP)]

    def back(step, slot):
        head, span = step_place(step, tile, per_head)

        sums = []

        def part(start):
            sums.append(dot(es[slot][:, start : start + 256], mixer[start : start + 256, :]))

        def mix():
            mixed = functools.reduce(jnp.add, sums)
            inverse = 1.0 / mixed[:, 96:97]
            inside = in_head(lanes(mixed.shape), head)
            o_ref[span, :] = jnp.where(inside, mixed * inverse, o_ref[span, :].astype(f32)).astype(bf16)
            r_ref[span, :] = jnp.where(inside, inverse, r_ref[span, :])

        return [functools.partial(part, start) for start in range(0, rows, 256)] + [mix]

    def enter(step, slot, first, second):
        if not first:
            out_copy(step - 1, 1 - slot).start()
        if not (first or second):
            out_copy(step - 2, slot).wait()

    run_pipeline(steps, logits, vector, back, enter)
    last = (steps - 1) % 2
    out_copy(jnp.int32(steps - 1), last).start()
    out_copy(jnp.int32(steps - 2), 1 - last).wait()
    out_copy(jnp.int32(steps - 1), last).wait()


def whole(shape):
    return pl.BlockSpec(shape, lambda *_: (0,) * len(shape))


SMEM = pl.BlockSpec(memory_space=pltpu.SMEM)
ANY = pl.BlockSpec(memory_space=pl.ANY)


def cost(micros):
    return pl.CostEstimate(flops=int(micros * 0.04e9), bytes_accessed=1024, transcendentals=0)


def attend_forward(length, x, w):
    rows, count = x.shape[0], w.shape[0]
    tile = min(WIDE_TILE, rows)
    narrow = jax.ShapeDtypeStruct((count, rows, 128), bf16)

    def share(shape):
        return pl.BlockSpec((1,) + shape, lambda s: (s,) + (0,) * len(shape))

    row = share((rows, 128))
    return pl.pallas_call(
        attend_forward_kernel,
        grid=(count,),
        in_specs=[SMEM, whole(x.shape), share(w.shape[1:])],
        out_specs=[row] * 3 + [ANY] + [row] * 2,
        out_shape=[
            narrow, narrow, narrow, jax.ShapeDtypeStruct((count, PART, rows, rows), bf16),
            jax.ShapeDtypeStruct((count, rows, 128), f32), narrow,
        ],
        scratch_shapes=[
            pltpu.VMEM((PART, rows, 128), bf16),
            pltpu.VMEM((rows, 128), bf16),
            pltpu.VMEM((rows, 128), bf16),
            pltpu.VMEM((tile, rows), f32),
            pltpu.VMEM((tile, rows), f32),
            pltpu.VMEM((tile, rows), bf16),
            pltpu.VMEM((tile, rows), bf16),
            pltpu.SemaphoreType.DMA((2,)),
        ],
        compiler_params=pltpu.CompilerParams(vmem_limit_bytes=VMEM),
        cost_estimate=cost(9 * count),
        name="attend_forward",
    )(length, x, w)


def attend_backward_kernel(
    q_ref, k_ref, v_ref, e_hbm, r_ref, a_ref, d_ref, x_hbm, w_hbm, acc_hbm, tail_ref, g_ref, in_ref,
    lhs, rhs, keys, qt, dt, zs0, zs1, gs0, gs1, dq, dkt, dvt, e_all, x_ref, w_ref, acc_ref, sems, late, *, share,
):
    q_ref, k_ref, v_ref, r_ref, a_ref = (t.at[0] for t in (q_ref, k_ref, v_ref, r_ref, a_ref))
    rows = q_ref.shape[0]
    zs, gs = (zs0, zs1), (gs0, gs1)
    tile = zs0.shape[0]
    per_head = rows // tile
    steps = PART * per_head

    def in_copy(step):
        head, span = step_place(step, tile, per_head)
        return pltpu.make_async_copy(e_hbm.at[share, head, span], e_all.at[head, span], sems.at[step])

    for step in range(2):
        in_copy(jnp.int32(step)).start()
    late_copies = [
        pltpu.make_async_copy(source, target, late.at[index])
        for index, (source, target) in enumerate(((x_hbm, x_ref), (w_hbm.at[share], w_ref), (acc_hbm, acc_ref)))
    ]

    def enter(step, slot, first, second):
        if second:
            for copy in late_copies:
                copy.start()

        @pl.when(step + 2 < steps)
        def _():
            in_copy(step + 2).start()

        in_copy(step).wait()

    lane = lanes((rows, 128))
    grads = r_ref[...] * d_ref[...].astype(f32)
    shifts = grads * a_ref[...].astype(f32)
    k = k_ref[...].astype(f32)
    def one_head(head, carry):
        inside = in_head(lane, head)
        shift = -jnp.sum(jnp.where(inside, shifts, 0.0), axis=1, keepdims=True)
        high = shift.astype(bf16).astype(f32)
        lhs[head] = split_terms(
            grads, head, HEAD_DIM, jnp.where(lane == 96, high, jnp.where(lane == 97, shift - high, 0.0))
        )
        keys[head] = jnp.where(inside, k, 0.0).astype(bf16)
        return carry

    lax.fori_loop(0, PART, one_head, 0)
    rhs[:, :128] = jnp.where((lane == 96) | (lane == 97), 1.0, v_ref[...].astype(f32)).astype(bf16)
    rhs[:, 128:] = v_ref[...]
    qt[...] = q_ref[...].T
    dt[...] = grads.astype(bf16).T

    def reset():
        dq[...] = jnp.zeros_like(dq)
        dkt[...] = jnp.zeros_like(dkt)
        dvt[...] = jnp.zeros_like(dvt)

    reset()

    def logits(step, slot):
        head, span = step_place(step, tile, per_head)

        def chunk(start):
            zs[slot][:, start : start + 256] = dot(lhs[head, span, :], rhs[start : start + 256, :], NT)

        return [functools.partial(chunk, start) for start in range(0, rows, 256)]

    def vector(step, slot):
        head, span = step_place(step, tile, per_head)
        base = lax.rem(step, per_head) * tile

        def strip(start):
            here = pl.ds(pl.multiple_of(base + start, STRIP), STRIP)
            weights = e_all[head, here, :].astype(f32)
            gs[slot][start : start + STRIP, :] = (weights * zs[slot][start : start + STRIP, :]).astype(bf16)

        return [functools.partial(strip, start) for start in range(0, tile, STRIP)]

    def back(step, slot):
        head, span = step_place(step, tile, per_head)
        own = pl.ds(pl.multiple_of(head * HEAD_DIM, HEAD_DIM), HEAD_DIM)

        def first():
            dq[span, :] += dot(gs[slot][...], keys[head])

        def second(start):
            part = slice(start, start + 256)
            dkt[own, part] += dot(qt[own, span], gs[slot][:, part])

        def third(start):
            part = slice(start, start + 256)
            dvt[own, part] += dot(dt[own, span], e_all[head, span, part])

        starts = range(0, rows, 256)
        return [first] + [functools.partial(second, s) for s in starts] + [functools.partial(third, s) for s in starts]

    run_pipeline(steps, logits, vector, back, enter)
    for copy in late_copies:
        copy.wait()
    grads = (
        (dq[...] * STUDENT_SCALE).astype(bf16),
        (dkt[...] * STUDENT_SCALE).T.astype(bf16),
        dvt[...].T.astype(bf16),
    )
    weight_grads(grads, x_ref[...], g_ref, tail_ref[:16, :].astype(f32), tail_ref[16:, :].astype(f32))
    in_ref[...] = acc_ref[...] + spread(grads, w_ref)


def weight_grads(grads, x, g_ref, tail_high=0.0, tail_low=0.0):
    for index, grad in enumerate(grads):
        g_ref[index * 96 : (index + 1) * 96, :] = dot(grad, x, TN)[:96].astype(bf16)
    ones = jnp.ones((16, x.shape[0]), bf16)
    row = lax.broadcasted_iota(jnp.int32, (16, 128), 0)
    sums = jnp.where(row == 0, dot(ones, grads[0]), jnp.where(row == 1, dot(ones, grads[2]), 0.0))
    sums = jnp.concatenate([sums, jnp.zeros((16, x.shape[1] - 128), f32)], axis=1) + tail_high
    high = sums.astype(bf16).astype(f32)
    g_ref[288:304, :] = high.astype(bf16)
    g_ref[304:320, :] = (sums - high + tail_low).astype(bf16)


def spread(grads, w_ref):
    total = None
    for index, grad in enumerate(grads):
        term = dot(grad[:, :96], w_ref[index * 96 : (index + 1) * 96, :])
        total = term if total is None else total + term
    return total


def attend_backward(share, q, k, v, e, r, attended, d_attended, x, w, grad_in, tail):
    rows = x.shape[0]
    tile = min(TILE, rows // 2)
    row = pl.BlockSpec((1, rows, 128), lambda i: (share, 0, 0))
    return pl.pallas_call(
        functools.partial(attend_backward_kernel, share=share),
        grid=(1,),
        in_specs=[row, row, row, ANY, row, row, whole((rows, 128)), ANY, ANY, ANY, whole(tail.shape)],
        out_specs=[whole((320, x.shape[1])), whole(x.shape)],
        out_shape=[jax.ShapeDtypeStruct((320, x.shape[1]), bf16), jax.ShapeDtypeStruct(x.shape, f32)],
        scratch_shapes=[
            pltpu.VMEM((PART, rows, 256), bf16),
            pltpu.VMEM((rows, 256), bf16),
            pltpu.VMEM((PART, rows, 128), bf16),
            pltpu.VMEM((128, rows), bf16),
            pltpu.VMEM((128, rows), bf16),
            pltpu.VMEM((tile, rows), f32),
            pltpu.VMEM((tile, rows), f32),
            pltpu.VMEM((tile, rows), bf16),
            pltpu.VMEM((tile, rows), bf16),
            pltpu.VMEM((rows, 128), f32),
            pltpu.VMEM((128, rows), f32),
            pltpu.VMEM((128, rows), f32),
            pltpu.VMEM((PART, rows, rows), bf16),
            pltpu.VMEM(x.shape, bf16),
            pltpu.VMEM(w.shape[1:], bf16),
            pltpu.VMEM(x.shape, f32),
            pltpu.SemaphoreType.DMA((PART * (rows // tile),)),
            pltpu.SemaphoreType.DMA((3,)),
        ],
        compiler_params=pltpu.CompilerParams(vmem_limit_bytes=VMEM),
        cost_estimate=cost(10),
        name="attend_backward",
    )(q, k, v, e, r, attended, d_attended, x, w, grad_in, tail)


def relation_kernel(
    length_ref, split_ref, block_ref, teacher_ref, packed_ref, small_ref, *rest, all_rows, gathered,
):
    before = None
    if gathered:
        before, rest = rest[:3], rest[3:]
    (
    d_ref, g_ref, kl_ref, kl_row_ref, pack, lefts, rights, t_lefts, t_rights, ls, rs, lt, rt, keys, left_t, zs0, zs1, zt0, zt1, gs0, gs1,
    left_sum, right_t, es_all, et_all, parts, columns, factors, rows_s, weight, weight_row, grads_s,
    ) = rest
    rows = block_ref.shape[0]
    tile = zs0.shape[0]
    per_head = rows // tile
    steps = PART * per_head
    zs, zt, gs = (zs0, zs1), (zt0, zt1), (gs0.at[:tile], gs1)
    length, split = own_number(length_ref), own_number(split_ref)

    @pl.when(pl.program_id(0) == 0)
    def _():
        position = lax.broadcasted_iota(jnp.int32, (rows, 1), 0)
        counted = (position < length) & (position != 0) & (position != split - 1) & (position != length - 1)
        share = 1.0 / ((length - 3).astype(f32) * float(all_rows))
        weight[...] = jnp.where(counted, share, 0.0)
        position = lanes((1, rows))
        counted = (position < length) & (position != 0) & (position != split - 1) & (position != length - 1)
        weight_row[...] = jnp.where(counted, share, 0.0)
        for index, ref in enumerate((d_ref, kl_ref, kl_row_ref)):
            ref[...] = before[index][...] if gathered else jnp.zeros_like(ref)

    if gathered:
        unpack(packed_ref, 0, pack)
    else:
        pack[...] = packed_ref[...]

    g_ref = g_ref.at[0]
    small = small_ref[0].astype(f32)

    def largest(low, size):
        square = low.astype(f32)
        same = lax.broadcasted_iota(jnp.int32, (128, 128), 0) // size == lanes((128, 128)) // size
        return jnp.max(dot((square * square).astype(bf16), jnp.where(same, 1.0, 0.0).astype(bf16)), axis=0, keepdims=True)

    def project(index, carry):
        here = pl.ds(pl.multiple_of(index * tile, tile), tile)
        block, teacher = block_ref[here, :], teacher_ref[here, :]

        def student(part, b):
            flat = dot(block, pack[part * 96 : (part + 1) * 96, :], NT)
            return wide_rows(flat if b is None else flat + b).astype(bf16)

        def taught(part, b):
            start = 288 + part * 192
            flat = dot(teacher[:, :D], pack[start : start + 192, :], NT)
            flat = flat + dot(teacher[:, D:], pack[start + 576 : start + 768, :], NT)
            flat = (flat if b is None else flat + b).astype(bf16)
            return flat[:, :128], wide_rows(flat[:, 128:])

        q, k, v = student(0, small[2:3, :96]), student(1, None), student(2, small[3:4, :96])
        lefts[0, here, :] = q
        rights[0, here, :] = k
        lefts[1, here, :] = v
        rights[1, here, :] = v
        tq, tk, tv = taught(0, small[5:6, :192]), taught(1, None), taught(2, small[6:7, :192])
        for half in range(2):
            t_lefts[0, half, here, :] = tq[half]
            t_rights[0, half, here, :] = tk[half]
            t_lefts[1, half, here, :] = tv[half]
            t_rights[1, half, here, :] = tv[half]
        found = [largest(value, HEAD_DIM) for value in (q, k, v)]
        found += [largest(value, TEACHER_HEAD_DIM) for value in tq + tk + tv]
        return tuple(jnp.maximum(old, new) for old, new in zip(carry, found))

    top = lax.fori_loop(0, rows // tile, project, (jnp.zeros((1, 128), f32),) * 9)
    bounds = []
    for s_left, s_right, t_left, t_right in ((0, 1, 3, 5), (2, 2, 7, 7)):
        bound = jnp.max(top[s_left] * top[s_right]) * STUDENT_LOG**2
        for half in range(2):
            bound = jnp.maximum(bound, jnp.max(top[t_left + half] * top[t_right + half]) * TEACHER_LOG**2)
        bounds.append(bound)

    def operands(relation, student_scale, teacher_scale, row_bias, everything):
        band = min(128, rows)
        line = lanes((1, 128))

        def terms(value, inside, extra):
            high, low = value
            return jnp.where(inside, high, extra).astype(bf16), jnp.where(inside, low, 0.0).astype(bf16)

        def halves(value, scale):
            value = value * scale
            high = value.astype(bf16).astype(f32)
            return high, value - high

        def one_band(index, carry):
            here = pl.ds(pl.multiple_of(index * band, band), band)
            position = lax.broadcasted_iota(jnp.int32, (band, 128), 0) + index * band
            bias = jnp.where(position < length, 0.0, MASKED)
            row = jnp.where(row_bias, bias, 0.0)
            left, right = lefts[relation, here, :].astype(f32), rights[relation, here, :].astype(f32)
            value = halves(left, student_scale)
            extra = jnp.where(line == 97, row, jnp.where(line == 96, 1.0, 0.0))
            if everything:
                rs[here, :128] = jnp.where(line == 97, 1.0, jnp.where(line == 96, bias, right)).astype(bf16)
                rs[here, 128:] = rights[relation, here, :]
            for head in range(PART):
                inside = in_head(line, head)
                ls[head, here, :128], ls[head, here, 128:] = terms(value, inside, extra)
                if everything:
                    keys[head, here, :] = jnp.where(inside, right, 0.0).astype(bf16)
            for half in range(2):
                t_left = t_lefts[relation, half, here, :].astype(f32)
                t_right = t_rights[relation, half, here, :].astype(f32)
                value = halves(t_left, teacher_scale)
                for head in range(2 * half, min(2 * half + 2, PART)):
                    own = head % 2
                    spare = (1 - own) * TEACHER_HEAD_DIM
                    extra = jnp.where(line == spare + 1, row, jnp.where(line == spare, 1.0, 0.0))
                    inside = in_head(line, own, TEACHER_HEAD_DIM)
                    lt[head, here, :128], lt[head, here, 128:] = terms(value, inside, extra)
                    if everything:
                        first = jnp.where(line == spare + 1, 1.0, jnp.where(line == spare, bias, t_right))
                        rt[head, here, :128] = first.astype(bf16)
                        rt[head, here, 128:] = t_rights[relation, half, here, :]
            return carry

        lax.fori_loop(0, rows // band, one_band, 0)

    def relate(relation, carry):
        symmetric = relation == 1
        left_t[...] = lefts[relation].T
        operands(relation, STUDENT_LOG, TEACHER_LOG, symmetric, True)
        near = jnp.where(symmetric, bounds[1], bounds[0]) < SAFE * SAFE
        reset()

        @pl.when(near & jnp.logical_not(symmetric))
        def _():
            run_pipeline(steps, logits, vector, grad_products)

        @pl.when(near & symmetric)
        def _():
            lax.fori_loop(0, PART, symmetric_head, 0)

        @pl.when(jnp.logical_not(near))
        def _():
            operands(relation, 1.0, 1.0, False, False)
            lax.fori_loop(0, steps, shifted_step, 0)

        @pl.when(jnp.logical_not(symmetric))
        def _():
            grads_s[0] = (left_sum[...] * STUDENT_SCALE).astype(bf16)
            grads_s[1] = (right_t[...] * STUDENT_SCALE).T.astype(bf16)

        @pl.when(symmetric)
        def _():
            grads_s[2] = ((left_sum[...] + right_t[...].T) * STUDENT_SCALE).astype(bf16)

        return carry

    def reset():
        left_sum[...] = jnp.zeros_like(left_sum)
        right_t[...] = jnp.zeros_like(right_t)

    def logits(step, slot):
        head, span = step_place(step, tile, per_head)

        def student(start):
            zs[slot][:, start : start + 256] = dot(ls[head, span, :], rs[start : start + 256, :], NT)

        def taught(start):
            zt[slot][:, start : start + 256] = dot(lt[head, span, :], rt[head, start : start + 256, :], NT)

        chunks = []
        for start in range(0, rows, 256):
            chunks += [functools.partial(student, start), functools.partial(taught, start)]
        return chunks

    def vector(step, slot):
        base = lax.rem(step, per_head) * tile
        z, t, g = zs[slot], zt[slot], gs[slot]
        scales = {}

        def both(start):
            strip = slice(start, start + STRIP)
            student, taught = z[strip, :], t[strip, :]
            es, et = jnp.exp2(student), jnp.exp2(taught)
            sum_s, sum_t, cross = row_sum(es), row_sum(et), row_sum(et * (taught - student))
            here = pl.ds(pl.multiple_of(base + start, STRIP), STRIP)
            w = weight[here, :]
            inverse = 1.0 / sum_t
            kl_ref[here, :] += w * (LN2 * cross * inverse + jnp.log(sum_s) - jnp.log(sum_t))
            g[strip, :] = (es * (w / sum_s) - et * (w * inverse)).astype(bf16)

        return [functools.partial(both, s) for s in range(0, tile, STRIP)]

    def grad_products(step, slot):
        head, span = step_place(step, tile, per_head)
        own = pl.ds(pl.multiple_of(head * HEAD_DIM, HEAD_DIM), HEAD_DIM)

        def first():
            left_sum[span, :] += dot(gs[slot][...], keys[head])

        def second(start):
            part = slice(start, start + 256)
            right_t[own, part] += dot(left_t[own, span], gs[slot][:, part])

        return [first] + [functools.partial(second, start) for start in range(0, rows, 256)]

    def shifted_step(step, carry):
        head, span = step_place(step, tile, per_head)
        student = dot(ls[head, span, :], rs[...], NT)
        zs0[...] = (student - jnp.max(student, axis=1, keepdims=True)) * STUDENT_LOG
        taught = dot(lt[head, span, :], rt[head], NT)
        zt0[...] = (taught - jnp.max(taught, axis=1, keepdims=True)) * TEACHER_LOG

        def strip(index, carry):
            here = pl.ds(pl.multiple_of(index * STRIP, STRIP), STRIP)
            student, taught = zs0[here, :], zt0[here, :]
            es, et = jnp.exp2(student), jnp.exp2(taught)
            sum_s, sum_t = row_sum(es), row_sum(et)
            cross = row_sum(et * (taught - student))
            there = pl.ds(pl.multiple_of(lax.rem(step, per_head) * tile + index * STRIP, STRIP), STRIP)
            w = weight[there, :]
            row = LN2 * cross / sum_t + jnp.log(sum_s) - jnp.log(sum_t)
            kl_ref[there, :] += jnp.where(w > 0.0, w * row, 0.0)
            gs0[here, :] = (es * (w / sum_s) - et * (w / sum_t)).astype(bf16)
            return carry

        lax.fori_loop(0, tile // STRIP, strip, 0)
        for chunk in grad_products(step, 0):
            chunk()
        return carry

    def symmetric_head(head, carry):
        size, band = min(256, rows), 32
        count = rows // size
        own = pl.ds(pl.multiple_of(head * HEAD_DIM, HEAD_DIM), HEAD_DIM)
        columns[...] = jnp.zeros_like(columns)

        def logit_chunks(i):
            here = slice(i * size, (i + 1) * size)

            def student(part):
                es_all[here, part] = dot(ls[head, here, :], rs[part, :], NT)

            def taught(part):
                et_all[here, part] = dot(lt[head, here, :], rt[head, part, :], NT)

            chunks = []
            for j in range(i, count):
                part = slice(j * size, (j + 1) * size)
                chunks += [functools.partial(student, part), functools.partial(taught, part)]
            return chunks

        def weigh(i, start):
            strip = slice(start, start + band)
            totals = [0.0, 0.0, 0.0]
            for column in range(i * size, rows, 128):
                part = slice(column, column + 128)
                student, taught = es_all[strip, part], et_all[strip, part]
                es, et = jnp.exp2(student), jnp.exp2(taught)
                es_all[strip, part] = es
                et_all[strip, part] = et
                for index, value in enumerate((es, et, et * (taught - student))):
                    totals[index] = totals[index] + value
                    if column >= (i + 1) * size:
                        eight = value[:8]
                        for line in range(8, band, 8):
                            eight = eight + value[line : line + 8]
                        columns[index, :, part] += eight
            for index in range(3):
                parts[index, strip, :] = totals[index]

        def combine(i, start):
            strip = slice(start, start + STRIP)
            a, b = factors[0, strip, :], factors[1, strip, :]
            for column in range(i * size, rows, 128):
                part = slice(column, column + 128)
                both = es_all[strip, part] * (a + rows_s[0, :, part])
                both = both - et_all[strip, part] * (b + rows_s[1, :, part])
                gs0[strip, part] = both.astype(bf16)

        def products(i):
            here = slice(i * size, (i + 1) * size)

            def first(j):
                part = slice(j * size, (j + 1) * size)
                left_sum[here, :] += dot(gs_all[here, part], keys[head, part, :])

            def second(j):
                part = slice(j * size, (j + 1) * size)
                right_t[own, part] += dot(left_t[own, here], gs_all[here, part])

            chunks = [functools.partial(first, j) for j in range(i, count)]
            return chunks + [functools.partial(second, j) for j in range(i + 1, count)]

        gs_all = gs0
        for chunk in logit_chunks(0):
            chunk()
        for i in range(count):
            ahead = logit_chunks(i + 1) if i + 1 < count else []
            weave(ahead, [functools.partial(weigh, i, s) for s in range(i * size, (i + 1) * size, band)])
        sums = [
            jnp.sum(parts[index].T, axis=0, keepdims=True) + jnp.sum(columns[index], axis=0, keepdims=True)
            for index in range(3)
        ]
        w = weight_row[...]
        sum_s, sum_t = (jnp.where(w > 0.0, value, 1.0) for value in sums[:2])
        inverse = 1.0 / sum_t
        kl_row_ref[...] += w * (LN2 * sums[2] * inverse + jnp.log(sum_s) - jnp.log(sum_t))
        for index, value in enumerate((w / sum_s, w * inverse)):
            factors[index] = jnp.broadcast_to(value, (128, rows)).T
            rows_s[index] = jnp.broadcast_to(value, (STRIP, rows))
        for i in range(count):
            behind = products(i - 1) if i else []
            weave(behind, [functools.partial(combine, i, s) for s in range(i * size, (i + 1) * size, STRIP)])
        for chunk in products(count - 1):
            chunk()
        return carry

    lax.fori_loop(0, 2, relate, 0)
    grads = tuple(grads_s[i] for i in range(3))
    weight_grads(grads, block_ref[...], g_ref)
    d_ref[...] += spread(grads, pack)


def part_rows(rows, batch):
    return -(-rows // (16 * batch)) * 16


def unpack(packed_ref, share, target):
    rows, batch = target.shape[0], packed_ref.shape[0]
    part = part_rows(rows, batch)
    for start in range(0, rows, part):
        size = min(part, rows - start)
        target[start : start + size, :] = packed_ref[start // part, share, :size, :]


def relations(length, split, block, teacher, packed, small, all_rows, before=()):
    rows = block.shape[0]
    tile = min(TILE, rows // 2)
    shares = small.shape[0]

    def share(shape):
        return pl.BlockSpec((1,) + shape[1:], lambda s: (s,) + (0,) * (len(shape) - 1))

    gathered = len(before) > 0
    if gathered:
        place = pl.BlockSpec((packed.shape[0], 1) + packed.shape[2:], lambda s: (0, s, 0, 0))
    else:
        place = whole(packed.shape)
    return pl.pallas_call(
        functools.partial(relation_kernel, all_rows=all_rows, gathered=gathered),
        grid=(shares,),
        in_specs=[
            SMEM, SMEM, whole(block.shape), whole(teacher.shape), place, share(small.shape),
        ] + [whole(b.shape) for b in before],
        out_specs=[whole(block.shape), share((shares, 320, D)), whole((rows, 1)), whole((1, rows))],
        out_shape=[
            jax.ShapeDtypeStruct(block.shape, f32),
            jax.ShapeDtypeStruct((shares, 320, D), bf16),
            jax.ShapeDtypeStruct((rows, 1), f32),
            jax.ShapeDtypeStruct((1, rows), f32),
        ],
        scratch_shapes=[
            pltpu.VMEM((1440, D), bf16),
            pltpu.VMEM((2, rows, 128), bf16),
            pltpu.VMEM((2, rows, 128), bf16),
            pltpu.VMEM((2, 2, rows, 128), bf16),
            pltpu.VMEM((2, 2, rows, 128), bf16),
            pltpu.VMEM((PART, rows, 256), bf16),
            pltpu.VMEM((rows, 256), bf16),
            pltpu.VMEM((PART, rows, 256), bf16),
            pltpu.VMEM((PART, rows, 256), bf16),
            pltpu.VMEM((PART, rows, 128), bf16),
            pltpu.VMEM((128, rows), bf16),
            pltpu.VMEM((tile, rows), f32),
            pltpu.VMEM((tile, rows), f32),
            pltpu.VMEM((tile, rows), f32),
            pltpu.VMEM((tile, rows), f32),
            pltpu.VMEM((rows, rows), bf16),
            pltpu.VMEM((tile, rows), bf16),
            pltpu.VMEM((rows, 128), f32),
            pltpu.VMEM((128, rows), f32),
            pltpu.VMEM((rows, rows), f32),
            pltpu.VMEM((rows, rows), f32),
            pltpu.VMEM((3, rows, 128), f32),
            pltpu.VMEM((3, 8, rows), f32),
            pltpu.VMEM((2, rows, 128), f32),
            pltpu.VMEM((2, STRIP, rows), f32),
            pltpu.VMEM((rows, 1), f32),
            pltpu.VMEM((1, rows), f32),
            pltpu.VMEM((3, rows, 128), bf16),
        ],
        compiler_params=pltpu.CompilerParams(vmem_limit_bytes=VMEM),
        cost_estimate=cost(30 * shares),
        name="relations",
    )(length, split, block, teacher, packed, small, *before)


def norm_forward(rows, gain, shift):
    center = jnp.mean(rows, axis=1, keepdims=True)
    offsets = rows - center
    rstd = lax.rsqrt(jnp.mean(offsets * offsets, axis=1, keepdims=True) + NORM_EPS)
    normed = offsets * rstd
    return normed * gain + shift, normed, rstd


def norm_backward(grad, normed, rstd, gain):
    inner = grad * gain
    mean = jnp.mean(inner, axis=1, keepdims=True)
    slope = jnp.mean(inner * normed, axis=1, keepdims=True)
    return rstd * (inner - mean - normed * slope)


def gelu_terms(x):
    t = 1.0 / (1.0 + (0.3275911 * math.sqrt(0.5)) * jnp.abs(x))
    bell = jnp.exp2((x * x) * (-0.5 * math.log2(math.e)))
    poly = 0.5 * -1.453152027 + t * (0.5 * 1.061405429)
    for term in (0.5 * 1.421413741, 0.5 * -0.284496736, 0.5 * 0.254829592):
        poly = term + t * poly
    tail = (t * poly) * bell
    share = jnp.where(x >= 0.0, 1.0 - tail, tail)
    return x * share, share + x * (bell * (1.0 / math.sqrt(2.0 * math.pi)))


def unpack_all(own_ref, packed_ref, pack):
    pack[0] = own_ref[...]
    for share in range(1, pack.shape[0]):
        unpack(packed_ref, share - 1, pack.at[share])


def split_pack(pack):
    return pack.at[:, :D], pack.at[:, D : 2 * D], pack.at[:, 2 * D :]


def block_kernel(
    length_ref, x_ref, own_ref, packed_ref, small_ref, branch_ref, gain_ref, shift_ref, first_ref, other_ref,
    block_ref, n1_ref, r1_ref, n2_ref, r2_ref, act_ref, slope_ref, sums_ref, pack,
):
    shares = small_ref.shape[0]
    a_refs = [first_ref.at[0]] + [other_ref.at[s] for s in range(shares - 1)]
    tile = x_ref.shape[0]

    @pl.when(pl.program_id(0) == 0)
    def _():
        unpack_all(own_ref, packed_ref, pack)

    wide_ref, narrow_ref, out_ref = split_pack(pack)
    x = x_ref[...].astype(f32)
    mixing = branch_ref[0:1, :]
    for s in range(shares):
        mixing = mixing + dot(a_refs[s][:, :96], out_ref[s, :96, :])
    middle, normed, rstd = norm_forward(x + mixing, gain_ref[0:1, :], shift_ref[0:1, :])
    n1_ref[...] = normed
    r1_ref[...] = rstd
    low = middle.astype(bf16)
    branch = branch_ref[1:2, :]
    width = D
    for s in range(shares):
        value, slope = gelu_terms(dot(low, wide_ref[s]) + small_ref[s, 4:5, :].astype(f32))
        value = value.astype(bf16)
        act_ref[:, s * width : (s + 1) * width] = value
        slope_ref[:, s * width : (s + 1) * width] = slope.astype(bf16)
        branch = branch + dot(value, narrow_ref[s])
    block, normed, rstd = norm_forward(middle + branch, gain_ref[1:2, :], shift_ref[1:2, :])
    n2_ref[...] = normed
    r2_ref[...] = rstd
    block_ref[...] = block.astype(bf16)
    position = lax.broadcasted_iota(jnp.int32, (tile, 1), 0) + pl.program_id(0) * tile
    kept = jnp.where(position < own_number(length_ref), 1.0, 0.0)
    row = lax.broadcasted_iota(jnp.int32, (8, x.shape[1]), 0)
    total = jnp.zeros((8, x.shape[1]), f32)
    for index, part in enumerate((x, mixing, branch)):
        total = jnp.where(row == index, jnp.sum(kept * part * part, axis=0, keepdims=True), total)

    @pl.when(pl.program_id(0) == 0)
    def _():
        sums_ref[...] = jnp.zeros_like(sums_ref)

    sums_ref[...] += total


def by_tile(tile, width):
    return pl.BlockSpec((tile, width), lambda i: (i, 0))


def block_forward(length, x, attended, own, packed, small, branch_bias, gain, shift):
    rows, width = x.shape
    tile = min(256, rows)
    shares = small.shape[0]
    units = shares * D
    row, column = by_tile(tile, width), by_tile(tile, 1)
    return pl.pallas_call(
        block_kernel,
        grid=(rows // tile,),
        in_specs=[
            SMEM, row, whole(own.shape), whole(packed.shape), whole(small.shape), whole(branch_bias.shape), whole(gain.shape), whole(shift.shape),
        ] + [pl.BlockSpec((a.shape[0], tile, 128), lambda i: (0, i, 0)) for a in attended],
        out_specs=[row, row, column, row, column, by_tile(tile, units), by_tile(tile, units), whole((8, width))],
        out_shape=[
            jax.ShapeDtypeStruct((rows, width), bf16),
            jax.ShapeDtypeStruct((rows, width), f32),
            jax.ShapeDtypeStruct((rows, 1), f32),
            jax.ShapeDtypeStruct((rows, width), f32),
            jax.ShapeDtypeStruct((rows, 1), f32),
            jax.ShapeDtypeStruct((rows, units), bf16),
            jax.ShapeDtypeStruct((rows, units), bf16),
            jax.ShapeDtypeStruct((8, width), f32),
        ],
        scratch_shapes=[pltpu.VMEM((shares, 2 * D + 128, D), bf16)],
        compiler_params=pltpu.CompilerParams(vmem_limit_bytes=VMEM),
        cost_estimate=cost(20),
        name="block_forward",
    )(length, x, own, packed, small, branch_bias, gain, shift, *attended)


def block_backward_kernel(
    length_ref, d_ref, n1_ref, r1_ref, n2_ref, r2_ref, act_ref, slope_ref, own_ref, packed_ref, gain_ref,
    shift_ref, kl_ref, kl_row_ref, square_ref, six_own_ref, six_ref, first_ref, other_ref, *rest,
):
    step = pl.program_id(0)
    pack = rest[-1]
    shares = pack.shape[0]
    a_refs = [first_ref.at[0]] + [other_ref.at[s] for s in range(shares - 1)]
    sum_ref, da_refs = rest[0], rest[1 : shares + 1]
    g_ref, tail_ref, vec_ref, g_sum, low_s, branch_s, pre_s, mix_s = rest[shares + 1 : -1]
    tile, width = d_ref.shape
    units = D
    span = pl.ds(pl.multiple_of(step * tile, tile), tile)

    @pl.when(step == 0)
    def _():
        unpack_all(own_ref, packed_ref, pack)
        vec_ref[...] = jnp.zeros_like(vec_ref)
        g_sum[...] = jnp.zeros_like(g_sum)

    wide_ref, narrow_ref, out_ref = split_pack(pack)

    def column(value):
        return jnp.sum(value, axis=0, keepdims=True)

    row = lax.broadcasted_iota(jnp.int32, (8, width), 0)
    d_block = d_ref[...]
    normed_two = n2_ref[...]
    d_two = norm_backward(d_block, normed_two, r2_ref[...], gain_ref[1:2, :])
    d_branch = d_two.astype(bf16)
    branch_s[span, :] = d_branch
    normed_one = n1_ref[...]
    low = (normed_one * gain_ref[0:1, :] + shift_ref[0:1, :]).astype(bf16)
    low_s[span, :] = low
    d_middle = d_two
    for s in range(shares):
        grad = dot(d_branch, narrow_ref[s], NT) * slope_ref[:, s * units : (s + 1) * units].astype(f32)
        grad = grad.astype(bf16)
        pre_s[span, s * units : (s + 1) * units] = grad
        g_sum[s : s + 1, :] += column(grad.astype(f32))
        d_middle = d_middle + dot(grad, wide_ref[s], NT)
    d_one = norm_backward(d_middle, normed_one, r1_ref[...], gain_ref[0:1, :])
    sum_ref[...] = d_one
    d_mixing = d_one.astype(bf16)
    mix_s[span, :] = d_mixing
    for s in range(shares):
        da_refs[s][...] = wide_rows(dot(d_mixing, out_ref[s, :96, :], NT)).astype(bf16)
    parts = (
        d_mixing.astype(f32), d_branch.astype(f32), d_middle * normed_one, d_block * normed_two, d_middle, d_block,
    )
    total = jnp.zeros((8, width), f32)
    for index, part in enumerate(parts):
        total = jnp.where(row == index, column(part), total)
    vec_ref[...] += total

    @pl.when(step == pl.num_programs(0) - 1)
    def _():
        for s in range(shares):
            part = slice(s * units, (s + 1) * units)
            own = slice(s * width, (s + 1) * width)
            g_ref[0:units, own] = dot(act_ref[:, part], branch_s[...], TN).astype(bf16)
            g_ref[units : 2 * units, own] = dot(low_s[...], pre_s[:, part], TN).astype(bf16)
            g_ref[2 * units : 2 * units + 96, own] = dot(a_refs[s][...], mix_s[...], TN)[:96].astype(bf16)
            g_ref[2 * units + 128 :, own] = six_own_ref[0] if s == 0 else six_ref[s - 1]
            first = lax.broadcasted_iota(jnp.int32, (32, units), 0) == 0
            g_ref[2 * units + 96 : 2 * units + 128, own] = jnp.where(first, g_sum[s : s + 1, :], 0.0).astype(bf16)
        scalars = [jnp.sum(kl_ref[...], axis=0, keepdims=True) + jnp.sum(kl_row_ref[...], axis=1, keepdims=True)]
        scalars += [jnp.sum(square_ref[i : i + 1, :], axis=1, keepdims=True) for i in range(3)]
        scalars += [jnp.broadcast_to(own_number(length_ref).astype(f32), (1, 1))]
        lane = lanes((8, width))
        total = vec_ref[...]
        for index, value in enumerate(scalars):
            total = jnp.where((row == 6) & (lane == index), value, total)
        total = jnp.concatenate([jnp.zeros((2, width), f32), total, jnp.zeros((6, width), f32)], axis=0)
        high = total.astype(bf16).astype(f32)
        tail_ref[:16, :] = high.astype(bf16)
        tail_ref[16:, :] = (total - high).astype(bf16)


def block_backward(
    length, d_block, n1, r1, n2, r2, act, slope, attended, own, packed, gain, shift, divergence, squares, six_own, six,
):
    rows, width = d_block.shape
    tile = min(256, rows)
    shares, units = six.shape[0] + 1, D
    row, column = by_tile(tile, width), by_tile(tile, 1)
    return pl.pallas_call(
        block_backward_kernel,
        grid=(rows // tile,),
        in_specs=[
            SMEM, row, row, column, row, column, whole(act.shape), by_tile(tile, shares * units), whole(own.shape), whole(packed.shape), whole(gain.shape), whole(shift.shape),
            whole(divergence[0].shape), whole(divergence[1].shape), whole(squares.shape), whole(six_own.shape),
            whole(six.shape),
        ] + [whole(a.shape) for a in attended],
        out_specs=[
            row, *[by_tile(tile, 128)] * shares, whole((2 * units + 448, shares * width)), whole((32, width)),
        ],
        out_shape=[
            jax.ShapeDtypeStruct((rows, width), f32),
            *[jax.ShapeDtypeStruct((rows, 128), bf16)] * shares,
            jax.ShapeDtypeStruct((2 * units + 448, shares * width), bf16),
            jax.ShapeDtypeStruct((32, width), bf16),
        ],
        scratch_shapes=[
            pltpu.VMEM((8, width), f32),
            pltpu.VMEM((8, units), f32),
            pltpu.VMEM((rows, width), bf16),
            pltpu.VMEM((rows, width), bf16),
            pltpu.VMEM((rows, shares * units), bf16),
            pltpu.VMEM((rows, width), bf16),
            pltpu.VMEM((shares, 2 * D + 128, D), bf16),
        ],
        compiler_params=pltpu.CompilerParams(vmem_limit_bytes=VMEM),
        cost_estimate=cost(25),
        name="block_backward",
    )(
        length, d_block, n1, r1, n2, r2, act, slope, own, packed, gain, shift, *divergence, squares, six_own, six,
        *attended
    )


def after(value, *others):
    return lax.optimization_barrier((value,) + others)[0]


def shift_shares(value, by):
    shares = lax.axis_size("heads")
    return lax.ppermute(value, "heads", [((i + by) % shares, i) for i in range(shares)])


def exchange(value, bit):
    size = lax.axis_size("batch")
    return lax.ppermute(value, "batch", [(i, i ^ bit) for i in range(size)])


def last_sum_kernel(rows_ref, grad_ref, bias_ref, branch_ref, gain_ref, shift_ref, summary_ref):
    total = rows_ref[...]
    end = total.shape[0] - 32
    sums = total[end : end + 16] + total[end + 16 :]
    grad_ref[...] = total[:end]
    bias_ref[...] = sums[0:2, :96]
    branch_ref[...] = sums[2:4]
    gain_ref[...] = sums[4:6]
    shift_ref[...] = sums[6:8]
    scalars = sums[8:9, :8]
    roots = jnp.sqrt(scalars / (scalars[:, 4:5] * D))
    summary_ref[...] = jnp.where(lanes((1, 8)) == 0, scalars, roots)[:, :4]


def last_sum(rows):
    count, width = rows.shape
    shapes = [(count - 32, width), (2, 96), (2, width), (2, width), (2, width), (1, 4)]
    return pl.pallas_call(
        last_sum_kernel, out_shape=[jax.ShapeDtypeStruct(s, f32) for s in shapes], cost_estimate=cost(1),
        name="last_sum", compiler_params=pltpu.CompilerParams(vmem_limit_bytes=VMEM),
    )(rows)


def rounded(total):
    end = total.shape[0] - 32
    sums = total[end : end + 16] + total[end + 16 :]
    high = lax.reduce_precision(sums, exponent_bits=8, mantissa_bits=7)
    return jnp.concatenate([total[:end], high, sums - high], axis=0).astype(bf16)


def finish_mid_kernel(rows_ref, narrow_ref, wide_ref, out_ref, bias_ref, six_ref, six_bias_ref):
    units = narrow_ref.shape[0]
    narrow_ref[...] = rows_ref[:units, :].astype(f32)
    wide_ref[...] = rows_ref[units : 2 * units, :].astype(f32)
    out_ref[...] = rows_ref[2 * units : 2 * units + 96, :].astype(f32)
    bias_ref[...] = rows_ref[2 * units + 96 : 2 * units + 112, :].astype(f32)[:1]
    six = 2 * units + 128
    six_ref[...] = rows_ref[six : six + 288, :].astype(f32)
    sums = rows_ref[six + 288 : six + 304, :].astype(f32) + rows_ref[six + 304 :, :].astype(f32)
    six_bias_ref[...] = sums[0:2, :96]


def finish_mid(rows):
    width = rows.shape[1]
    shapes = [(D, width), (D, width), (96, width), (1, width), (288, width), (2, 96)]
    return pl.pallas_call(
        finish_mid_kernel, out_shape=[jax.ShapeDtypeStruct(s, f32) for s in shapes], cost_estimate=cost(1),
        name="finish_mid", compiler_params=pltpu.CompilerParams(vmem_limit_bytes=VMEM),
    )(rows)


def body(
    student_rows, teacher_rows, valid_length, split_point, project_five, bias_five, output_five, branch_bias,
    norm_gain, norm_bias, widen_weight, widen_bias, narrow_weight, project_six, bias_six, teacher_project,
    teacher_bias,
):
    shares = lax.axis_size("heads")
    batch = lax.axis_size("batch")
    place = lax.axis_index("batch")
    all_rows = shares * batch * HEADS
    x = student_rows[0]
    teacher = teacher_rows[0]

    def turned(weight):
        return jnp.transpose(weight, (1, 2, 0)).reshape(-1, weight.shape[0])

    def placed(rows, at, count):
        return jnp.pad(rows, ((at, count - at - rows.shape[0]), (0, D - rows.shape[1])))

    biases = (bias_five, bias_six, widen_bias[None], teacher_bias)
    five = placed(turned(project_five), 0, 304)
    at = 288
    for bias in biases:
        five = five + placed(bias, at, 304)
        at += bias.shape[0]

    def part_of(rows):
        count = part_rows(rows.shape[0], batch)
        rows = jnp.pad(rows, ((0, count * batch - rows.shape[0]), (0, 0)))
        return lax.dynamic_slice_in_dim(rows, place * count, count)

    def others(rows):
        return [shift_shares(rows, by) for by in range(1, shares)]

    half = five.shape[0] // 2
    core = lax.rem(place, 2)
    mid = jnp.concatenate([widen_weight, narrow_weight, jnp.pad(output_five, ((0, 32), (0, 0)))], axis=0)
    taught = turned(teacher_project)
    rest = jnp.concatenate([turned(project_six), taught[:, :D], taught[:, D:]], axis=0)
    parts = others(jnp.concatenate([lax.dynamic_slice_in_dim(five, core * half, half), part_of(mid)], axis=0))

    first = attend_forward(valid_length, x, five[None])
    parts = jnp.stack([after(p, first[5]) for p in parts])
    halves, mid_parts = parts[:, :half], parts[:, half:]
    swapped = exchange(halves, 1)
    mid_all = lax.all_gather(mid_parts, "batch", axis=0)
    rest_parts = others(after(part_of(rest), mid_parts))
    low, high = jnp.where(core == 0, halves, swapped), jnp.where(core == 0, swapped, halves)
    fives = jnp.concatenate([low, high], axis=1)
    smalls = jnp.concatenate([five[None, 288:], fives[:, 288:]], axis=0)
    other = attend_forward(valid_length, after(x, mid_parts), fives)
    rest_parts = jnp.stack([after(p, other[5]) for p in rest_parts])
    rest_all = lax.all_gather(rest_parts, "batch", axis=0)
    attended = (first[5], other[5])
    block, n1, r1, n2, r2, act, slope, squares = block_forward(
        valid_length, after(x, rest_parts), attended, mid, mid_all, smalls, branch_bias, norm_gain, norm_bias
    )
    d_block, g_six_own, *divergence = relations(
        valid_length, split_point, block, teacher, rest, smalls[:1], all_rows
    )
    d_block, g_six, *divergence = relations(
        valid_length, split_point, block, teacher, rest_all, smalls[1:], all_rows, (d_block, *divergence)
    )
    result = block_backward(
        valid_length, d_block, n1, r1, n2, r2, act, slope, attended, mid, mid_all, norm_gain, norm_bias,
        divergence, squares, g_six_own, g_six,
    )
    d_sum_one, d_attended, (g_both, tail) = result[0], result[1 : 1 + shares], result[1 + shares :]

    def to_owner(parts):
        return [parts[0]] + [shift_shares(parts[by], shares - by) for by in range(1, shares)]

    units = widen_weight.shape[1]
    both = lax.psum_scatter(g_both, "batch", scatter_dimension=0, tiled=True)

    grad_in = d_sum_one
    g_five = [None] * shares
    for s in list(range(1, shares)) + [0]:
        q, k, v, e, r, a = other if s else first
        rows, w = after(x, *g_five[1 : shares - 1]) if s == 0 else x, fives if s else five[None]
        grad, grad_in = attend_backward(max(s - 1, 0), q, k, v, e, r, a, d_attended[s], rows, w, grad_in, tail)
        g_five[s] = shift_shares(grad, shares - s) if s else grad

    g_five = [g.astype(f32) for g in g_five]
    five_sum = rounded((g_five[0] + g_five[1]) + functools.reduce(jnp.add, g_five[2:]))
    both = after(both, five_sum)
    five_sum = after(five_sum, both)
    both = to_owner([both[:, s * D : (s + 1) * D] for s in range(shares)])
    bits = [1 << i for i in range(batch.bit_length() - 1)]
    groups = [bits[:1]] + [bits[i : i + 2] for i in range(1, len(bits), 2)]
    for index, group in enumerate(groups):
        received = [exchange(five_sum, bit) for bit in group]
        if len(group) == 2:
            received.append(exchange(five_sum, group[0] + group[1]))
        if index == 1:
            both = [after(p, five_sum) for p in both]
            both = sum(p.astype(f32) for p in both).astype(bf16)
        if index == len(groups) - 1:
            both = lax.all_gather(after(both, five_sum), "batch", axis=0, tiled=True)
            five_sum = after(five_sum, both)
        total = five_sum.astype(f32) + received[0].astype(f32)
        if len(group) == 2:
            total = total + (received[1].astype(f32) + received[2].astype(f32))
        five_sum = total if index == len(groups) - 1 else rounded(total)
    grad_five, five_bias, branch, gain, shift, summary = last_sum(five_sum)
    grad_narrow, grad_wide, grad_out, wide_bias, grad_six, six_bias = finish_mid(both)

    def unturned(grad):
        return jnp.transpose(grad.reshape(3, -1, grad.shape[1]), (2, 0, 1))

    return (
        block[None], grad_in[None], unturned(grad_five), five_bias, grad_out, branch, gain, shift,
        grad_wide, wide_bias[0], grad_narrow, unturned(grad_six), six_bias, summary[0],
    )


def solution(mesh):
    return jax.shard_map(
        body,
        mesh=mesh,
        in_specs=(
            P(("batch", "heads"), None, None),
            P(("batch", "heads"), None, None),
            P("batch"),
            P("batch"),
            P(None, None, "heads"),
            P(None, "heads"),
            P("heads", None),
            P(),
            P(),
            P(),
            P(None, "heads"),
            P("heads"),
            P("heads", None),
            P(None, None, "heads"),
            P(None, "heads"),
            P(None, None, "heads"),
            P(None, "heads"),
        ),
        out_specs=(
            P(("batch", "heads"), None, None),
            P(("batch", "heads"), None, None),
            P(None, None, "heads"),
            P(None, "heads"),
            P("heads", None),
            P(),
            P(),
            P(),
            P(None, "heads"),
            P("heads"),
            P("heads", None),
            P(None, None, "heads"),
            P(None, "heads"),
            P(),
        ),
        check_vma=False,
    )
```

```python
import functools
import math

import jax
import jax.numpy as jnp
from jax import lax
from jax.experimental import pallas as pl
from jax.experimental.pallas import tpu as pltpu
from jax.sharding import PartitionSpec as P

D = 384
HEADS = 12
HEAD_DIM = 32
TEACHER_HEAD_DIM = 64
PART = 3
TILE = 512
WIDE_TILE = 1024
STRIP = 16
NORM_EPS = 1e-12
MASKED = -1e30
SAFE = 64.0
LN2 = math.log(2.0)
STUDENT_SCALE = 1.0 / math.sqrt(HEAD_DIM)
STUDENT_LOG = math.log2(math.e) / math.sqrt(HEAD_DIM)
TEACHER_LOG = math.log2(math.e) / math.sqrt(TEACHER_HEAD_DIM)
VMEM = 56 * 2**20

f32 = jnp.float32
bf16 = jnp.bfloat16

NN = (((1,), (0,)), ((), ()))
NT = (((1,), (1,)), ((), ()))
TN = (((0,), (0,)), ((), ()))


def dot(left, right, dims=NN):
    return lax.dot_general(left, right, dims, preferred_element_type=f32)


def lanes(shape):
    return lax.broadcasted_iota(jnp.int32, shape, 1)


def wide_rows(rows):
    return jnp.concatenate([rows, jnp.zeros((rows.shape[0], 128 - rows.shape[1]), rows.dtype)], axis=1)


def in_head(lane, head, size=HEAD_DIM):
    return (lane >= head * size) & (lane < (head + 1) * size)


def split_terms(rows, head, size, extra):
    inside = in_head(lanes(rows.shape), head, size)
    high = rows.astype(bf16).astype(f32)
    first = jnp.where(inside, high, extra).astype(bf16)
    second = jnp.where(inside, rows - high, 0.0).astype(bf16)
    return jnp.concatenate([first, second], axis=1)


def own_number(ref):
    return ref[lax.axis_index("heads")]


def key_bias(rows, length):
    position = lax.broadcasted_iota(jnp.int32, (rows, 1), 0)
    return jnp.where(position < length, 0.0, MASKED)


def fold(tile, combine):
    total = tile[:, :128]
    for column in range(128, tile.shape[1], 128):
        total = combine(total, tile[:, column : column + 128])
    return total


def row_sum(tile):
    return jnp.sum(fold(tile, jnp.add), axis=1, keepdims=True)


def weave(first, second):
    done = 0
    for index, step in enumerate(second):
        while done < len(first) and done * len(second) < len(first) * (index + 1):
            first[done]()
            done += 1
        step()
    for step in first[done:]:
        step()


def step_place(step, tile, per_head):
    head = step // per_head
    return head, pl.ds(pl.multiple_of(lax.rem(step, per_head) * tile, tile), tile)


def skew(first, second):
    steps = [first[0]]
    for index in range(1, len(first)):
        steps += [first[index], second[index - 1]]
    return steps + [second[-1]]


def run_rolled(steps, logits, vector, back, reset=None, enter=None):
    def pair(index, carry):
        for slot in range(2):
            step = 2 * index + slot
            if enter is not None:
                enter(step, slot, index)
            ahead = logits(jnp.minimum(step + 1, steps - 1), 1 - slot)
            weave(ahead + back(jnp.maximum(step - 1, 0), 1 - slot), vector(step, slot))
            if slot == 0 and reset is not None:
                pl.when(index == 0)(reset)
        return carry

    for chunk in logits(jnp.int32(0), 0):
        chunk()
    lax.fori_loop(0, steps // 2, pair, 0)
    for chunk in back(jnp.int32(steps - 1), 1):
        chunk()


def run_pipeline(steps, logits, vector, back, enter=None):
    def stage(step, slot, before, after, second=False):
        if enter is not None:
            enter(step, slot, not before, second)
        ahead = logits(step + 1, 1 - slot) if after else []
        behind = back(step - 1, 1 - slot) if before else []
        weave(ahead + behind, vector(step, slot))

    for chunk in logits(jnp.int32(0), 0):
        chunk()
    if steps < 4:
        for step in range(steps):
            stage(jnp.int32(step), step % 2, step > 0, step + 1 < steps, second=step == 1)
        for chunk in back(jnp.int32(steps - 1), (steps - 1) % 2):
            chunk()
        return
    stage(jnp.int32(0), 0, False, True)
    stage(jnp.int32(1), 1, True, True, second=True)

    def pair(index, carry):
        stage(2 * index + 2, 0, True, True)
        stage(2 * index + 3, 1, True, True)
        return carry

    lax.fori_loop(0, (steps - 4) // 2, pair, 0)
    stage(jnp.int32(steps - 2), 0, True, True)
    stage(jnp.int32(steps - 1), 1, True, False)
    for chunk in back(jnp.int32(steps - 1), 1):
        chunk()


def project_part(x, w_ref, index, bias):
    flat = dot(x, w_ref[index * 96 : (index + 1) * 96, :], NT)
    if bias is not None:
        flat = flat + bias
    return wide_rows(flat).astype(bf16)


def attend_forward_kernel(
    length_ref, x_ref, w_ref, q_ref, k_ref, v_ref, e_hbm, r_ref, o_ref, lhs, rhs, mixer, zs0, zs1, es0, es1, sems
):
    share = pl.program_id(0)
    w_ref, q_ref, k_ref, v_ref, r_ref, o_ref = (t.at[0] for t in (w_ref, q_ref, k_ref, v_ref, r_ref, o_ref))
    zs, es = (zs0, zs1), (es0, es1)
    rows = x_ref.shape[0]
    tile = zs0.shape[0]
    per_head = rows // tile
    steps = PART * per_head
    x = x_ref[...]
    small = w_ref[288:304, :].astype(f32)
    q = project_part(x, w_ref, 0, small[0:1, :96])
    k = project_part(x, w_ref, 1, None)
    v = project_part(x, w_ref, 2, small[1:2, :96])
    q_ref[...] = q
    k_ref[...] = k
    v_ref[...] = v
    lane = lanes((rows, 128))
    one = jnp.where(lane == 96, 1.0, 0.0)
    for head in range(PART):
        lhs[head] = jnp.where(in_head(lane, head), q.astype(f32), one).astype(bf16)
    rhs[...] = jnp.where(lane == 96, key_bias(rows, own_number(length_ref)), k.astype(f32)).astype(bf16)
    mixer[...] = jnp.where(lane == 96, 1.0, v.astype(f32)).astype(bf16)
    o_ref[...] = jnp.zeros_like(o_ref)
    r_ref[...] = jnp.zeros_like(r_ref)

    def out_copy(step, slot):
        head, span = step_place(step, tile, per_head)
        return pltpu.make_async_copy(es[slot], e_hbm.at[share, head, span], sems.at[slot])

    def logits(step, slot):
        head, span = step_place(step, tile, per_head)

        def chunk(start):
            zs[slot][:, start : start + 256] = dot(lhs[head, span, :], rhs[start : start + 256, :], NT)

        return [functools.partial(chunk, start) for start in range(0, rows, 256)]

    def vector(step, slot):
        def strip(start):
            z = zs[slot][start : start + STRIP, :]
            highest = jnp.max(fold(z, jnp.maximum), axis=1, keepdims=True)
            es[slot][start : start + STRIP, :] = jnp.exp2((z - highest) * STUDENT_LOG).astype(bf16)

        return [functools.partial(strip, start) for start in range(0, tile, STRIP)]

    def back(step, slot):
        head, span = step_place(step, tile, per_head)

        sums = []

        def part(start):
            sums.append(dot(es[slot][:, start : start + 256], mixer[start : start + 256, :]))

        def mix():
            mixed = functools.reduce(jnp.add, sums)
            inverse = 1.0 / mixed[:, 96:97]
            inside = in_head(lanes(mixed.shape), head)
            o_ref[span, :] = jnp.where(inside, mixed * inverse, o_ref[span, :].astype(f32)).astype(bf16)
            r_ref[span, :] = jnp.where(inside, inverse, r_ref[span, :])

        return [functools.partial(part, start) for start in range(0, rows, 256)] + [mix]

    def enter(step, slot, first, second):
        if not first:
            out_copy(step - 1, 1 - slot).start()
        if not (first or second):
            out_copy(step - 2, slot).wait()

    run_pipeline(steps, logits, vector, back, enter)
    last = (steps - 1) % 2
    out_copy(jnp.int32(steps - 1), last).start()
    out_copy(jnp.int32(steps - 2), 1 - last).wait()
    out_copy(jnp.int32(steps - 1), last).wait()


def whole(shape):
    return pl.BlockSpec(shape, lambda *_: (0,) * len(shape))


SMEM = pl.BlockSpec(memory_space=pltpu.SMEM)
ANY = pl.BlockSpec(memory_space=pl.ANY)


def cost(micros):
    return pl.CostEstimate(flops=int(micros * 0.04e9), bytes_accessed=1024, transcendentals=0)


def attend_forward(length, x, w):
    rows, count = x.shape[0], w.shape[0]
    tile = min(WIDE_TILE, rows)
    narrow = jax.ShapeDtypeStruct((count, rows, 128), bf16)

    def share(shape):
        return pl.BlockSpec((1,) + shape, lambda s: (s,) + (0,) * len(shape))

    row = share((rows, 128))
    return pl.pallas_call(
        attend_forward_kernel,
        grid=(count,),
        in_specs=[SMEM, whole(x.shape), share(w.shape[1:])],
        out_specs=[row] * 3 + [ANY] + [row] * 2,
        out_shape=[
            narrow, narrow, narrow, jax.ShapeDtypeStruct((count, PART, rows, rows), bf16),
            jax.ShapeDtypeStruct((count, rows, 128), f32), narrow,
        ],
        scratch_shapes=[
            pltpu.VMEM((PART, rows, 128), bf16),
            pltpu.VMEM((rows, 128), bf16),
            pltpu.VMEM((rows, 128), bf16),
            pltpu.VMEM((tile, rows), f32),
            pltpu.VMEM((tile, rows), f32),
            pltpu.VMEM((tile, rows), bf16),
            pltpu.VMEM((tile, rows), bf16),
            pltpu.SemaphoreType.DMA((2,)),
        ],
        compiler_params=pltpu.CompilerParams(vmem_limit_bytes=VMEM),
        cost_estimate=cost(9 * count),
        name="attend_forward",
    )(length, x, w)


def attend_backward_kernel(
    q_ref, k_ref, v_ref, e_hbm, r_ref, a_ref, d_ref, x_hbm, w_hbm, acc_hbm, tail_ref, g_ref, in_ref,
    lhs, rhs, keys, qt, dt, zs0, zs1, gs0, gs1, dq, dkt, dvt, e_all, x_ref, w_ref, acc_ref, sems, late, *, share,
):
    q_ref, k_ref, v_ref, r_ref, a_ref = (t.at[0] for t in (q_ref, k_ref, v_ref, r_ref, a_ref))
    rows = q_ref.shape[0]
    zs, gs = (zs0, zs1), (gs0, gs1)
    tile = zs0.shape[0]
    per_head = rows // tile
    steps = PART * per_head

    def in_copy(step):
        head, span = step_place(step, tile, per_head)
        return pltpu.make_async_copy(e_hbm.at[share, head, span], e_all.at[head, span], sems.at[step])

    for step in range(2):
        in_copy(jnp.int32(step)).start()
    late_copies = [
        pltpu.make_async_copy(source, target, late.at[index])
        for index, (source, target) in enumerate(((x_hbm, x_ref), (w_hbm.at[share], w_ref), (acc_hbm, acc_ref)))
    ]

    def enter(step, slot, first, second):
        if second:
            for copy in late_copies:
                copy.start()

        @pl.when(step + 2 < steps)
        def _():
            in_copy(step + 2).start()

        in_copy(step).wait()

    lane = lanes((rows, 128))
    grads = r_ref[...] * d_ref[...].astype(f32)
    shifts = grads * a_ref[...].astype(f32)
    k = k_ref[...].astype(f32)
    def one_head(head, carry):
        inside = in_head(lane, head)
        shift = -jnp.sum(jnp.where(inside, shifts, 0.0), axis=1, keepdims=True)
        high = shift.astype(bf16).astype(f32)
        lhs[head] = split_terms(
            grads, head, HEAD_DIM, jnp.where(lane == 96, high, jnp.where(lane == 97, shift - high, 0.0))
        )
        keys[head] = jnp.where(inside, k, 0.0).astype(bf16)
        return carry

    lax.fori_loop(0, PART, one_head, 0)
    rhs[:, :128] = jnp.where((lane == 96) | (lane == 97), 1.0, v_ref[...].astype(f32)).astype(bf16)
    rhs[:, 128:] = v_ref[...]
    qt[...] = q_ref[...].T
    dt[...] = grads.astype(bf16).T

    def reset():
        dq[...] = jnp.zeros_like(dq)
        dkt[...] = jnp.zeros_like(dkt)
        dvt[...] = jnp.zeros_like(dvt)

    reset()

    def logits(step, slot):
        head, span = step_place(step, tile, per_head)

        def chunk(start):
            zs[slot][:, start : start + 256] = dot(lhs[head, span, :], rhs[start : start + 256, :], NT)

        return [functools.partial(chunk, start) for start in range(0, rows, 256)]

    def vector(step, slot):
        head, span = step_place(step, tile, per_head)
        base = lax.rem(step, per_head) * tile

        def strip(start):
            here = pl.ds(pl.multiple_of(base + start, STRIP), STRIP)
            weights = e_all[head, here, :].astype(f32)
            gs[slot][start : start + STRIP, :] = (weights * zs[slot][start : start + STRIP, :]).astype(bf16)

        return [functools.partial(strip, start) for start in range(0, tile, STRIP)]

    def back(step, slot):
        head, span = step_place(step, tile, per_head)
        own = pl.ds(pl.multiple_of(head * HEAD_DIM, HEAD_DIM), HEAD_DIM)

        def first():
            dq[span, :] += dot(gs[slot][...], keys[head])

        def second(start):
            part = slice(start, start + 256)
            dkt[own, part] += dot(qt[own, span], gs[slot][:, part])

        def third(start):
            part = slice(start, start + 256)
            dvt[own, part] += dot(dt[own, span], e_all[head, span, part])

        starts = range(0, rows, 256)
        return [first] + [functools.partial(second, s) for s in starts] + [functools.partial(third, s) for s in starts]

    run_pipeline(steps, logits, vector, back, enter)
    for copy in late_copies:
        copy.wait()
    grads = (
        (dq[...] * STUDENT_SCALE).astype(bf16),
        (dkt[...] * STUDENT_SCALE).T.astype(bf16),
        dvt[...].T.astype(bf16),
    )
    weight_grads(grads, x_ref[...], g_ref, tail_ref[:16, :].astype(f32), tail_ref[16:, :].astype(f32))
    in_ref[...] = acc_ref[...] + spread(grads, w_ref)


def weight_grads(grads, x, g_ref, tail_high=0.0, tail_low=0.0):
    for index, grad in enumerate(grads):
        g_ref[index * 96 : (index + 1) * 96, :] = dot(grad, x, TN)[:96].astype(bf16)
    ones = jnp.ones((16, x.shape[0]), bf16)
    row = lax.broadcasted_iota(jnp.int32, (16, 128), 0)
    sums = jnp.where(row == 0, dot(ones, grads[0]), jnp.where(row == 1, dot(ones, grads[2]), 0.0))
    sums = jnp.concatenate([sums, jnp.zeros((16, x.shape[1] - 128), f32)], axis=1) + tail_high
    high = sums.astype(bf16).astype(f32)
    g_ref[288:304, :] = high.astype(bf16)
    g_ref[304:320, :] = (sums - high + tail_low).astype(bf16)


def spread(grads, w_ref):
    total = None
    for index, grad in enumerate(grads):
        term = dot(grad[:, :96], w_ref[index * 96 : (index + 1) * 96, :])
        total = term if total is None else total + term
    return total


def attend_backward(share, q, k, v, e, r, attended, d_attended, x, w, grad_in, tail):
    rows = x.shape[0]
    tile = min(TILE, rows // 2)
    row = pl.BlockSpec((1, rows, 128), lambda i: (share, 0, 0))
    return pl.pallas_call(
        functools.partial(attend_backward_kernel, share=share),
        grid=(1,),
        in_specs=[row, row, row, ANY, row, row, whole((rows, 128)), ANY, ANY, ANY, whole(tail.shape)],
        out_specs=[whole((320, x.shape[1])), whole(x.shape)],
        out_shape=[jax.ShapeDtypeStruct((320, x.shape[1]), bf16), jax.ShapeDtypeStruct(x.shape, f32)],
        scratch_shapes=[
            pltpu.VMEM((PART, rows, 256), bf16),
            pltpu.VMEM((rows, 256), bf16),
            pltpu.VMEM((PART, rows, 128), bf16),
            pltpu.VMEM((128, rows), bf16),
            pltpu.VMEM((128, rows), bf16),
            pltpu.VMEM((tile, rows), f32),
            pltpu.VMEM((tile, rows), f32),
            pltpu.VMEM((tile, rows), bf16),
            pltpu.VMEM((tile, rows), bf16),
            pltpu.VMEM((rows, 128), f32),
            pltpu.VMEM((128, rows), f32),
            pltpu.VMEM((128, rows), f32),
            pltpu.VMEM((PART, rows, rows), bf16),
            pltpu.VMEM(x.shape, bf16),
            pltpu.VMEM(w.shape[1:], bf16),
            pltpu.VMEM(x.shape, f32),
            pltpu.SemaphoreType.DMA((PART * (rows // tile),)),
            pltpu.SemaphoreType.DMA((3,)),
        ],
        compiler_params=pltpu.CompilerParams(vmem_limit_bytes=VMEM),
        cost_estimate=cost(10),
        name="attend_backward",
    )(q, k, v, e, r, attended, d_attended, x, w, grad_in, tail)


def relation_kernel(
    length_ref, split_ref, block_ref, teacher_ref, packed_ref, small_ref, *rest, all_rows, gathered,
):
    before = None
    if gathered:
        before, rest = rest[:3], rest[3:]
    (
    d_ref, g_ref, kl_ref, kl_row_ref, pack, lefts, rights, t_lefts, t_rights, ls, rs, lt, rt, keys, left_t, zs0, zs1, zt0, zt1, gs0, gs1,
    left_sum, right_t, es_all, et_all, parts, columns, factors, rows_s, weight, weight_row, grads_s,
    ) = rest
    rows = block_ref.shape[0]
    tile = zs0.shape[0]
    per_head = rows // tile
    steps = PART * per_head
    zs, zt, gs = (zs0, zs1), (zt0, zt1), (gs0.at[:tile], gs1)
    length, split = own_number(length_ref), own_number(split_ref)

    @pl.when(pl.program_id(0) == 0)
    def _():
        position = lax.broadcasted_iota(jnp.int32, (rows, 1), 0)
        counted = (position < length) & (position != 0) & (position != split - 1) & (position != length - 1)
        share = 1.0 / ((length - 3).astype(f32) * float(all_rows))
        weight[...] = jnp.where(counted, share, 0.0)
        position = lanes((1, rows))
        counted = (position < length) & (position != 0) & (position != split - 1) & (position != length - 1)
        weight_row[...] = jnp.where(counted, share, 0.0)
        for index, ref in enumerate((d_ref, kl_ref, kl_row_ref)):
            ref[...] = before[index][...] if gathered else jnp.zeros_like(ref)

    if gathered:
        unpack(packed_ref, 0, pack)
    else:
        pack[...] = packed_ref[...]

    g_ref = g_ref.at[0]
    small = small_ref[0].astype(f32)

    def head_mask(size):
        shift = size.bit_length() - 1
        same = (lax.broadcasted_iota(jnp.int32, (128, 128), 0) >> shift) == (lanes((128, 128)) >> shift)
        return jnp.where(same, 1.0, 0.0).astype(bf16)

    masks = {size: head_mask(size) for size in (HEAD_DIM, TEACHER_HEAD_DIM)}

    def largest(low, size):
        square = low.astype(f32)
        return jnp.max(dot((square * square).astype(bf16), masks[size]), axis=0, keepdims=True)

    def project(index, carry):
        here = pl.ds(pl.multiple_of(index * tile, tile), tile)
        block, teacher = block_ref[here, :], teacher_ref[here, :]

        def student(part, b):
            flat = dot(block, pack[part * 96 : (part + 1) * 96, :], NT)
            return wide_rows(flat if b is None else flat + b).astype(bf16)

        def taught(part, b):
            start = 288 + part * 192
            flat = dot(teacher[:, :D], pack[start : start + 192, :], NT)
            flat = flat + dot(teacher[:, D:], pack[start + 576 : start + 768, :], NT)
            flat = (flat if b is None else flat + b).astype(bf16)
            return flat[:, :128], wide_rows(flat[:, 128:])

        q, k, v = student(0, small[2:3, :96]), student(1, None), student(2, small[3:4, :96])
        lefts[0, here, :] = q
        rights[0, here, :] = k
        lefts[1, here, :] = v
        rights[1, here, :] = v
        tq, tk, tv = taught(0, small[5:6, :192]), taught(1, None), taught(2, small[6:7, :192])
        for half in range(2):
            t_lefts[0, half, here, :] = tq[half]
            t_rights[0, half, here, :] = tk[half]
            t_lefts[1, half, here, :] = tv[half]
            t_rights[1, half, here, :] = tv[half]
        found = [largest(value, HEAD_DIM) for value in (q, k, v)]
        found += [largest(value, TEACHER_HEAD_DIM) for value in tq + tk + tv]
        return tuple(jnp.maximum(old, new) for old, new in zip(carry, found))

    top = lax.fori_loop(0, rows // tile, project, (jnp.zeros((1, 128), f32),) * 9)
    bounds = []
    for s_left, s_right, t_left, t_right in ((0, 1, 3, 5), (2, 2, 7, 7)):
        bound = jnp.max(top[s_left] * top[s_right]) * STUDENT_LOG**2
        for half in range(2):
            bound = jnp.maximum(bound, jnp.max(top[t_left + half] * top[t_right + half]) * TEACHER_LOG**2)
        bounds.append(bound)

    def operands(relation, student_scale, teacher_scale, row_bias, everything):
        band = min(128, rows)
        line = lanes((1, 128))

        def terms(value, inside, extra):
            high, low = value
            return jnp.where(inside, high, extra).astype(bf16), jnp.where(inside, low, 0.0).astype(bf16)

        def halves(value, scale):
            value = value * scale
            high = value.astype(bf16).astype(f32)
            return high, value - high

        def one_band(index, carry):
            here = pl.ds(pl.multiple_of(index * band, band), band)
            position = lax.broadcasted_iota(jnp.int32, (band, 128), 0) + index * band
            bias = jnp.where(position < length, 0.0, MASKED)
            row = jnp.where(row_bias, bias, 0.0)
            left, right = lefts[relation, here, :].astype(f32), rights[relation, here, :].astype(f32)
            value = halves(left, student_scale)
            extra = jnp.where(line == 97, row, jnp.where(line == 96, 1.0, 0.0))
            if everything:
                rs[here, :128] = jnp.where(line == 97, 1.0, jnp.where(line == 96, bias, right)).astype(bf16)
                rs[here, 128:] = rights[relation, here, :]
            for head in range(PART):
                inside = in_head(line, head)
                ls[head, here, :128], ls[head, here, 128:] = terms(value, inside, extra)
                if everything:
                    keys[head, here, :] = jnp.where(inside, right, 0.0).astype(bf16)
            for half in range(2):
                t_left = t_lefts[relation, half, here, :].astype(f32)
                t_right = t_rights[relation, half, here, :].astype(f32)
                value = halves(t_left, teacher_scale)
                for head in range(2 * half, min(2 * half + 2, PART)):
                    own = head % 2
                    spare = (1 - own) * TEACHER_HEAD_DIM
                    extra = jnp.where(line == spare + 1, row, jnp.where(line == spare, 1.0, 0.0))
                    inside = in_head(line, own, TEACHER_HEAD_DIM)
                    lt[head, here, :128], lt[head, here, 128:] = terms(value, inside, extra)
                    if everything:
                        first = jnp.where(line == spare + 1, 1.0, jnp.where(line == spare, bias, t_right))
                        rt[head, here, :128] = first.astype(bf16)
                        rt[head, here, 128:] = t_rights[relation, half, here, :]
            return carry

        lax.fori_loop(0, rows // band, one_band, 0)

    def relate(relation, carry):
        symmetric = relation == 1
        left_t[...] = lefts[relation].T
        operands(relation, STUDENT_LOG, TEACHER_LOG, symmetric, True)
        near = jnp.where(symmetric, bounds[1], bounds[0]) < SAFE * SAFE
        reset()

        @pl.when(near & jnp.logical_not(symmetric))
        def _():
            run_pipeline(steps, logits, vector, grad_products)

        @pl.when(near & symmetric)
        def _():
            lax.fori_loop(0, PART, symmetric_head, 0)

        @pl.when(jnp.logical_not(near))
        def _():
            operands(relation, 1.0, 1.0, False, False)
            lax.fori_loop(0, steps, shifted_step, 0)

        @pl.when(jnp.logical_not(symmetric))
        def _():
            grads_s[0] = (left_sum[...] * STUDENT_SCALE).astype(bf16)
            grads_s[1] = (right_t[...] * STUDENT_SCALE).T.astype(bf16)

        @pl.when(symmetric)
        def _():
            grads_s[2] = ((left_sum[...] + right_t[...].T) * STUDENT_SCALE).astype(bf16)

        return carry

    def reset():
        left_sum[...] = jnp.zeros_like(left_sum)
        right_t[...] = jnp.zeros_like(right_t)

    def logits(step, slot):
        head, span = step_place(step, tile, per_head)

        def student(start):
            zs[slot][:, start : start + 256] = dot(ls[head, span, :], rs[start : start + 256, :], NT)

        def taught(start):
            zt[slot][:, start : start + 256] = dot(lt[head, span, :], rt[head, start : start + 256, :], NT)

        chunks = []
        for start in range(0, rows, 256):
            chunks += [functools.partial(student, start), functools.partial(taught, start)]
        return chunks

    def vector(step, slot):
        base = lax.rem(step, per_head) * tile
        z, t, g = zs[slot], zt[slot], gs[slot]
        scales = {}

        def both(start):
            strip = slice(start, start + STRIP)
            student, taught = z[strip, :], t[strip, :]
            es, et = jnp.exp2(student), jnp.exp2(taught)
            sum_s, sum_t, cross = row_sum(es), row_sum(et), row_sum(et * (taught - student))
            here = pl.ds(pl.multiple_of(base + start, STRIP), STRIP)
            w = weight[here, :]
            inverse = 1.0 / sum_t
            kl_ref[here, :] += w * (LN2 * cross * inverse + jnp.log(sum_s) - jnp.log(sum_t))
            g[strip, :] = (es * (w / sum_s) - et * (w * inverse)).astype(bf16)

        return [functools.partial(both, s) for s in range(0, tile, STRIP)]

    def grad_products(step, slot):
        head, span = step_place(step, tile, per_head)
        own = pl.ds(pl.multiple_of(head * HEAD_DIM, HEAD_DIM), HEAD_DIM)

        def first():
            left_sum[span, :] += dot(gs[slot][...], keys[head])

        def second(start):
            part = slice(start, start + 256)
            right_t[own, part] += dot(left_t[own, span], gs[slot][:, part])

        return [first] + [functools.partial(second, start) for start in range(0, rows, 256)]

    def shifted_step(step, carry):
        head, span = step_place(step, tile, per_head)
        student = dot(ls[head, span, :], rs[...], NT)
        zs0[...] = (student - jnp.max(student, axis=1, keepdims=True)) * STUDENT_LOG
        taught = dot(lt[head, span, :], rt[head], NT)
        zt0[...] = (taught - jnp.max(taught, axis=1, keepdims=True)) * TEACHER_LOG

        def strip(index, carry):
            here = pl.ds(pl.multiple_of(index * STRIP, STRIP), STRIP)
            student, taught = zs0[here, :], zt0[here, :]
            es, et = jnp.exp2(student), jnp.exp2(taught)
            sum_s, sum_t = row_sum(es), row_sum(et)
            cross = row_sum(et * (taught - student))
            there = pl.ds(pl.multiple_of(lax.rem(step, per_head) * tile + index * STRIP, STRIP), STRIP)
            w = weight[there, :]
            row = LN2 * cross / sum_t + jnp.log(sum_s) - jnp.log(sum_t)
            kl_ref[there, :] += jnp.where(w > 0.0, w * row, 0.0)
            gs0[here, :] = (es * (w / sum_s) - et * (w / sum_t)).astype(bf16)
            return carry

        lax.fori_loop(0, tile // STRIP, strip, 0)
        for chunk in grad_products(step, 0):
            chunk()
        return carry

    def symmetric_head(head, carry):
        size, band = min(256, rows), 32
        count = rows // size
        own = pl.ds(pl.multiple_of(head * HEAD_DIM, HEAD_DIM), HEAD_DIM)
        columns[...] = jnp.zeros_like(columns)

        def logit_chunks(i):
            here = slice(i * size, (i + 1) * size)

            def student(part):
                es_all[here, part] = dot(ls[head, here, :], rs[part, :], NT)

            def taught(part):
                et_all[here, part] = dot(lt[head, here, :], rt[head, part, :], NT)

            chunks = []
            for j in range(i, count):
                part = slice(j * size, (j + 1) * size)
                chunks += [functools.partial(student, part), functools.partial(taught, part)]
            return chunks

        def weigh(i, start):
            strip = slice(start, start + band)
            totals = [0.0, 0.0, 0.0]
            for column in range(i * size, rows, 128):
                part = slice(column, column + 128)
                student, taught = es_all[strip, part], et_all[strip, part]
                es, et = jnp.exp2(student), jnp.exp2(taught)
                es_all[strip, part] = es
                et_all[strip, part] = et
                for index, value in enumerate((es, et, et * (taught - student))):
                    totals[index] = totals[index] + value
                    if column >= (i + 1) * size:
                        eight = value[:8]
                        for line in range(8, band, 8):
                            eight = eight + value[line : line + 8]
                        columns[index, :, part] += eight
            for index in range(3):
                parts[index, strip, :] = totals[index]

        def combine(i, start):
            strip = slice(start, start + STRIP)
            a, b = factors[0, strip, :], factors[1, strip, :]
            for column in range(i * size, rows, 128):
                part = slice(column, column + 128)
                both = es_all[strip, part] * (a + rows_s[0, :, part])
                both = both - et_all[strip, part] * (b + rows_s[1, :, part])
                gs0[strip, part] = both.astype(bf16)

        def products(i):
            here = slice(i * size, (i + 1) * size)

            def first(j):
                part = slice(j * size, (j + 1) * size)
                left_sum[here, :] += dot(gs_all[here, part], keys[head, part, :])

            def second(j):
                part = slice(j * size, (j + 1) * size)
                right_t[own, part] += dot(left_t[own, here], gs_all[here, part])

            chunks = [functools.partial(first, j) for j in range(i, count)]
            return chunks + [functools.partial(second, j) for j in range(i + 1, count)]

        gs_all = gs0
        for chunk in logit_chunks(0):
            chunk()
        for i in range(count):
            ahead = logit_chunks(i + 1) if i + 1 < count else []
            weave(ahead, [functools.partial(weigh, i, s) for s in range(i * size, (i + 1) * size, band)])
        sums = [
            jnp.sum(parts[index].T, axis=0, keepdims=True) + jnp.sum(columns[index], axis=0, keepdims=True)
            for index in range(3)
        ]
        w = weight_row[...]
        sum_s, sum_t = (jnp.where(w > 0.0, value, 1.0) for value in sums[:2])
        inverse = 1.0 / sum_t
        kl_row_ref[...] += w * (LN2 * sums[2] * inverse + jnp.log(sum_s) - jnp.log(sum_t))
        for index, value in enumerate((w / sum_s, w * inverse)):
            factors[index] = jnp.broadcast_to(value, (128, rows)).T
            rows_s[index] = jnp.broadcast_to(value, (STRIP, rows))
        for i in range(count):
            behind = products(i - 1) if i else []
            weave(behind, [functools.partial(combine, i, s) for s in range(i * size, (i + 1) * size, STRIP)])
        for chunk in products(count - 1):
            chunk()
        return carry

    lax.fori_loop(0, 2, relate, 0)
    grads = tuple(grads_s[i] for i in range(3))
    weight_grads(grads, block_ref[...], g_ref)
    d_ref[...] += spread(grads, pack)


def part_rows(rows, batch):
    return -(-rows // (16 * batch)) * 16


def unpack(packed_ref, share, target):
    rows, batch = target.shape[0], packed_ref.shape[0]
    part = part_rows(rows, batch)
    for start in range(0, rows, part):
        size = min(part, rows - start)
        target[start : start + size, :] = packed_ref[start // part, share, :size, :]


def relations(length, split, block, teacher, packed, small, all_rows, before=()):
    rows = block.shape[0]
    tile = min(TILE, rows // 2)
    shares = small.shape[0]

    def share(shape):
        return pl.BlockSpec((1,) + shape[1:], lambda s: (s,) + (0,) * (len(shape) - 1))

    gathered = len(before) > 0
    if gathered:
        place = pl.BlockSpec((packed.shape[0], 1) + packed.shape[2:], lambda s: (0, s, 0, 0))
    else:
        place = whole(packed.shape)
    return pl.pallas_call(
        functools.partial(relation_kernel, all_rows=all_rows, gathered=gathered),
        grid=(shares,),
        in_specs=[
            SMEM, SMEM, whole(block.shape), whole(teacher.shape), place, share(small.shape),
        ] + [whole(b.shape) for b in before],
        out_specs=[whole(block.shape), share((shares, 320, D)), whole((rows, 1)), whole((1, rows))],
        out_shape=[
            jax.ShapeDtypeStruct(block.shape, f32),
            jax.ShapeDtypeStruct((shares, 320, D), bf16),
            jax.ShapeDtypeStruct((rows, 1), f32),
            jax.ShapeDtypeStruct((1, rows), f32),
        ],
        scratch_shapes=[
            pltpu.VMEM((1440, D), bf16),
            pltpu.VMEM((2, rows, 128), bf16),
            pltpu.VMEM((2, rows, 128), bf16),
            pltpu.VMEM((2, 2, rows, 128), bf16),
            pltpu.VMEM((2, 2, rows, 128), bf16),
            pltpu.VMEM((PART, rows, 256), bf16),
            pltpu.VMEM((rows, 256), bf16),
            pltpu.VMEM((PART, rows, 256), bf16),
            pltpu.VMEM((PART, rows, 256), bf16),
            pltpu.VMEM((PART, rows, 128), bf16),
            pltpu.VMEM((128, rows), bf16),
            pltpu.VMEM((tile, rows), f32),
            pltpu.VMEM((tile, rows), f32),
            pltpu.VMEM((tile, rows), f32),
            pltpu.VMEM((tile, rows), f32),
            pltpu.VMEM((rows, rows), bf16),
            pltpu.VMEM((tile, rows), bf16),
            pltpu.VMEM((rows, 128), f32),
            pltpu.VMEM((128, rows), f32),
            pltpu.VMEM((rows, rows), f32),
            pltpu.VMEM((rows, rows), f32),
            pltpu.VMEM((3, rows, 128), f32),
            pltpu.VMEM((3, 8, rows), f32),
            pltpu.VMEM((2, rows, 128), f32),
            pltpu.VMEM((2, STRIP, rows), f32),
            pltpu.VMEM((rows, 1), f32),
            pltpu.VMEM((1, rows), f32),
            pltpu.VMEM((3, rows, 128), bf16),
        ],
        compiler_params=pltpu.CompilerParams(vmem_limit_bytes=VMEM),
        cost_estimate=cost(30 * shares),
        name="relations",
    )(length, split, block, teacher, packed, small, *before)


def norm_forward(rows, gain, shift):
    center = jnp.mean(rows, axis=1, keepdims=True)
    offsets = rows - center
    rstd = lax.rsqrt(jnp.mean(offsets * offsets, axis=1, keepdims=True) + NORM_EPS)
    normed = offsets * rstd
    return normed * gain + shift, normed, rstd


def norm_backward(grad, normed, rstd, gain):
    inner = grad * gain
    mean = jnp.mean(inner, axis=1, keepdims=True)
    slope = jnp.mean(inner * normed, axis=1, keepdims=True)
    return rstd * (inner - mean - normed * slope)


def gelu_terms(x):
    t = 1.0 / (1.0 + (0.3275911 * math.sqrt(0.5)) * jnp.abs(x))
    bell = jnp.exp2((x * x) * (-0.5 * math.log2(math.e)))
    poly = 0.5 * -1.453152027 + t * (0.5 * 1.061405429)
    for term in (0.5 * 1.421413741, 0.5 * -0.284496736, 0.5 * 0.254829592):
        poly = term + t * poly
    tail = (t * poly) * bell
    share = jnp.where(x >= 0.0, 1.0 - tail, tail)
    return x * share, share + x * (bell * (1.0 / math.sqrt(2.0 * math.pi)))


def unpack_all(own_ref, packed_ref, pack):
    pack[0] = own_ref[...]
    for share in range(1, pack.shape[0]):
        unpack(packed_ref, share - 1, pack.at[share])


def split_pack(pack):
    return pack.at[:, :D], pack.at[:, D : 2 * D], pack.at[:, 2 * D :]


def block_kernel(
    length_ref, x_ref, own_ref, packed_ref, small_ref, branch_ref, gain_ref, shift_ref, first_ref, other_ref,
    block_ref, n1_ref, r1_ref, n2_ref, r2_ref, act_ref, slope_ref, sums_ref, pack,
):
    shares = small_ref.shape[0]
    a_refs = [first_ref.at[0]] + [other_ref.at[s] for s in range(shares - 1)]
    tile = x_ref.shape[0]

    @pl.when(pl.program_id(0) == 0)
    def _():
        unpack_all(own_ref, packed_ref, pack)

    wide_ref, narrow_ref, out_ref = split_pack(pack)
    x = x_ref[...].astype(f32)
    mixing = branch_ref[0:1, :]
    for s in range(shares):
        mixing = mixing + dot(a_refs[s][:, :96], out_ref[s, :96, :])
    middle, normed, rstd = norm_forward(x + mixing, gain_ref[0:1, :], shift_ref[0:1, :])
    n1_ref[...] = normed
    r1_ref[...] = rstd
    low = middle.astype(bf16)
    branch = branch_ref[1:2, :]
    width = D
    for s in range(shares):
        value, slope = gelu_terms(dot(low, wide_ref[s]) + small_ref[s, 4:5, :].astype(f32))
        value = value.astype(bf16)
        act_ref[:, s * width : (s + 1) * width] = value
        slope_ref[:, s * width : (s + 1) * width] = slope.astype(bf16)
        branch = branch + dot(value, narrow_ref[s])
    block, normed, rstd = norm_forward(middle + branch, gain_ref[1:2, :], shift_ref[1:2, :])
    n2_ref[...] = normed
    r2_ref[...] = rstd
    block_ref[...] = block.astype(bf16)
    position = lax.broadcasted_iota(jnp.int32, (tile, 1), 0) + pl.program_id(0) * tile
    kept = jnp.where(position < own_number(length_ref), 1.0, 0.0)
    row = lax.broadcasted_iota(jnp.int32, (8, x.shape[1]), 0)
    total = jnp.zeros((8, x.shape[1]), f32)
    for index, part in enumerate((x, mixing, branch)):
        total = jnp.where(row == index, jnp.sum(kept * part * part, axis=0, keepdims=True), total)

    @pl.when(pl.program_id(0) == 0)
    def _():
        sums_ref[...] = jnp.zeros_like(sums_ref)

    sums_ref[...] += total


def by_tile(tile, width):
    return pl.BlockSpec((tile, width), lambda i: (i, 0))


def block_forward(length, x, attended, own, packed, small, branch_bias, gain, shift):
    rows, width = x.shape
    tile = min(256, rows)
    shares = small.shape[0]
    units = shares * D
    row, column = by_tile(tile, width), by_tile(tile, 1)
    return pl.pallas_call(
        block_kernel,
        grid=(rows // tile,),
        in_specs=[
            SMEM, row, whole(own.shape), whole(packed.shape), whole(small.shape), whole(branch_bias.shape), whole(gain.shape), whole(shift.shape),
        ] + [pl.BlockSpec((a.shape[0], tile, 128), lambda i: (0, i, 0)) for a in attended],
        out_specs=[row, row, column, row, column, by_tile(tile, units), by_tile(tile, units), whole((8, width))],
        out_shape=[
            jax.ShapeDtypeStruct((rows, width), bf16),
            jax.ShapeDtypeStruct((rows, width), f32),
            jax.ShapeDtypeStruct((rows, 1), f32),
            jax.ShapeDtypeStruct((rows, width), f32),
            jax.ShapeDtypeStruct((rows, 1), f32),
            jax.ShapeDtypeStruct((rows, units), bf16),
            jax.ShapeDtypeStruct((rows, units), bf16),
            jax.ShapeDtypeStruct((8, width), f32),
        ],
        scratch_shapes=[pltpu.VMEM((shares, 2 * D + 128, D), bf16)],
        compiler_params=pltpu.CompilerParams(vmem_limit_bytes=VMEM),
        cost_estimate=cost(20),
        name="block_forward",
    )(length, x, own, packed, small, branch_bias, gain, shift, *attended)


def block_backward_kernel(
    length_ref, d_ref, n1_ref, r1_ref, n2_ref, r2_ref, act_ref, slope_ref, own_ref, packed_ref, gain_ref,
    shift_ref, kl_ref, kl_row_ref, square_ref, six_own_ref, six_ref, first_ref, other_ref, *rest,
):
    step = pl.program_id(0)
    pack = rest[-1]
    shares = pack.shape[0]
    a_refs = [first_ref.at[0]] + [other_ref.at[s] for s in range(shares - 1)]
    sum_ref, da_refs = rest[0], rest[1 : shares + 1]
    g_ref, tail_ref, vec_ref, g_sum, low_s, branch_s, pre_s, mix_s = rest[shares + 1 : -1]
    tile, width = d_ref.shape
    units = D
    span = pl.ds(pl.multiple_of(step * tile, tile), tile)

    @pl.when(step == 0)
    def _():
        unpack_all(own_ref, packed_ref, pack)
        vec_ref[...] = jnp.zeros_like(vec_ref)
        g_sum[...] = jnp.zeros_like(g_sum)

    wide_ref, narrow_ref, out_ref = split_pack(pack)

    def column(value):
        return jnp.sum(value, axis=0, keepdims=True)

    row = lax.broadcasted_iota(jnp.int32, (8, width), 0)
    d_block = d_ref[...]
    normed_two = n2_ref[...]
    d_two = norm_backward(d_block, normed_two, r2_ref[...], gain_ref[1:2, :])
    d_branch = d_two.astype(bf16)
    branch_s[span, :] = d_branch
    normed_one = n1_ref[...]
    low = (normed_one * gain_ref[0:1, :] + shift_ref[0:1, :]).astype(bf16)
    low_s[span, :] = low
    d_middle = d_two
    for s in range(shares):
        grad = dot(d_branch, narrow_ref[s], NT) * slope_ref[:, s * units : (s + 1) * units].astype(f32)
        grad = grad.astype(bf16)
        pre_s[span, s * units : (s + 1) * units] = grad
        g_sum[s : s + 1, :] += column(grad.astype(f32))
        d_middle = d_middle + dot(grad, wide_ref[s], NT)
    d_one = norm_backward(d_middle, normed_one, r1_ref[...], gain_ref[0:1, :])
    sum_ref[...] = d_one
    d_mixing = d_one.astype(bf16)
    mix_s[span, :] = d_mixing
    for s in range(shares):
        da_refs[s][...] = wide_rows(dot(d_mixing, out_ref[s, :96, :], NT)).astype(bf16)
    parts = (
        d_mixing.astype(f32), d_branch.astype(f32), d_middle * normed_one, d_block * normed_two, d_middle, d_block,
    )
    total = jnp.zeros((8, width), f32)
    for index, part in enumerate(parts):
        total = jnp.where(row == index, column(part), total)
    vec_ref[...] += total

    @pl.when(step == pl.num_programs(0) - 1)
    def _():
        narrow = dot(act_ref[...], branch_s[...], TN).astype(bf16)
        wide = dot(low_s[...], pre_s[...], TN).astype(bf16)
        out = dot(jnp.concatenate([a[...] for a in a_refs], axis=1), mix_s[...], TN).astype(bf16)
        first = lax.broadcasted_iota(jnp.int32, (32, units), 0) == 0
        for s in range(shares):
            own = slice(s * width, (s + 1) * width)
            g_ref[0:units, own] = narrow[s * units : (s + 1) * units]
            g_ref[units : 2 * units, own] = wide[:, s * units : (s + 1) * units]
            g_ref[2 * units : 2 * units + 96, own] = out[s * 128 : s * 128 + 96]
            g_ref[2 * units + 128 :, own] = six_own_ref[0] if s == 0 else six_ref[s - 1]
            g_ref[2 * units + 96 : 2 * units + 128, own] = jnp.where(first, g_sum[s : s + 1, :], 0.0).astype(bf16)
        scalars = [jnp.sum(kl_ref[...], axis=0, keepdims=True) + jnp.sum(kl_row_ref[...], axis=1, keepdims=True)]
        scalars += [jnp.sum(square_ref[i : i + 1, :], axis=1, keepdims=True) for i in range(3)]
        scalars += [jnp.broadcast_to(own_number(length_ref).astype(f32), (1, 1))]
        lane = lanes((8, width))
        total = vec_ref[...]
        for index, value in enumerate(scalars):
            total = jnp.where((row == 6) & (lane == index), value, total)
        total = jnp.concatenate([jnp.zeros((2, width), f32), total, jnp.zeros((6, width), f32)], axis=0)
        high = total.astype(bf16).astype(f32)
        tail_ref[:16, :] = high.astype(bf16)
        tail_ref[16:, :] = (total - high).astype(bf16)


def block_backward(
    length, d_block, n1, r1, n2, r2, act, slope, attended, own, packed, gain, shift, divergence, squares, six_own, six,
):
    rows, width = d_block.shape
    tile = min(256, rows)
    shares, units = six.shape[0] + 1, D
    row, column = by_tile(tile, width), by_tile(tile, 1)
    return pl.pallas_call(
        block_backward_kernel,
        grid=(rows // tile,),
        in_specs=[
            SMEM, row, row, column, row, column, whole(act.shape), by_tile(tile, shares * units), whole(own.shape), whole(packed.shape), whole(gain.shape), whole(shift.shape),
            whole(divergence[0].shape), whole(divergence[1].shape), whole(squares.shape), whole(six_own.shape),
            whole(six.shape),
        ] + [whole(a.shape) for a in attended],
        out_specs=[
            row, *[by_tile(tile, 128)] * shares, whole((2 * units + 448, shares * width)), whole((32, width)),
        ],
        out_shape=[
            jax.ShapeDtypeStruct((rows, width), f32),
            *[jax.ShapeDtypeStruct((rows, 128), bf16)] * shares,
            jax.ShapeDtypeStruct((2 * units + 448, shares * width), bf16),
            jax.ShapeDtypeStruct((32, width), bf16),
        ],
        scratch_shapes=[
            pltpu.VMEM((8, width), f32),
            pltpu.VMEM((8, units), f32),
            pltpu.VMEM((rows, width), bf16),
            pltpu.VMEM((rows, width), bf16),
            pltpu.VMEM((rows, shares * units), bf16),
            pltpu.VMEM((rows, width), bf16),
            pltpu.VMEM((shares, 2 * D + 128, D), bf16),
        ],
        compiler_params=pltpu.CompilerParams(vmem_limit_bytes=VMEM),
        cost_estimate=cost(25),
        name="block_backward",
    )(
        length, d_block, n1, r1, n2, r2, act, slope, own, packed, gain, shift, *divergence, squares, six_own, six,
        *attended
    )


def after(value, *others):
    return lax.optimization_barrier((value,) + others)[0]


def shift_shares(value, by):
    shares = lax.axis_size("heads")
    return lax.ppermute(value, "heads", [((i + by) % shares, i) for i in range(shares)])


def exchange(value, bit):
    size = lax.axis_size("batch")
    return lax.ppermute(value, "batch", [(i, i ^ bit) for i in range(size)])


def rounded(total):
    end = total.shape[0] - 32
    sums = total[end : end + 16] + total[end + 16 :]
    high = lax.reduce_precision(sums, exponent_bits=8, mantissa_bits=7)
    return jnp.concatenate([total[:end], high, sums - high], axis=0).astype(bf16)


def finish_kernel(*refs, count):
    (
        rows_ref, grad_ref, bias_ref, branch_ref, gain_ref, shift_ref, summary_ref,
        narrow_ref, wide_ref, out_ref, wide_bias_ref, six_ref, six_bias_ref,
    ) = refs[count:]
    terms = [ref[...].astype(f32) for ref in refs[:count]]
    total = terms[0] + terms[1]
    if count == 4:
        total = total + (terms[2] + terms[3])
    end = total.shape[0] - 32
    sums = total[end : end + 16] + total[end + 16 :]
    grad_ref[...] = total[:end]
    bias_ref[...] = sums[0:2, :96]
    branch_ref[...] = sums[2:4]
    gain_ref[...] = sums[4:6]
    shift_ref[...] = sums[6:8]
    scalars = sums[8:9, :8]
    roots = jnp.sqrt(scalars / (scalars[:, 4:5] * D))
    summary_ref[...] = jnp.where(lanes((1, 8)) == 0, scalars, roots)[:, :4]
    units = narrow_ref.shape[0]
    narrow_ref[...] = rows_ref[:units, :].astype(f32)
    wide_ref[...] = rows_ref[units : 2 * units, :].astype(f32)
    out_ref[...] = rows_ref[2 * units : 2 * units + 96, :].astype(f32)
    wide_bias_ref[...] = rows_ref[2 * units + 96 : 2 * units + 112, :].astype(f32)[:1]
    six = 2 * units + 128
    six_ref[...] = rows_ref[six : six + 288, :].astype(f32)
    sums = rows_ref[six + 288 : six + 304, :].astype(f32) + rows_ref[six + 304 :, :].astype(f32)
    six_bias_ref[...] = sums[0:2, :96]


def finish(terms, rows):
    width = rows.shape[1]
    shapes = [(288, width), (2, 96), (2, width), (2, width), (2, width), (1, 4)]
    shapes += [(D, width), (D, width), (96, width), (1, width), (288, width), (2, 96)]
    return pl.pallas_call(
        functools.partial(finish_kernel, count=len(terms)),
        out_shape=[jax.ShapeDtypeStruct(s, f32) for s in shapes], cost_estimate=cost(1),
        name="finish", compiler_params=pltpu.CompilerParams(vmem_limit_bytes=VMEM),
    )(*terms, rows)


def body(
    student_rows, teacher_rows, valid_length, split_point, project_five, bias_five, output_five, branch_bias,
    norm_gain, norm_bias, widen_weight, widen_bias, narrow_weight, project_six, bias_six, teacher_project,
    teacher_bias,
):
    shares = lax.axis_size("heads")
    batch = lax.axis_size("batch")
    place = lax.axis_index("batch")
    all_rows = shares * batch * HEADS
    x = student_rows[0]
    teacher = teacher_rows[0]

    def turned(weight):
        return jnp.transpose(weight, (1, 2, 0)).reshape(-1, weight.shape[0])

    def placed(rows, at, count):
        return jnp.pad(rows, ((at, count - at - rows.shape[0]), (0, D - rows.shape[1])))

    biases = (bias_five, bias_six, widen_bias[None], teacher_bias)
    five = placed(turned(project_five), 0, 304)
    at = 288
    for bias in biases:
        five = five + placed(bias, at, 304)
        at += bias.shape[0]

    def part_of(rows):
        count = part_rows(rows.shape[0], batch)
        rows = jnp.pad(rows, ((0, count * batch - rows.shape[0]), (0, 0)))
        return lax.dynamic_slice_in_dim(rows, place * count, count)

    def others(rows):
        return [shift_shares(rows, by) for by in range(1, shares)]

    half = five.shape[0] // 2
    core = lax.rem(place, 2)
    mid = jnp.concatenate([widen_weight, narrow_weight, jnp.pad(output_five, ((0, 32), (0, 0)))], axis=0)
    taught = turned(teacher_project)
    rest = jnp.concatenate([turned(project_six), taught[:, :D], taught[:, D:]], axis=0)
    parts = others(jnp.concatenate([lax.dynamic_slice_in_dim(five, core * half, half), part_of(mid)], axis=0))

    first = attend_forward(valid_length, x, five[None])
    parts = jnp.stack([after(p, first[5]) for p in parts])
    halves, mid_parts = parts[:, :half], parts[:, half:]
    swapped = exchange(halves, 1)
    mid_all = lax.all_gather(mid_parts, "batch", axis=0)
    rest_parts = others(after(part_of(rest), mid_parts))
    low, high = jnp.where(core == 0, halves, swapped), jnp.where(core == 0, swapped, halves)
    fives = jnp.concatenate([low, high], axis=1)
    smalls = jnp.concatenate([five[None, 288:], fives[:, 288:]], axis=0)
    other = attend_forward(valid_length, after(x, mid_parts), fives)
    rest_parts = jnp.stack([after(p, other[5]) for p in rest_parts])
    rest_all = lax.all_gather(rest_parts, "batch", axis=0)
    attended = (first[5], other[5])
    block, n1, r1, n2, r2, act, slope, squares = block_forward(
        valid_length, after(x, rest_parts), attended, mid, mid_all, smalls, branch_bias, norm_gain, norm_bias
    )
    d_block, g_six_own, *divergence = relations(
        valid_length, split_point, block, teacher, rest, smalls[:1], all_rows
    )
    d_block, g_six, *divergence = relations(
        valid_length, split_point, block, teacher, rest_all, smalls[1:], all_rows, (d_block, *divergence)
    )
    result = block_backward(
        valid_length, d_block, n1, r1, n2, r2, act, slope, attended, mid, mid_all, norm_gain, norm_bias,
        divergence, squares, g_six_own, g_six,
    )
    d_sum_one, d_attended, (g_both, tail) = result[0], result[1 : 1 + shares], result[1 + shares :]

    def to_owner(parts):
        return [parts[0]] + [shift_shares(parts[by], shares - by) for by in range(1, shares)]

    units = widen_weight.shape[1]
    both = lax.psum_scatter(g_both, "batch", scatter_dimension=0, tiled=True)

    grad_in = d_sum_one
    g_five = [None] * shares
    for s in list(range(1, shares)) + [0]:
        q, k, v, e, r, a = other if s else first
        rows, w = after(x, *g_five[1 : shares - 1]) if s == 0 else x, fives if s else five[None]
        grad, grad_in = attend_backward(max(s - 1, 0), q, k, v, e, r, a, d_attended[s], rows, w, grad_in, tail)
        g_five[s] = shift_shares(grad, shares - s) if s else grad

    g_five = [g.astype(f32) for g in g_five]
    five_sum = rounded((g_five[0] + g_five[1]) + functools.reduce(jnp.add, g_five[2:]))
    both = after(both, five_sum)
    five_sum = after(five_sum, both)
    both = to_owner([both[:, s * D : (s + 1) * D] for s in range(shares)])
    bits = [1 << i for i in range(batch.bit_length() - 1)]
    groups = [bits[:1]] + [bits[i : i + 2] for i in range(1, len(bits), 2)]
    for index, group in enumerate(groups):
        received = [exchange(five_sum, bit) for bit in group]
        if len(group) == 2:
            received.append(exchange(five_sum, group[0] + group[1]))
        if index == 1:
            both = [after(p, five_sum) for p in both]
            both = sum(p.astype(f32) for p in both).astype(bf16)
        if index == len(groups) - 1:
            both = lax.all_gather(after(both, five_sum), "batch", axis=0, tiled=True)
            five_sum = after(five_sum, both)
        if index == len(groups) - 1:
            break
        total = five_sum.astype(f32) + received[0].astype(f32)
        if len(group) == 2:
            total = total + (received[1].astype(f32) + received[2].astype(f32))
        five_sum = rounded(total)
    (
        grad_five, five_bias, branch, gain, shift, summary, grad_narrow, grad_wide, grad_out, wide_bias, grad_six,
        six_bias,
    ) = finish([five_sum] + received, both)

    def unturned(grad):
        return jnp.transpose(grad.reshape(3, -1, grad.shape[1]), (2, 0, 1))

    return (
        block[None], grad_in[None], unturned(grad_five), five_bias, grad_out, branch, gain, shift,
        grad_wide, wide_bias.reshape(-1), grad_narrow, unturned(grad_six), six_bias, summary.reshape(-1),
    )


def solution(mesh):
    return jax.shard_map(
        body,
        mesh=mesh,
        in_specs=(
            P(("batch", "heads"), None, None),
            P(("batch", "heads"), None, None),
            P("batch"),
            P("batch"),
            P(None, None, "heads"),
            P(None, "heads"),
            P("heads", None),
            P(),
            P(),
            P(),
            P(None, "heads"),
            P("heads"),
            P("heads", None),
            P(None, None, "heads"),
            P(None, "heads"),
            P(None, None, "heads"),
            P(None, "heads"),
        ),
        out_specs=(
            P(("batch", "heads"), None, None),
            P(("batch", "heads"), None, None),
            P(None, None, "heads"),
            P(None, "heads"),
            P("heads", None),
            P(),
            P(),
            P(),
            P(None, "heads"),
            P("heads"),
            P("heads", None),
            P(None, None, "heads"),
            P(None, "heads"),
            P(),
        ),
        check_vma=False,
    )
```

```python
import functools
import math

import jax
import jax.numpy as jnp
from jax import lax
from jax.experimental import pallas as pl
from jax.experimental.pallas import tpu as pltpu
from jax.sharding import PartitionSpec as P

D = 384
HEADS = 12
HEAD_DIM = 32
TEACHER_HEAD_DIM = 64
PART = 3
TILE = 512
WIDE_TILE = 1024
STRIP = 16
NORM_EPS = 1e-12
MASKED = -1e30
SAFE = 64.0
LN2 = math.log(2.0)
STUDENT_SCALE = 1.0 / math.sqrt(HEAD_DIM)
STUDENT_LOG = math.log2(math.e) / math.sqrt(HEAD_DIM)
TEACHER_LOG = math.log2(math.e) / math.sqrt(TEACHER_HEAD_DIM)
VMEM = 56 * 2**20

f32 = jnp.float32
bf16 = jnp.bfloat16

NN = (((1,), (0,)), ((), ()))
NT = (((1,), (1,)), ((), ()))
TN = (((0,), (0,)), ((), ()))


def dot(left, right, dims=NN):
    return lax.dot_general(left, right, dims, preferred_element_type=f32)


def lanes(shape):
    return lax.broadcasted_iota(jnp.int32, shape, 1)


def wide_rows(rows):
    return jnp.concatenate([rows, jnp.zeros((rows.shape[0], 128 - rows.shape[1]), rows.dtype)], axis=1)


def in_head(lane, head, size=HEAD_DIM):
    return (lane >= head * size) & (lane < (head + 1) * size)


def split_terms(rows, head, size, extra):
    inside = in_head(lanes(rows.shape), head, size)
    high = rows.astype(bf16).astype(f32)
    first = jnp.where(inside, high, extra).astype(bf16)
    second = jnp.where(inside, rows - high, 0.0).astype(bf16)
    return jnp.concatenate([first, second], axis=1)


def own_number(ref):
    return ref[lax.axis_index("heads")]


def key_bias(rows, length):
    position = lax.broadcasted_iota(jnp.int32, (rows, 1), 0)
    return jnp.where(position < length, 0.0, MASKED)


def fold(tile, combine):
    total = tile[:, :128]
    for column in range(128, tile.shape[1], 128):
        total = combine(total, tile[:, column : column + 128])
    return total


def row_sum(tile):
    return jnp.sum(fold(tile, jnp.add), axis=1, keepdims=True)


def weave(first, second):
    done = 0
    for index, step in enumerate(second):
        while done < len(first) and done * len(second) < len(first) * (index + 1):
            first[done]()
            done += 1
        step()
    for step in first[done:]:
        step()


def step_place(step, tile, per_head):
    head = step // per_head
    return head, pl.ds(pl.multiple_of(lax.rem(step, per_head) * tile, tile), tile)


def skew(first, second):
    steps = [first[0]]
    for index in range(1, len(first)):
        steps += [first[index], second[index - 1]]
    return steps + [second[-1]]


def run_rolled(steps, logits, vector, back, reset=None, enter=None):
    def pair(index, carry):
        for slot in range(2):
            step = 2 * index + slot
            if enter is not None:
                enter(step, slot, index)
            ahead = logits(jnp.minimum(step + 1, steps - 1), 1 - slot)
            weave(ahead + back(jnp.maximum(step - 1, 0), 1 - slot), vector(step, slot))
            if slot == 0 and reset is not None:
                pl.when(index == 0)(reset)
        return carry

    for chunk in logits(jnp.int32(0), 0):
        chunk()
    lax.fori_loop(0, steps // 2, pair, 0)
    for chunk in back(jnp.int32(steps - 1), 1):
        chunk()


def run_pipeline(steps, logits, vector, back, enter=None):
    def stage(step, slot, before, after, second=False):
        if enter is not None:
            enter(step, slot, not before, second)
        ahead = logits(step + 1, 1 - slot) if after else []
        behind = back(step - 1, 1 - slot) if before else []
        weave(ahead + behind, vector(step, slot))

    for chunk in logits(jnp.int32(0), 0):
        chunk()
    if steps < 4:
        for step in range(steps):
            stage(jnp.int32(step), step % 2, step > 0, step + 1 < steps, second=step == 1)
        for chunk in back(jnp.int32(steps - 1), (steps - 1) % 2):
            chunk()
        return
    stage(jnp.int32(0), 0, False, True)
    stage(jnp.int32(1), 1, True, True, second=True)

    def pair(index, carry):
        stage(2 * index + 2, 0, True, True)
        stage(2 * index + 3, 1, True, True)
        return carry

    lax.fori_loop(0, (steps - 4) // 2, pair, 0)
    stage(jnp.int32(steps - 2), 0, True, True)
    stage(jnp.int32(steps - 1), 1, True, False)
    for chunk in back(jnp.int32(steps - 1), 1):
        chunk()


def project_part(x, w_ref, index, bias):
    flat = dot(x, w_ref[index * 96 : (index + 1) * 96, :], NT)
    if bias is not None:
        flat = flat + bias
    return wide_rows(flat).astype(bf16)


def attend_forward_kernel(
    length_ref, x_ref, w_ref, q_ref, k_ref, v_ref, e_hbm, r_ref, o_ref, lhs, rhs, mixer, zs0, zs1, es0, es1, sems
):
    share = pl.program_id(0)
    w_ref, q_ref, k_ref, v_ref, r_ref, o_ref = (t.at[0] for t in (w_ref, q_ref, k_ref, v_ref, r_ref, o_ref))
    zs, es = (zs0, zs1), (es0, es1)
    rows = x_ref.shape[0]
    tile = zs0.shape[0]
    per_head = rows // tile
    steps = PART * per_head
    x = x_ref[...]
    small = w_ref[288:304, :].astype(f32)
    q = project_part(x, w_ref, 0, small[0:1, :96])
    k = project_part(x, w_ref, 1, None)
    v = project_part(x, w_ref, 2, small[1:2, :96])
    q_ref[...] = q
    k_ref[...] = k
    v_ref[...] = v
    lane = lanes((rows, 128))
    one = jnp.where(lane == 96, 1.0, 0.0)
    for head in range(PART):
        lhs[head] = jnp.where(in_head(lane, head), q.astype(f32), one).astype(bf16)
    rhs[...] = jnp.where(lane == 96, key_bias(rows, own_number(length_ref)), k.astype(f32)).astype(bf16)
    mixer[...] = jnp.where(lane == 96, 1.0, v.astype(f32)).astype(bf16)
    o_ref[...] = jnp.zeros_like(o_ref)
    r_ref[...] = jnp.zeros_like(r_ref)

    def out_copy(step, slot):
        head, span = step_place(step, tile, per_head)
        return pltpu.make_async_copy(es[slot], e_hbm.at[share, head, span], sems.at[slot])

    def logits(step, slot):
        head, span = step_place(step, tile, per_head)

        def chunk(start):
            zs[slot][:, start : start + 256] = dot(lhs[head, span, :], rhs[start : start + 256, :], NT)

        return [functools.partial(chunk, start) for start in range(0, rows, 256)]

    def vector(step, slot):
        def strip(start):
            z = zs[slot][start : start + STRIP, :]
            highest = jnp.max(fold(z, jnp.maximum), axis=1, keepdims=True)
            es[slot][start : start + STRIP, :] = jnp.exp2((z - highest) * STUDENT_LOG).astype(bf16)

        return [functools.partial(strip, start) for start in range(0, tile, STRIP)]

    def back(step, slot):
        head, span = step_place(step, tile, per_head)

        sums = []

        def part(start):
            sums.append(dot(es[slot][:, start : start + 256], mixer[start : start + 256, :]))

        def mix():
            mixed = functools.reduce(jnp.add, sums)
            inverse = 1.0 / mixed[:, 96:97]
            inside = in_head(lanes(mixed.shape), head)
            o_ref[span, :] = jnp.where(inside, mixed * inverse, o_ref[span, :].astype(f32)).astype(bf16)
            r_ref[span, :] = jnp.where(inside, inverse, r_ref[span, :])

        return [functools.partial(part, start) for start in range(0, rows, 256)] + [mix]

    def enter(step, slot, first, second):
        if not first:
            out_copy(step - 1, 1 - slot).start()
        if not (first or second):
            out_copy(step - 2, slot).wait()

    run_pipeline(steps, logits, vector, back, enter)
    last = (steps - 1) % 2
    out_copy(jnp.int32(steps - 1), last).start()
    out_copy(jnp.int32(steps - 2), 1 - last).wait()
    out_copy(jnp.int32(steps - 1), last).wait()


def whole(shape):
    return pl.BlockSpec(shape, lambda *_: (0,) * len(shape))


SMEM = pl.BlockSpec(memory_space=pltpu.SMEM)
ANY = pl.BlockSpec(memory_space=pl.ANY)


def cost(micros):
    return pl.CostEstimate(flops=int(micros * 0.04e9), bytes_accessed=1024, transcendentals=0)


def attend_forward(length, x, w):
    rows, count = x.shape[0], w.shape[0]
    tile = min(WIDE_TILE, rows)
    narrow = jax.ShapeDtypeStruct((count, rows, 128), bf16)

    def share(shape):
        return pl.BlockSpec((1,) + shape, lambda s: (s,) + (0,) * len(shape))

    row = share((rows, 128))
    return pl.pallas_call(
        attend_forward_kernel,
        grid=(count,),
        in_specs=[SMEM, whole(x.shape), share(w.shape[1:])],
        out_specs=[row] * 3 + [ANY] + [row] * 2,
        out_shape=[
            narrow, narrow, narrow, jax.ShapeDtypeStruct((count, PART, rows, rows), bf16),
            jax.ShapeDtypeStruct((count, rows, 128), f32), narrow,
        ],
        scratch_shapes=[
            pltpu.VMEM((PART, rows, 128), bf16),
            pltpu.VMEM((rows, 128), bf16),
            pltpu.VMEM((rows, 128), bf16),
            pltpu.VMEM((tile, rows), f32),
            pltpu.VMEM((tile, rows), f32),
            pltpu.VMEM((tile, rows), bf16),
            pltpu.VMEM((tile, rows), bf16),
            pltpu.SemaphoreType.DMA((2,)),
        ],
        compiler_params=pltpu.CompilerParams(vmem_limit_bytes=VMEM),
        cost_estimate=cost(9 * count),
        name="attend_forward",
    )(length, x, w)


def attend_backward_kernel(
    q_ref, k_ref, v_ref, e_hbm, r_ref, a_ref, d_ref, x_hbm, w_hbm, acc_hbm, tail_ref, g_ref, in_ref,
    lhs, rhs, keys, qt, dt, zs0, zs1, gs0, gs1, dq, dkt, dvt, e_all, x_ref, w_ref, acc_ref, sems, late, *, share,
):
    q_ref, k_ref, v_ref, r_ref, a_ref = (t.at[0] for t in (q_ref, k_ref, v_ref, r_ref, a_ref))
    rows = q_ref.shape[0]
    zs, gs = (zs0, zs1), (gs0, gs1)
    tile = zs0.shape[0]
    per_head = rows // tile
    steps = PART * per_head

    def in_copy(step):
        head, span = step_place(step, tile, per_head)
        return pltpu.make_async_copy(e_hbm.at[share, head, span], e_all.at[head, span], sems.at[step])

    for step in range(2):
        in_copy(jnp.int32(step)).start()
    late_copies = [
        pltpu.make_async_copy(source, target, late.at[index])
        for index, (source, target) in enumerate(((x_hbm, x_ref), (w_hbm.at[share], w_ref), (acc_hbm, acc_ref)))
    ]

    def enter(step, slot, first, second):
        if second:
            for copy in late_copies:
                copy.start()

        @pl.when(step + 2 < steps)
        def _():
            in_copy(step + 2).start()

        in_copy(step).wait()

    lane = lanes((rows, 128))
    grads = r_ref[...] * d_ref[...].astype(f32)
    shifts = grads * a_ref[...].astype(f32)
    k = k_ref[...].astype(f32)
    def one_head(head, carry):
        inside = in_head(lane, head)
        shift = -jnp.sum(jnp.where(inside, shifts, 0.0), axis=1, keepdims=True)
        high = shift.astype(bf16).astype(f32)
        lhs[head] = split_terms(
            grads, head, HEAD_DIM, jnp.where(lane == 96, high, jnp.where(lane == 97, shift - high, 0.0))
        )
        keys[head] = jnp.where(inside, k, 0.0).astype(bf16)
        return carry

    lax.fori_loop(0, PART, one_head, 0)
    rhs[:, :128] = jnp.where((lane == 96) | (lane == 97), 1.0, v_ref[...].astype(f32)).astype(bf16)
    rhs[:, 128:] = v_ref[...]
    qt[...] = q_ref[...].T
    dt[...] = grads.astype(bf16).T

    def reset():
        dq[...] = jnp.zeros_like(dq)
        dkt[...] = jnp.zeros_like(dkt)
        dvt[...] = jnp.zeros_like(dvt)

    reset()

    def logits(step, slot):
        head, span = step_place(step, tile, per_head)

        def chunk(start):
            zs[slot][:, start : start + 256] = dot(lhs[head, span, :], rhs[start : start + 256, :], NT)

        return [functools.partial(chunk, start) for start in range(0, rows, 256)]

    def vector(step, slot):
        head, span = step_place(step, tile, per_head)
        base = lax.rem(step, per_head) * tile

        def strip(start):
            here = pl.ds(pl.multiple_of(base + start, STRIP), STRIP)
            weights = e_all[head, here, :].astype(f32)
            gs[slot][start : start + STRIP, :] = (weights * zs[slot][start : start + STRIP, :]).astype(bf16)

        return [functools.partial(strip, start) for start in range(0, tile, STRIP)]

    def back(step, slot):
        head, span = step_place(step, tile, per_head)
        own = pl.ds(pl.multiple_of(head * HEAD_DIM, HEAD_DIM), HEAD_DIM)

        def first():
            dq[span, :] += dot(gs[slot][...], keys[head])

        def second(start):
            part = slice(start, start + 256)
            dkt[own, part] += dot(qt[own, span], gs[slot][:, part])

        def third(start):
            part = slice(start, start + 256)
            dvt[own, part] += dot(dt[own, span], e_all[head, span, part])

        starts = range(0, rows, 256)
        return [first] + [functools.partial(second, s) for s in starts] + [functools.partial(third, s) for s in starts]

    run_pipeline(steps, logits, vector, back, enter)
    for copy in late_copies:
        copy.wait()
    grads = (
        (dq[...] * STUDENT_SCALE).astype(bf16),
        (dkt[...] * STUDENT_SCALE).T.astype(bf16),
        dvt[...].T.astype(bf16),
    )
    weight_grads(grads, x_ref[...], g_ref, tail_ref[:16, :].astype(f32), tail_ref[16:, :].astype(f32))
    in_ref[...] = acc_ref[...] + spread(grads, w_ref)


def weight_grads(grads, x, g_ref, tail_high=0.0, tail_low=0.0):
    for index, grad in enumerate(grads):
        g_ref[index * 96 : (index + 1) * 96, :] = dot(grad, x, TN)[:96].astype(bf16)
    ones = jnp.ones((16, x.shape[0]), bf16)
    row = lax.broadcasted_iota(jnp.int32, (16, 128), 0)
    sums = jnp.where(row == 0, dot(ones, grads[0]), jnp.where(row == 1, dot(ones, grads[2]), 0.0))
    sums = jnp.concatenate([sums, jnp.zeros((16, x.shape[1] - 128), f32)], axis=1) + tail_high
    high = sums.astype(bf16).astype(f32)
    g_ref[288:304, :] = high.astype(bf16)
    g_ref[304:320, :] = (sums - high + tail_low).astype(bf16)


def spread(grads, w_ref):
    total = None
    for index, grad in enumerate(grads):
        term = dot(grad[:, :96], w_ref[index * 96 : (index + 1) * 96, :])
        total = term if total is None else total + term
    return total


def attend_backward(share, q, k, v, e, r, attended, d_attended, x, w, grad_in, tail):
    rows = x.shape[0]
    tile = min(TILE, rows // 2)
    row = pl.BlockSpec((1, rows, 128), lambda i: (share, 0, 0))
    return pl.pallas_call(
        functools.partial(attend_backward_kernel, share=share),
        grid=(1,),
        in_specs=[row, row, row, ANY, row, row, whole((rows, 128)), ANY, ANY, ANY, whole(tail.shape)],
        out_specs=[whole((320, x.shape[1])), whole(x.shape)],
        out_shape=[jax.ShapeDtypeStruct((320, x.shape[1]), bf16), jax.ShapeDtypeStruct(x.shape, f32)],
        scratch_shapes=[
            pltpu.VMEM((PART, rows, 256), bf16),
            pltpu.VMEM((rows, 256), bf16),
            pltpu.VMEM((PART, rows, 128), bf16),
            pltpu.VMEM((128, rows), bf16),
            pltpu.VMEM((128, rows), bf16),
            pltpu.VMEM((tile, rows), f32),
            pltpu.VMEM((tile, rows), f32),
            pltpu.VMEM((tile, rows), bf16),
            pltpu.VMEM((tile, rows), bf16),
            pltpu.VMEM((rows, 128), f32),
            pltpu.VMEM((128, rows), f32),
            pltpu.VMEM((128, rows), f32),
            pltpu.VMEM((PART, rows, rows), bf16),
            pltpu.VMEM(x.shape, bf16),
            pltpu.VMEM(w.shape[1:], bf16),
            pltpu.VMEM(x.shape, f32),
            pltpu.SemaphoreType.DMA((PART * (rows // tile),)),
            pltpu.SemaphoreType.DMA((3,)),
        ],
        compiler_params=pltpu.CompilerParams(vmem_limit_bytes=VMEM),
        cost_estimate=cost(10),
        name="attend_backward",
    )(q, k, v, e, r, attended, d_attended, x, w, grad_in, tail)


def relation_kernel(
    length_ref, split_ref, block_ref, teacher_ref, packed_ref, small_ref, *rest, all_rows, gathered,
):
    before = None
    if gathered:
        before, rest = rest[:3], rest[3:]
    (
    d_ref, g_ref, kl_ref, kl_row_ref, pack, lefts, rights, t_lefts, t_rights, ls, rs, lt, rt, keys, left_t, zs0, zs1, zt0, zt1, gs0, gs1,
    left_sum, right_t, es_all, et_all, parts, columns, factors, rows_s, weight, weight_row, grads_s,
    ) = rest
    rows = block_ref.shape[0]
    tile = zs0.shape[0]
    per_head = rows // tile
    steps = PART * per_head
    zs, zt, gs = (zs0, zs1), (zt0, zt1), (gs0.at[:tile], gs1)
    length, split = own_number(length_ref), own_number(split_ref)

    @pl.when(pl.program_id(0) == 0)
    def _():
        position = lax.broadcasted_iota(jnp.int32, (rows, 1), 0)
        counted = (position < length) & (position != 0) & (position != split - 1) & (position != length - 1)
        share = 1.0 / ((length - 3).astype(f32) * float(all_rows))
        weight[...] = jnp.where(counted, share, 0.0)
        position = lanes((1, rows))
        counted = (position < length) & (position != 0) & (position != split - 1) & (position != length - 1)
        weight_row[...] = jnp.where(counted, share, 0.0)
        for index, ref in enumerate((d_ref, kl_ref, kl_row_ref)):
            ref[...] = before[index][...] if gathered else jnp.zeros_like(ref)

    if gathered:
        unpack(packed_ref, 0, pack)
    else:
        pack[...] = packed_ref[...]

    g_ref = g_ref.at[0]
    small = small_ref[0].astype(f32)

    def head_mask(size):
        shift = size.bit_length() - 1
        same = (lax.broadcasted_iota(jnp.int32, (128, 128), 0) >> shift) == (lanes((128, 128)) >> shift)
        return jnp.where(same, 1.0, 0.0).astype(bf16)

    masks = {size: head_mask(size) for size in (HEAD_DIM, TEACHER_HEAD_DIM)}

    def largest(low, size):
        square = low.astype(f32)
        return jnp.max(dot((square * square).astype(bf16), masks[size]), axis=0, keepdims=True)

    def project(index, carry):
        here = pl.ds(pl.multiple_of(index * tile, tile), tile)
        block, teacher = block_ref[here, :], teacher_ref[here, :]

        def student(part, b):
            flat = dot(block, pack[part * 96 : (part + 1) * 96, :], NT)
            return wide_rows(flat if b is None else flat + b).astype(bf16)

        def taught(part, b):
            start = 288 + part * 192
            flat = dot(teacher[:, :D], pack[start : start + 192, :], NT)
            flat = flat + dot(teacher[:, D:], pack[start + 576 : start + 768, :], NT)
            flat = (flat if b is None else flat + b).astype(bf16)
            return flat[:, :128], wide_rows(flat[:, 128:])

        q, k, v = student(0, small[2:3, :96]), student(1, None), student(2, small[3:4, :96])
        lefts[0, here, :] = q
        rights[0, here, :] = k
        lefts[1, here, :] = v
        rights[1, here, :] = v
        tq, tk, tv = taught(0, small[5:6, :192]), taught(1, None), taught(2, small[6:7, :192])
        for half in range(2):
            t_lefts[0, half, here, :] = tq[half]
            t_rights[0, half, here, :] = tk[half]
            t_lefts[1, half, here, :] = tv[half]
            t_rights[1, half, here, :] = tv[half]
        found = [largest(value, HEAD_DIM) for value in (q, k, v)]
        found += [largest(value, TEACHER_HEAD_DIM) for value in tq + tk + tv]
        return tuple(jnp.maximum(old, new) for old, new in zip(carry, found))

    top = lax.fori_loop(0, rows // tile, project, (jnp.zeros((1, 128), f32),) * 9)
    bounds = []
    for s_left, s_right, t_left, t_right in ((0, 1, 3, 5), (2, 2, 7, 7)):
        bound = jnp.max(top[s_left] * top[s_right]) * STUDENT_LOG**2
        for half in range(2):
            bound = jnp.maximum(bound, jnp.max(top[t_left + half] * top[t_right + half]) * TEACHER_LOG**2)
        bounds.append(bound)

    def operands(relation, student_scale, teacher_scale, row_bias, everything):
        band = min(128, rows)
        line = lanes((1, 128))

        def terms(value, inside, extra):
            high, low = value
            return jnp.where(inside, high, extra).astype(bf16), jnp.where(inside, low, 0.0).astype(bf16)

        def halves(value, scale):
            value = value * scale
            high = value.astype(bf16).astype(f32)
            return high, value - high

        def one_band(index, carry):
            here = pl.ds(pl.multiple_of(index * band, band), band)
            position = lax.broadcasted_iota(jnp.int32, (band, 128), 0) + index * band
            bias = jnp.where(position < length, 0.0, MASKED)
            row = jnp.where(row_bias, bias, 0.0)
            left, right = lefts[relation, here, :].astype(f32), rights[relation, here, :].astype(f32)
            value = halves(left, student_scale)
            extra = jnp.where(line == 97, row, jnp.where(line == 96, 1.0, 0.0))
            if everything:
                rs[here, :128] = jnp.where(line == 97, 1.0, jnp.where(line == 96, bias, right)).astype(bf16)
                rs[here, 128:] = rights[relation, here, :]
            for head in range(PART):
                inside = in_head(line, head)
                ls[head, here, :128], ls[head, here, 128:] = terms(value, inside, extra)
                if everything:
                    keys[head, here, :] = jnp.where(inside, right, 0.0).astype(bf16)
            for half in range(2):
                t_left = t_lefts[relation, half, here, :].astype(f32)
                t_right = t_rights[relation, half, here, :].astype(f32)
                value = halves(t_left, teacher_scale)
                for head in range(2 * half, min(2 * half + 2, PART)):
                    own = head % 2
                    spare = (1 - own) * TEACHER_HEAD_DIM
                    extra = jnp.where(line == spare + 1, row, jnp.where(line == spare, 1.0, 0.0))
                    inside = in_head(line, own, TEACHER_HEAD_DIM)
                    lt[head, here, :128], lt[head, here, 128:] = terms(value, inside, extra)
                    if everything:
                        first = jnp.where(line == spare + 1, 1.0, jnp.where(line == spare, bias, t_right))
                        rt[head, here, :128] = first.astype(bf16)
                        rt[head, here, 128:] = t_rights[relation, half, here, :]
            return carry

        lax.fori_loop(0, rows // band, one_band, 0)

    def relate(relation, carry):
        symmetric = relation == 1
        left_t[...] = lefts[relation].T
        operands(relation, STUDENT_LOG, TEACHER_LOG, symmetric, True)
        near = jnp.where(symmetric, bounds[1], bounds[0]) < SAFE * SAFE
        reset()

        @pl.when(near & jnp.logical_not(symmetric))
        def _():
            run_pipeline(steps, logits, vector, grad_products)

        @pl.when(near & symmetric)
        def _():
            lax.fori_loop(0, PART, symmetric_head, 0)

        @pl.when(jnp.logical_not(near))
        def _():
            operands(relation, 1.0, 1.0, False, False)
            lax.fori_loop(0, steps, shifted_step, 0)

        @pl.when(jnp.logical_not(symmetric))
        def _():
            grads_s[0] = (left_sum[...] * STUDENT_SCALE).astype(bf16)
            grads_s[1] = (right_t[...] * STUDENT_SCALE).T.astype(bf16)

        @pl.when(symmetric)
        def _():
            grads_s[2] = ((left_sum[...] + right_t[...].T) * STUDENT_SCALE).astype(bf16)

        return carry

    def reset():
        left_sum[...] = jnp.zeros_like(left_sum)
        right_t[...] = jnp.zeros_like(right_t)

    def logits(step, slot):
        head, span = step_place(step, tile, per_head)

        def student(start):
            zs[slot][:, start : start + 256] = dot(ls[head, span, :], rs[start : start + 256, :], NT)

        def taught(start):
            zt[slot][:, start : start + 256] = dot(lt[head, span, :], rt[head, start : start + 256, :], NT)

        chunks = []
        for start in range(0, rows, 256):
            chunks += [functools.partial(student, start), functools.partial(taught, start)]
        return chunks

    def vector(step, slot):
        base = lax.rem(step, per_head) * tile
        z, t, g = zs[slot], zt[slot], gs[slot]
        scales = {}

        def both(start):
            strip = slice(start, start + STRIP)
            student, taught = z[strip, :], t[strip, :]
            es, et = jnp.exp2(student), jnp.exp2(taught)
            sum_s, sum_t, cross = row_sum(es), row_sum(et), row_sum(et * (taught - student))
            here = pl.ds(pl.multiple_of(base + start, STRIP), STRIP)
            w = weight[here, :]
            inverse = 1.0 / sum_t
            kl_ref[here, :] += w * (LN2 * cross * inverse + jnp.log(sum_s) - jnp.log(sum_t))
            g[strip, :] = (es * (w / sum_s) - et * (w * inverse)).astype(bf16)

        return [functools.partial(both, s) for s in range(0, tile, STRIP)]

    def grad_products(step, slot):
        head, span = step_place(step, tile, per_head)
        own = pl.ds(pl.multiple_of(head * HEAD_DIM, HEAD_DIM), HEAD_DIM)

        def first():
            left_sum[span, :] += dot(gs[slot][...], keys[head])

        def second(start):
            part = slice(start, start + 256)
            right_t[own, part] += dot(left_t[own, span], gs[slot][:, part])

        return [first] + [functools.partial(second, start) for start in range(0, rows, 256)]

    def shifted_step(step, carry):
        head, span = step_place(step, tile, per_head)
        student = dot(ls[head, span, :], rs[...], NT)
        zs0[...] = (student - jnp.max(student, axis=1, keepdims=True)) * STUDENT_LOG
        taught = dot(lt[head, span, :], rt[head], NT)
        zt0[...] = (taught - jnp.max(taught, axis=1, keepdims=True)) * TEACHER_LOG

        def strip(index, carry):
            here = pl.ds(pl.multiple_of(index * STRIP, STRIP), STRIP)
            student, taught = zs0[here, :], zt0[here, :]
            es, et = jnp.exp2(student), jnp.exp2(taught)
            sum_s, sum_t = row_sum(es), row_sum(et)
            cross = row_sum(et * (taught - student))
            there = pl.ds(pl.multiple_of(lax.rem(step, per_head) * tile + index * STRIP, STRIP), STRIP)
            w = weight[there, :]
            row = LN2 * cross / sum_t + jnp.log(sum_s) - jnp.log(sum_t)
            kl_ref[there, :] += jnp.where(w > 0.0, w * row, 0.0)
            gs0[here, :] = (es * (w / sum_s) - et * (w / sum_t)).astype(bf16)
            return carry

        lax.fori_loop(0, tile // STRIP, strip, 0)
        for chunk in grad_products(step, 0):
            chunk()
        return carry

    def symmetric_head(head, carry):
        size, band = min(256, rows), 32
        count = rows // size
        own = pl.ds(pl.multiple_of(head * HEAD_DIM, HEAD_DIM), HEAD_DIM)
        columns[...] = jnp.zeros_like(columns)

        def logit_chunks(i):
            here = slice(i * size, (i + 1) * size)

            def student(part):
                es_all[here, part] = dot(ls[head, here, :], rs[part, :], NT)

            def taught(part):
                et_all[here, part] = dot(lt[head, here, :], rt[head, part, :], NT)

            chunks = []
            for j in range(i, count):
                part = slice(j * size, (j + 1) * size)
                chunks += [functools.partial(student, part), functools.partial(taught, part)]
            return chunks

        def weigh(i, start):
            strip = slice(start, start + band)
            totals = [0.0, 0.0, 0.0]
            for column in range(i * size, rows, 128):
                part = slice(column, column + 128)
                student, taught = es_all[strip, part], et_all[strip, part]
                es, et = jnp.exp2(student), jnp.exp2(taught)
                es_all[strip, part] = es
                et_all[strip, part] = et
                for index, value in enumerate((es, et, et * (taught - student))):
                    totals[index] = totals[index] + value
                    if column >= (i + 1) * size:
                        eight = value[:8]
                        for line in range(8, band, 8):
                            eight = eight + value[line : line + 8]
                        columns[index, :, part] += eight
            for index in range(3):
                parts[index, strip, :] = totals[index]

        def combine(i, start):
            strip = slice(start, start + STRIP)
            a, b = factors[0, strip, :], factors[1, strip, :]
            for column in range(i * size, rows, 128):
                part = slice(column, column + 128)
                both = es_all[strip, part] * (a + rows_s[0, :, part])
                both = both - et_all[strip, part] * (b + rows_s[1, :, part])
                gs0[strip, part] = both.astype(bf16)

        def products(i):
            here = slice(i * size, (i + 1) * size)

            def first(j):
                part = slice(j * size, (j + 1) * size)
                left_sum[here, :] += dot(gs_all[here, part], keys[head, part, :])

            def second(j):
                part = slice(j * size, (j + 1) * size)
                right_t[own, part] += dot(left_t[own, here], gs_all[here, part])

            chunks = [functools.partial(first, j) for j in range(i, count)]
            return chunks + [functools.partial(second, j) for j in range(i + 1, count)]

        gs_all = gs0
        for chunk in logit_chunks(0):
            chunk()
        for i in range(count):
            ahead = logit_chunks(i + 1) if i + 1 < count else []
            weave(ahead, [functools.partial(weigh, i, s) for s in range(i * size, (i + 1) * size, band)])
        sums = [
            jnp.sum(parts[index].T, axis=0, keepdims=True) + jnp.sum(columns[index], axis=0, keepdims=True)
            for index in range(3)
        ]
        w = weight_row[...]
        sum_s, sum_t = (jnp.where(w > 0.0, value, 1.0) for value in sums[:2])
        inverse = 1.0 / sum_t
        kl_row_ref[...] += w * (LN2 * sums[2] * inverse + jnp.log(sum_s) - jnp.log(sum_t))
        for index, value in enumerate((w / sum_s, w * inverse)):
            factors[index] = jnp.broadcast_to(value, (128, rows)).T
            rows_s[index] = jnp.broadcast_to(value, (STRIP, rows))
        for i in range(count):
            behind = products(i - 1) if i else []
            weave(behind, [functools.partial(combine, i, s) for s in range(i * size, (i + 1) * size, STRIP)])
        for chunk in products(count - 1):
            chunk()
        return carry

    lax.fori_loop(0, 2, relate, 0)
    grads = tuple(grads_s[i] for i in range(3))
    weight_grads(grads, block_ref[...], g_ref)
    d_ref[...] += spread(grads, pack)


def part_rows(rows, batch):
    return -(-rows // (16 * batch)) * 16


def unpack(packed_ref, share, target):
    rows, batch = target.shape[0], packed_ref.shape[0]
    part = part_rows(rows, batch)
    for start in range(0, rows, part):
        size = min(part, rows - start)
        target[start : start + size, :] = packed_ref[start // part, share, :size, :]


def relations(length, split, block, teacher, packed, small, all_rows, before=()):
    rows = block.shape[0]
    tile = min(TILE, rows // 2)
    shares = small.shape[0]

    def share(shape):
        return pl.BlockSpec((1,) + shape[1:], lambda s: (s,) + (0,) * (len(shape) - 1))

    gathered = len(before) > 0
    if gathered:
        place = pl.BlockSpec((packed.shape[0], 1) + packed.shape[2:], lambda s: (0, s, 0, 0))
    else:
        place = whole(packed.shape)
    return pl.pallas_call(
        functools.partial(relation_kernel, all_rows=all_rows, gathered=gathered),
        grid=(shares,),
        in_specs=[
            SMEM, SMEM, whole(block.shape), whole(teacher.shape), place, share(small.shape),
        ] + [whole(b.shape) for b in before],
        out_specs=[whole(block.shape), share((shares, 320, D)), whole((rows, 1)), whole((1, rows))],
        out_shape=[
            jax.ShapeDtypeStruct(block.shape, f32),
            jax.ShapeDtypeStruct((shares, 320, D), bf16),
            jax.ShapeDtypeStruct((rows, 1), f32),
            jax.ShapeDtypeStruct((1, rows), f32),
        ],
        scratch_shapes=[
            pltpu.VMEM((1440, D), bf16),
            pltpu.VMEM((2, rows, 128), bf16),
            pltpu.VMEM((2, rows, 128), bf16),
            pltpu.VMEM((2, 2, rows, 128), bf16),
            pltpu.VMEM((2, 2, rows, 128), bf16),
            pltpu.VMEM((PART, rows, 256), bf16),
            pltpu.VMEM((rows, 256), bf16),
            pltpu.VMEM((PART, rows, 256), bf16),
            pltpu.VMEM((PART, rows, 256), bf16),
            pltpu.VMEM((PART, rows, 128), bf16),
            pltpu.VMEM((128, rows), bf16),
            pltpu.VMEM((tile, rows), f32),
            pltpu.VMEM((tile, rows), f32),
            pltpu.VMEM((tile, rows), f32),
            pltpu.VMEM((tile, rows), f32),
            pltpu.VMEM((rows, rows), bf16),
            pltpu.VMEM((tile, rows), bf16),
            pltpu.VMEM((rows, 128), f32),
            pltpu.VMEM((128, rows), f32),
            pltpu.VMEM((rows, rows), f32),
            pltpu.VMEM((rows, rows), f32),
            pltpu.VMEM((3, rows, 128), f32),
            pltpu.VMEM((3, 8, rows), f32),
            pltpu.VMEM((2, rows, 128), f32),
            pltpu.VMEM((2, STRIP, rows), f32),
            pltpu.VMEM((rows, 1), f32),
            pltpu.VMEM((1, rows), f32),
            pltpu.VMEM((3, rows, 128), bf16),
        ],
        compiler_params=pltpu.CompilerParams(vmem_limit_bytes=VMEM),
        cost_estimate=cost(30 * shares),
        name="relations",
    )(length, split, block, teacher, packed, small, *before)


def norm_forward(rows, gain, shift):
    center = jnp.mean(rows, axis=1, keepdims=True)
    offsets = rows - center
    rstd = lax.rsqrt(jnp.mean(offsets * offsets, axis=1, keepdims=True) + NORM_EPS)
    normed = offsets * rstd
    return normed * gain + shift, normed, rstd


def norm_backward(grad, normed, rstd, gain):
    inner = grad * gain
    mean = jnp.mean(inner, axis=1, keepdims=True)
    slope = jnp.mean(inner * normed, axis=1, keepdims=True)
    return rstd * (inner - mean - normed * slope)


def gelu_terms(x):
    t = 1.0 / (1.0 + (0.3275911 * math.sqrt(0.5)) * jnp.abs(x))
    bell = jnp.exp2((x * x) * (-0.5 * math.log2(math.e)))
    poly = 0.5 * -1.453152027 + t * (0.5 * 1.061405429)
    for term in (0.5 * 1.421413741, 0.5 * -0.284496736, 0.5 * 0.254829592):
        poly = term + t * poly
    tail = (t * poly) * bell
    share = jnp.where(x >= 0.0, 1.0 - tail, tail)
    return x * share, share + x * (bell * (1.0 / math.sqrt(2.0 * math.pi)))


def unpack_all(own_ref, packed_ref, pack):
    pack[0] = own_ref[...]
    for share in range(1, pack.shape[0]):
        unpack(packed_ref, share - 1, pack.at[share])


def split_pack(pack):
    return pack.at[:, :D], pack.at[:, D : 2 * D], pack.at[:, 2 * D :]


def block_kernel(
    length_ref, x_ref, own_ref, packed_ref, small_ref, branch_ref, gain_ref, shift_ref, first_ref, other_ref,
    block_ref, n1_ref, r1_ref, n2_ref, r2_ref, act_ref, slope_ref, sums_ref, pack,
):
    shares = small_ref.shape[0]
    a_refs = [first_ref.at[0]] + [other_ref.at[s] for s in range(shares - 1)]
    tile = x_ref.shape[0]

    @pl.when(pl.program_id(0) == 0)
    def _():
        unpack_all(own_ref, packed_ref, pack)

    wide_ref, narrow_ref, out_ref = split_pack(pack)
    x = x_ref[...].astype(f32)
    mixing = branch_ref[0:1, :]
    for s in range(shares):
        mixing = mixing + dot(a_refs[s][:, :96], out_ref[s, :96, :])
    middle, normed, rstd = norm_forward(x + mixing, gain_ref[0:1, :], shift_ref[0:1, :])
    n1_ref[...] = normed
    r1_ref[...] = rstd
    low = middle.astype(bf16)
    branch = branch_ref[1:2, :]
    width = D
    for s in range(shares):
        value, slope = gelu_terms(dot(low, wide_ref[s]) + small_ref[s, 4:5, :].astype(f32))
        value = value.astype(bf16)
        act_ref[:, s * width : (s + 1) * width] = value
        slope_ref[:, s * width : (s + 1) * width] = slope.astype(bf16)
        branch = branch + dot(value, narrow_ref[s])
    block, normed, rstd = norm_forward(middle + branch, gain_ref[1:2, :], shift_ref[1:2, :])
    n2_ref[...] = normed
    r2_ref[...] = rstd
    block_ref[...] = block.astype(bf16)
    position = lax.broadcasted_iota(jnp.int32, (tile, 1), 0) + pl.program_id(0) * tile
    kept = jnp.where(position < own_number(length_ref), 1.0, 0.0)
    row = lax.broadcasted_iota(jnp.int32, (8, x.shape[1]), 0)
    total = jnp.zeros((8, x.shape[1]), f32)
    for index, part in enumerate((x, mixing, branch)):
        total = jnp.where(row == index, jnp.sum(kept * part * part, axis=0, keepdims=True), total)

    @pl.when(pl.program_id(0) == 0)
    def _():
        sums_ref[...] = jnp.zeros_like(sums_ref)

    sums_ref[...] += total


def by_tile(tile, width):
    return pl.BlockSpec((tile, width), lambda i: (i, 0))


def block_forward(length, x, attended, own, packed, small, branch_bias, gain, shift):
    rows, width = x.shape
    tile = min(256, rows)
    shares = small.shape[0]
    units = shares * D
    row, column = by_tile(tile, width), by_tile(tile, 1)
    return pl.pallas_call(
        block_kernel,
        grid=(rows // tile,),
        in_specs=[
            SMEM, row, whole(own.shape), whole(packed.shape), whole(small.shape), whole(branch_bias.shape), whole(gain.shape), whole(shift.shape),
        ] + [pl.BlockSpec((a.shape[0], tile, 128), lambda i: (0, i, 0)) for a in attended],
        out_specs=[row, row, column, row, column, by_tile(tile, units), by_tile(tile, units), whole((8, width))],
        out_shape=[
            jax.ShapeDtypeStruct((rows, width), bf16),
            jax.ShapeDtypeStruct((rows, width), f32),
            jax.ShapeDtypeStruct((rows, 1), f32),
            jax.ShapeDtypeStruct((rows, width), f32),
            jax.ShapeDtypeStruct((rows, 1), f32),
            jax.ShapeDtypeStruct((rows, units), bf16),
            jax.ShapeDtypeStruct((rows, units), bf16),
            jax.ShapeDtypeStruct((8, width), f32),
        ],
        scratch_shapes=[pltpu.VMEM((shares, 2 * D + 128, D), bf16)],
        compiler_params=pltpu.CompilerParams(vmem_limit_bytes=VMEM),
        cost_estimate=cost(20),
        name="block_forward",
    )(length, x, own, packed, small, branch_bias, gain, shift, *attended)


def block_backward_kernel(
    length_ref, d_ref, n1_ref, r1_ref, n2_ref, r2_ref, act_ref, slope_ref, own_ref, packed_ref, gain_ref,
    shift_ref, kl_ref, kl_row_ref, square_ref, six_own_ref, six_ref, first_ref, other_ref, *rest,
):
    step = pl.program_id(0)
    pack = rest[-1]
    shares = pack.shape[0]
    a_refs = [first_ref.at[0]] + [other_ref.at[s] for s in range(shares - 1)]
    sum_ref, da_refs = rest[0], rest[1 : shares + 1]
    g_ref, tail_ref, vec_ref, g_sum, low_s, branch_s, pre_s, mix_s = rest[shares + 1 : -1]
    tile, width = d_ref.shape
    units = D
    span = pl.ds(pl.multiple_of(step * tile, tile), tile)

    @pl.when(step == 0)
    def _():
        unpack_all(own_ref, packed_ref, pack)
        vec_ref[...] = jnp.zeros_like(vec_ref)
        g_sum[...] = jnp.zeros_like(g_sum)

    wide_ref, narrow_ref, out_ref = split_pack(pack)

    def column(value):
        return jnp.sum(value, axis=0, keepdims=True)

    row = lax.broadcasted_iota(jnp.int32, (8, width), 0)
    d_block = d_ref[...]
    normed_two = n2_ref[...]
    d_two = norm_backward(d_block, normed_two, r2_ref[...], gain_ref[1:2, :])
    d_branch = d_two.astype(bf16)
    branch_s[span, :] = d_branch
    normed_one = n1_ref[...]
    low = (normed_one * gain_ref[0:1, :] + shift_ref[0:1, :]).astype(bf16)
    low_s[span, :] = low
    d_middle = d_two
    for s in range(shares):
        grad = dot(d_branch, narrow_ref[s], NT) * slope_ref[:, s * units : (s + 1) * units].astype(f32)
        grad = grad.astype(bf16)
        pre_s[span, s * units : (s + 1) * units] = grad
        g_sum[s : s + 1, :] += column(grad.astype(f32))
        d_middle = d_middle + dot(grad, wide_ref[s], NT)
    d_one = norm_backward(d_middle, normed_one, r1_ref[...], gain_ref[0:1, :])
    sum_ref[...] = d_one
    d_mixing = d_one.astype(bf16)
    mix_s[span, :] = d_mixing
    for s in range(shares):
        da_refs[s][...] = wide_rows(dot(d_mixing, out_ref[s, :96, :], NT)).astype(bf16)
    parts = (
        d_mixing.astype(f32), d_branch.astype(f32), d_middle * normed_one, d_block * normed_two, d_middle, d_block,
    )
    total = jnp.zeros((8, width), f32)
    for index, part in enumerate(parts):
        total = jnp.where(row == index, column(part), total)
    vec_ref[...] += total

    @pl.when(step == pl.num_programs(0) - 1)
    def _():
        narrow = dot(act_ref[...], branch_s[...], TN).astype(bf16)
        wide = dot(low_s[...], pre_s[...], TN).astype(bf16)
        out = dot(jnp.concatenate([a[...] for a in a_refs], axis=1), mix_s[...], TN).astype(bf16)
        first = lax.broadcasted_iota(jnp.int32, (32, units), 0) == 0
        for s in range(shares):
            own = slice(s * width, (s + 1) * width)
            g_ref[0:units, own] = narrow[s * units : (s + 1) * units]
            g_ref[units : 2 * units, own] = wide[:, s * units : (s + 1) * units]
            g_ref[2 * units : 2 * units + 96, own] = out[s * 128 : s * 128 + 96]
            g_ref[2 * units + 128 :, own] = six_own_ref[0] if s == 0 else six_ref[s - 1]
            g_ref[2 * units + 96 : 2 * units + 128, own] = jnp.where(first, g_sum[s : s + 1, :], 0.0).astype(bf16)
        scalars = [jnp.sum(kl_ref[...], axis=0, keepdims=True) + jnp.sum(kl_row_ref[...], axis=1, keepdims=True)]
        scalars += [jnp.sum(square_ref[i : i + 1, :], axis=1, keepdims=True) for i in range(3)]
        scalars += [jnp.broadcast_to(own_number(length_ref).astype(f32), (1, 1))]
        lane = lanes((8, width))
        total = vec_ref[...]
        for index, value in enumerate(scalars):
            total = jnp.where((row == 6) & (lane == index), value, total)
        total = jnp.concatenate([jnp.zeros((2, width), f32), total, jnp.zeros((6, width), f32)], axis=0)
        high = total.astype(bf16).astype(f32)
        tail_ref[:16, :] = high.astype(bf16)
        tail_ref[16:, :] = (total - high).astype(bf16)


def block_backward(
    length, d_block, n1, r1, n2, r2, act, slope, attended, own, packed, gain, shift, divergence, squares, six_own, six,
):
    rows, width = d_block.shape
    tile = min(256, rows)
    shares, units = six.shape[0] + 1, D
    row, column = by_tile(tile, width), by_tile(tile, 1)
    return pl.pallas_call(
        block_backward_kernel,
        grid=(rows // tile,),
        in_specs=[
            SMEM, row, row, column, row, column, whole(act.shape), by_tile(tile, shares * units), whole(own.shape), whole(packed.shape), whole(gain.shape), whole(shift.shape),
            whole(divergence[0].shape), whole(divergence[1].shape), whole(squares.shape), whole(six_own.shape),
            whole(six.shape),
        ] + [whole(a.shape) for a in attended],
        out_specs=[
            row, *[by_tile(tile, 128)] * shares, whole((2 * units + 448, shares * width)), whole((32, width)),
        ],
        out_shape=[
            jax.ShapeDtypeStruct((rows, width), f32),
            *[jax.ShapeDtypeStruct((rows, 128), bf16)] * shares,
            jax.ShapeDtypeStruct((2 * units + 448, shares * width), bf16),
            jax.ShapeDtypeStruct((32, width), bf16),
        ],
        scratch_shapes=[
            pltpu.VMEM((8, width), f32),
            pltpu.VMEM((8, units), f32),
            pltpu.VMEM((rows, width), bf16),
            pltpu.VMEM((rows, width), bf16),
            pltpu.VMEM((rows, shares * units), bf16),
            pltpu.VMEM((rows, width), bf16),
            pltpu.VMEM((shares, 2 * D + 128, D), bf16),
        ],
        compiler_params=pltpu.CompilerParams(vmem_limit_bytes=VMEM),
        cost_estimate=cost(25),
        name="block_backward",
    )(
        length, d_block, n1, r1, n2, r2, act, slope, own, packed, gain, shift, *divergence, squares, six_own, six,
        *attended
    )


def after(value, *others):
    return lax.optimization_barrier((value,) + others)[0]


def shift_shares(value, by):
    shares = lax.axis_size("heads")
    return lax.ppermute(value, "heads", [((i + by) % shares, i) for i in range(shares)])


def exchange(value, bit):
    size = lax.axis_size("batch")
    return lax.ppermute(value, "batch", [(i, i ^ bit) for i in range(size)])


def rounded(total):
    end = total.shape[0] - 32
    sums = total[end : end + 16] + total[end + 16 :]
    high = lax.reduce_precision(sums, exponent_bits=8, mantissa_bits=7)
    return jnp.concatenate([total[:end], high, sums - high], axis=0).astype(bf16)


def finish_kernel(*refs, count):
    (
        rows_ref, grad_ref, bias_ref, branch_ref, gain_ref, shift_ref, summary_ref,
        narrow_ref, wide_ref, out_ref, wide_bias_ref, six_ref, six_bias_ref,
    ) = refs[count:]
    terms = [ref[...].astype(f32) for ref in refs[:count]]
    total = terms[0] + terms[1]
    if count == 4:
        total = total + (terms[2] + terms[3])
    end = total.shape[0] - 32
    sums = total[end : end + 16] + total[end + 16 :]
    grad_ref[...] = total[:end]
    bias_ref[...] = sums[0:2, :96]
    branch_ref[...] = sums[2:4]
    gain_ref[...] = sums[4:6]
    shift_ref[...] = sums[6:8]
    scalars = sums[8:9, :8]
    roots = jnp.sqrt(scalars / (scalars[:, 4:5] * D))
    summary_ref[...] = jnp.where(lanes((1, 8)) == 0, scalars, roots)[:, :4]
    units = narrow_ref.shape[0]
    narrow_ref[...] = rows_ref[:units, :].astype(f32)
    wide_ref[...] = rows_ref[units : 2 * units, :].astype(f32)
    out_ref[...] = rows_ref[2 * units : 2 * units + 96, :].astype(f32)
    wide_bias_ref[...] = rows_ref[2 * units + 96 : 2 * units + 112, :].astype(f32)[0]
    six = 2 * units + 128
    six_ref[...] = rows_ref[six : six + 288, :].astype(f32)
    sums = rows_ref[six + 288 : six + 304, :].astype(f32) + rows_ref[six + 304 :, :].astype(f32)
    six_bias_ref[...] = sums[0:2, :96]


def finish(terms, rows):
    width = rows.shape[1]
    shapes = [(288, width), (2, 96), (2, width), (2, width), (2, width), (1, 4)]
    shapes += [(D, width), (D, width), (96, width), (width,), (288, width), (2, 96)]
    return pl.pallas_call(
        functools.partial(finish_kernel, count=len(terms)),
        in_specs=[pl.BlockSpec(memory_space=pltpu.VMEM)] * (len(terms) + 1),
        out_shape=[jax.ShapeDtypeStruct(s, f32) for s in shapes], cost_estimate=cost(1),
        name="finish", compiler_params=pltpu.CompilerParams(vmem_limit_bytes=16 * 2**20),
    )(*terms, rows)


def body(
    student_rows, teacher_rows, valid_length, split_point, project_five, bias_five, output_five, branch_bias,
    norm_gain, norm_bias, widen_weight, widen_bias, narrow_weight, project_six, bias_six, teacher_project,
    teacher_bias,
):
    shares = lax.axis_size("heads")
    batch = lax.axis_size("batch")
    place = lax.axis_index("batch")
    all_rows = shares * batch * HEADS
    x = student_rows[0]
    teacher = teacher_rows[0]

    def turned(weight):
        return jnp.transpose(weight, (1, 2, 0)).reshape(-1, weight.shape[0])

    def placed(rows, at, count):
        return jnp.pad(rows, ((at, count - at - rows.shape[0]), (0, D - rows.shape[1])))

    biases = (bias_five, bias_six, widen_bias[None], teacher_bias)
    five = placed(turned(project_five), 0, 304)
    at = 288
    for bias in biases:
        five = five + placed(bias, at, 304)
        at += bias.shape[0]

    def part_of(rows):
        count = part_rows(rows.shape[0], batch)
        rows = jnp.pad(rows, ((0, count * batch - rows.shape[0]), (0, 0)))
        return lax.dynamic_slice_in_dim(rows, place * count, count)

    def others(rows):
        return [shift_shares(rows, by) for by in range(1, shares)]

    half = five.shape[0] // 2
    core = lax.rem(place, 2)
    mid = jnp.concatenate([widen_weight, narrow_weight, jnp.pad(output_five, ((0, 32), (0, 0)))], axis=0)
    taught = turned(teacher_project)
    rest = jnp.concatenate([turned(project_six), taught[:, :D], taught[:, D:]], axis=0)
    parts = others(jnp.concatenate([lax.dynamic_slice_in_dim(five, core * half, half), part_of(mid)], axis=0))

    first = attend_forward(valid_length, x, five[None])
    parts = jnp.stack([after(p, first[5]) for p in parts])
    halves, mid_parts = parts[:, :half], parts[:, half:]
    swapped = exchange(halves, 1)
    mid_all = lax.all_gather(mid_parts, "batch", axis=0)
    rest_parts = others(after(part_of(rest), mid_parts))
    low, high = jnp.where(core == 0, halves, swapped), jnp.where(core == 0, swapped, halves)
    fives = jnp.concatenate([low, high], axis=1)
    smalls = jnp.concatenate([five[None, 288:], fives[:, 288:]], axis=0)
    other = attend_forward(valid_length, after(x, mid_parts), fives)
    rest_parts = jnp.stack([after(p, other[5]) for p in rest_parts])
    rest_all = lax.all_gather(rest_parts, "batch", axis=0)
    attended = (first[5], other[5])
    block, n1, r1, n2, r2, act, slope, squares = block_forward(
        valid_length, after(x, rest_parts), attended, mid, mid_all, smalls, branch_bias, norm_gain, norm_bias
    )
    d_block, g_six_own, *divergence = relations(
        valid_length, split_point, block, teacher, rest, smalls[:1], all_rows
    )
    d_block, g_six, *divergence = relations(
        valid_length, split_point, block, teacher, rest_all, smalls[1:], all_rows, (d_block, *divergence)
    )
    result = block_backward(
        valid_length, d_block, n1, r1, n2, r2, act, slope, attended, mid, mid_all, norm_gain, norm_bias,
        divergence, squares, g_six_own, g_six,
    )
    d_sum_one, d_attended, (g_both, tail) = result[0], result[1 : 1 + shares], result[1 + shares :]

    def to_owner(parts):
        return [parts[0]] + [shift_shares(parts[by], shares - by) for by in range(1, shares)]

    units = widen_weight.shape[1]
    both = lax.psum_scatter(g_both, "batch", scatter_dimension=0, tiled=True)

    grad_in = d_sum_one
    g_five = [None] * shares
    for s in list(range(1, shares)) + [0]:
        q, k, v, e, r, a = other if s else first
        rows, w = after(x, *g_five[1 : shares - 1]) if s == 0 else x, fives if s else five[None]
        grad, grad_in = attend_backward(max(s - 1, 0), q, k, v, e, r, a, d_attended[s], rows, w, grad_in, tail)
        g_five[s] = shift_shares(grad, shares - s) if s else grad

    g_five = [g.astype(f32) for g in g_five]
    five_sum = rounded((g_five[0] + g_five[1]) + functools.reduce(jnp.add, g_five[2:]))
    both = after(both, five_sum)
    five_sum = after(five_sum, both)
    both = to_owner([both[:, s * D : (s + 1) * D] for s in range(shares)])
    bits = [1 << i for i in range(batch.bit_length() - 1)]
    groups = [bits[:1]] + [bits[i : i + 2] for i in range(1, len(bits), 2)]
    for index, group in enumerate(groups):
        received = [exchange(five_sum, bit) for bit in group]
        if len(group) == 2:
            received.append(exchange(five_sum, group[0] + group[1]))
        if index == 1:
            both = [after(p, five_sum) for p in both]
            both = sum(p.astype(f32) for p in both).astype(bf16)
        if index == len(groups) - 1:
            both = lax.all_gather(after(both, five_sum), "batch", axis=0, tiled=True)
            five_sum = after(five_sum, both)
        if index == len(groups) - 1:
            break
        total = five_sum.astype(f32) + received[0].astype(f32)
        if len(group) == 2:
            total = total + (received[1].astype(f32) + received[2].astype(f32))
        five_sum = rounded(total)
    (
        grad_five, five_bias, branch, gain, shift, summary, grad_narrow, grad_wide, grad_out, wide_bias, grad_six,
        six_bias,
    ) = finish([five_sum] + received, both)

    def unturned(grad):
        return jnp.transpose(grad.reshape(3, -1, grad.shape[1]), (2, 0, 1))

    return (
        block[None], grad_in[None], unturned(grad_five), five_bias, grad_out, branch, gain, shift,
        grad_wide, wide_bias, grad_narrow, unturned(grad_six), six_bias, summary.reshape(-1),
    )


def solution(mesh):
    return jax.shard_map(
        body,
        mesh=mesh,
        in_specs=(
            P(("batch", "heads"), None, None),
            P(("batch", "heads"), None, None),
            P("batch"),
            P("batch"),
            P(None, None, "heads"),
            P(None, "heads"),
            P("heads", None),
            P(),
            P(),
            P(),
            P(None, "heads"),
            P("heads"),
            P("heads", None),
            P(None, None, "heads"),
            P(None, "heads"),
            P(None, None, "heads"),
            P(None, "heads"),
        ),
        out_specs=(
            P(("batch", "heads"), None, None),
            P(("batch", "heads"), None, None),
            P(None, None, "heads"),
            P(None, "heads"),
            P("heads", None),
            P(),
            P(),
            P(),
            P(None, "heads"),
            P("heads"),
            P("heads", None),
            P(None, None, "heads"),
            P(None, "heads"),
            P(),
        ),
        check_vma=False,
    )
```
